32 devices in a mesh: runs: 2 (over x), gx: 16 (over z, y, core).
Axes of the slice: x: 2, y: 2, z: 4, core: 2. Of those that a mesh axis runs over, the one named last changes fastest.
Arguments:
- frac: float32 [3, 524288], P(None, ('runs', 'gx')), parts along dimension 1, may hold values from 0 to 1
- velocity: float32 [3, 524288], P(None, ('runs', 'gx')), parts along dimension 1, may hold values from -6 to 6
- mass: float32 [524288], P(('runs', 'gx')), parts along dimension 0, may hold values from 0.5 to 2
- particle_cell: int32 [524288], P(('runs', 'gx')), parts along dimension 0, may hold values from 0 to 8191, as said below
- tile_count: int32 [32], P(('runs', 'gx')), parts along dimension 0, may hold values from 2048 to 16384, as said below
- time_step: float32 [2], P('runs'), parts along dimension 0, may hold values from 0.1 to 0.2
Outputs:
- new_frac: float32 [3, 524288], P(None, ('runs', 'gx')), parts along dimension 1
- new_velocity: float32 [3, 524288], P(None, ('runs', 'gx')), parts along dimension 1
- next_step: float32 [2], P('runs'), parts along dimension 0
The draws below stay inside these ranges and needn't reach their ends.
There are 2 independent parts, one for each index of `runs`. The reference program is written for one: setup_inputs(seed, part) draws one part's arguments, and reference() takes and returns one part's arrays. A program takes and returns all parts, laid end to end along the dimension named above; each array names one. Nothing has to cross between parts.
Inputs may be any that keep to these rules, and one draw needn't show every extreme that they name: `particle_cell`: within each tile the slots' cell numbers never fall; live slots come first and lie in cells with z <= 126; empty slots name the tile's last cell. `tile_count`: some tile is full in every run.
All inputs are finite; a program needn't handle non-finite values.
Results may differ from the reference program's by a relative error of at most 0.0003.
Values sent between devices are 32-bit elements; how exact they have to be, the bound alone decides.
No kernel may reach another device: no remote copies, remote signals or barrier semaphores. Data moves between devices by JAX's collectives and lax.ppermute only.
A program may use at most 64 MiB of HBM per device.

```python
import math
import jax
import jax.numpy as jnp
from jax import lax

CX = 2
NY = 32
NZ = 128
NP_DEV = 16384
NX = 32
NP = 262144
N_GX = 16


def tile_counts_from(key):
    first, second = jax.random.split(key)
    drawn = jax.random.randint(first, (N_GX,), 0, 1024)
    spread = drawn * drawn // 1024 * (NP_DEV - NP_DEV // 8) // 1024
    counts = NP_DEV // 8 + spread
    fullest = jax.random.randint(second, (), 0, N_GX)
    return jnp.where(jnp.arange(N_GX) == fullest, NP_DEV, counts).astype(jnp.int32)


def draw_tile_count(key, part):
    return tile_counts_from(key)


def draw_particle_cell(key, part):
    counts = tile_counts_from(key)
    key = jax.random.fold_in(key, 5)
    key_x, key_y, key_z, key_pick, key_share, key_centre = jax.random.split(key, 6)
    shape = (N_GX, NP_DEV)
    along = jax.random.randint(key_x, shape, 0, CX)
    across = jax.random.randint(key_y, shape, 0, NY)
    upward = jax.random.randint(key_z, shape, 0, NZ - 1)
    scattered = (along * NY + across) * NZ + upward
    centre_x, centre_y, centre_z = jax.random.split(key_centre, 3)
    clusters = 4
    near_x = jax.random.randint(centre_x, (N_GX, clusters), 0, CX)
    near_y = jax.random.randint(centre_y, (N_GX, clusters), 0, NY)
    near_z = jax.random.randint(centre_z, (N_GX, clusters), 1, NZ - 2)
    centres = (near_x * NY + near_y) * NZ + near_z
    pick = jax.random.randint(key_pick, shape, 0, clusters)
    which = jnp.arange(clusters, dtype=jnp.int32)[None, None, :]
    chosen = jnp.sum(jnp.where(pick[:, :, None] == which, centres[:, None, :], 0), axis=2)
    into = jax.random.randint(key_share, shape, 0, 4) < 3
    local = jnp.where(into, chosen, scattered)
    slots = jnp.arange(NP_DEV, dtype=jnp.int32)[None, :]
    local = jnp.where(slots < counts[:, None], local, CX * NY * NZ - 1)
    local = jnp.sort(local, axis=1)
    return local.reshape(-1).astype(jnp.int32)


def shard_levels(key, shape, cuts, smallest, high):
    def one(axis_at, parts):
        steps = jax.random.uniform(jax.random.fold_in(jax.random.fold_in(key, 6), axis_at), (parts,), jnp.float32, smallest / len(cuts), high / len(cuts))
        return jnp.repeat(jnp.exp(steps), shape[axis_at] // parts).reshape((-1,) + (1,) * (len(shape) - axis_at - 1))

    level = one(*cuts[0])
    for cut in cuts[1:]:
        level = level * one(*cut)
    return level


def normal_values(key, dims, scale, limit, cuts=(), kind=jnp.bfloat16):
    values = scale * jax.random.normal(key, dims, jnp.float32)
    if cuts:
        values = values * shard_levels(key, dims, cuts, -0.22, 0.18)
    return jnp.clip(values, -limit, limit).astype(kind)


def setup_inputs(seed: int = 0, part: int = 0) -> dict:
    key_list = jax.random.split(jax.random.key(seed), 7)
    part_keys = jax.random.split(jax.random.fold_in(key_list[6], part), 7)
    return {
        "frac": jnp.clip(1.0 * jax.random.uniform(part_keys[0], (3, NP), jnp.float32) ** shard_levels(part_keys[0], (3, NP), ((1, 16),), -0.2, 0.2), 0.0, 1.0),
        "velocity": normal_values(part_keys[1], (3, NP), 1.0, 6.0, ((1, 16),), jnp.float32),
        "mass": jnp.clip(jnp.exp(math.log(2.0) - 1.3862944 * jax.random.uniform(part_keys[2], (NP,), jnp.float32) ** shard_levels(part_keys[2], (NP,), ((0, 16),), -0.2, 0.2)), 0.5, 2.0),
        "particle_cell": draw_particle_cell(jax.random.fold_in(jax.random.fold_in(key_list[6], part), 71), part),
        "tile_count": draw_tile_count(jax.random.fold_in(jax.random.fold_in(key_list[6], part), 71), part),
        "time_step": jnp.clip(jax.random.uniform(part_keys[5], (1,), jnp.float32, 0.1, 0.2), 0.1, 0.2),
    }


mass_floor = 0.25
stiffness = 2.0
press_floor = 1.0
grain_size = 0.5
inertia_ref = 0.3
mu_static = 0.38
mu_limit = 0.64
rate_floor = 0.5
gravity_x = 0.5
gravity_z = -0.866
flip_share = 0.95
courant = 0.4
wave_speed = 2.0
components = ((0, 3, 4), (3, 1, 5), (4, 5, 2))

def pair_up(field, axis):
    return field + jnp.roll(field, -1, axis)

def step_up(field, axis):
    return jnp.roll(field, -1, axis) - field

def pair_down(field, axis):
    return field + jnp.roll(field, 1, axis)

def step_down(field, axis):
    return field - jnp.roll(field, 1, axis)

def cell_gradient(field, direction):
    if direction == 0:
        grad = pair_up(pair_up(step_up(field, 0), 1), 2)
    elif direction == 1:
        grad = pair_up(step_up(pair_up(field, 0), 1), 2)
    else:
        grad = step_up(pair_up(pair_up(field, 0), 1), 2)
    return 0.25 * grad

def node_divergence(stress, direction):
    if direction == 0:
        result = step_down(pair_down(pair_down(stress, 1), 2), 0)
    elif direction == 1:
        result = step_down(pair_down(pair_down(stress, 0), 2), 1)
    else:
        result = step_down(pair_down(pair_down(stress, 0), 1), 2)
    return 0.25 * result

def stresses(grads, density, keep):
    dxx = grads[0][0]
    dyy = grads[1][1]
    dzz = grads[2][2]
    dxy = 0.5 * (grads[0][1] + grads[1][0])
    dxz = 0.5 * (grads[0][2] + grads[2][0])
    dyz = 0.5 * (grads[1][2] + grads[2][1])
    second = dxx * dxx + dyy * dyy + dzz * dzz + 2.0 * (dxy * dxy + dxz * dxz + dyz * dyz)
    rate = jnp.sqrt(2.0 * second + rate_floor * rate_floor)
    pressure = stiffness * density
    inertial = rate * grain_size / jnp.sqrt(pressure + press_floor)
    friction = mu_static + (mu_limit - mu_static) * inertial / (inertia_ref + inertial)
    twice = 2.0 * friction * pressure / rate
    sigma = jnp.stack([twice * dxx - pressure, twice * dyy - pressure, twice * dzz - pressure, twice * dxy, twice * dxz, twice * dyz])
    return jnp.where(keep, sigma, 0.0)

def corners(frac, cell_i, cell_j, cell_k, xsize):
    listed = []
    for a in range(2):
        wx = frac[0] if a else 1.0 - frac[0]
        for b in range(2):
            wy = frac[1] if b else 1.0 - frac[1]
            for c in range(2):
                wz = frac[2] if c else 1.0 - frac[2]
                index = ((cell_i + a) % xsize * NY + (cell_j + b) % NY) * NZ + (cell_k + c) % NZ
                listed.append((wx * wy * wz, index.astype(jnp.int32)))
    return listed

def reference(frac, velocity, mass, particle_cell, tile_count, time_step):
    step = time_step[0]
    total = NP_DEV * N_GX
    slots = jnp.arange(total, dtype=jnp.int32)
    tiles = (slots // NP_DEV).astype(jnp.int32)
    live = slots % NP_DEV < tile_count[tiles]
    cell_i = (tiles * CX + particle_cell // (NY * NZ)).astype(jnp.int32)
    cell_j = particle_cell // NZ % NY
    cell_k = particle_cell % NZ
    listed = corners(frac, cell_i, cell_j, cell_k, NX)
    held = jnp.where(live, mass, 0.0)
    carried = jnp.stack([held, held * velocity[0], held * velocity[1], held * velocity[2]])
    grid = jnp.zeros((4, NX * NY * NZ), jnp.float32)
    for weight, index in listed:
        grid = grid.at[:, index].add(carried * weight)
    grid = grid.reshape(4, NX, NY, NZ)
    node_mass = grid[0]
    momentum = grid[1:]
    v_old = momentum / jnp.maximum(node_mass, mass_floor)
    grads = [[cell_gradient(v_old[a], b) for b in range(3)] for a in range(3)]
    density = 0.125 * pair_up(pair_up(pair_up(node_mass, 0), 1), 2)
    keep = lax.broadcasted_iota(jnp.int32, (NX, NY, NZ), 2) < NZ - 1
    sigma = stresses(grads, density, keep)
    force = jnp.stack([node_divergence(sigma[components[a][0]], 0) + node_divergence(sigma[components[a][1]], 1) + node_divergence(sigma[components[a][2]], 2) for a in range(3)])
    gravity = jnp.array([gravity_x, 0.0, gravity_z], jnp.float32)[:, None, None, None]
    v_new = (momentum + step * (force + node_mass[None] * gravity)) / jnp.maximum(node_mass, mass_floor)
    above_bed = lax.broadcasted_iota(jnp.int32, (NX, NY, NZ), 2) > 0
    v_new = jnp.where(above_bed, v_new, 0.0)
    table = jnp.concatenate([v_new, v_new - v_old]).reshape(6, NX * NY * NZ)
    picked = jnp.zeros((6, total), jnp.float32)
    for weight, index in listed:
        picked = picked + weight * jnp.take(table, index, axis=1)
    moved = picked[:3]
    change = picked[3:]
    new_velocity = jnp.where(live, flip_share * (velocity + change) + (1.0 - flip_share) * moved, 0.0)
    new_frac = jnp.where(live, frac + step * moved, 0.0)
    speed = jnp.sqrt(lax.optimization_barrier(jnp.sum(new_velocity * new_velocity, axis=0)))
    top = jnp.max(jnp.where(live, speed, 0.0))
    next_step = (courant / (top + wave_speed)).reshape(1).astype(jnp.float32)
    return (new_frac, new_velocity, next_step)
```

```python
import functools

import jax
import jax.numpy as jnp
from jax import lax
from jax.experimental import pallas as pl
from jax.experimental.pallas import tpu as pltpu
from jax.sharding import PartitionSpec as P

CX = 2
NY = 32
NZ = 128
ROWS = CX * NY
BLOCK = 256
UNROLL = 8
SPREAD = 32
TABLE = 64

mass_floor = 0.25
stiffness = 2.0
press_floor = 1.0
grain_size = 0.5
inertia_ref = 0.3
mu_static = 0.38
mu_limit = 0.64
rate_floor = 0.5
gravity = (0.5, 0.0, -0.866)
flip_share = 0.95
courant = 0.4
wave_speed = 2.0
components = ((0, 3, 4), (3, 1, 5), (4, 5, 2))
f32 = jnp.float32
bf16 = jnp.bfloat16


def shifted(array, axis, by):
    devices = lax.axis_size(axis)
    return lax.ppermute(array, axis, [(i, (i + by) % devices) for i in range(devices)])


def visit_list(particle_cell, count):
    slots = particle_cell.shape[0]
    blocks = slots // BLOCK
    size = blocks + ROWS
    number = jnp.arange(blocks, dtype=jnp.int32)
    cells = particle_cell.reshape(blocks, BLOCK)
    live = jnp.arange(slots, dtype=jnp.int32).reshape(blocks, BLOCK) < count
    first = cells[:, 0] // NZ
    last = jnp.max(jnp.where(live, cells, 0), axis=1) // NZ
    visits = jnp.where(number * BLOCK < count, last - first + 1, 0)
    before = number[:, None] < number[None, :]
    starts = jnp.sum(jnp.where(before, visits[:, None], 0), axis=0)
    total = jnp.sum(visits)
    order = jnp.arange(size, dtype=jnp.int32)
    inside = (starts[None, :] <= order[:, None]) & (order[:, None] < (starts + visits)[None, :])
    block = jnp.sum(jnp.where(inside, number[None, :], 0), axis=1)
    row = jnp.sum(jnp.where(inside, (first - starts)[None, :], 0), axis=1) + order
    row = jnp.where(order < total, row, ROWS)
    return block, row, total.reshape(1)


def split_pair(values):
    high = values.astype(bf16)
    low = (values - high.astype(f32)).astype(bf16)
    return high, low


def one_hot(cells_ref, block, row):
    rel = cells_ref[pl.ds(block * 2, 2), :] - row * NZ
    nodes = lax.broadcasted_iota(jnp.int32, (NZ, 128), 0)
    halves = [jnp.where(nodes == rel[h : h + 1, :], 1.0, 0.0) for h in range(2)]
    return jnp.concatenate(halves, axis=1).astype(bf16)


def pair_lines(ref, block):
    both = ref[pl.ds(block * 2, 2), :]
    return jnp.concatenate([both[0:1, :], both[1:2, :]], axis=1)


def spread_kernel(
    count_ref, block_ref, row_ref, total_ref, frac_ref, vel_ref, mass_ref, cells_ref,
    low_ref, high_ref, q_ref, acc_ref,
):
    blocks = frac_ref.shape[1] // BLOCK
    count = count_ref[0]
    acc_ref[...] = jnp.zeros_like(acc_ref)
    corner = lax.broadcasted_iota(jnp.int32, (8, BLOCK), 0)
    upper = [(corner // part) % 2 == 1 for part in (4, 2, 1)]
    lane = lax.broadcasted_iota(jnp.int32, (1, BLOCK), 1)

    def prepare(block, carry):
        at = pl.multiple_of(block * BLOCK, BLOCK)
        frac = frac_ref[:, pl.ds(at, BLOCK)]
        vel = vel_ref[:, pl.ds(at, BLOCK)]
        mass = pair_lines(mass_ref, block)
        held = jnp.where(at + lane < count, mass, 0.0)
        parts = [
            jnp.where(upper[d], frac[d : d + 1, :], 1.0 - frac[d : d + 1, :]) for d in range(3)
        ]
        weight = parts[0] * parts[1] * parts[2] * held
        carried = jnp.concatenate([weight] + [weight * vel[a : a + 1, :] for a in range(3)], axis=0)
        high, low = split_pair(carried)
        q_ref[pl.ds(block, 1)] = jnp.concatenate([high, low], axis=0)[None]
        return carry

    lax.fori_loop(0, blocks, prepare, 0, unroll=4)

    def visit(group, carry):
        found = []
        for u in range(UNROLL):
            v = group * UNROLL + u
            block = block_ref[v]
            row = row_ref[v]
            hot = one_hot(cells_ref, block, row)
            both = lax.dot_general(
                q_ref[pl.ds(block, 1)][0], hot, (((1,), (1,)), ((), ())), preferred_element_type=f32
            )
            found.append((row, both[:SPREAD] + both[SPREAD:]))
        for row, part in found:
            at = pl.ds(pl.multiple_of(row * SPREAD, SPREAD), SPREAD)
            acc_ref[at, :] += part
        return carry

    lax.fori_loop(0, (total_ref[0] + UNROLL - 1) // UNROLL, visit, 0)

    for field in range(4):
        layers = [None] * 3
        for i in range(CX):
            for a in range(2):
                summed = None
                for b in range(2):
                    line = None
                    for c in range(2):
                        start = i * NY * SPREAD + field * 8 + a * 4 + b * 2 + c
                        got = acc_ref[pl.ds(start, NY, stride=SPREAD), :]
                        line = got if c == 0 else line + pltpu.roll(got, 1, 1)
                    summed = line if b == 0 else summed + pltpu.roll(line, 1, 0)
                there = layers[i + a]
                layers[i + a] = summed if there is None else there + summed
        for l in range(2):
            low_ref[field * 2 + l] = layers[l]
            high_ref[field * 2 + l] = layers[l + 1]


def pair_up(field, axis):
    return field + pltpu.roll(field, field.shape[axis] - 1, axis)


def step_up(field, axis):
    return pltpu.roll(field, field.shape[axis] - 1, axis) - field


def pair_down(field, axis):
    return field + pltpu.roll(field, 1, axis)


def step_down(field, axis):
    return field - pltpu.roll(field, 1, axis)


def cell_stress(vel_lo, vel_hi, mass_lo, mass_hi, keep):
    grads = []
    for a in range(3):
        diff = vel_hi[a] - vel_lo[a]
        both = vel_hi[a] + vel_lo[a]
        grads.append(
            [
                0.25 * pair_up(pair_up(diff, 0), 1),
                0.25 * pair_up(step_up(both, 0), 1),
                0.25 * step_up(pair_up(both, 0), 1),
            ]
        )
    density = 0.125 * pair_up(pair_up(mass_hi + mass_lo, 0), 1)
    dxx = grads[0][0]
    dyy = grads[1][1]
    dzz = grads[2][2]
    dxy = 0.5 * (grads[0][1] + grads[1][0])
    dxz = 0.5 * (grads[0][2] + grads[2][0])
    dyz = 0.5 * (grads[1][2] + grads[2][1])
    second = dxx * dxx + dyy * dyy + dzz * dzz + 2.0 * (dxy * dxy + dxz * dxz + dyz * dyz)
    rate = jnp.sqrt(2.0 * second + rate_floor * rate_floor)
    pressure = stiffness * density
    inertial = rate * grain_size / jnp.sqrt(pressure + press_floor)
    friction = mu_static + (mu_limit - mu_static) * inertial / (inertia_ref + inertial)
    twice = 2.0 * friction * pressure / rate
    sigma = [
        twice * dxx - pressure,
        twice * dyy - pressure,
        twice * dzz - pressure,
        twice * dxy,
        twice * dxz,
        twice * dyz,
    ]
    return [jnp.where(keep, s, 0.0) for s in sigma]


def node_force(lower, upper):
    force = []
    for a in range(3):
        sx, sy, sz = (components[a][b] for b in range(3))
        along = pair_down(pair_down(upper[sx] - lower[sx], 0), 1)
        across = step_down(pair_down(upper[sy] + lower[sy], 1), 0)
        upward = step_down(pair_down(upper[sz] + lower[sz], 0), 1)
        force.append(0.25 * (along + across + upward))
    return force


def collect_kernel(
    count_ref, block_ref, row_ref, total_ref, step_ref,
    low_ref, high_ref, left_ref, right_ref, frac_ref, vel_ref, cells_ref,
    new_frac_ref, new_vel_ref, top_ref, tab_ref, out_ref,
):
    blocks = frac_ref.shape[1] // BLOCK
    count = count_ref[0]
    step = step_ref[0]
    nodes = [
        [left_ref[f * 2] for f in range(4)],
        [low_ref[f * 2] + left_ref[f * 2 + 1] for f in range(4)],
        [low_ref[f * 2 + 1] for f in range(4)],
        [high_ref[f * 2 + 1] + right_ref[f * 2] for f in range(4)],
        [right_ref[f * 2 + 1] for f in range(4)],
    ]
    height = lax.broadcasted_iota(jnp.int32, (NY, NZ), 1)
    keep = height < NZ - 1
    above_bed = height > 0
    floor = [jnp.maximum(layer[0], mass_floor) for layer in nodes]
    v_old = [[layer[1 + a] / floor[l] for a in range(3)] for l, layer in enumerate(nodes)]
    sigma = [
        cell_stress(v_old[l], v_old[l + 1], nodes[l][0], nodes[l + 1][0], keep) for l in range(4)
    ]
    tab_ref[...] = jnp.zeros_like(tab_ref)
    for l in range(1, 4):
        force = node_force(sigma[l - 1], sigma[l])
        for a in range(3):
            fresh = (
                nodes[l][1 + a] + step * (force[a] + nodes[l][0] * gravity[a])
            ) / floor[l]
            fresh = jnp.where(above_bed, fresh, 0.0)
            for field, value in ((a, fresh - flip_share * v_old[l][a]), (4 + a, step * fresh)):
                for b in range(2):
                    line = value if b == 0 else pltpu.roll(value, NY - 1, 0)
                    for c in range(2):
                        put = line if c == 0 else pltpu.roll(line, NZ - 1, 1)
                        for i in range(CX):
                            corner_a = l - 1 - i
                            if corner_a not in (0, 1):
                                continue
                            corner = corner_a * 4 + b * 2 + c
                            start = i * NY * TABLE + corner * 8 + field
                            tab_ref[pl.ds(start, NY, stride=TABLE), :] = put

    out_ref[...] = jnp.zeros_like(out_ref)

    def visit(group, carry):
        found = []
        for u in range(UNROLL):
            v = group * UNROLL + u
            block = block_ref[v]
            row = row_ref[v]
            hot = one_hot(cells_ref, block, row)
            at = pl.ds(pl.multiple_of(jnp.minimum(row, ROWS - 1) * TABLE, TABLE), TABLE)
            high, low = split_pair(tab_ref[at, :])
            both = jnp.dot(jnp.concatenate([high, low], axis=0), hot, preferred_element_type=f32)
            value = both[:TABLE] + both[TABLE:]
            frac = frac_ref[:, pl.ds(pl.multiple_of(block * BLOCK, BLOCK), BLOCK)]
            corners = [value[8 * k : 8 * k + 8] for k in range(8)]
            for d in (2, 1, 0):
                share = frac[d : d + 1, :]
                corners = [
                    corners[k] + share * (corners[k + 1] - corners[k])
                    for k in range(0, len(corners), 2)
                ]
            found.append((block, corners[0]))
        for block, part in found:
            out_ref[pl.ds(block, 1)] += part[None]
        return carry

    lax.fori_loop(0, (total_ref[0] + UNROLL - 1) // UNROLL, visit, 0)

    lane = lax.broadcasted_iota(jnp.int32, (1, BLOCK), 1)

    def finish(block, top):
        at = pl.multiple_of(block * BLOCK, BLOCK)
        alive = at + lane < count
        got = out_ref[pl.ds(block, 1)][0]
        fresh = jnp.where(alive, flip_share * vel_ref[:, pl.ds(at, BLOCK)] + got[0:3], 0.0)
        new_vel_ref[:, pl.ds(at, BLOCK)] = fresh
        placed = jnp.where(alive, frac_ref[:, pl.ds(at, BLOCK)] + got[4:7], 0.0)
        new_frac_ref[:, pl.ds(at, BLOCK)] = placed
        square = fresh[0:1] * fresh[0:1] + fresh[1:2] * fresh[1:2] + fresh[2:3] * fresh[2:3]
        return jnp.maximum(top, square)

    top = lax.fori_loop(0, blocks, finish, jnp.zeros((1, BLOCK), f32), unroll=4)
    top = jnp.sqrt(jnp.max(top, axis=1, keepdims=True))
    top_ref[...] = jnp.broadcast_to(top, top_ref.shape)


def largest(value, axis):
    devices = lax.axis_size(axis)
    reach = 1
    while reach < devices:
        if devices & (devices - 1) == 0:
            pairs = [(i, i ^ reach) for i in range(devices)]
        else:
            pairs = [(i, (i + reach) % devices) for i in range(devices)]
        value = jnp.maximum(value, lax.ppermute(value, axis, pairs))
        reach *= 2
    return value


smem = pl.BlockSpec(memory_space=pltpu.SMEM)
vmem = pl.BlockSpec(memory_space=pltpu.VMEM)


def body(frac, velocity, mass, particle_cell, tile_count, time_step):
    slots = frac.shape[1]
    blocks = slots // BLOCK
    count = tile_count[0]
    block, row, total = visit_list(particle_cell, count)
    mass_rows = mass.reshape(slots // 128, 128)
    cell_rows = particle_cell.reshape(slots // 128, 128)
    layer_pair = jax.ShapeDtypeStruct((8, NY, NZ), f32)
    low, high = pl.pallas_call(
        spread_kernel,
        out_shape=(layer_pair, layer_pair),
        in_specs=[smem] * 4 + [vmem] * 4,
        out_specs=(vmem, vmem),
        scratch_shapes=[
            pltpu.VMEM((blocks, 2 * SPREAD, BLOCK), bf16),
            pltpu.VMEM(((ROWS + 1) * SPREAD, NZ), f32),
        ],
        compiler_params=pltpu.CompilerParams(vmem_limit_bytes=32 * 1024 * 1024),
        name="spread",
    )(tile_count, block, row, total, frac, velocity, mass_rows, cell_rows)
    from_left = shifted(high, "gx", 1)
    from_right = shifted(low, "gx", -1)
    new_frac, new_velocity, top = pl.pallas_call(
        collect_kernel,
        out_shape=(
            jax.ShapeDtypeStruct(frac.shape, f32),
            jax.ShapeDtypeStruct(velocity.shape, f32),
            jax.ShapeDtypeStruct((8, 128), f32),
        ),
        in_specs=[smem] * 5 + [vmem] * 7,
        out_specs=(vmem, vmem, vmem),
        scratch_shapes=[
            pltpu.VMEM((ROWS * TABLE, NZ), f32),
            pltpu.VMEM((blocks, 8, BLOCK), f32),
        ],
        compiler_params=pltpu.CompilerParams(vmem_limit_bytes=32 * 1024 * 1024),
        name="collect",
    )(
        tile_count, block, row, total, time_step,
        low, high, from_left, from_right, frac, velocity, cell_rows,
    )
    fastest = largest(top[0, :1], "gx")
    next_step = courant / (fastest + wave_speed)
    return (new_frac, new_velocity, next_step)


def solution(mesh):
    placed = (
        P(None, ("runs", "gx")),
        P(None, ("runs", "gx")),
        P(("runs", "gx")),
        P(("runs", "gx")),
        P(("runs", "gx")),
        P("runs"),
    )
    return jax.shard_map(
        body,
        mesh=mesh,
        in_specs=placed,
        out_specs=(P(None, ("runs", "gx")), P(None, ("runs", "gx")), P("runs")),
        check_vma=False,
    )
```

```python
import functools

import jax
import jax.numpy as jnp
from jax import lax
from jax.experimental import pallas as pl
from jax.experimental.pallas import tpu as pltpu
from jax.sharding import PartitionSpec as P

CX = 2
NY = 32
NZ = 128
ROWS = CX * NY
BLOCK = 256
UNROLL = 8
SPREAD = 32
TABLE = 64

mass_floor = 0.25
stiffness = 2.0
press_floor = 1.0
grain_size = 0.5
inertia_ref = 0.3
mu_static = 0.38
mu_limit = 0.64
rate_floor = 0.5
gravity = (0.5, 0.0, -0.866)
flip_share = 0.95
courant = 0.4
wave_speed = 2.0
components = ((0, 3, 4), (3, 1, 5), (4, 5, 2))
f32 = jnp.float32
bf16 = jnp.bfloat16


def shifted(array, axis, by):
    devices = lax.axis_size(axis)
    return lax.ppermute(array, axis, [(i, (i + by) % devices) for i in range(devices)])


def visit_list(particle_cell, count):
    slots = particle_cell.shape[0]
    blocks = slots // BLOCK
    size = blocks + ROWS
    number = jnp.arange(blocks, dtype=jnp.int32)
    cells = particle_cell.reshape(blocks, BLOCK)
    live = jnp.arange(slots, dtype=jnp.int32).reshape(blocks, BLOCK) < count
    first = cells[:, 0] // NZ
    last = jnp.max(jnp.where(live, cells, 0), axis=1) // NZ
    visits = jnp.where(number * BLOCK < count, last - first + 1, 0)
    before = number[:, None] < number[None, :]
    starts = jnp.sum(jnp.where(before, visits[:, None], 0), axis=0)
    total = jnp.sum(visits)
    order = jnp.arange(size, dtype=jnp.int32)
    inside = (starts[None, :] <= order[:, None]) & (order[:, None] < (starts + visits)[None, :])
    block = jnp.sum(jnp.where(inside, number[None, :], 0), axis=1)
    row = jnp.sum(jnp.where(inside, (first - starts)[None, :], 0), axis=1) + order
    row = jnp.where(order < total, row, ROWS)
    return block, row, total.reshape(1)


def split_pair(values):
    high = values.astype(bf16)
    low = (values - high.astype(f32)).astype(bf16)
    return high, low


def one_hot(cells_ref, block, row):
    rel = cells_ref[pl.ds(block * 2, 2), :] - row * NZ
    nodes = lax.broadcasted_iota(jnp.int32, (NZ, 128), 0)
    halves = [jnp.where(nodes == rel[h : h + 1, :], 1.0, 0.0) for h in range(2)]
    return jnp.concatenate(halves, axis=1).astype(bf16)


def pair_lines(ref, block):
    both = ref[pl.ds(block * 2, 2), :]
    return jnp.concatenate([both[0:1, :], both[1:2, :]], axis=1)


def spread_kernel(
    count_ref, block_ref, row_ref, total_ref, frac_ref, vel_ref, mass_ref, cells_ref,
    low_ref, high_ref, q_ref, acc_ref,
):
    blocks = frac_ref.shape[1] // BLOCK
    count = count_ref[0]
    acc_ref[...] = jnp.zeros_like(acc_ref)
    corner = lax.broadcasted_iota(jnp.int32, (8, BLOCK), 0)
    upper = [(corner // part) % 2 == 1 for part in (4, 2, 1)]
    lane = lax.broadcasted_iota(jnp.int32, (1, BLOCK), 1)

    def prepare(block, carry):
        at = pl.multiple_of(block * BLOCK, BLOCK)
        frac = frac_ref[:, pl.ds(at, BLOCK)]
        vel = vel_ref[:, pl.ds(at, BLOCK)]
        mass = pair_lines(mass_ref, block)
        held = jnp.where(at + lane < count, mass, 0.0)
        parts = [
            jnp.where(upper[d], frac[d : d + 1, :], 1.0 - frac[d : d + 1, :]) for d in range(3)
        ]
        weight = parts[0] * parts[1] * parts[2] * held
        carried = jnp.concatenate([weight] + [weight * vel[a : a + 1, :] for a in range(3)], axis=0)
        high, low = split_pair(carried)
        q_ref[pl.ds(block, 1)] = jnp.concatenate([high, low], axis=0)[None]
        return carry

    lax.fori_loop(0, blocks, prepare, 0, unroll=4)

    def visit(group, carry):
        found = []
        for u in range(UNROLL):
            v = group * UNROLL + u
            block = block_ref[v]
            row = row_ref[v]
            hot = one_hot(cells_ref, block, row)
            both = lax.dot_general(
                q_ref[pl.ds(block, 1)][0], hot, (((1,), (1,)), ((), ())), preferred_element_type=f32
            )
            found.append((row, both[:SPREAD] + both[SPREAD:]))
        for row, part in found:
            at = pl.ds(pl.multiple_of(row * SPREAD, SPREAD), SPREAD)
            acc_ref[at, :] += part
        return carry

    lax.fori_loop(0, (total_ref[0] + UNROLL - 1) // UNROLL, visit, 0)

    for field in range(4):
        layers = [None] * 3
        for i in range(CX):
            for a in range(2):
                summed = None
                for b in range(2):
                    line = None
                    for c in range(2):
                        start = i * NY * SPREAD + field * 8 + a * 4 + b * 2 + c
                        got = acc_ref[pl.ds(start, NY, stride=SPREAD), :]
                        line = got if c == 0 else line + pltpu.roll(got, 1, 1)
                    summed = line if b == 0 else summed + pltpu.roll(line, 1, 0)
                there = layers[i + a]
                layers[i + a] = summed if there is None else there + summed
        for l in range(2):
            low_ref[field * 2 + l] = layers[l]
            high_ref[field * 2 + l] = layers[l + 1]


def pair_up(field, axis):
    return field + pltpu.roll(field, field.shape[axis] - 1, axis)


def step_up(field, axis):
    return pltpu.roll(field, field.shape[axis] - 1, axis) - field


def pair_down(field, axis):
    return field + pltpu.roll(field, 1, axis)


def step_down(field, axis):
    return field - pltpu.roll(field, 1, axis)


def cell_stress(vel_lo, vel_hi, mass_lo, mass_hi, keep):
    grads = []
    for a in range(3):
        diff = vel_hi[a] - vel_lo[a]
        both = vel_hi[a] + vel_lo[a]
        grads.append(
            [
                0.25 * pair_up(pair_up(diff, 0), 1),
                0.25 * pair_up(step_up(both, 0), 1),
                0.25 * step_up(pair_up(both, 0), 1),
            ]
        )
    density = 0.125 * pair_up(pair_up(mass_hi + mass_lo, 0), 1)
    dxx = grads[0][0]
    dyy = grads[1][1]
    dzz = grads[2][2]
    dxy = 0.5 * (grads[0][1] + grads[1][0])
    dxz = 0.5 * (grads[0][2] + grads[2][0])
    dyz = 0.5 * (grads[1][2] + grads[2][1])
    second = dxx * dxx + dyy * dyy + dzz * dzz + 2.0 * (dxy * dxy + dxz * dxz + dyz * dyz)
    rate = jnp.sqrt(2.0 * second + rate_floor * rate_floor)
    pressure = stiffness * density
    inertial = rate * grain_size / jnp.sqrt(pressure + press_floor)
    friction = mu_static + (mu_limit - mu_static) * inertial / (inertia_ref + inertial)
    twice = 2.0 * friction * pressure / rate
    sigma = [
        twice * dxx - pressure,
        twice * dyy - pressure,
        twice * dzz - pressure,
        twice * dxy,
        twice * dxz,
        twice * dyz,
    ]
    return [jnp.where(keep, s, 0.0) for s in sigma]


def node_force(lower, upper):
    force = []
    for a in range(3):
        sx, sy, sz = (components[a][b] for b in range(3))
        along = pair_down(pair_down(upper[sx] - lower[sx], 0), 1)
        across = step_down(pair_down(upper[sy] + lower[sy], 1), 0)
        upward = step_down(pair_down(upper[sz] + lower[sz], 0), 1)
        force.append(0.25 * (along + across + upward))
    return force


def collect_kernel(
    count_ref, block_ref, row_ref, total_ref, step_ref,
    low_ref, high_ref, left_ref, right_ref, frac_ref, vel_ref, cells_ref,
    new_frac_ref, new_vel_ref, top_ref, tab_ref, out_ref,
):
    blocks = frac_ref.shape[1] // BLOCK
    count = count_ref[0]
    step = step_ref[0]
    nodes = [
        [left_ref[f * 2] for f in range(4)],
        [low_ref[f * 2] + left_ref[f * 2 + 1] for f in range(4)],
        [low_ref[f * 2 + 1] for f in range(4)],
        [high_ref[f * 2 + 1] + right_ref[f * 2] for f in range(4)],
        [right_ref[f * 2 + 1] for f in range(4)],
    ]
    height = lax.broadcasted_iota(jnp.int32, (NY, NZ), 1)
    keep = height < NZ - 1
    above_bed = height > 0
    floor = [jnp.maximum(layer[0], mass_floor) for layer in nodes]
    v_old = [[layer[1 + a] / floor[l] for a in range(3)] for l, layer in enumerate(nodes)]
    sigma = [
        cell_stress(v_old[l], v_old[l + 1], nodes[l][0], nodes[l + 1][0], keep) for l in range(4)
    ]
    tab_ref[...] = jnp.zeros_like(tab_ref)
    for l in range(1, 4):
        force = node_force(sigma[l - 1], sigma[l])
        for a in range(3):
            fresh = (
                nodes[l][1 + a] + step * (force[a] + nodes[l][0] * gravity[a])
            ) / floor[l]
            fresh = jnp.where(above_bed, fresh, 0.0)
            for field, value in ((a, fresh - flip_share * v_old[l][a]), (4 + a, step * fresh)):
                for b in range(2):
                    line = value if b == 0 else pltpu.roll(value, NY - 1, 0)
                    for c in range(2):
                        put = line if c == 0 else pltpu.roll(line, NZ - 1, 1)
                        for i in range(CX):
                            corner_a = l - 1 - i
                            if corner_a not in (0, 1):
                                continue
                            corner = corner_a * 4 + b * 2 + c
                            start = i * NY * TABLE + corner * 8 + field
                            tab_ref[pl.ds(start, NY, stride=TABLE), :] = put

    out_ref[...] = jnp.zeros_like(out_ref)

    def visit(group, carry):
        found = []
        for u in range(UNROLL):
            v = group * UNROLL + u
            block = block_ref[v]
            row = row_ref[v]
            hot = one_hot(cells_ref, block, row)
            at = pl.ds(pl.multiple_of(jnp.minimum(row, ROWS - 1) * TABLE, TABLE), TABLE)
            high, low = split_pair(tab_ref[at, :])
            both = jnp.dot(jnp.concatenate([high, low], axis=0), hot, preferred_element_type=f32)
            value = both[:TABLE] + both[TABLE:]
            frac = frac_ref[:, pl.ds(pl.multiple_of(block * BLOCK, BLOCK), BLOCK)]
            corners = [value[8 * k : 8 * k + 8] for k in range(8)]
            for d in (2, 1, 0):
                share = frac[d : d + 1, :]
                corners = [
                    corners[k] + share * (corners[k + 1] - corners[k])
                    for k in range(0, len(corners), 2)
                ]
            found.append((block, corners[0]))
        for block, part in found:
            out_ref[pl.ds(block, 1)] += part[None]
        return carry

    lax.fori_loop(0, (total_ref[0] + UNROLL - 1) // UNROLL, visit, 0)

    lane = lax.broadcasted_iota(jnp.int32, (1, BLOCK), 1)

    def finish(block, top):
        at = pl.multiple_of(block * BLOCK, BLOCK)
        alive = at + lane < count
        got = out_ref[pl.ds(block, 1)][0]
        fresh = jnp.where(alive, flip_share * vel_ref[:, pl.ds(at, BLOCK)] + got[0:3], 0.0)
        new_vel_ref[:, pl.ds(at, BLOCK)] = fresh
        placed = jnp.where(alive, frac_ref[:, pl.ds(at, BLOCK)] + got[4:7], 0.0)
        new_frac_ref[:, pl.ds(at, BLOCK)] = placed
        square = fresh[0:1] * fresh[0:1] + fresh[1:2] * fresh[1:2] + fresh[2:3] * fresh[2:3]
        return jnp.maximum(top, square)

    top = lax.fori_loop(0, blocks, finish, jnp.zeros((1, BLOCK), f32), unroll=4)
    top = jnp.sqrt(jnp.max(top, axis=1, keepdims=True))
    top_ref[...] = jnp.broadcast_to(top[None], top_ref.shape)


smem = pl.BlockSpec(memory_space=pltpu.SMEM)
vmem = pl.BlockSpec(memory_space=pltpu.VMEM)


def body(frac, velocity, mass, particle_cell, tile_count, time_step):
    slots = frac.shape[1]
    blocks = slots // BLOCK
    count = tile_count[0]
    block, row, total = visit_list(particle_cell, count)
    mass_rows = mass.reshape(slots // 128, 128)
    cell_rows = particle_cell.reshape(slots // 128, 128)
    layer_pair = jax.ShapeDtypeStruct((8, NY, NZ), f32)
    low, high = pl.pallas_call(
        spread_kernel,
        out_shape=(layer_pair, layer_pair),
        in_specs=[smem] * 4 + [vmem] * 4,
        out_specs=(vmem, vmem),
        scratch_shapes=[
            pltpu.VMEM((blocks, 2 * SPREAD, BLOCK), bf16),
            pltpu.VMEM(((ROWS + 1) * SPREAD, NZ), f32),
        ],
        compiler_params=pltpu.CompilerParams(vmem_limit_bytes=32 * 1024 * 1024),
        name="spread",
    )(tile_count, block, row, total, frac, velocity, mass_rows, cell_rows)
    from_left = shifted(high, "gx", 1)
    from_right = shifted(low, "gx", -1)
    new_frac, new_velocity, top = pl.pallas_call(
        collect_kernel,
        out_shape=(
            jax.ShapeDtypeStruct(frac.shape, f32),
            jax.ShapeDtypeStruct(velocity.shape, f32),
            jax.ShapeDtypeStruct((lax.axis_size("gx"), 8, 128), f32),
        ),
        in_specs=[smem] * 5 + [vmem] * 7,
        out_specs=(vmem, vmem, vmem),
        scratch_shapes=[
            pltpu.VMEM((ROWS * TABLE, NZ), f32),
            pltpu.VMEM((blocks, 8, BLOCK), f32),
        ],
        compiler_params=pltpu.CompilerParams(vmem_limit_bytes=32 * 1024 * 1024),
        name="collect",
    )(
        tile_count, block, row, total, time_step,
        low, high, from_left, from_right, frac, velocity, cell_rows,
    )
    tops = lax.all_to_all(top, "gx", 0, 0, tiled=True)
    next_step = (courant / (jnp.max(tops) + wave_speed)).reshape(1)
    return (new_frac, new_velocity, next_step)


def solution(mesh):
    placed = (
        P(None, ("runs", "gx")),
        P(None, ("runs", "gx")),
        P(("runs", "gx")),
        P(("runs", "gx")),
        P(("runs", "gx")),
        P("runs"),
    )
    return jax.shard_map(
        body,
        mesh=mesh,
        in_specs=placed,
        out_specs=(P(None, ("runs", "gx")), P(None, ("runs", "gx")), P("runs")),
        check_vma=False,
    )
```

```python
import functools

import jax
import jax.numpy as jnp
from jax import lax
from jax.experimental import pallas as pl
from jax.experimental.pallas import tpu as pltpu
from jax.sharding import PartitionSpec as P

CX = 2
NY = 32
NZ = 128
ROWS = CX * NY
BLOCK = 256
UNROLL = 8
SPREAD = 32
TABLE = 64

mass_floor = 0.25
stiffness = 2.0
press_floor = 1.0
grain_size = 0.5
inertia_ref = 0.3
mu_static = 0.38
mu_limit = 0.64
rate_floor = 0.5
gravity = (0.5, 0.0, -0.866)
flip_share = 0.95
courant = 0.4
wave_speed = 2.0
components = ((0, 3, 4), (3, 1, 5), (4, 5, 2))
f32 = jnp.float32
bf16 = jnp.bfloat16


def shifted(array, axis, by):
    devices = lax.axis_size(axis)
    return lax.ppermute(array, axis, [(i, (i + by) % devices) for i in range(devices)])


def visit_list(particle_cell, count):
    slots = particle_cell.shape[0]
    blocks = slots // BLOCK
    size = blocks + ROWS
    number = jnp.arange(blocks, dtype=jnp.int32)
    cells = particle_cell.reshape(blocks, BLOCK)
    live = jnp.arange(slots, dtype=jnp.int32).reshape(blocks, BLOCK) < count
    first = cells[:, 0] // NZ
    last = jnp.max(jnp.where(live, cells, 0), axis=1) // NZ
    visits = jnp.where(number * BLOCK < count, last - first + 1, 0)
    before = number[:, None] < number[None, :]
    starts = jnp.sum(jnp.where(before, visits[:, None], 0), axis=0)
    total = jnp.sum(visits)
    order = jnp.arange(size, dtype=jnp.int32)
    inside = (starts[None, :] <= order[:, None]) & (order[:, None] < (starts + visits)[None, :])
    block = jnp.sum(jnp.where(inside, number[None, :], 0), axis=1)
    row = jnp.sum(jnp.where(inside, (first - starts)[None, :], 0), axis=1) + order
    row = jnp.where(order < total, row, ROWS)
    return block, row, total.reshape(1)


def split_pair(values):
    high = values.astype(bf16)
    low = (values - high.astype(f32)).astype(bf16)
    return high, low


def one_hot(cells_ref, block, row):
    rel = cells_ref[pl.ds(block * 2, 2), :] - row * NZ
    nodes = lax.broadcasted_iota(jnp.int32, (NZ, 128), 0)
    halves = [jnp.where(nodes == rel[h : h + 1, :], 1.0, 0.0) for h in range(2)]
    return jnp.concatenate(halves, axis=1).astype(bf16)


def pair_lines(ref, block):
    both = ref[pl.ds(block * 2, 2), :]
    return jnp.concatenate([both[0:1, :], both[1:2, :]], axis=1)


def spread_kernel(
    count_ref, block_ref, row_ref, total_ref, frac_ref, vel_ref, mass_ref, cells_ref,
    low_ref, high_ref, q_ref, acc_ref,
):
    blocks = frac_ref.shape[1] // BLOCK
    count = count_ref[0]
    acc_ref[...] = jnp.zeros_like(acc_ref)
    corner = lax.broadcasted_iota(jnp.int32, (8, BLOCK), 0)
    upper = [(corner // part) % 2 == 1 for part in (4, 2, 1)]
    lane = lax.broadcasted_iota(jnp.int32, (1, BLOCK), 1)

    def prepare(block, carry):
        at = pl.multiple_of(block * BLOCK, BLOCK)
        frac = frac_ref[:, pl.ds(at, BLOCK)]
        vel = vel_ref[:, pl.ds(at, BLOCK)]
        mass = pair_lines(mass_ref, block)
        held = jnp.where(at + lane < count, mass, 0.0)
        parts = [
            jnp.where(upper[d], frac[d : d + 1, :], 1.0 - frac[d : d + 1, :]) for d in range(3)
        ]
        weight = parts[0] * parts[1] * parts[2] * held
        carried = jnp.concatenate([weight] + [weight * vel[a : a + 1, :] for a in range(3)], axis=0)
        high, low = split_pair(carried)
        q_ref[pl.ds(block, 1)] = jnp.concatenate([high, low], axis=0)[None]
        return carry

    lax.fori_loop(0, blocks, prepare, 0, unroll=4)

    def visit(group, carry):
        found = []
        for u in range(UNROLL):
            v = group * UNROLL + u
            block = block_ref[v]
            row = row_ref[v]
            hot = one_hot(cells_ref, block, row)
            both = lax.dot_general(
                q_ref[pl.ds(block, 1)][0], hot, (((1,), (1,)), ((), ())), preferred_element_type=f32
            )
            found.append((row, both[:SPREAD] + both[SPREAD:]))
        for row, part in found:
            at = pl.ds(pl.multiple_of(row * SPREAD, SPREAD), SPREAD)
            acc_ref[at, :] += part
        return carry

    lax.fori_loop(0, (total_ref[0] + UNROLL - 1) // UNROLL, visit, 0)

    for field in range(4):
        layers = [None] * 3
        for i in range(CX):
            for a in range(2):
                summed = None
                for b in range(2):
                    line = None
                    for c in range(2):
                        start = i * NY * SPREAD + field * 8 + a * 4 + b * 2 + c
                        got = acc_ref[pl.ds(start, NY, stride=SPREAD), :]
                        line = got if c == 0 else line + pltpu.roll(got, 1, 1)
                    summed = line if b == 0 else summed + pltpu.roll(line, 1, 0)
                there = layers[i + a]
                layers[i + a] = summed if there is None else there + summed
        for l in range(2):
            low_ref[field * 2 + l] = layers[l]
            high_ref[field * 2 + l] = layers[l + 1]


def pair_up(field, axis):
    return field + pltpu.roll(field, field.shape[axis] - 1, axis)


def step_up(field, axis):
    return pltpu.roll(field, field.shape[axis] - 1, axis) - field


def pair_down(field, axis):
    return field + pltpu.roll(field, 1, axis)


def step_down(field, axis):
    return field - pltpu.roll(field, 1, axis)


def cell_stress(vel_lo, vel_hi, mass_lo, mass_hi, keep):
    grads = []
    for a in range(3):
        diff = vel_hi[a] - vel_lo[a]
        both = vel_hi[a] + vel_lo[a]
        grads.append(
            [
                0.25 * pair_up(pair_up(diff, 0), 1),
                0.25 * pair_up(step_up(both, 0), 1),
                0.25 * step_up(pair_up(both, 0), 1),
            ]
        )
    density = 0.125 * pair_up(pair_up(mass_hi + mass_lo, 0), 1)
    dxx = grads[0][0]
    dyy = grads[1][1]
    dzz = grads[2][2]
    dxy = 0.5 * (grads[0][1] + grads[1][0])
    dxz = 0.5 * (grads[0][2] + grads[2][0])
    dyz = 0.5 * (grads[1][2] + grads[2][1])
    second = dxx * dxx + dyy * dyy + dzz * dzz + 2.0 * (dxy * dxy + dxz * dxz + dyz * dyz)
    rate = jnp.sqrt(2.0 * second + rate_floor * rate_floor)
    pressure = stiffness * density
    inertial = rate * grain_size / jnp.sqrt(pressure + press_floor)
    friction = mu_static + (mu_limit - mu_static) * inertial / (inertia_ref + inertial)
    twice = 2.0 * friction * pressure / rate
    sigma = [
        twice * dxx - pressure,
        twice * dyy - pressure,
        twice * dzz - pressure,
        twice * dxy,
        twice * dxz,
        twice * dyz,
    ]
    return [jnp.where(keep, s, 0.0) for s in sigma]


def node_force(lower, upper):
    force = []
    for a in range(3):
        sx, sy, sz = (components[a][b] for b in range(3))
        along = pair_down(pair_down(upper[sx] - lower[sx], 0), 1)
        across = step_down(pair_down(upper[sy] + lower[sy], 1), 0)
        upward = step_down(pair_down(upper[sz] + lower[sz], 0), 1)
        force.append(0.25 * (along + across + upward))
    return force


def collect_kernel(
    count_ref, block_ref, row_ref, total_ref, step_ref,
    low_ref, high_ref, left_ref, right_ref, frac_ref, vel_ref, cells_ref,
    out_ref, top_ref, tab_ref,
):
    blocks = frac_ref.shape[1] // BLOCK
    count = count_ref[0]
    step = step_ref[0]
    nodes = [
        [left_ref[f * 2] for f in range(4)],
        [low_ref[f * 2] + left_ref[f * 2 + 1] for f in range(4)],
        [low_ref[f * 2 + 1] for f in range(4)],
        [high_ref[f * 2 + 1] + right_ref[f * 2] for f in range(4)],
        [right_ref[f * 2 + 1] for f in range(4)],
    ]
    height = lax.broadcasted_iota(jnp.int32, (NY, NZ), 1)
    keep = height < NZ - 1
    above_bed = height > 0
    floor = [jnp.maximum(layer[0], mass_floor) for layer in nodes]
    v_old = [[layer[1 + a] / floor[l] for a in range(3)] for l, layer in enumerate(nodes)]
    sigma = [
        cell_stress(v_old[l], v_old[l + 1], nodes[l][0], nodes[l + 1][0], keep) for l in range(4)
    ]
    tab_ref[...] = jnp.zeros_like(tab_ref)
    for l in range(1, 4):
        force = node_force(sigma[l - 1], sigma[l])
        for a in range(3):
            fresh = (
                nodes[l][1 + a] + step * (force[a] + nodes[l][0] * gravity[a])
            ) / floor[l]
            fresh = jnp.where(above_bed, fresh, 0.0)
            for field, value in ((a, fresh - flip_share * v_old[l][a]), (4 + a, step * fresh)):
                for b in range(2):
                    line = value if b == 0 else pltpu.roll(value, NY - 1, 0)
                    for c in range(2):
                        put = line if c == 0 else pltpu.roll(line, NZ - 1, 1)
                        for i in range(CX):
                            corner_a = l - 1 - i
                            if corner_a not in (0, 1):
                                continue
                            corner = corner_a * 4 + b * 2 + c
                            start = i * NY * TABLE + corner * 8 + field
                            tab_ref[pl.ds(start, NY, stride=TABLE), :] = put

    out_ref[...] = jnp.zeros_like(out_ref)

    def visit(group, carry):
        found = []
        for u in range(UNROLL):
            v = group * UNROLL + u
            block = block_ref[v]
            row = row_ref[v]
            hot = one_hot(cells_ref, block, row)
            at = pl.ds(pl.multiple_of(jnp.minimum(row, ROWS - 1) * TABLE, TABLE), TABLE)
            high, low = split_pair(tab_ref[at, :])
            both = jnp.dot(jnp.concatenate([high, low], axis=0), hot, preferred_element_type=f32)
            value = both[:TABLE] + both[TABLE:]
            frac = frac_ref[:, pl.ds(pl.multiple_of(block * BLOCK, BLOCK), BLOCK)]
            corners = [value[8 * k : 8 * k + 8] for k in range(8)]
            for d in (2, 1, 0):
                share = frac[d : d + 1, :]
                corners = [
                    corners[k] + share * (corners[k + 1] - corners[k])
                    for k in range(0, len(corners), 2)
                ]
            found.append((block, corners[0]))
        for block, part in found:
            out_ref[pl.ds(block, 1)] += part[None]
        return carry

    lax.fori_loop(0, (total_ref[0] + UNROLL - 1) // UNROLL, visit, 0)

    lane = lax.broadcasted_iota(jnp.int32, (1, BLOCK), 1)

    def finish(block, top):
        at = pl.multiple_of(block * BLOCK, BLOCK)
        alive = at + lane < count
        got = out_ref[pl.ds(block, 1)][0]
        fresh = jnp.where(alive, flip_share * vel_ref[:, pl.ds(at, BLOCK)] + got[0:3], 0.0)
        out_ref[pl.ds(block, 1), 0:3] = fresh[None]
        square = fresh[0:1] * fresh[0:1] + fresh[1:2] * fresh[1:2] + fresh[2:3] * fresh[2:3]
        return jnp.maximum(top, square)

    top = lax.fori_loop(0, blocks, finish, jnp.zeros((1, BLOCK), f32), unroll=4)
    top = jnp.sqrt(jnp.max(top, axis=1, keepdims=True))
    top_ref[...] = jnp.broadcast_to(top, top_ref.shape)


def finish_kernel(count_ref, moved_ref, frac_ref, new_frac_ref, new_vel_ref):
    blocks = frac_ref.shape[1] // BLOCK
    count = count_ref[0]
    lane = lax.broadcasted_iota(jnp.int32, (1, BLOCK), 1)

    def finish(block, carry):
        at = pl.multiple_of(block * BLOCK, BLOCK)
        got = moved_ref[pl.ds(block, 1)][0]
        new_vel_ref[:, pl.ds(at, BLOCK)] = got[0:3]
        placed = jnp.where(at + lane < count, frac_ref[:, pl.ds(at, BLOCK)] + got[4:7], 0.0)
        new_frac_ref[:, pl.ds(at, BLOCK)] = placed
        return carry

    lax.fori_loop(0, blocks, finish, 0, unroll=4)


def largest(value, axis):
    devices = lax.axis_size(axis)
    reach = 1
    while reach < devices:
        if devices & (devices - 1) == 0:
            pairs = [(i, i ^ reach) for i in range(devices)]
        else:
            pairs = [(i, (i + reach) % devices) for i in range(devices)]
        value = jnp.maximum(value, lax.ppermute(value, axis, pairs))
        reach *= 2
    return value


smem = pl.BlockSpec(memory_space=pltpu.SMEM)
vmem = pl.BlockSpec(memory_space=pltpu.VMEM)


def body(frac, velocity, mass, particle_cell, tile_count, time_step):
    slots = frac.shape[1]
    blocks = slots // BLOCK
    count = tile_count[0]
    block, row, total = visit_list(particle_cell, count)
    mass_rows = mass.reshape(slots // 128, 128)
    cell_rows = particle_cell.reshape(slots // 128, 128)
    layer_pair = jax.ShapeDtypeStruct((8, NY, NZ), f32)
    low, high = pl.pallas_call(
        spread_kernel,
        out_shape=(layer_pair, layer_pair),
        in_specs=[smem] * 4 + [vmem] * 4,
        out_specs=(vmem, vmem),
        scratch_shapes=[
            pltpu.VMEM((blocks, 2 * SPREAD, BLOCK), bf16),
            pltpu.VMEM(((ROWS + 1) * SPREAD, NZ), f32),
        ],
        compiler_params=pltpu.CompilerParams(vmem_limit_bytes=32 * 1024 * 1024),
        name="spread",
    )(tile_count, block, row, total, frac, velocity, mass_rows, cell_rows)
    from_left = shifted(high, "gx", 1)
    from_right = shifted(low, "gx", -1)
    moved, top = pl.pallas_call(
        collect_kernel,
        out_shape=(
            jax.ShapeDtypeStruct((blocks, 8, BLOCK), f32),
            jax.ShapeDtypeStruct((8, 128), f32),
        ),
        in_specs=[smem] * 5 + [vmem] * 7,
        out_specs=(vmem, vmem),
        scratch_shapes=[pltpu.VMEM((ROWS * TABLE, NZ), f32)],
        compiler_params=pltpu.CompilerParams(vmem_limit_bytes=32 * 1024 * 1024),
        name="collect",
    )(
        tile_count, block, row, total, time_step,
        low, high, from_left, from_right, frac, velocity, cell_rows,
    )
    new_frac, new_velocity = pl.pallas_call(
        finish_kernel,
        out_shape=(
            jax.ShapeDtypeStruct(frac.shape, f32),
            jax.ShapeDtypeStruct(velocity.shape, f32),
        ),
        in_specs=[smem] + [vmem] * 2,
        out_specs=(vmem, vmem),
        compiler_params=pltpu.CompilerParams(vmem_limit_bytes=32 * 1024 * 1024),
        cost_estimate=pl.CostEstimate(flops=0, bytes_accessed=8000000, transcendentals=0),
        name="finish",
    )(tile_count, moved, frac)
    fastest = largest(top, "gx")
    next_step = (courant / (fastest + wave_speed))[0, :1]
    return (new_frac, new_velocity, next_step)


def solution(mesh):
    placed = (
        P(None, ("runs", "gx")),
        P(None, ("runs", "gx")),
        P(("runs", "gx")),
        P(("runs", "gx")),
        P(("runs", "gx")),
        P("runs"),
    )
    return jax.shard_map(
        body,
        mesh=mesh,
        in_specs=placed,
        out_specs=(P(None, ("runs", "gx")), P(None, ("runs", "gx")), P("runs")),
        check_vma=False,
    )
```

```python
import functools

import jax
import jax.numpy as jnp
from jax import lax
from jax.experimental import pallas as pl
from jax.experimental.pallas import tpu as pltpu
from jax.sharding import PartitionSpec as P

CX = 2
NY = 32
NZ = 128
ROWS = CX * NY
BLOCK = 256
UNROLL = 8
SPREAD = 32
TABLE = 64

mass_floor = 0.25
stiffness = 2.0
press_floor = 1.0
grain_size = 0.5
inertia_ref = 0.3
mu_static = 0.38
mu_limit = 0.64
rate_floor = 0.5
gravity = (0.5, 0.0, -0.866)
flip_share = 0.95
courant = 0.4
wave_speed = 2.0
components = ((0, 3, 4), (3, 1, 5), (4, 5, 2))
f32 = jnp.float32
bf16 = jnp.bfloat16


def shifted(array, axis, by):
    devices = lax.axis_size(axis)
    return lax.ppermute(array, axis, [(i, (i + by) % devices) for i in range(devices)])


def visit_list(particle_cell, count):
    slots = particle_cell.shape[0]
    blocks = slots // BLOCK
    size = blocks + ROWS
    number = jnp.arange(blocks, dtype=jnp.int32)
    cells = particle_cell.reshape(blocks, BLOCK)
    live = jnp.arange(slots, dtype=jnp.int32).reshape(blocks, BLOCK) < count
    first = cells[:, 0] // NZ
    last = jnp.max(jnp.where(live, cells, 0), axis=1) // NZ
    visits = jnp.where(number * BLOCK < count, last - first + 1, 0)
    before = number[:, None] < number[None, :]
    starts = jnp.sum(jnp.where(before, visits[:, None], 0), axis=0)
    total = jnp.sum(visits)
    order = jnp.arange(size, dtype=jnp.int32)
    inside = (starts[None, :] <= order[:, None]) & (order[:, None] < (starts + visits)[None, :])
    block = jnp.sum(jnp.where(inside, number[None, :], 0), axis=1)
    row = jnp.sum(jnp.where(inside, (first - starts)[None, :], 0), axis=1) + order
    row = jnp.where(order < total, row, ROWS)
    return block, row, total.reshape(1)


def split_pair(values):
    high = values.astype(bf16)
    low = (values - high.astype(f32)).astype(bf16)
    return high, low


def one_hot(cells_ref, block, row):
    rel = cells_ref[pl.ds(block * 2, 2), :] - row * NZ
    nodes = lax.broadcasted_iota(jnp.int32, (NZ, 128), 0)
    halves = [jnp.where(nodes == rel[h : h + 1, :], 1.0, 0.0) for h in range(2)]
    return jnp.concatenate(halves, axis=1).astype(bf16)


def pair_lines(ref, block):
    both = ref[pl.ds(block * 2, 2), :]
    return jnp.concatenate([both[0:1, :], both[1:2, :]], axis=1)


def spread_kernel(
    count_ref, block_ref, row_ref, total_ref, frac_ref, vel_ref, mass_ref, cells_ref,
    low_ref, high_ref, q_ref, acc_ref,
):
    blocks = frac_ref.shape[1] // BLOCK
    count = count_ref[0]
    acc_ref[...] = jnp.zeros_like(acc_ref)
    corner = lax.broadcasted_iota(jnp.int32, (8, BLOCK), 0)
    upper = [(corner // part) % 2 == 1 for part in (4, 2, 1)]
    lane = lax.broadcasted_iota(jnp.int32, (1, BLOCK), 1)

    def prepare(block, carry):
        at = pl.multiple_of(block * BLOCK, BLOCK)
        frac = frac_ref[:, pl.ds(at, BLOCK)]
        vel = vel_ref[:, pl.ds(at, BLOCK)]
        mass = pair_lines(mass_ref, block)
        held = jnp.where(at + lane < count, mass, 0.0)
        parts = [
            jnp.where(upper[d], frac[d : d + 1, :], 1.0 - frac[d : d + 1, :]) for d in range(3)
        ]
        weight = parts[0] * parts[1] * parts[2] * held
        carried = jnp.concatenate([weight] + [weight * vel[a : a + 1, :] for a in range(3)], axis=0)
        high, low = split_pair(carried)
        q_ref[pl.ds(block, 1)] = jnp.concatenate([high, low], axis=0)[None]
        return carry

    lax.fori_loop(0, blocks, prepare, 0, unroll=4)

    def visit(group, carry):
        found = []
        for u in range(UNROLL):
            v = group * UNROLL + u
            block = block_ref[v]
            row = row_ref[v]
            hot = one_hot(cells_ref, block, row)
            both = lax.dot_general(
                q_ref[pl.ds(block, 1)][0], hot, (((1,), (1,)), ((), ())), preferred_element_type=f32
            )
            found.append((row, both[:SPREAD] + both[SPREAD:]))
        for row, part in found:
            at = pl.ds(pl.multiple_of(row * SPREAD, SPREAD), SPREAD)
            acc_ref[at, :] += part
        return carry

    lax.fori_loop(0, (total_ref[0] + UNROLL - 1) // UNROLL, visit, 0)

    for field in range(4):
        layers = [None] * 3
        for i in range(CX):
            for a in range(2):
                summed = None
                for b in range(2):
                    line = None
                    for c in range(2):
                        start = i * NY * SPREAD + field * 8 + a * 4 + b * 2 + c
                        got = acc_ref[pl.ds(start, NY, stride=SPREAD), :]
                        line = got if c == 0 else line + pltpu.roll(got, 1, 1)
                    summed = line if b == 0 else summed + pltpu.roll(line, 1, 0)
                there = layers[i + a]
                layers[i + a] = summed if there is None else there + summed
        for l in range(2):
            low_ref[field * 2 + l] = layers[l]
            high_ref[field * 2 + l] = layers[l + 1]


def pair_up(field, axis):
    return field + pltpu.roll(field, field.shape[axis] - 1, axis)


def step_up(field, axis):
    return pltpu.roll(field, field.shape[axis] - 1, axis) - field


def pair_down(field, axis):
    return field + pltpu.roll(field, 1, axis)


def step_down(field, axis):
    return field - pltpu.roll(field, 1, axis)


def cell_stress(vel_lo, vel_hi, mass_lo, mass_hi, keep):
    grads = []
    for a in range(3):
        diff = vel_hi[a] - vel_lo[a]
        both = vel_hi[a] + vel_lo[a]
        grads.append(
            [
                0.25 * pair_up(pair_up(diff, 0), 1),
                0.25 * pair_up(step_up(both, 0), 1),
                0.25 * step_up(pair_up(both, 0), 1),
            ]
        )
    density = 0.125 * pair_up(pair_up(mass_hi + mass_lo, 0), 1)
    dxx = grads[0][0]
    dyy = grads[1][1]
    dzz = grads[2][2]
    dxy = 0.5 * (grads[0][1] + grads[1][0])
    dxz = 0.5 * (grads[0][2] + grads[2][0])
    dyz = 0.5 * (grads[1][2] + grads[2][1])
    second = dxx * dxx + dyy * dyy + dzz * dzz + 2.0 * (dxy * dxy + dxz * dxz + dyz * dyz)
    rate = jnp.sqrt(2.0 * second + rate_floor * rate_floor)
    pressure = stiffness * density
    inertial = rate * grain_size / jnp.sqrt(pressure + press_floor)
    friction = mu_static + (mu_limit - mu_static) * inertial / (inertia_ref + inertial)
    twice = 2.0 * friction * pressure / rate
    sigma = [
        twice * dxx - pressure,
        twice * dyy - pressure,
        twice * dzz - pressure,
        twice * dxy,
        twice * dxz,
        twice * dyz,
    ]
    return [jnp.where(keep, s, 0.0) for s in sigma]


def node_force(lower, upper):
    force = []
    for a in range(3):
        sx, sy, sz = (components[a][b] for b in range(3))
        along = pair_down(pair_down(upper[sx] - lower[sx], 0), 1)
        across = step_down(pair_down(upper[sy] + lower[sy], 1), 0)
        upward = step_down(pair_down(upper[sz] + lower[sz], 0), 1)
        force.append(0.25 * (along + across + upward))
    return force


def collect_kernel(
    count_ref, block_ref, row_ref, total_ref, step_ref,
    low_ref, high_ref, left_ref, right_ref, frac_ref, vel_ref, cells_ref,
    out_ref, top_ref, tab_ref,
):
    blocks = frac_ref.shape[1] // BLOCK
    count = count_ref[0]
    step = step_ref[0]
    nodes = [
        [left_ref[f * 2] for f in range(4)],
        [low_ref[f * 2] + left_ref[f * 2 + 1] for f in range(4)],
        [low_ref[f * 2 + 1] for f in range(4)],
        [high_ref[f * 2 + 1] + right_ref[f * 2] for f in range(4)],
        [right_ref[f * 2 + 1] for f in range(4)],
    ]
    height = lax.broadcasted_iota(jnp.int32, (NY, NZ), 1)
    keep = height < NZ - 1
    above_bed = height > 0
    floor = [jnp.maximum(layer[0], mass_floor) for layer in nodes]
    v_old = [[layer[1 + a] / floor[l] for a in range(3)] for l, layer in enumerate(nodes)]
    sigma = [
        cell_stress(v_old[l], v_old[l + 1], nodes[l][0], nodes[l + 1][0], keep) for l in range(4)
    ]
    tab_ref[...] = jnp.zeros_like(tab_ref)
    for l in range(1, 4):
        force = node_force(sigma[l - 1], sigma[l])
        for a in range(3):
            fresh = (
                nodes[l][1 + a] + step * (force[a] + nodes[l][0] * gravity[a])
            ) / floor[l]
            fresh = jnp.where(above_bed, fresh, 0.0)
            for field, value in ((a, fresh - flip_share * v_old[l][a]), (4 + a, step * fresh)):
                for b in range(2):
                    line = value if b == 0 else pltpu.roll(value, NY - 1, 0)
                    for c in range(2):
                        put = line if c == 0 else pltpu.roll(line, NZ - 1, 1)
                        for i in range(CX):
                            corner_a = l - 1 - i
                            if corner_a not in (0, 1):
                                continue
                            corner = corner_a * 4 + b * 2 + c
                            start = i * NY * TABLE + corner * 8 + field
                            tab_ref[pl.ds(start, NY, stride=TABLE), :] = put

    out_ref[...] = jnp.zeros_like(out_ref)

    def visit(group, carry):
        found = []
        for u in range(UNROLL):
            v = group * UNROLL + u
            block = block_ref[v]
            row = row_ref[v]
            hot = one_hot(cells_ref, block, row)
            at = pl.ds(pl.multiple_of(jnp.minimum(row, ROWS - 1) * TABLE, TABLE), TABLE)
            high, low = split_pair(tab_ref[at, :])
            both = jnp.dot(jnp.concatenate([high, low], axis=0), hot, preferred_element_type=f32)
            value = both[:TABLE] + both[TABLE:]
            frac = frac_ref[:, pl.ds(pl.multiple_of(block * BLOCK, BLOCK), BLOCK)]
            corners = [value[8 * k : 8 * k + 8] for k in range(8)]
            for d in (2, 1, 0):
                share = frac[d : d + 1, :]
                corners = [
                    corners[k] + share * (corners[k + 1] - corners[k])
                    for k in range(0, len(corners), 2)
                ]
            found.append((block, corners[0]))
        for block, part in found:
            out_ref[pl.ds(block, 1)] += part[None]
        return carry

    lax.fori_loop(0, (total_ref[0] + UNROLL - 1) // UNROLL, visit, 0)

    lane = lax.broadcasted_iota(jnp.int32, (1, BLOCK), 1)

    def finish(block, top):
        at = pl.multiple_of(block * BLOCK, BLOCK)
        alive = at + lane < count
        got = out_ref[pl.ds(block, 1)][0]
        fresh = jnp.where(alive, flip_share * vel_ref[:, pl.ds(at, BLOCK)] + got[0:3], 0.0)
        out_ref[pl.ds(block, 1), 0:3] = fresh[None]
        square = fresh[0:1] * fresh[0:1] + fresh[1:2] * fresh[1:2] + fresh[2:3] * fresh[2:3]
        return jnp.maximum(top, square)

    top = lax.fori_loop(0, blocks, finish, jnp.zeros((1, BLOCK), f32), unroll=4)
    top = jnp.sqrt(jnp.max(top, axis=1, keepdims=True))
    top_ref[...] = jnp.broadcast_to(top, top_ref.shape)


def finish_kernel(count_ref, moved_ref, frac_ref, new_frac_ref, new_vel_ref):
    blocks = frac_ref.shape[1] // BLOCK
    count = count_ref[0]
    lane = lax.broadcasted_iota(jnp.int32, (1, BLOCK), 1)

    def finish(block, carry):
        at = pl.multiple_of(block * BLOCK, BLOCK)
        got = moved_ref[pl.ds(block, 1)][0]
        new_vel_ref[:, pl.ds(at, BLOCK)] = got[0:3]
        placed = jnp.where(at + lane < count, frac_ref[:, pl.ds(at, BLOCK)] + got[4:7], 0.0)
        new_frac_ref[:, pl.ds(at, BLOCK)] = placed
        return carry

    lax.fori_loop(0, blocks, finish, 0, unroll=4)


def largest(value, axis):
    devices = lax.axis_size(axis)
    reach, radix = 1, 2
    while reach < devices:
        ahead = [k * reach for k in range(1, radix) if k * reach < devices]
        if devices & (devices - 1) == 0:
            pairs = [[(i, i ^ by) for i in range(devices)] for by in ahead]
        else:
            pairs = [[(i, (i + by) % devices) for i in range(devices)] for by in ahead]
        arrived = [lax.ppermute(value, axis, listed) for listed in pairs]
        for other in arrived:
            value = jnp.maximum(value, other)
        reach, radix = reach * radix, 8
    return value


smem = pl.BlockSpec(memory_space=pltpu.SMEM)
vmem = pl.BlockSpec(memory_space=pltpu.VMEM)


def body(frac, velocity, mass, particle_cell, tile_count, time_step):
    slots = frac.shape[1]
    blocks = slots // BLOCK
    count = tile_count[0]
    block, row, total = visit_list(particle_cell, count)
    mass_rows = mass.reshape(slots // 128, 128)
    cell_rows = particle_cell.reshape(slots // 128, 128)
    layer_pair = jax.ShapeDtypeStruct((8, NY, NZ), f32)
    low, high = pl.pallas_call(
        spread_kernel,
        out_shape=(layer_pair, layer_pair),
        in_specs=[smem] * 4 + [vmem] * 4,
        out_specs=(vmem, vmem),
        scratch_shapes=[
            pltpu.VMEM((blocks, 2 * SPREAD, BLOCK), bf16),
            pltpu.VMEM(((ROWS + 1) * SPREAD, NZ), f32),
        ],
        compiler_params=pltpu.CompilerParams(vmem_limit_bytes=32 * 1024 * 1024),
        name="spread",
    )(tile_count, block, row, total, frac, velocity, mass_rows, cell_rows)
    from_left = shifted(high, "gx", 1)
    from_right = shifted(low, "gx", -1)
    moved, top = pl.pallas_call(
        collect_kernel,
        out_shape=(
            jax.ShapeDtypeStruct((blocks, 8, BLOCK), f32),
            jax.ShapeDtypeStruct((8, 128), f32),
        ),
        in_specs=[smem] * 5 + [vmem] * 7,
        out_specs=(vmem, vmem),
        scratch_shapes=[pltpu.VMEM((ROWS * TABLE, NZ), f32)],
        compiler_params=pltpu.CompilerParams(vmem_limit_bytes=32 * 1024 * 1024),
        name="collect",
    )(
        tile_count, block, row, total, time_step,
        low, high, from_left, from_right, frac, velocity, cell_rows,
    )
    new_frac, new_velocity = pl.pallas_call(
        finish_kernel,
        out_shape=(
            jax.ShapeDtypeStruct(frac.shape, f32),
            jax.ShapeDtypeStruct(velocity.shape, f32),
        ),
        in_specs=[smem] + [vmem] * 2,
        out_specs=(vmem, vmem),
        compiler_params=pltpu.CompilerParams(vmem_limit_bytes=32 * 1024 * 1024),
        cost_estimate=pl.CostEstimate(flops=0, bytes_accessed=8000000, transcendentals=0),
        name="finish",
    )(tile_count, moved, frac)
    fastest = largest(top, "gx")
    next_step = (courant / (fastest + wave_speed))[0, :1]
    return (new_frac, new_velocity, next_step)


def solution(mesh):
    placed = (
        P(None, ("runs", "gx")),
        P(None, ("runs", "gx")),
        P(("runs", "gx")),
        P(("runs", "gx")),
        P(("runs", "gx")),
        P("runs"),
    )
    return jax.shard_map(
        body,
        mesh=mesh,
        in_specs=placed,
        out_specs=(P(None, ("runs", "gx")), P(None, ("runs", "gx")), P("runs")),
        check_vma=False,
    )
```

```python
import functools

import jax
import jax.numpy as jnp
from jax import lax
from jax.experimental import pallas as pl
from jax.experimental.pallas import tpu as pltpu
from jax.sharding import PartitionSpec as P

CX = 2
NY = 32
NZ = 128
ROWS = CX * NY
BLOCK = 256
LANES = 128
UNROLL = 8
SPREAD = 32
TABLE = 16

mass_floor = 0.25
stiffness = 2.0
press_floor = 1.0
grain_size = 0.5
inertia_ref = 0.3
mu_static = 0.38
mu_limit = 0.64
rate_floor = 0.5
gravity = (0.5, 0.0, -0.866)
flip_share = 0.95
courant = 0.4
wave_speed = 2.0
components = ((0, 3, 4), (3, 1, 5), (4, 5, 2))
f32 = jnp.float32
bf16 = jnp.bfloat16


def shifted(array, axis, by):
    devices = lax.axis_size(axis)
    return lax.ppermute(array, axis, [(i, (i + by) % devices) for i in range(devices)])


def split_pair(values):
    high = values.astype(bf16)
    low = (values - high.astype(f32)).astype(bf16)
    return high, low


def one_hot(cells_ref, block, offset):
    rel = cells_ref[pl.ds(block * 2, 2), :] - offset
    nodes = lax.broadcasted_iota(jnp.int32, (NZ, LANES), 0)
    halves = [jnp.where(nodes == rel[h : h + 1, :], 1.0, 0.0) for h in range(2)]
    return jnp.concatenate(halves, axis=1).astype(bf16)


def spread_kernel(
    count_hbm, frac_hbm, vel_hbm, mass_hbm, cells_hbm,
    low_ref, high_ref, plan_ref,
    count_ref, listed_ref, frac_ref, vel_ref, mass_ref, cells_ref, q_ref, acc_ref, sems,
):
    slots = frac_ref.shape[1]
    blocks = slots // BLOCK
    steps = blocks + ROWS
    arrivals = [
        pltpu.make_async_copy(source, target, sems.at[k])
        for k, (source, target) in enumerate(
            (
                (count_hbm, count_ref),
                (cells_hbm, listed_ref),
                (frac_hbm, frac_ref),
                (vel_hbm, vel_ref),
                (mass_hbm, mass_ref),
                (cells_hbm, cells_ref),
            )
        )
    ]
    for arrival in arrivals:
        arrival.start()
    acc_ref[...] = jnp.zeros_like(acc_ref)
    for arrival in arrivals:
        arrival.wait()
    count = count_ref[0]
    live_blocks = (count + BLOCK - 1) >> 8
    sublane = lax.broadcasted_iota(jnp.int32, (8, LANES), 0)
    lane = lax.broadcasted_iota(jnp.int32, (1, LANES), 1)
    top_z = sublane >= 4
    field = sublane & 3

    def list_visit(v, block, row, total):
        valid = block < live_blocks
        plan_ref[v] = jnp.where(valid, block, 0)
        plan_ref[steps + v] = jnp.where(valid, row + (row >> 5), 0)
        plan_ref[2 * steps + v] = jnp.where(valid, row, ROWS) * NZ
        end = jnp.minimum(block * BLOCK + BLOCK, count) - 1
        after = jnp.minimum(block * BLOCK + BLOCK, slots - 1)
        last = listed_ref[end >> 7, end & 127] >> 7
        following = listed_ref[after >> 7, after & 127] >> 7
        ahead = valid & (row >= last)
        return (
            jnp.where(ahead, block + 1, block),
            jnp.where(ahead, following, row + 1),
            jnp.where(valid, v + 1, total),
        )

    def weigh(part):
        at = pl.multiple_of(part * LANES, LANES)
        here = pl.ds(at, LANES)

        def spread_out(line):
            return jnp.broadcast_to(line, (8, LANES))

        fx, fy, fz = (spread_out(frac_ref[d : d + 1, here]) for d in range(3))
        vx, vy, vz = (spread_out(vel_ref[d : d + 1, here]) for d in range(3))
        held = spread_out(jnp.where(at + lane < count, mass_ref[pl.ds(part, 1), :], 0.0))
        carried = jnp.where(
            field == 0, held, held * jnp.where(field == 1, vx, jnp.where(field == 2, vy, vz))
        )
        carried = carried * jnp.where(top_z, fz, 1.0 - fz)
        lower, upper = carried * (1.0 - fx), carried * fx
        rows = jnp.concatenate(
            [lower * (1.0 - fy), lower * fy, upper * (1.0 - fy), upper * fy], axis=0
        )
        high, low = split_pair(rows)
        q_ref[pl.ds(part, 1)] = jnp.concatenate([high, low], axis=0)[None]

    def prepare(group, carry):
        block, row, total = carry
        for u in range(UNROLL):
            v = group * UNROLL + u
            block, row, total = list_visit(v, block, row, total)
            weigh(v)
        return block, row, total

    start = (jnp.int32(0), listed_ref[0, 0] >> 7, jnp.int32(0))
    total = lax.fori_loop(0, steps // UNROLL, prepare, start)[2]
    plan_ref[3 * steps] = total
    plan_ref[3 * steps + 1] = count

    def visit(group, carry):
        found = []
        for u in range(UNROLL):
            v = group * UNROLL + u
            block = plan_ref[v]
            hot = one_hot(cells_ref, block, plan_ref[2 * steps + v])
            both = q_ref[pl.ds(block * 2, 2)]
            both = lax.dot_general(
                jnp.concatenate([both[0], both[1]], axis=1),
                hot,
                (((1,), (1,)), ((), ())),
                preferred_element_type=f32,
            )
            found.append((plan_ref[steps + v], both[:SPREAD] + both[SPREAD:]))
        for base, part in found:
            for k, ahead in enumerate((0, 1, NY + 1, NY + 2)):
                at = pl.ds(pl.multiple_of((base + ahead) * 8, 8), 8)
                acc_ref[at, :] += part[8 * k : 8 * k + 8]
        return carry

    lax.fori_loop(0, (total + UNROLL - 1) // UNROLL, visit, 0)

    for l in range(CX + 1):
        first = l * (NY + 1) * 8
        acc_ref[first : first + 8, :] += acc_ref[first + NY * 8 : first + NY * 8 + 8, :]
        for f in range(4):
            lower = acc_ref[pl.ds(first + f, NY, stride=8), :]
            upper = acc_ref[pl.ds(first + 4 + f, NY, stride=8), :]
            summed = lower + pltpu.roll(upper, 1, 1)
            if l < CX:
                low_ref[f * CX + l] = summed
            if l > 0:
                high_ref[f * CX + l - 1] = summed


def pair_up(field, axis):
    return field + pltpu.roll(field, field.shape[axis] - 1, axis)


def step_up(field, axis):
    return pltpu.roll(field, field.shape[axis] - 1, axis) - field


def pair_down(field, axis):
    return field + pltpu.roll(field, 1, axis)


def step_down(field, axis):
    return field - pltpu.roll(field, 1, axis)


def cell_stress(vel_lo, vel_hi, mass_lo, mass_hi, keep):
    grads = []
    for a in range(3):
        diff = vel_hi[a] - vel_lo[a]
        both = vel_hi[a] + vel_lo[a]
        grads.append(
            [
                0.25 * pair_up(pair_up(diff, 0), 1),
                0.25 * pair_up(step_up(both, 0), 1),
                0.25 * step_up(pair_up(both, 0), 1),
            ]
        )
    density = 0.125 * pair_up(pair_up(mass_hi + mass_lo, 0), 1)
    dxx = grads[0][0]
    dyy = grads[1][1]
    dzz = grads[2][2]
    dxy = 0.5 * (grads[0][1] + grads[1][0])
    dxz = 0.5 * (grads[0][2] + grads[2][0])
    dyz = 0.5 * (grads[1][2] + grads[2][1])
    second = dxx * dxx + dyy * dyy + dzz * dzz + 2.0 * (dxy * dxy + dxz * dxz + dyz * dyz)
    rate = jnp.sqrt(2.0 * second + rate_floor * rate_floor)
    pressure = stiffness * density
    inertial = rate * grain_size / jnp.sqrt(pressure + press_floor)
    friction = mu_static + (mu_limit - mu_static) * inertial / (inertia_ref + inertial)
    twice = 2.0 * friction * pressure / rate
    sigma = [
        twice * dxx - pressure,
        twice * dyy - pressure,
        twice * dzz - pressure,
        twice * dxy,
        twice * dxz,
        twice * dyz,
    ]
    return [jnp.where(keep, s, 0.0) for s in sigma]


def node_force(lower, upper):
    force = []
    for a in range(3):
        sx, sy, sz = (components[a][b] for b in range(3))
        along = pair_down(pair_down(upper[sx] - lower[sx], 0), 1)
        across = step_down(pair_down(upper[sy] + lower[sy], 1), 0)
        upward = step_down(pair_down(upper[sz] + lower[sz], 0), 1)
        force.append(0.25 * (along + across + upward))
    return force


def collect_kernel(
    plan_ref, step_ref, low_ref, high_ref, left_ref, right_ref, frac_ref, vel_ref, cells_ref,
    out_ref, top_ref, tab_ref, pair_ref,
):
    blocks = frac_ref.shape[1] // BLOCK
    steps = blocks + ROWS
    total = plan_ref[3 * steps]
    count = plan_ref[3 * steps + 1]
    step = step_ref[0]
    nodes = [
        [left_ref[f * 2] for f in range(4)],
        [low_ref[f * 2] + left_ref[f * 2 + 1] for f in range(4)],
        [low_ref[f * 2 + 1] for f in range(4)],
        [high_ref[f * 2 + 1] + right_ref[f * 2] for f in range(4)],
        [right_ref[f * 2 + 1] for f in range(4)],
    ]
    height = lax.broadcasted_iota(jnp.int32, (NY, NZ), 1)
    keep = height < NZ - 1
    above_bed = height > 0
    floor = [jnp.maximum(layer[0], mass_floor) for layer in nodes]
    v_old = [[layer[1 + a] / floor[l] for a in range(3)] for l, layer in enumerate(nodes)]
    sigma = [
        cell_stress(v_old[l], v_old[l + 1], nodes[l][0], nodes[l + 1][0], keep) for l in range(4)
    ]
    blank = jnp.zeros((NY, NZ), f32)
    for l in range(CX + 1):
        force = node_force(sigma[l], sigma[l + 1])
        fields = [blank] * 8
        for a in range(3):
            layer = nodes[l + 1]
            fresh = (layer[1 + a] + step * (force[a] + layer[0] * gravity[a])) / floor[l + 1]
            fresh = jnp.where(above_bed, fresh, 0.0)
            fields[a] = fresh - flip_share * v_old[l + 1][a]
            fields[4 + a] = step * fresh
        for k, value in enumerate(fields):
            start = l * NY * TABLE + k
            tab_ref[pl.ds(start, NY, stride=TABLE), :] = value
            tab_ref[pl.ds(start + 8, NY, stride=TABLE), :] = pltpu.roll(value, NZ - 1, 1)

    for l in range(CX + 1):

        def split_row(j, carry):
            at = pl.ds(pl.multiple_of((l * NY + j) * TABLE, TABLE), TABLE)
            high, low = split_pair(tab_ref[at, :])
            pair_ref[pl.ds(l * (NY + 1) + j, 1)] = jnp.concatenate([high, low], axis=0)[None]
            return carry

        lax.fori_loop(0, NY, split_row, 0, unroll=8)
        pair_ref[l * (NY + 1) + NY] = pair_ref[l * (NY + 1)]

    out_ref[...] = jnp.zeros_like(out_ref)

    def visit(group, carry):
        found = []
        for u in range(UNROLL):
            v = group * UNROLL + u
            block = plan_ref[v]
            base = plan_ref[steps + v]
            hot = one_hot(cells_ref, block, plan_ref[2 * steps + v])
            rows = [pair_ref[base + ahead] for ahead in (0, 1, NY + 1, NY + 2)]
            both = jnp.dot(jnp.concatenate(rows, axis=0), hot, preferred_element_type=f32)
            corners = []
            for k in range(4):
                four = both[4 * 8 * k : 4 * 8 * (k + 1)]
                corners += [four[0:8] + four[16:24], four[8:16] + four[24:32]]
            frac = frac_ref[:, pl.ds(pl.multiple_of(block * BLOCK, BLOCK), BLOCK)]
            for d in (2, 1, 0):
                share = frac[d : d + 1, :]
                corners = [
                    corners[k] + share * (corners[k + 1] - corners[k])
                    for k in range(0, len(corners), 2)
                ]
            found.append((block, corners[0]))
        for block, part in found:
            out_ref[pl.ds(block, 1)] += part[None]
        return carry

    lax.fori_loop(0, (total + UNROLL - 1) // UNROLL, visit, 0)

    lane = lax.broadcasted_iota(jnp.int32, (1, BLOCK), 1)

    def finish(block, top):
        at = pl.multiple_of(block * BLOCK, BLOCK)
        alive = at + lane < count
        got = out_ref[pl.ds(block, 1)][0]
        fresh = jnp.where(alive, flip_share * vel_ref[:, pl.ds(at, BLOCK)] + got[0:3], 0.0)
        out_ref[pl.ds(block, 1), 0:3] = fresh[None]
        square = fresh[0:1] * fresh[0:1] + fresh[1:2] * fresh[1:2] + fresh[2:3] * fresh[2:3]
        return jnp.maximum(top, square)

    top = lax.fori_loop(0, blocks, finish, jnp.zeros((1, BLOCK), f32), unroll=4)
    top = jnp.sqrt(jnp.max(top, axis=1, keepdims=True))
    top_ref[...] = jnp.broadcast_to(top, top_ref.shape)


def finish_kernel(plan_ref, moved_ref, frac_ref, new_frac_ref, new_vel_ref):
    blocks = frac_ref.shape[1] // BLOCK
    count = plan_ref[3 * (blocks + ROWS) + 1]
    lane = lax.broadcasted_iota(jnp.int32, (1, BLOCK), 1)

    def finish(block, carry):
        at = pl.multiple_of(block * BLOCK, BLOCK)
        got = moved_ref[pl.ds(block, 1)][0]
        new_vel_ref[:, pl.ds(at, BLOCK)] = got[0:3]
        placed = jnp.where(at + lane < count, frac_ref[:, pl.ds(at, BLOCK)] + got[4:7], 0.0)
        new_frac_ref[:, pl.ds(at, BLOCK)] = placed
        return carry

    lax.fori_loop(0, blocks, finish, 0, unroll=4)


def largest(value, axis):
    devices = lax.axis_size(axis)
    reach = 1
    while reach < devices:
        if devices & (devices - 1) == 0:
            pairs = [(i, i ^ reach) for i in range(devices)]
        else:
            pairs = [(i, (i + reach) % devices) for i in range(devices)]
        value = jnp.maximum(value, lax.ppermute(value, axis, pairs))
        reach *= 2
    return value


smem = pl.BlockSpec(memory_space=pltpu.SMEM)
vmem = pl.BlockSpec(memory_space=pltpu.VMEM)
hbm = pl.BlockSpec(memory_space=pltpu.HBM)


def body(frac, velocity, mass, particle_cell, tile_count, time_step):
    slots = frac.shape[1]
    blocks = slots // BLOCK
    steps = blocks + ROWS
    mass_rows = mass.reshape(slots // LANES, LANES)
    cell_rows = particle_cell.reshape(slots // LANES, LANES)
    layer_pair = jax.ShapeDtypeStruct((4 * CX, NY, NZ), f32)
    low, high, plan = pl.pallas_call(
        spread_kernel,
        out_shape=(layer_pair, layer_pair, jax.ShapeDtypeStruct((4 * steps,), jnp.int32)),
        in_specs=[hbm] * 5,
        out_specs=(vmem, vmem, smem),
        scratch_shapes=[
            pltpu.SMEM((1,), jnp.int32),
            pltpu.SMEM((slots // LANES, LANES), jnp.int32),
            pltpu.VMEM((3, slots), f32),
            pltpu.VMEM((3, slots), f32),
            pltpu.VMEM((slots // LANES, LANES), f32),
            pltpu.VMEM((slots // LANES, LANES), jnp.int32),
            pltpu.VMEM((slots // LANES, 2 * SPREAD, LANES), bf16),
            pltpu.VMEM(((CX + 1) * (NY + 1) * 8, NZ), f32),
            pltpu.SemaphoreType.DMA((6,)),
        ],
        compiler_params=pltpu.CompilerParams(vmem_limit_bytes=32 * 1024 * 1024),
        name="spread",
    )(tile_count, frac, velocity, mass_rows, cell_rows)
    from_left = shifted(high, "gx", 1)
    from_right = shifted(low, "gx", -1)
    moved, top = pl.pallas_call(
        collect_kernel,
        out_shape=(
            jax.ShapeDtypeStruct((blocks, 8, BLOCK), f32),
            jax.ShapeDtypeStruct((8, LANES), f32),
        ),
        in_specs=[smem] * 2 + [vmem] * 7,
        out_specs=(vmem, vmem),
        scratch_shapes=[
            pltpu.VMEM(((CX + 1) * NY * TABLE, NZ), f32),
            pltpu.VMEM(((CX + 1) * (NY + 1), 2 * TABLE, NZ), bf16),
        ],
        compiler_params=pltpu.CompilerParams(vmem_limit_bytes=32 * 1024 * 1024),
        name="collect",
    )(plan, time_step, low, high, from_left, from_right, frac, velocity, cell_rows)
    new_frac, new_velocity = pl.pallas_call(
        finish_kernel,
        out_shape=(
            jax.ShapeDtypeStruct(frac.shape, f32),
            jax.ShapeDtypeStruct(velocity.shape, f32),
        ),
        in_specs=[smem] + [vmem] * 2,
        out_specs=(vmem, vmem),
        compiler_params=pltpu.CompilerParams(vmem_limit_bytes=32 * 1024 * 1024),
        cost_estimate=pl.CostEstimate(flops=0, bytes_accessed=8000000, transcendentals=0),
        name="finish",
    )(plan, moved, frac)
    fastest = largest(top, "gx")
    next_step = (courant / (fastest + wave_speed))[0, :1]
    return (new_frac, new_velocity, next_step)


def solution(mesh):
    placed = (
        P(None, ("runs", "gx")),
        P(None, ("runs", "gx")),
        P(("runs", "gx")),
        P(("runs", "gx")),
        P(("runs", "gx")),
        P("runs"),
    )
    return jax.shard_map(
        body,
        mesh=mesh,
        in_specs=placed,
        out_specs=(P(None, ("runs", "gx")), P(None, ("runs", "gx")), P("runs")),
        check_vma=False,
    )
```

```python
import functools

import jax
import jax.numpy as jnp
from jax import lax
from jax.experimental import pallas as pl
from jax.experimental.pallas import tpu as pltpu
from jax.sharding import PartitionSpec as P

CX = 2
NY = 32
NZ = 128
ROWS = CX * NY
BLOCK = 256
LANES = 128
UNROLL = 8
SPREAD = 32
TABLE = 16

mass_floor = 0.25
stiffness = 2.0
press_floor = 1.0
grain_size = 0.5
inertia_ref = 0.3
mu_static = 0.38
mu_limit = 0.64
rate_floor = 0.5
gravity = (0.5, 0.0, -0.866)
flip_share = 0.95
courant = 0.4
wave_speed = 2.0
components = ((0, 3, 4), (3, 1, 5), (4, 5, 2))
f32 = jnp.float32
bf16 = jnp.bfloat16


def shifted(array, axis, by):
    devices = lax.axis_size(axis)
    return lax.ppermute(array, axis, [(i, (i + by) % devices) for i in range(devices)])


def split_pair(values):
    high = values.astype(bf16)
    low = (values - high.astype(f32)).astype(bf16)
    return high, low


def one_hot(cells_ref, block, offset):
    rel = cells_ref[pl.ds(block * 2, 2), :] - offset
    nodes = lax.broadcasted_iota(jnp.int32, (NZ, LANES), 0)
    halves = [jnp.where(nodes == rel[h : h + 1, :], 1.0, 0.0) for h in range(2)]
    return jnp.concatenate(halves, axis=1).astype(bf16)


def list_visits(cells_ref, count, plan_ref):
    blocks = cells_ref.shape[0] // 2
    shape = (blocks, LANES)
    number = lax.broadcasted_iota(jnp.int32, shape, 0)
    lane = lax.broadcasted_iota(jnp.int32, shape, 1)
    first_half = cells_ref[pl.ds(0, blocks, stride=2), :]
    second_half = cells_ref[pl.ds(1, blocks, stride=2), :]
    slot = number * BLOCK + lane
    reached = jnp.maximum(
        jnp.where(slot < count, first_half, 0), jnp.where(slot + LANES < count, second_half, 0)
    )
    live = number * BLOCK < count
    first = jnp.min(first_half, axis=1, keepdims=True) >> 7
    last = jnp.max(reached, axis=1, keepdims=True) >> 7
    low = jnp.where(live, first + number, 2 * LANES)
    high = jnp.where(live, last + number, -1)
    inside = (low <= lane) & (lane <= high)
    place = lane[:1]
    block = jnp.max(jnp.where(inside, number, -1), axis=0, keepdims=True)
    valid = block >= 0
    row = place - block
    plan_ref[0:1, :] = jnp.where(valid, block, 0)
    plan_ref[1:2, :] = jnp.where(valid, row + (row >> 5), 0)
    plan_ref[2:3, :] = jnp.where(valid, row, ROWS) * NZ
    plan_ref[3:4, :] = jnp.max(high, axis=0, keepdims=True) + 1
    plan_ref[4:5, :] = jnp.broadcast_to(count, (1, LANES))
    plan_ref[5:8, :] = jnp.zeros((3, LANES), jnp.int32)


def spread_kernel(
    count_ref, frac_hbm, vel_hbm, mass_hbm, cells_hbm,
    low_ref, high_ref, plan_ref, frac_ref, vel_ref, cells_ref,
    listed_ref, mass_ref, q_ref, acc_ref, sems,
):
    slots = frac_ref.shape[1]
    sources = (cells_hbm, frac_hbm, vel_hbm, mass_hbm)
    targets = (cells_ref, frac_ref, vel_ref, mass_ref)
    arrivals = [
        pltpu.make_async_copy(source, target, sems.at[k])
        for k, (source, target) in enumerate(zip(sources, targets))
    ]
    for arrival in arrivals:
        arrival.start()
    acc_ref[...] = jnp.zeros_like(acc_ref)
    arrivals[0].wait()
    count = count_ref[0]
    list_visits(cells_ref, count, plan_ref)
    listing = pltpu.make_async_copy(plan_ref, listed_ref, sems.at[4])
    listing.start()
    for arrival in arrivals[1:]:
        arrival.wait()
    sublane = lax.broadcasted_iota(jnp.int32, (8, LANES), 0)
    lane = lax.broadcasted_iota(jnp.int32, (1, LANES), 1)
    top_z = sublane >= 4
    field = sublane & 3

    def weigh(part):
        at = pl.multiple_of(part * LANES, LANES)
        here = pl.ds(at, LANES)

        def spread_out(line):
            return jnp.broadcast_to(line, (8, LANES))

        fx, fy, fz = (spread_out(frac_ref[d : d + 1, here]) for d in range(3))
        vx, vy, vz = (spread_out(vel_ref[d : d + 1, here]) for d in range(3))
        held = spread_out(jnp.where(at + lane < count, mass_ref[pl.ds(part, 1), :], 0.0))
        carried = jnp.where(
            field == 0, held, held * jnp.where(field == 1, vx, jnp.where(field == 2, vy, vz))
        )
        carried = carried * jnp.where(top_z, fz, 1.0 - fz)
        lower, upper = carried * (1.0 - fx), carried * fx
        rows = jnp.concatenate(
            [lower * (1.0 - fy), lower * fy, upper * (1.0 - fy), upper * fy], axis=0
        )
        high, low = split_pair(rows)
        q_ref[pl.ds(part, 1)] = jnp.concatenate([high, low], axis=0)[None]

    def prepare(group, carry):
        for u in range(UNROLL):
            weigh(group * UNROLL + u)
        return carry

    lax.fori_loop(0, slots // LANES // UNROLL, prepare, 0)
    listing.wait()
    total = listed_ref[3, 0]

    def visit(group, carry):
        found = []
        for u in range(UNROLL):
            v = group * UNROLL + u
            block = listed_ref[0, v]
            hot = one_hot(cells_ref, block, listed_ref[2, v])
            both = q_ref[pl.ds(block * 2, 2)]
            both = lax.dot_general(
                jnp.concatenate([both[0], both[1]], axis=1),
                hot,
                (((1,), (1,)), ((), ())),
                preferred_element_type=f32,
            )
            found.append((listed_ref[1, v], both[:SPREAD] + both[SPREAD:]))
        for base, part in found:
            for k, ahead in enumerate((0, 1, NY + 1, NY + 2)):
                at = pl.ds(pl.multiple_of((base + ahead) * 8, 8), 8)
                acc_ref[at, :] += part[8 * k : 8 * k + 8]
        return carry

    lax.fori_loop(0, (total + UNROLL - 1) // UNROLL, visit, 0)

    for l in range(CX + 1):
        first = l * (NY + 1) * 8
        acc_ref[first : first + 8, :] += acc_ref[first + NY * 8 : first + NY * 8 + 8, :]
        for f in range(4):
            lower = acc_ref[pl.ds(first + f, NY, stride=8), :]
            upper = acc_ref[pl.ds(first + 4 + f, NY, stride=8), :]
            summed = lower + pltpu.roll(upper, 1, 1)
            if l < CX:
                low_ref[f * CX + l] = summed
            if l > 0:
                high_ref[f * CX + l - 1] = summed


def pair_up(field, axis):
    return field + pltpu.roll(field, field.shape[axis] - 1, axis)


def step_up(field, axis):
    return pltpu.roll(field, field.shape[axis] - 1, axis) - field


def pair_down(field, axis):
    return field + pltpu.roll(field, 1, axis)


def step_down(field, axis):
    return field - pltpu.roll(field, 1, axis)


def cell_stress(vel_lo, vel_hi, mass_lo, mass_hi, keep):
    grads = []
    for a in range(3):
        diff = vel_hi[a] - vel_lo[a]
        both = vel_hi[a] + vel_lo[a]
        grads.append(
            [
                0.25 * pair_up(pair_up(diff, 0), 1),
                0.25 * pair_up(step_up(both, 0), 1),
                0.25 * step_up(pair_up(both, 0), 1),
            ]
        )
    density = 0.125 * pair_up(pair_up(mass_hi + mass_lo, 0), 1)
    dxx = grads[0][0]
    dyy = grads[1][1]
    dzz = grads[2][2]
    dxy = 0.5 * (grads[0][1] + grads[1][0])
    dxz = 0.5 * (grads[0][2] + grads[2][0])
    dyz = 0.5 * (grads[1][2] + grads[2][1])
    second = dxx * dxx + dyy * dyy + dzz * dzz + 2.0 * (dxy * dxy + dxz * dxz + dyz * dyz)
    rate = jnp.sqrt(2.0 * second + rate_floor * rate_floor)
    pressure = stiffness * density
    inertial = rate * grain_size / jnp.sqrt(pressure + press_floor)
    friction = mu_static + (mu_limit - mu_static) * inertial / (inertia_ref + inertial)
    twice = 2.0 * friction * pressure / rate
    sigma = [
        twice * dxx - pressure,
        twice * dyy - pressure,
        twice * dzz - pressure,
        twice * dxy,
        twice * dxz,
        twice * dyz,
    ]
    return [jnp.where(keep, s, 0.0) for s in sigma]


def node_force(lower, upper):
    force = []
    for a in range(3):
        sx, sy, sz = (components[a][b] for b in range(3))
        along = pair_down(pair_down(upper[sx] - lower[sx], 0), 1)
        across = step_down(pair_down(upper[sy] + lower[sy], 1), 0)
        upward = step_down(pair_down(upper[sz] + lower[sz], 0), 1)
        force.append(0.25 * (along + across + upward))
    return force


def collect_kernel(
    step_ref, plan_ref, low_ref, high_ref, left_ref, right_ref, frac_ref, vel_ref, cells_ref,
    out_ref, top_ref, listed_ref, tab_ref, pair_ref, sem,
):
    blocks = frac_ref.shape[1] // BLOCK
    listing = pltpu.make_async_copy(plan_ref, listed_ref, sem)
    listing.start()
    step = step_ref[0]
    nodes = [
        [left_ref[f * 2] for f in range(4)],
        [low_ref[f * 2] + left_ref[f * 2 + 1] for f in range(4)],
        [low_ref[f * 2 + 1] for f in range(4)],
        [high_ref[f * 2 + 1] + right_ref[f * 2] for f in range(4)],
        [right_ref[f * 2 + 1] for f in range(4)],
    ]
    height = lax.broadcasted_iota(jnp.int32, (NY, NZ), 1)
    keep = height < NZ - 1
    above_bed = height > 0
    floor = [jnp.maximum(layer[0], mass_floor) for layer in nodes]
    v_old = [[layer[1 + a] / floor[l] for a in range(3)] for l, layer in enumerate(nodes)]
    sigma = [
        cell_stress(v_old[l], v_old[l + 1], nodes[l][0], nodes[l + 1][0], keep) for l in range(4)
    ]
    blank = jnp.zeros((NY, NZ), f32)
    for l in range(CX + 1):
        force = node_force(sigma[l], sigma[l + 1])
        fields = [blank] * 8
        for a in range(3):
            layer = nodes[l + 1]
            fresh = (layer[1 + a] + step * (force[a] + layer[0] * gravity[a])) / floor[l + 1]
            fresh = jnp.where(above_bed, fresh, 0.0)
            fields[a] = fresh - flip_share * v_old[l + 1][a]
            fields[4 + a] = step * fresh
        for k, value in enumerate(fields):
            start = l * NY * TABLE + k
            tab_ref[pl.ds(start, NY, stride=TABLE), :] = value
            tab_ref[pl.ds(start + 8, NY, stride=TABLE), :] = pltpu.roll(value, NZ - 1, 1)

    for l in range(CX + 1):

        def split_row(j, carry):
            at = pl.ds(pl.multiple_of((l * NY + j) * TABLE, TABLE), TABLE)
            high, low = split_pair(tab_ref[at, :])
            pair_ref[pl.ds(l * (NY + 1) + j, 1)] = jnp.concatenate([high, low], axis=0)[None]
            return carry

        lax.fori_loop(0, NY, split_row, 0, unroll=8)
        pair_ref[l * (NY + 1) + NY] = pair_ref[l * (NY + 1)]

    out_ref[...] = jnp.zeros_like(out_ref)
    listing.wait()
    total = listed_ref[3, 0]
    count = listed_ref[4, 0]

    def visit(group, carry):
        found = []
        for u in range(UNROLL):
            v = group * UNROLL + u
            block = listed_ref[0, v]
            base = listed_ref[1, v]
            hot = one_hot(cells_ref, block, listed_ref[2, v])
            rows = [pair_ref[base + ahead] for ahead in (0, 1, NY + 1, NY + 2)]
            both = jnp.dot(jnp.concatenate(rows, axis=0), hot, preferred_element_type=f32)
            corners = []
            for k in range(4):
                four = both[4 * 8 * k : 4 * 8 * (k + 1)]
                corners += [four[0:8] + four[16:24], four[8:16] + four[24:32]]
            frac = frac_ref[:, pl.ds(pl.multiple_of(block * BLOCK, BLOCK), BLOCK)]
            for d in (2, 1, 0):
                share = frac[d : d + 1, :]
                corners = [
                    corners[k] + share * (corners[k + 1] - corners[k])
                    for k in range(0, len(corners), 2)
                ]
            found.append((block, corners[0]))
        for block, part in found:
            out_ref[pl.ds(block, 1)] += part[None]
        return carry

    lax.fori_loop(0, (total + UNROLL - 1) // UNROLL, visit, 0)

    lane = lax.broadcasted_iota(jnp.int32, (1, BLOCK), 1)

    def finish(block, top):
        at = pl.multiple_of(block * BLOCK, BLOCK)
        alive = at + lane < count
        got = out_ref[pl.ds(block, 1)][0]
        fresh = jnp.where(alive, flip_share * vel_ref[:, pl.ds(at, BLOCK)] + got[0:3], 0.0)
        out_ref[pl.ds(block, 1), 0:3] = fresh[None]
        square = fresh[0:1] * fresh[0:1] + fresh[1:2] * fresh[1:2] + fresh[2:3] * fresh[2:3]
        return jnp.maximum(top, square)

    top = lax.fori_loop(0, blocks, finish, jnp.zeros((1, BLOCK), f32), unroll=4)
    top = jnp.sqrt(jnp.max(top, axis=1, keepdims=True))
    top_ref[...] = jnp.broadcast_to(top, top_ref.shape)


def finish_kernel(plan_ref, moved_ref, frac_ref, new_frac_ref, new_vel_ref):
    blocks = frac_ref.shape[1] // BLOCK
    count = plan_ref[4:5, :]
    count = jnp.concatenate([count, count], axis=1)
    lane = lax.broadcasted_iota(jnp.int32, (1, BLOCK), 1)

    def finish(block, carry):
        at = pl.multiple_of(block * BLOCK, BLOCK)
        got = moved_ref[pl.ds(block, 1)][0]
        new_vel_ref[:, pl.ds(at, BLOCK)] = got[0:3]
        placed = jnp.where(at + lane < count, frac_ref[:, pl.ds(at, BLOCK)] + got[4:7], 0.0)
        new_frac_ref[:, pl.ds(at, BLOCK)] = placed
        return carry

    lax.fori_loop(0, blocks, finish, 0, unroll=4)


def largest(value, axis):
    devices = lax.axis_size(axis)
    reach = 1
    while reach < devices:
        if devices & (devices - 1) == 0:
            pairs = [(i, i ^ reach) for i in range(devices)]
        else:
            pairs = [(i, (i + reach) % devices) for i in range(devices)]
        value = jnp.maximum(value, lax.ppermute(value, axis, pairs))
        reach *= 2
    return value


smem = pl.BlockSpec(memory_space=pltpu.SMEM)
vmem = pl.BlockSpec(memory_space=pltpu.VMEM)
hbm = pl.BlockSpec(memory_space=pltpu.HBM)


def body(frac, velocity, mass, particle_cell, tile_count, time_step):
    slots = frac.shape[1]
    blocks = slots // BLOCK
    rows = slots // LANES
    inputs = (frac, velocity, mass.reshape(rows, LANES), particle_cell.reshape(rows, LANES))
    layer_pair = pltpu.VMEM((4 * CX, NY, NZ), f32)
    low, high, plan, frac_here, vel_here, cells_here = pl.pallas_call(
        spread_kernel,
        out_shape=(
            layer_pair,
            layer_pair,
            pltpu.VMEM((8, LANES), jnp.int32),
            pltpu.VMEM(frac.shape, f32),
            pltpu.VMEM(velocity.shape, f32),
            pltpu.VMEM((rows, LANES), jnp.int32),
        ),
        in_specs=[smem] + [hbm] * 4,
        out_specs=(vmem,) * 6,
        scratch_shapes=[
            pltpu.SMEM((8, LANES), jnp.int32),
            pltpu.VMEM((rows, LANES), f32),
            pltpu.VMEM((rows, 2 * SPREAD, LANES), bf16),
            pltpu.VMEM(((CX + 1) * (NY + 1) * 8, NZ), f32),
            pltpu.SemaphoreType.DMA((5,)),
        ],
        compiler_params=pltpu.CompilerParams(vmem_limit_bytes=32 * 1024 * 1024),
        name="spread",
    )(tile_count, *[pltpu.with_memory_space_constraint(x, pltpu.HBM) for x in inputs])
    from_left = shifted(high, "gx", 1)
    from_right = shifted(low, "gx", -1)
    moved, top = pl.pallas_call(
        collect_kernel,
        out_shape=(
            jax.ShapeDtypeStruct((blocks, 8, BLOCK), f32),
            jax.ShapeDtypeStruct((8, LANES), f32),
        ),
        in_specs=[smem] + [vmem] * 8,
        out_specs=(vmem, vmem),
        scratch_shapes=[
            pltpu.SMEM((8, LANES), jnp.int32),
            pltpu.VMEM(((CX + 1) * NY * TABLE, NZ), f32),
            pltpu.VMEM(((CX + 1) * (NY + 1), 2 * TABLE, NZ), bf16),
            pltpu.SemaphoreType.DMA,
        ],
        compiler_params=pltpu.CompilerParams(vmem_limit_bytes=32 * 1024 * 1024),
        name="collect",
    )(time_step, plan, low, high, from_left, from_right, frac_here, vel_here, cells_here)
    new_frac, new_velocity = pl.pallas_call(
        finish_kernel,
        out_shape=(
            jax.ShapeDtypeStruct(frac.shape, f32),
            jax.ShapeDtypeStruct(velocity.shape, f32),
        ),
        in_specs=[vmem] * 3,
        out_specs=(vmem, vmem),
        compiler_params=pltpu.CompilerParams(vmem_limit_bytes=32 * 1024 * 1024),
        cost_estimate=pl.CostEstimate(flops=0, bytes_accessed=8000000, transcendentals=0),
        name="finish",
    )(plan, moved, frac_here)
    fastest = largest(top, "gx")
    next_step = (courant / (fastest + wave_speed))[0, :1]
    return (new_frac, new_velocity, next_step)


def solution(mesh):
    placed = (
        P(None, ("runs", "gx")),
        P(None, ("runs", "gx")),
        P(("runs", "gx")),
        P(("runs", "gx")),
        P(("runs", "gx")),
        P("runs"),
    )
    return jax.shard_map(
        body,
        mesh=mesh,
        in_specs=placed,
        out_specs=(P(None, ("runs", "gx")), P(None, ("runs", "gx")), P("runs")),
        check_vma=False,
    )
```

```python
import functools

import jax
import jax.numpy as jnp
from jax import lax
from jax.experimental import pallas as pl
from jax.experimental.pallas import tpu as pltpu
from jax.sharding import PartitionSpec as P

CX = 2
NY = 32
NZ = 128
ROWS = CX * NY
BLOCK = 256
LANES = 128
UNROLL = 8
SPREAD = 32
TABLE = 16

mass_floor = 0.25
stiffness = 2.0
press_floor = 1.0
grain_size = 0.5
inertia_ref = 0.3
mu_static = 0.38
mu_limit = 0.64
rate_floor = 0.5
gravity = (0.5, 0.0, -0.866)
flip_share = 0.95
courant = 0.4
wave_speed = 2.0
components = ((0, 3, 4), (3, 1, 5), (4, 5, 2))
f32 = jnp.float32
bf16 = jnp.bfloat16


def split_pair(values):
    high = values.astype(bf16)
    low = (values - high.astype(f32)).astype(bf16)
    return high, low


def one_hot(cells_ref, block, offset):
    rel = cells_ref[pl.ds(block * 2, 2), :] - offset
    nodes = lax.broadcasted_iota(jnp.int32, (NZ, LANES), 0)
    halves = [jnp.where(nodes == rel[h : h + 1, :], 1.0, 0.0) for h in range(2)]
    return jnp.concatenate(halves, axis=1).astype(bf16)


def list_visits(cells_ref, count, plan_ref):
    blocks = cells_ref.shape[0] // 2
    shape = (blocks, LANES)
    number = lax.broadcasted_iota(jnp.int32, shape, 0)
    lane = lax.broadcasted_iota(jnp.int32, shape, 1)
    first_half = cells_ref[pl.ds(0, blocks, stride=2), :]
    second_half = cells_ref[pl.ds(1, blocks, stride=2), :]
    slot = number * BLOCK + lane
    reached = jnp.maximum(
        jnp.where(slot < count, first_half, 0), jnp.where(slot + LANES < count, second_half, 0)
    )
    live = number * BLOCK < count
    first = jnp.min(first_half, axis=1, keepdims=True) >> 7
    last = jnp.max(reached, axis=1, keepdims=True) >> 7
    low = jnp.where(live, first + number, 2 * LANES)
    high = jnp.where(live, last + number, -1)
    inside = (low <= lane) & (lane <= high)
    place = lane[:1]
    block = jnp.max(jnp.where(inside, number, -1), axis=0, keepdims=True)
    valid = block >= 0
    row = place - block
    plan_ref[0:1, :] = jnp.where(valid, block, 0)
    plan_ref[1:2, :] = jnp.where(valid, row + (row >> 5), 0)
    plan_ref[2:3, :] = jnp.where(valid, row, ROWS) * NZ
    plan_ref[3:4, :] = jnp.max(high, axis=0, keepdims=True) + 1
    plan_ref[4:5, :] = jnp.broadcast_to(count, (1, LANES))
    plan_ref[5:8, :] = jnp.zeros((3, LANES), jnp.int32)


def spread_kernel(
    count_ref, frac_hbm, vel_hbm, mass_hbm, cells_hbm,
    far_ref, near_ref, plan_ref, frac_ref, vel_ref, cells_ref,
    listed_ref, mass_ref, q_ref, acc_ref, sems,
):
    slots = frac_ref.shape[1]
    sources = (cells_hbm, frac_hbm, vel_hbm, mass_hbm)
    targets = (cells_ref, frac_ref, vel_ref, mass_ref)
    arrivals = [
        pltpu.make_async_copy(source, target, sems.at[k])
        for k, (source, target) in enumerate(zip(sources, targets))
    ]
    for arrival in arrivals:
        arrival.start()
    acc_ref[...] = jnp.zeros_like(acc_ref)
    arrivals[0].wait()
    count = count_ref[0]
    list_visits(cells_ref, count, plan_ref)
    listing = pltpu.make_async_copy(plan_ref, listed_ref, sems.at[4])
    listing.start()
    for arrival in arrivals[1:]:
        arrival.wait()
    sublane = lax.broadcasted_iota(jnp.int32, (8, LANES), 0)
    lane = lax.broadcasted_iota(jnp.int32, (1, LANES), 1)
    top_z = sublane >= 4
    field = sublane & 3

    def weigh(part):
        at = pl.multiple_of(part * LANES, LANES)
        here = pl.ds(at, LANES)

        def spread_out(line):
            return jnp.broadcast_to(line, (8, LANES))

        fx, fy, fz = (spread_out(frac_ref[d : d + 1, here]) for d in range(3))
        vx, vy, vz = (spread_out(vel_ref[d : d + 1, here]) for d in range(3))
        held = spread_out(jnp.where(at + lane < count, mass_ref[pl.ds(part, 1), :], 0.0))
        carried = jnp.where(
            field == 0, held, held * jnp.where(field == 1, vx, jnp.where(field == 2, vy, vz))
        )
        carried = carried * jnp.where(top_z, fz, 1.0 - fz)
        lower, upper = carried * (1.0 - fx), carried * fx
        rows = jnp.concatenate(
            [lower * (1.0 - fy), lower * fy, upper * (1.0 - fy), upper * fy], axis=0
        )
        high, low = split_pair(rows)
        q_ref[pl.ds(part, 1)] = jnp.concatenate([high, low], axis=0)[None]

    def prepare(group, carry):
        for u in range(UNROLL):
            weigh(group * UNROLL + u)
        return carry

    lax.fori_loop(0, slots // LANES // UNROLL, prepare, 0)
    listing.wait()
    total = listed_ref[3, 0]

    def visit(group, carry):
        found = []
        for u in range(UNROLL):
            v = group * UNROLL + u
            block = listed_ref[0, v]
            hot = one_hot(cells_ref, block, listed_ref[2, v])
            both = q_ref[pl.ds(block * 2, 2)]
            both = lax.dot_general(
                jnp.concatenate([both[0], both[1]], axis=1),
                hot,
                (((1,), (1,)), ((), ())),
                preferred_element_type=f32,
            )
            found.append((listed_ref[1, v], both[:SPREAD] + both[SPREAD:]))
        for base, part in found:
            for k, ahead in enumerate((0, 1, NY + 1, NY + 2)):
                at = pl.ds(pl.multiple_of((base + ahead) * 8, 8), 8)
                acc_ref[at, :] += part[8 * k : 8 * k + 8]
        return carry

    lax.fori_loop(0, (total + UNROLL - 1) // UNROLL, visit, 0)

    layers = []
    for l in range(CX + 1):
        first = l * (NY + 1) * 8
        acc_ref[first : first + 8, :] += acc_ref[first + NY * 8 : first + NY * 8 + 8, :]
        for f in range(4):
            lower = acc_ref[pl.ds(first + f, NY, stride=8), :]
            upper = acc_ref[pl.ds(first + 4 + f, NY, stride=8), :]
            layers.append(lower + pltpu.roll(upper, 1, 1))
    odd = lax.axis_index("gx") % 2 == 1
    for l in range(CX):
        for f in range(4):
            low, high = layers[l * 4 + f], layers[(l + 1) * 4 + f]
            near_ref[f * CX + l] = jnp.where(odd, low, high)
            far_ref[f * CX + l] = jnp.where(odd, high, low)


def pair_up(field, axis):
    return field + pltpu.roll(field, field.shape[axis] - 1, axis)


def step_up(field, axis):
    return pltpu.roll(field, field.shape[axis] - 1, axis) - field


def pair_down(field, axis):
    return field + pltpu.roll(field, 1, axis)


def step_down(field, axis):
    return field - pltpu.roll(field, 1, axis)


def cell_stress(vel_lo, vel_hi, mass_lo, mass_hi, keep):
    grads = []
    for a in range(3):
        diff = vel_hi[a] - vel_lo[a]
        both = vel_hi[a] + vel_lo[a]
        grads.append(
            [
                0.25 * pair_up(pair_up(diff, 0), 1),
                0.25 * pair_up(step_up(both, 0), 1),
                0.25 * step_up(pair_up(both, 0), 1),
            ]
        )
    density = 0.125 * pair_up(pair_up(mass_hi + mass_lo, 0), 1)
    dxx = grads[0][0]
    dyy = grads[1][1]
    dzz = grads[2][2]
    dxy = 0.5 * (grads[0][1] + grads[1][0])
    dxz = 0.5 * (grads[0][2] + grads[2][0])
    dyz = 0.5 * (grads[1][2] + grads[2][1])
    second = dxx * dxx + dyy * dyy + dzz * dzz + 2.0 * (dxy * dxy + dxz * dxz + dyz * dyz)
    rate = jnp.sqrt(2.0 * second + rate_floor * rate_floor)
    pressure = stiffness * density
    inertial = rate * grain_size / jnp.sqrt(pressure + press_floor)
    friction = mu_static + (mu_limit - mu_static) * inertial / (inertia_ref + inertial)
    twice = 2.0 * friction * pressure / rate
    sigma = [
        twice * dxx - pressure,
        twice * dyy - pressure,
        twice * dzz - pressure,
        twice * dxy,
        twice * dxz,
        twice * dyz,
    ]
    return [jnp.where(keep, s, 0.0) for s in sigma]


def node_force(lower, upper):
    force = []
    for a in range(3):
        sx, sy, sz = (components[a][b] for b in range(3))
        along = pair_down(pair_down(upper[sx] - lower[sx], 0), 1)
        across = step_down(pair_down(upper[sy] + lower[sy], 1), 0)
        upward = step_down(pair_down(upper[sz] + lower[sz], 0), 1)
        force.append(0.25 * (along + across + upward))
    return force


def collect_kernel(
    step_ref, plan_ref, near_ref, far_ref, far_new_ref, near_new_ref, frac_ref, vel_ref, cells_ref,
    out_ref, top_ref, listed_ref, tab_ref, pair_ref, sem,
):
    blocks = frac_ref.shape[1] // BLOCK
    listing = pltpu.make_async_copy(plan_ref, listed_ref, sem)
    listing.start()
    step = step_ref[0]
    odd = lax.axis_index("gx") % 2 == 1

    def pick(if_odd, if_even):
        return [jnp.where(odd, if_odd[k], if_even[k]) for k in range(4 * CX)]

    low, high = pick(near_ref, far_ref), pick(far_ref, near_ref)
    left, right = pick(near_new_ref, far_new_ref), pick(far_new_ref, near_new_ref)
    nodes = [
        [left[f * 2] for f in range(4)],
        [low[f * 2] + left[f * 2 + 1] for f in range(4)],
        [low[f * 2 + 1] for f in range(4)],
        [high[f * 2 + 1] + right[f * 2] for f in range(4)],
        [right[f * 2 + 1] for f in range(4)],
    ]
    height = lax.broadcasted_iota(jnp.int32, (NY, NZ), 1)
    keep = height < NZ - 1
    above_bed = height > 0
    floor = [jnp.maximum(layer[0], mass_floor) for layer in nodes]
    v_old = [[layer[1 + a] / floor[l] for a in range(3)] for l, layer in enumerate(nodes)]
    sigma = [
        cell_stress(v_old[l], v_old[l + 1], nodes[l][0], nodes[l + 1][0], keep) for l in range(4)
    ]
    blank = jnp.zeros((NY, NZ), f32)
    for l in range(CX + 1):
        force = node_force(sigma[l], sigma[l + 1])
        fields = [blank] * 8
        for a in range(3):
            layer = nodes[l + 1]
            fresh = (layer[1 + a] + step * (force[a] + layer[0] * gravity[a])) / floor[l + 1]
            fresh = jnp.where(above_bed, fresh, 0.0)
            fields[a] = fresh - flip_share * v_old[l + 1][a]
            fields[4 + a] = step * fresh
        for k, value in enumerate(fields):
            start = l * NY * TABLE + k
            tab_ref[pl.ds(start, NY, stride=TABLE), :] = value
            tab_ref[pl.ds(start + 8, NY, stride=TABLE), :] = pltpu.roll(value, NZ - 1, 1)

    for l in range(CX + 1):

        def split_row(j, carry):
            at = pl.ds(pl.multiple_of((l * NY + j) * TABLE, TABLE), TABLE)
            high, low = split_pair(tab_ref[at, :])
            pair_ref[pl.ds(l * (NY + 1) + j, 1)] = jnp.concatenate([high, low], axis=0)[None]
            return carry

        lax.fori_loop(0, NY, split_row, 0, unroll=8)
        pair_ref[l * (NY + 1) + NY] = pair_ref[l * (NY + 1)]

    out_ref[...] = jnp.zeros_like(out_ref)
    listing.wait()
    total = listed_ref[3, 0]
    count = listed_ref[4, 0]

    def visit(group, carry):
        found = []
        for u in range(UNROLL):
            v = group * UNROLL + u
            block = listed_ref[0, v]
            base = listed_ref[1, v]
            hot = one_hot(cells_ref, block, listed_ref[2, v])
            rows = [pair_ref[base + ahead] for ahead in (0, 1, NY + 1, NY + 2)]
            both = jnp.dot(jnp.concatenate(rows, axis=0), hot, preferred_element_type=f32)
            corners = []
            for k in range(4):
                four = both[4 * 8 * k : 4 * 8 * (k + 1)]
                corners += [four[0:8] + four[16:24], four[8:16] + four[24:32]]
            frac = frac_ref[:, pl.ds(pl.multiple_of(block * BLOCK, BLOCK), BLOCK)]
            for d in (2, 1, 0):
                share = frac[d : d + 1, :]
                corners = [
                    corners[k] + share * (corners[k + 1] - corners[k])
                    for k in range(0, len(corners), 2)
                ]
            found.append((block, corners[0]))
        for block, part in found:
            out_ref[pl.ds(block, 1)] += part[None]
        return carry

    lax.fori_loop(0, (total + UNROLL - 1) // UNROLL, visit, 0)

    lane = lax.broadcasted_iota(jnp.int32, (1, BLOCK), 1)

    def finish(block, top):
        at = pl.multiple_of(block * BLOCK, BLOCK)
        alive = at + lane < count
        got = out_ref[pl.ds(block, 1)][0]
        fresh = jnp.where(alive, flip_share * vel_ref[:, pl.ds(at, BLOCK)] + got[0:3], 0.0)
        out_ref[pl.ds(block, 1), 0:3] = fresh[None]
        square = fresh[0:1] * fresh[0:1] + fresh[1:2] * fresh[1:2] + fresh[2:3] * fresh[2:3]
        return jnp.maximum(top, square)

    top = lax.fori_loop(0, blocks, finish, jnp.zeros((1, BLOCK), f32), unroll=4)
    top = jnp.sqrt(jnp.max(top, axis=1, keepdims=True))
    top_ref[...] = jnp.broadcast_to(top, top_ref.shape)


def finish_kernel(plan_ref, moved_ref, frac_ref, new_frac_ref, new_vel_ref):
    blocks = frac_ref.shape[1] // BLOCK
    count = plan_ref[4:5, :]
    count = jnp.concatenate([count, count], axis=1)
    lane = lax.broadcasted_iota(jnp.int32, (1, BLOCK), 1)

    def finish(block, carry):
        at = pl.multiple_of(block * BLOCK, BLOCK)
        got = moved_ref[pl.ds(block, 1)][0]
        new_vel_ref[:, pl.ds(at, BLOCK)] = got[0:3]
        placed = jnp.where(at + lane < count, frac_ref[:, pl.ds(at, BLOCK)] + got[4:7], 0.0)
        new_frac_ref[:, pl.ds(at, BLOCK)] = placed
        return carry

    lax.fori_loop(0, blocks, finish, 0, unroll=4)


def largest(value, axis):
    devices = lax.axis_size(axis)
    reach = 1
    while reach < devices:
        if devices & (devices - 1) == 0:
            pairs = [(i, i ^ reach) for i in range(devices)]
        else:
            pairs = [(i, (i + reach) % devices) for i in range(devices)]
        value = jnp.maximum(value, lax.ppermute(value, axis, pairs))
        reach *= 2
    return value


smem = pl.BlockSpec(memory_space=pltpu.SMEM)
vmem = pl.BlockSpec(memory_space=pltpu.VMEM)
hbm = pl.BlockSpec(memory_space=pltpu.HBM)


def body(frac, velocity, mass, particle_cell, tile_count, time_step):
    slots = frac.shape[1]
    blocks = slots // BLOCK
    rows = slots // LANES
    inputs = (frac, velocity, mass.reshape(rows, LANES), particle_cell.reshape(rows, LANES))
    layer_pair = pltpu.VMEM((4 * CX, NY, NZ), f32)
    far, near, plan, frac_here, vel_here, cells_here = pl.pallas_call(
        spread_kernel,
        out_shape=(
            layer_pair,
            layer_pair,
            pltpu.VMEM((8, LANES), jnp.int32),
            pltpu.VMEM(frac.shape, f32),
            pltpu.VMEM(velocity.shape, f32),
            pltpu.VMEM((rows, LANES), jnp.int32),
        ),
        in_specs=[smem] + [hbm] * 4,
        out_specs=(vmem,) * 6,
        scratch_shapes=[
            pltpu.SMEM((8, LANES), jnp.int32),
            pltpu.VMEM((rows, LANES), f32),
            pltpu.VMEM((rows, 2 * SPREAD, LANES), bf16),
            pltpu.VMEM(((CX + 1) * (NY + 1) * 8, NZ), f32),
            pltpu.SemaphoreType.DMA((5,)),
        ],
        compiler_params=pltpu.CompilerParams(vmem_limit_bytes=32 * 1024 * 1024),
        name="spread",
    )(tile_count, *[pltpu.with_memory_space_constraint(x, pltpu.HBM) for x in inputs])
    devices = lax.axis_size("gx")
    far_pairs = [(i, (i + (1 if i % 2 else -1)) % devices) for i in range(devices)]
    near_pairs = [(i, i ^ 1) for i in range(devices)]
    near_new = lax.ppermute(near, "gx", near_pairs)
    far_new = lax.ppermute(far, "gx", far_pairs)
    moved, top = pl.pallas_call(
        collect_kernel,
        out_shape=(
            jax.ShapeDtypeStruct((blocks, 8, BLOCK), f32),
            jax.ShapeDtypeStruct((8, LANES), f32),
        ),
        in_specs=[smem] + [vmem] * 8,
        out_specs=(vmem, vmem),
        scratch_shapes=[
            pltpu.SMEM((8, LANES), jnp.int32),
            pltpu.VMEM(((CX + 1) * NY * TABLE, NZ), f32),
            pltpu.VMEM(((CX + 1) * (NY + 1), 2 * TABLE, NZ), bf16),
            pltpu.SemaphoreType.DMA,
        ],
        compiler_params=pltpu.CompilerParams(vmem_limit_bytes=32 * 1024 * 1024),
        name="collect",
    )(time_step, plan, near, far, far_new, near_new, frac_here, vel_here, cells_here)
    new_frac, new_velocity = pl.pallas_call(
        finish_kernel,
        out_shape=(
            jax.ShapeDtypeStruct(frac.shape, f32),
            jax.ShapeDtypeStruct(velocity.shape, f32),
        ),
        in_specs=[vmem] * 3,
        out_specs=(vmem, vmem),
        compiler_params=pltpu.CompilerParams(vmem_limit_bytes=32 * 1024 * 1024),
        cost_estimate=pl.CostEstimate(flops=0, bytes_accessed=8000000, transcendentals=0),
        name="finish",
    )(plan, moved, frac_here)
    fastest = largest(top, "gx")
    next_step = (courant / (fastest + wave_speed))[0, :1]
    return (new_frac, new_velocity, next_step)


def solution(mesh):
    placed = (
        P(None, ("runs", "gx")),
        P(None, ("runs", "gx")),
        P(("runs", "gx")),
        P(("runs", "gx")),
        P(("runs", "gx")),
        P("runs"),
    )
    return jax.shard_map(
        body,
        mesh=mesh,
        in_specs=placed,
        out_specs=(P(None, ("runs", "gx")), P(None, ("runs", "gx")), P("runs")),
        check_vma=False,
    )
```

```python
import functools

import jax
import jax.numpy as jnp
from jax import lax
from jax.experimental import pallas as pl
from jax.experimental.pallas import tpu as pltpu
from jax.sharding import PartitionSpec as P

CX = 2
NY = 32
NZ = 128
ROWS = CX * NY
BLOCK = 256
LANES = 128
UNROLL = 8
SPREAD = 32
TABLE = 16

mass_floor = 0.25
stiffness = 2.0
press_floor = 1.0
grain_size = 0.5
inertia_ref = 0.3
mu_static = 0.38
mu_limit = 0.64
rate_floor = 0.5
gravity = (0.5, 0.0, -0.866)
flip_share = 0.95
courant = 0.4
wave_speed = 2.0
components = ((0, 3, 4), (3, 1, 5), (4, 5, 2))
f32 = jnp.float32
bf16 = jnp.bfloat16


def split_pair(values):
    high = values.astype(bf16)
    low = (values - high.astype(f32)).astype(bf16)
    return high, low


def one_hot(cells_ref, block, offset):
    rel = cells_ref[pl.ds(block * 2, 2), :] - offset
    nodes = lax.broadcasted_iota(jnp.int32, (NZ, LANES), 0)
    halves = [jnp.where(nodes == rel[h : h + 1, :], 1.0, 0.0) for h in range(2)]
    return jnp.concatenate(halves, axis=1).astype(bf16)


def list_visits(cells_ref, count, plan_ref):
    blocks = cells_ref.shape[0] // 2
    shape = (blocks, LANES)
    number = lax.broadcasted_iota(jnp.int32, shape, 0)
    lane = lax.broadcasted_iota(jnp.int32, shape, 1)
    first_half = cells_ref[pl.ds(0, blocks, stride=2), :]
    second_half = cells_ref[pl.ds(1, blocks, stride=2), :]
    slot = number * BLOCK + lane
    reached = jnp.maximum(
        jnp.where(slot < count, first_half, 0), jnp.where(slot + LANES < count, second_half, 0)
    )
    live = number * BLOCK < count
    first = jnp.min(first_half, axis=1, keepdims=True) >> 7
    last = jnp.max(reached, axis=1, keepdims=True) >> 7
    low = jnp.where(live, first + number, 2 * LANES)
    high = jnp.where(live, last + number, -1)
    inside = (low <= lane) & (lane <= high)
    place = lane[:1]
    block = jnp.max(jnp.where(inside, number, -1), axis=0, keepdims=True)
    valid = block >= 0
    row = place - block
    plan_ref[0:1, :] = jnp.where(valid, block, 0)
    plan_ref[1:2, :] = jnp.where(valid, row + (row >> 5), 0)
    plan_ref[2:3, :] = jnp.where(valid, row, ROWS) * NZ
    plan_ref[3:4, :] = jnp.max(high, axis=0, keepdims=True) + 1
    plan_ref[4:5, :] = jnp.broadcast_to(count, (1, LANES))
    plan_ref[5:8, :] = jnp.zeros((3, LANES), jnp.int32)


def spread_kernel(
    count_ref, frac_hbm, vel_hbm, mass_hbm, cells_hbm,
    far_ref, near_ref, plan_ref, frac_ref, vel_ref, cells_ref,
    listed_ref, mass_ref, q_ref, acc_ref, sems,
):
    slots = frac_ref.shape[1]
    sources = (cells_hbm, frac_hbm, vel_hbm, mass_hbm)
    targets = (cells_ref, frac_ref, vel_ref, mass_ref)
    arrivals = [
        pltpu.make_async_copy(source, target, sems.at[k])
        for k, (source, target) in enumerate(zip(sources, targets))
    ]
    for arrival in arrivals:
        arrival.start()
    acc_ref[...] = jnp.zeros_like(acc_ref)
    arrivals[0].wait()
    count = count_ref[0]
    list_visits(cells_ref, count, plan_ref)
    listing = pltpu.make_async_copy(plan_ref, listed_ref, sems.at[4])
    listing.start()
    for arrival in arrivals[1:]:
        arrival.wait()
    sublane = lax.broadcasted_iota(jnp.int32, (8, LANES), 0)
    lane = lax.broadcasted_iota(jnp.int32, (1, LANES), 1)
    top_z = sublane >= 4
    field = sublane & 3

    def weigh(part):
        at = pl.multiple_of(part * LANES, LANES)
        here = pl.ds(at, LANES)

        def spread_out(line):
            return jnp.broadcast_to(line, (8, LANES))

        fx, fy, fz = (spread_out(frac_ref[d : d + 1, here]) for d in range(3))
        vx, vy, vz = (spread_out(vel_ref[d : d + 1, here]) for d in range(3))
        held = spread_out(jnp.where(at + lane < count, mass_ref[pl.ds(part, 1), :], 0.0))
        carried = jnp.where(
            field == 0, held, held * jnp.where(field == 1, vx, jnp.where(field == 2, vy, vz))
        )
        carried = carried * jnp.where(top_z, fz, 1.0 - fz)
        lower, upper = carried * (1.0 - fx), carried * fx
        rows = jnp.concatenate(
            [lower * (1.0 - fy), lower * fy, upper * (1.0 - fy), upper * fy], axis=0
        )
        high, low = split_pair(rows)
        q_ref[pl.ds(part, 1)] = jnp.concatenate([high, low], axis=0)[None]

    def prepare(group, carry):
        for u in range(UNROLL):
            weigh(group * UNROLL + u)
        return carry

    lax.fori_loop(0, slots // LANES // UNROLL, prepare, 0)
    listing.wait()
    total = listed_ref[3, 0]

    def visit(group, carry):
        found = []
        for u in range(UNROLL):
            v = group * UNROLL + u
            block = listed_ref[0, v]
            hot = one_hot(cells_ref, block, listed_ref[2, v])
            both = q_ref[pl.ds(block * 2, 2)]
            both = lax.dot_general(
                jnp.concatenate([both[0], both[1]], axis=1),
                hot,
                (((1,), (1,)), ((), ())),
                preferred_element_type=f32,
            )
            found.append((listed_ref[1, v], both[:SPREAD] + both[SPREAD:]))
        for base, part in found:
            for k, ahead in enumerate((0, 1, NY + 1, NY + 2)):
                at = pl.ds(pl.multiple_of((base + ahead) * 8, 8), 8)
                acc_ref[at, :] += part[8 * k : 8 * k + 8]
        return carry

    lax.fori_loop(0, (total + UNROLL - 1) // UNROLL, visit, 0)

    layers = []
    for l in range(CX + 1):
        first = l * (NY + 1) * 8
        acc_ref[first : first + 8, :] += acc_ref[first + NY * 8 : first + NY * 8 + 8, :]
        for f in range(4):
            lower = acc_ref[pl.ds(first + f, NY, stride=8), :]
            upper = acc_ref[pl.ds(first + 4 + f, NY, stride=8), :]
            layers.append(lower + pltpu.roll(upper, 1, 1))
    odd = lax.axis_index("gx") % 2 == 1
    for l in range(CX):
        for f in range(4):
            low, high = layers[l * 4 + f], layers[(l + 1) * 4 + f]
            near_ref[f * CX + l] = jnp.where(odd, low, high)
            far_ref[f * CX + l] = jnp.where(odd, high, low)


def pair_up(field, axis):
    return field + pltpu.roll(field, field.shape[axis] - 1, axis)


def step_up(field, axis):
    return pltpu.roll(field, field.shape[axis] - 1, axis) - field


def pair_down(field, axis):
    return field + pltpu.roll(field, 1, axis)


def step_down(field, axis):
    return field - pltpu.roll(field, 1, axis)


def cell_stress(vel_lo, vel_hi, mass_lo, mass_hi, keep):
    grads = []
    for a in range(3):
        diff = vel_hi[a] - vel_lo[a]
        both = vel_hi[a] + vel_lo[a]
        grads.append(
            [
                0.25 * pair_up(pair_up(diff, 0), 1),
                0.25 * pair_up(step_up(both, 0), 1),
                0.25 * step_up(pair_up(both, 0), 1),
            ]
        )
    density = 0.125 * pair_up(pair_up(mass_hi + mass_lo, 0), 1)
    dxx = grads[0][0]
    dyy = grads[1][1]
    dzz = grads[2][2]
    dxy = 0.5 * (grads[0][1] + grads[1][0])
    dxz = 0.5 * (grads[0][2] + grads[2][0])
    dyz = 0.5 * (grads[1][2] + grads[2][1])
    second = dxx * dxx + dyy * dyy + dzz * dzz + 2.0 * (dxy * dxy + dxz * dxz + dyz * dyz)
    rate = jnp.sqrt(2.0 * second + rate_floor * rate_floor)
    pressure = stiffness * density
    inertial = rate * grain_size / jnp.sqrt(pressure + press_floor)
    friction = mu_static + (mu_limit - mu_static) * inertial / (inertia_ref + inertial)
    twice = 2.0 * friction * pressure / rate
    sigma = [
        twice * dxx - pressure,
        twice * dyy - pressure,
        twice * dzz - pressure,
        twice * dxy,
        twice * dxz,
        twice * dyz,
    ]
    return [jnp.where(keep, s, 0.0) for s in sigma]


def node_force(lower, upper):
    force = []
    for a in range(3):
        sx, sy, sz = (components[a][b] for b in range(3))
        along = pair_down(pair_down(upper[sx] - lower[sx], 0), 1)
        across = step_down(pair_down(upper[sy] + lower[sy], 1), 0)
        upward = step_down(pair_down(upper[sz] + lower[sz], 0), 1)
        force.append(0.25 * (along + across + upward))
    return force


def collect_kernel(
    step_ref, plan_ref, near_ref, far_ref, far_new_ref, near_new_ref, frac_ref, vel_ref, cells_ref,
    out_ref, top_ref, listed_ref, tab_ref, pair_ref, sem,
):
    blocks = frac_ref.shape[1] // BLOCK
    listing = pltpu.make_async_copy(plan_ref, listed_ref, sem)
    listing.start()
    step = step_ref[0]
    odd = lax.axis_index("gx") % 2 == 1

    def pick(if_odd, if_even):
        return [jnp.where(odd, if_odd[k], if_even[k]) for k in range(4 * CX)]

    low, high = pick(near_ref, far_ref), pick(far_ref, near_ref)
    left, right = pick(near_new_ref, far_new_ref), pick(far_new_ref, near_new_ref)
    nodes = [
        [left[f * 2] for f in range(4)],
        [low[f * 2] + left[f * 2 + 1] for f in range(4)],
        [low[f * 2 + 1] for f in range(4)],
        [high[f * 2 + 1] + right[f * 2] for f in range(4)],
        [right[f * 2 + 1] for f in range(4)],
    ]
    height = lax.broadcasted_iota(jnp.int32, (NY, NZ), 1)
    keep = height < NZ - 1
    above_bed = height > 0
    floor = [jnp.maximum(layer[0], mass_floor) for layer in nodes]
    v_old = [[layer[1 + a] / floor[l] for a in range(3)] for l, layer in enumerate(nodes)]
    sigma = [
        cell_stress(v_old[l], v_old[l + 1], nodes[l][0], nodes[l + 1][0], keep) for l in range(4)
    ]
    blank = jnp.zeros((NY, NZ), f32)
    for l in range(CX + 1):
        force = node_force(sigma[l], sigma[l + 1])
        fields = [blank] * 8
        for a in range(3):
            layer = nodes[l + 1]
            fresh = (layer[1 + a] + step * (force[a] + layer[0] * gravity[a])) / floor[l + 1]
            fresh = jnp.where(above_bed, fresh, 0.0)
            fields[a] = fresh - flip_share * v_old[l + 1][a]
            fields[4 + a] = step * fresh
        for k, value in enumerate(fields):
            start = l * NY * TABLE + k
            tab_ref[pl.ds(start, NY, stride=TABLE), :] = value
            tab_ref[pl.ds(start + 8, NY, stride=TABLE), :] = pltpu.roll(value, NZ - 1, 1)

    for l in range(CX + 1):

        def split_row(j, carry):
            at = pl.ds(pl.multiple_of((l * NY + j) * TABLE, TABLE), TABLE)
            high, low = split_pair(tab_ref[at, :])
            pair_ref[pl.ds(l * (NY + 1) + j, 1)] = jnp.concatenate([high, low], axis=0)[None]
            return carry

        lax.fori_loop(0, NY, split_row, 0, unroll=8)
        pair_ref[l * (NY + 1) + NY] = pair_ref[l * (NY + 1)]

    out_ref[...] = jnp.zeros_like(out_ref)
    listing.wait()
    total = listed_ref[3, 0]
    count = listed_ref[4, 0]

    def visit(group, carry):
        found = []
        for u in range(UNROLL):
            v = group * UNROLL + u
            block = listed_ref[0, v]
            base = listed_ref[1, v]
            hot = one_hot(cells_ref, block, listed_ref[2, v])
            rows = [pair_ref[base + ahead] for ahead in (0, 1, NY + 1, NY + 2)]
            both = jnp.dot(jnp.concatenate(rows, axis=0), hot, preferred_element_type=f32)
            corners = []
            for k in range(4):
                four = both[4 * 8 * k : 4 * 8 * (k + 1)]
                corners += [four[0:8] + four[16:24], four[8:16] + four[24:32]]
            frac = frac_ref[:, pl.ds(pl.multiple_of(block * BLOCK, BLOCK), BLOCK)]
            for d in (2, 1, 0):
                share = frac[d : d + 1, :]
                corners = [
                    corners[k] + share * (corners[k + 1] - corners[k])
                    for k in range(0, len(corners), 2)
                ]
            found.append((block, corners[0]))
        for block, part in found:
            out_ref[pl.ds(block, 1)] += part[None]
        return carry

    lax.fori_loop(0, (total + UNROLL - 1) // UNROLL, visit, 0)

    lane = lax.broadcasted_iota(jnp.int32, (1, BLOCK), 1)

    def finish(block, top):
        at = pl.multiple_of(block * BLOCK, BLOCK)
        alive = at + lane < count
        got = out_ref[pl.ds(block, 1)][0]
        fresh = jnp.where(alive, flip_share * vel_ref[:, pl.ds(at, BLOCK)] + got[0:3], 0.0)
        out_ref[pl.ds(block, 1), 0:3] = fresh[None]
        square = fresh[0:1] * fresh[0:1] + fresh[1:2] * fresh[1:2] + fresh[2:3] * fresh[2:3]
        return jnp.maximum(top, square)

    top = lax.fori_loop(0, blocks, finish, jnp.zeros((1, BLOCK), f32), unroll=4)
    top = jnp.sqrt(jnp.max(top, axis=1, keepdims=True))
    top_ref[...] = jnp.broadcast_to(top, top_ref.shape)


def finish_kernel(plan_ref, moved_ref, frac_ref, new_frac_ref, new_vel_ref):
    blocks = frac_ref.shape[1] // BLOCK
    count = plan_ref[4:5, :]
    count = jnp.concatenate([count, count], axis=1)
    lane = lax.broadcasted_iota(jnp.int32, (1, BLOCK), 1)

    def finish(block, carry):
        at = pl.multiple_of(block * BLOCK, BLOCK)
        got = moved_ref[pl.ds(block, 1)][0]
        new_vel_ref[:, pl.ds(at, BLOCK)] = got[0:3]
        placed = jnp.where(at + lane < count, frac_ref[:, pl.ds(at, BLOCK)] + got[4:7], 0.0)
        new_frac_ref[:, pl.ds(at, BLOCK)] = placed
        return carry

    lax.fori_loop(0, blocks, finish, 0, unroll=4)


def largest(value, axis):
    devices = lax.axis_size(axis)
    value = jnp.maximum(value, lax.ppermute(value, axis, [(i, i ^ 1) for i in range(devices)]))
    odd = range(1, devices, 2)
    reach = 2
    while reach < devices:
        if devices & (devices - 1) == 0:
            pairs = [(i, i ^ reach) for i in odd]
        else:
            pairs = [(i, (i + reach) % devices) for i in odd]
        value = jnp.maximum(value, lax.ppermute(value, axis, pairs))
        reach *= 2
    return jnp.maximum(value, lax.ppermute(value, axis, [(i, i - 1) for i in odd]))


smem = pl.BlockSpec(memory_space=pltpu.SMEM)
vmem = pl.BlockSpec(memory_space=pltpu.VMEM)
hbm = pl.BlockSpec(memory_space=pltpu.HBM)


def body(frac, velocity, mass, particle_cell, tile_count, time_step):
    slots = frac.shape[1]
    blocks = slots // BLOCK
    rows = slots // LANES
    inputs = (frac, velocity, mass.reshape(rows, LANES), particle_cell.reshape(rows, LANES))
    layer_pair = pltpu.VMEM((4 * CX, NY, NZ), f32)
    far, near, plan, frac_here, vel_here, cells_here = pl.pallas_call(
        spread_kernel,
        out_shape=(
            layer_pair,
            layer_pair,
            pltpu.VMEM((8, LANES), jnp.int32),
            pltpu.VMEM(frac.shape, f32),
            pltpu.VMEM(velocity.shape, f32),
            pltpu.VMEM((rows, LANES), jnp.int32),
        ),
        in_specs=[smem] + [hbm] * 4,
        out_specs=(vmem,) * 6,
        scratch_shapes=[
            pltpu.SMEM((8, LANES), jnp.int32),
            pltpu.VMEM((rows, LANES), f32),
            pltpu.VMEM((rows, 2 * SPREAD, LANES), bf16),
            pltpu.VMEM(((CX + 1) * (NY + 1) * 8, NZ), f32),
            pltpu.SemaphoreType.DMA((5,)),
        ],
        compiler_params=pltpu.CompilerParams(vmem_limit_bytes=32 * 1024 * 1024),
        name="spread",
    )(tile_count, *[pltpu.with_memory_space_constraint(x, pltpu.HBM) for x in inputs])
    devices = lax.axis_size("gx")
    far_pairs = [(i, (i + (1 if i % 2 else -1)) % devices) for i in range(devices)]
    near_pairs = [(i, i ^ 1) for i in range(devices)]
    near_new = lax.ppermute(near, "gx", near_pairs)
    far_new = lax.ppermute(far, "gx", far_pairs)
    moved, top = pl.pallas_call(
        collect_kernel,
        out_shape=(
            jax.ShapeDtypeStruct((blocks, 8, BLOCK), f32),
            jax.ShapeDtypeStruct((8, LANES), f32),
        ),
        in_specs=[smem] + [vmem] * 8,
        out_specs=(vmem, vmem),
        scratch_shapes=[
            pltpu.SMEM((8, LANES), jnp.int32),
            pltpu.VMEM(((CX + 1) * NY * TABLE, NZ), f32),
            pltpu.VMEM(((CX + 1) * (NY + 1), 2 * TABLE, NZ), bf16),
            pltpu.SemaphoreType.DMA,
        ],
        compiler_params=pltpu.CompilerParams(vmem_limit_bytes=32 * 1024 * 1024),
        name="collect",
    )(time_step, plan, near, far, far_new, near_new, frac_here, vel_here, cells_here)
    new_frac, new_velocity = pl.pallas_call(
        finish_kernel,
        out_shape=(
            jax.ShapeDtypeStruct(frac.shape, f32),
            jax.ShapeDtypeStruct(velocity.shape, f32),
        ),
        in_specs=[vmem] * 3,
        out_specs=(vmem, vmem),
        compiler_params=pltpu.CompilerParams(vmem_limit_bytes=32 * 1024 * 1024),
        cost_estimate=pl.CostEstimate(flops=0, bytes_accessed=8000000, transcendentals=0),
        name="finish",
    )(plan, moved, frac_here)
    fastest = largest(top, "gx")
    next_step = (courant / (fastest + wave_speed))[0, :1]
    return (new_frac, new_velocity, next_step)


def solution(mesh):
    placed = (
        P(None, ("runs", "gx")),
        P(None, ("runs", "gx")),
        P(("runs", "gx")),
        P(("runs", "gx")),
        P(("runs", "gx")),
        P("runs"),
    )
    return jax.shard_map(
        body,
        mesh=mesh,
        in_specs=placed,
        out_specs=(P(None, ("runs", "gx")), P(None, ("runs", "gx")), P("runs")),
        check_vma=False,
    )
```

```python
import functools

import jax
import jax.numpy as jnp
from jax import lax
from jax.experimental import pallas as pl
from jax.experimental.pallas import tpu as pltpu
from jax.sharding import PartitionSpec as P

CX = 2
NY = 32
NZ = 128
ROWS = CX * NY
BLOCK = 256
LANES = 128
UNROLL = 8
SPREAD = 32
TABLE = 16

mass_floor = 0.25
stiffness = 2.0
press_floor = 1.0
grain_size = 0.5
inertia_ref = 0.3
mu_static = 0.38
mu_limit = 0.64
rate_floor = 0.5
gravity = (0.5, 0.0, -0.866)
flip_share = 0.95
courant = 0.4
wave_speed = 2.0
components = ((0, 3, 4), (3, 1, 5), (4, 5, 2))
f32 = jnp.float32
bf16 = jnp.bfloat16


def split_pair(values):
    high = values.astype(bf16)
    low = (values - high.astype(f32)).astype(bf16)
    return high, low


def one_hot(cells_ref, block, offset):
    rel = cells_ref[pl.ds(block * 2, 2), :] - offset
    nodes = lax.broadcasted_iota(jnp.int32, (NZ, LANES), 0)
    halves = [jnp.where(nodes == rel[h : h + 1, :], 1.0, 0.0) for h in range(2)]
    return jnp.concatenate(halves, axis=1).astype(bf16)


def list_visits(cells_ref, count, plan_ref):
    blocks = cells_ref.shape[0] // 2
    shape = (blocks, LANES)
    number = lax.broadcasted_iota(jnp.int32, shape, 0)
    lane = lax.broadcasted_iota(jnp.int32, shape, 1)
    first_half = cells_ref[pl.ds(0, blocks, stride=2), :]
    second_half = cells_ref[pl.ds(1, blocks, stride=2), :]
    slot = number * BLOCK + lane
    reached = jnp.maximum(
        jnp.where(slot < count, first_half, 0), jnp.where(slot + LANES < count, second_half, 0)
    )
    live = number * BLOCK < count
    first = jnp.min(first_half, axis=1, keepdims=True) >> 7
    last = jnp.max(reached, axis=1, keepdims=True) >> 7
    low = jnp.where(live, first + number, 2 * LANES)
    high = jnp.where(live, last + number, -1)
    inside = (low <= lane) & (lane <= high)
    place = lane[:1]
    block = jnp.max(jnp.where(inside, number, -1), axis=0, keepdims=True)
    valid = block >= 0
    row = place - block
    plan_ref[0:1, :] = jnp.where(valid, block, 0)
    plan_ref[1:2, :] = jnp.where(valid, row + (row >> 5), 0)
    plan_ref[2:3, :] = jnp.where(valid, row, ROWS) * NZ
    plan_ref[3:4, :] = jnp.max(high, axis=0, keepdims=True) + 1
    plan_ref[4:5, :] = jnp.broadcast_to(count, (1, LANES))
    plan_ref[5:8, :] = jnp.zeros((3, LANES), jnp.int32)


def spread_kernel(
    count_ref, frac_hbm, vel_hbm, mass_hbm, cells_hbm,
    far_ref, near_ref, plan_ref, frac_ref, vel_ref, cells_ref,
    listed_ref, mass_ref, q_ref, acc_ref, sems,
):
    slots = frac_ref.shape[1]
    sources = (cells_hbm, frac_hbm, vel_hbm, mass_hbm)
    targets = (cells_ref, frac_ref, vel_ref, mass_ref)
    arrivals = [
        pltpu.make_async_copy(source, target, sems.at[k])
        for k, (source, target) in enumerate(zip(sources, targets))
    ]
    for arrival in arrivals:
        arrival.start()
    acc_ref[...] = jnp.zeros_like(acc_ref)
    arrivals[0].wait()
    count = count_ref[0]
    list_visits(cells_ref, count, plan_ref)
    listing = pltpu.make_async_copy(plan_ref, listed_ref, sems.at[4])
    listing.start()
    for arrival in arrivals[1:]:
        arrival.wait()
    sublane = lax.broadcasted_iota(jnp.int32, (8, LANES), 0)
    lane = lax.broadcasted_iota(jnp.int32, (1, LANES), 1)
    top_z = sublane >= 4
    field = sublane & 3

    def weigh(part):
        at = pl.multiple_of(part * LANES, LANES)
        here = pl.ds(at, LANES)

        def spread_out(line):
            return jnp.broadcast_to(line, (8, LANES))

        fx, fy, fz = (spread_out(frac_ref[d : d + 1, here]) for d in range(3))
        vx, vy, vz = (spread_out(vel_ref[d : d + 1, here]) for d in range(3))
        held = spread_out(jnp.where(at + lane < count, mass_ref[pl.ds(part, 1), :], 0.0))
        carried = jnp.where(
            field == 0, held, held * jnp.where(field == 1, vx, jnp.where(field == 2, vy, vz))
        )
        carried = carried * jnp.where(top_z, fz, 1.0 - fz)
        lower, upper = carried * (1.0 - fx), carried * fx
        rows = jnp.concatenate(
            [lower * (1.0 - fy), lower * fy, upper * (1.0 - fy), upper * fy], axis=0
        )
        high, low = split_pair(rows)
        q_ref[pl.ds(part, 1)] = jnp.concatenate([high, low], axis=0)[None]

    def prepare(group, carry):
        for u in range(UNROLL):
            weigh(group * UNROLL + u)
        return carry

    lax.fori_loop(0, slots // LANES // UNROLL, prepare, 0)
    listing.wait()
    total = listed_ref[3, 0]

    def visit(group, carry):
        found = []
        for u in range(UNROLL):
            v = group * UNROLL + u
            block = listed_ref[0, v]
            hot = one_hot(cells_ref, block, listed_ref[2, v])
            both = q_ref[pl.ds(block * 2, 2)]
            both = lax.dot_general(
                jnp.concatenate([both[0], both[1]], axis=1),
                hot,
                (((1,), (1,)), ((), ())),
                preferred_element_type=f32,
            )
            found.append((listed_ref[1, v], both[:SPREAD] + both[SPREAD:]))
        for base, part in found:
            for k, ahead in enumerate((0, 1, NY + 1, NY + 2)):
                at = pl.ds(pl.multiple_of((base + ahead) * 8, 8), 8)
                acc_ref[at, :] += part[8 * k : 8 * k + 8]
        return carry

    lax.fori_loop(0, (total + UNROLL - 1) // UNROLL, visit, 0)

    layers = []
    for l in range(CX + 1):
        first = l * (NY + 1) * 8
        acc_ref[first : first + 8, :] += acc_ref[first + NY * 8 : first + NY * 8 + 8, :]
        for f in range(4):
            lower = acc_ref[pl.ds(first + f, NY, stride=8), :]
            upper = acc_ref[pl.ds(first + 4 + f, NY, stride=8), :]
            layers.append(lower + pltpu.roll(upper, 1, 1))
    odd = lax.axis_index("gx") % 2 == 1
    for l in range(CX):
        for f in range(4):
            low, high = layers[l * 4 + f], layers[(l + 1) * 4 + f]
            near_ref[f * CX + l] = jnp.where(odd, low, high)
            far_ref[f * CX + l] = jnp.where(odd, high, low)


def pair_up(field, axis):
    return field + pltpu.roll(field, field.shape[axis] - 1, axis)


def step_up(field, axis):
    return pltpu.roll(field, field.shape[axis] - 1, axis) - field


def pair_down(field, axis):
    return field + pltpu.roll(field, 1, axis)


def step_down(field, axis):
    return field - pltpu.roll(field, 1, axis)


def cell_stress(vel_lo, vel_hi, mass_lo, mass_hi, keep):
    grads = []
    for a in range(3):
        diff = vel_hi[a] - vel_lo[a]
        both = vel_hi[a] + vel_lo[a]
        grads.append(
            [
                0.25 * pair_up(pair_up(diff, 0), 1),
                0.25 * pair_up(step_up(both, 0), 1),
                0.25 * step_up(pair_up(both, 0), 1),
            ]
        )
    density = 0.125 * pair_up(pair_up(mass_hi + mass_lo, 0), 1)
    dxx = grads[0][0]
    dyy = grads[1][1]
    dzz = grads[2][2]
    dxy = 0.5 * (grads[0][1] + grads[1][0])
    dxz = 0.5 * (grads[0][2] + grads[2][0])
    dyz = 0.5 * (grads[1][2] + grads[2][1])
    second = dxx * dxx + dyy * dyy + dzz * dzz + 2.0 * (dxy * dxy + dxz * dxz + dyz * dyz)
    rate = jnp.sqrt(2.0 * second + rate_floor * rate_floor)
    pressure = stiffness * density
    inertial = rate * grain_size / jnp.sqrt(pressure + press_floor)
    friction = mu_static + (mu_limit - mu_static) * inertial / (inertia_ref + inertial)
    twice = 2.0 * friction * pressure / rate
    sigma = [
        twice * dxx - pressure,
        twice * dyy - pressure,
        twice * dzz - pressure,
        twice * dxy,
        twice * dxz,
        twice * dyz,
    ]
    return [jnp.where(keep, s, 0.0) for s in sigma]


def node_force(lower, upper):
    force = []
    for a in range(3):
        sx, sy, sz = (components[a][b] for b in range(3))
        along = pair_down(pair_down(upper[sx] - lower[sx], 0), 1)
        across = step_down(pair_down(upper[sy] + lower[sy], 1), 0)
        upward = step_down(pair_down(upper[sz] + lower[sz], 0), 1)
        force.append(0.25 * (along + across + upward))
    return force


def collect_kernel(
    step_ref, plan_ref, near_ref, far_ref, far_new_ref, near_new_ref, frac_ref, vel_ref, cells_ref,
    out_ref, top_ref, listed_ref, tab_ref, pair_ref, sem,
):
    blocks = frac_ref.shape[1] // BLOCK
    listing = pltpu.make_async_copy(plan_ref, listed_ref, sem)
    listing.start()
    step = step_ref[0]
    odd = lax.axis_index("gx") % 2 == 1

    def pick(if_odd, if_even):
        return [jnp.where(odd, if_odd[k], if_even[k]) for k in range(4 * CX)]

    low, high = pick(near_ref, far_ref), pick(far_ref, near_ref)
    left, right = pick(near_new_ref, far_new_ref), pick(far_new_ref, near_new_ref)
    nodes = [
        [left[f * 2] for f in range(4)],
        [low[f * 2] + left[f * 2 + 1] for f in range(4)],
        [low[f * 2 + 1] for f in range(4)],
        [high[f * 2 + 1] + right[f * 2] for f in range(4)],
        [right[f * 2 + 1] for f in range(4)],
    ]
    height = lax.broadcasted_iota(jnp.int32, (NY, NZ), 1)
    keep = height < NZ - 1
    above_bed = height > 0
    floor = [jnp.maximum(layer[0], mass_floor) for layer in nodes]
    v_old = [[layer[1 + a] / floor[l] for a in range(3)] for l, layer in enumerate(nodes)]
    sigma = [
        cell_stress(v_old[l], v_old[l + 1], nodes[l][0], nodes[l + 1][0], keep) for l in range(4)
    ]
    blank = jnp.zeros((NY, NZ), f32)
    for l in range(CX + 1):
        force = node_force(sigma[l], sigma[l + 1])
        fields = [blank] * 8
        for a in range(3):
            layer = nodes[l + 1]
            fresh = (layer[1 + a] + step * (force[a] + layer[0] * gravity[a])) / floor[l + 1]
            fresh = jnp.where(above_bed, fresh, 0.0)
            fields[a] = fresh - flip_share * v_old[l + 1][a]
            fields[4 + a] = step * fresh
        for k, value in enumerate(fields):
            start = l * NY * TABLE + k
            tab_ref[pl.ds(start, NY, stride=TABLE), :] = value
            tab_ref[pl.ds(start + 8, NY, stride=TABLE), :] = pltpu.roll(value, NZ - 1, 1)

    for l in range(CX + 1):

        def split_row(j, carry):
            at = pl.ds(pl.multiple_of((l * NY + j) * TABLE, TABLE), TABLE)
            high, low = split_pair(tab_ref[at, :])
            pair_ref[pl.ds(l * (NY + 1) + j, 1)] = jnp.concatenate([high, low], axis=0)[None]
            return carry

        lax.fori_loop(0, NY, split_row, 0, unroll=8)
        pair_ref[l * (NY + 1) + NY] = pair_ref[l * (NY + 1)]

    out_ref[...] = jnp.zeros_like(out_ref)
    listing.wait()
    total = listed_ref[3, 0]
    count = listed_ref[4, 0]

    def visit(group, carry):
        found = []
        for u in range(UNROLL):
            v = group * UNROLL + u
            block = listed_ref[0, v]
            base = listed_ref[1, v]
            hot = one_hot(cells_ref, block, listed_ref[2, v])
            rows = [pair_ref[base + ahead] for ahead in (0, 1, NY + 1, NY + 2)]
            both = jnp.dot(jnp.concatenate(rows, axis=0), hot, preferred_element_type=f32)
            corners = []
            for k in range(4):
                four = both[4 * 8 * k : 4 * 8 * (k + 1)]
                corners += [four[0:8] + four[16:24], four[8:16] + four[24:32]]
            frac = frac_ref[:, pl.ds(pl.multiple_of(block * BLOCK, BLOCK), BLOCK)]
            for d in (2, 1, 0):
                share = frac[d : d + 1, :]
                corners = [
                    corners[k] + share * (corners[k + 1] - corners[k])
                    for k in range(0, len(corners), 2)
                ]
            found.append((block, corners[0]))
        for block, part in found:
            out_ref[pl.ds(block, 1)] += part[None]
        return carry

    lax.fori_loop(0, (total + UNROLL - 1) // UNROLL, visit, 0)

    lane = lax.broadcasted_iota(jnp.int32, (1, BLOCK), 1)

    def finish(block, top):
        at = pl.multiple_of(block * BLOCK, BLOCK)
        alive = at + lane < count
        got = out_ref[pl.ds(block, 1)][0]
        fresh = jnp.where(alive, flip_share * vel_ref[:, pl.ds(at, BLOCK)] + got[0:3], 0.0)
        out_ref[pl.ds(block, 1), 0:3] = fresh[None]
        square = fresh[0:1] * fresh[0:1] + fresh[1:2] * fresh[1:2] + fresh[2:3] * fresh[2:3]
        return jnp.maximum(top, square)

    top = lax.fori_loop(0, blocks, finish, jnp.zeros((1, BLOCK), f32), unroll=4)
    top = jnp.sqrt(jnp.max(top, axis=1, keepdims=True))
    top_ref[...] = jnp.broadcast_to(top, top_ref.shape)


def finish_kernel(plan_ref, moved_ref, frac_ref, new_frac_ref, new_vel_ref):
    blocks = frac_ref.shape[1] // BLOCK
    count = plan_ref[4:5, :]
    count = jnp.concatenate([count, count], axis=1)
    lane = lax.broadcasted_iota(jnp.int32, (1, BLOCK), 1)

    def finish(block, carry):
        at = pl.multiple_of(block * BLOCK, BLOCK)
        got = moved_ref[pl.ds(block, 1)][0]
        new_vel_ref[:, pl.ds(at, BLOCK)] = got[0:3]
        placed = jnp.where(at + lane < count, frac_ref[:, pl.ds(at, BLOCK)] + got[4:7], 0.0)
        new_frac_ref[:, pl.ds(at, BLOCK)] = placed
        return carry

    lax.fori_loop(0, blocks, finish, 0, unroll=4)


def largest(value, axis):
    devices = lax.axis_size(axis)
    swap = [(i, i ^ 1) for i in range(devices)]
    value = jnp.maximum(value, lax.ppermute(value, axis, swap))
    reach = 2
    while reach < devices:
        if devices & (devices - 1) == 0:
            pairs = [(i, i ^ reach if i % 2 else i) for i in range(devices)]
        else:
            pairs = [(i, (i + reach) % devices if i % 2 else i) for i in range(devices)]
        value = jnp.maximum(value, lax.ppermute(value, axis, pairs))
        reach *= 2
    return jnp.maximum(value, lax.ppermute(value, axis, swap))


smem = pl.BlockSpec(memory_space=pltpu.SMEM)
vmem = pl.BlockSpec(memory_space=pltpu.VMEM)
hbm = pl.BlockSpec(memory_space=pltpu.HBM)


def body(frac, velocity, mass, particle_cell, tile_count, time_step):
    slots = frac.shape[1]
    blocks = slots // BLOCK
    rows = slots // LANES
    inputs = (frac, velocity, mass.reshape(rows, LANES), particle_cell.reshape(rows, LANES))
    layer_pair = pltpu.VMEM((4 * CX, NY, NZ), f32)
    far, near, plan, frac_here, vel_here, cells_here = pl.pallas_call(
        spread_kernel,
        out_shape=(
            layer_pair,
            layer_pair,
            pltpu.VMEM((8, LANES), jnp.int32),
            pltpu.VMEM(frac.shape, f32),
            pltpu.VMEM(velocity.shape, f32),
            pltpu.VMEM((rows, LANES), jnp.int32),
        ),
        in_specs=[smem] + [hbm] * 4,
        out_specs=(vmem,) * 6,
        scratch_shapes=[
            pltpu.SMEM((8, LANES), jnp.int32),
            pltpu.VMEM((rows, LANES), f32),
            pltpu.VMEM((rows, 2 * SPREAD, LANES), bf16),
            pltpu.VMEM(((CX + 1) * (NY + 1) * 8, NZ), f32),
            pltpu.SemaphoreType.DMA((5,)),
        ],
        compiler_params=pltpu.CompilerParams(vmem_limit_bytes=32 * 1024 * 1024),
        name="spread",
    )(tile_count, *[pltpu.with_memory_space_constraint(x, pltpu.HBM) for x in inputs])
    devices = lax.axis_size("gx")
    far_pairs = [(i, (i + (1 if i % 2 else -1)) % devices) for i in range(devices)]
    near_pairs = [(i, i ^ 1) for i in range(devices)]
    near_new = lax.ppermute(near, "gx", near_pairs)
    far_new = lax.ppermute(far, "gx", far_pairs)
    moved, top = pl.pallas_call(
        collect_kernel,
        out_shape=(
            jax.ShapeDtypeStruct((blocks, 8, BLOCK), f32),
            jax.ShapeDtypeStruct((8, LANES), f32),
        ),
        in_specs=[smem] + [vmem] * 8,
        out_specs=(vmem, vmem),
        scratch_shapes=[
            pltpu.SMEM((8, LANES), jnp.int32),
            pltpu.VMEM(((CX + 1) * NY * TABLE, NZ), f32),
            pltpu.VMEM(((CX + 1) * (NY + 1), 2 * TABLE, NZ), bf16),
            pltpu.SemaphoreType.DMA,
        ],
        compiler_params=pltpu.CompilerParams(vmem_limit_bytes=32 * 1024 * 1024),
        name="collect",
    )(time_step, plan, near, far, far_new, near_new, frac_here, vel_here, cells_here)
    new_frac, new_velocity = pl.pallas_call(
        finish_kernel,
        out_shape=(
            jax.ShapeDtypeStruct(frac.shape, f32),
            jax.ShapeDtypeStruct(velocity.shape, f32),
        ),
        in_specs=[vmem] * 3,
        out_specs=(vmem, vmem),
        compiler_params=pltpu.CompilerParams(vmem_limit_bytes=32 * 1024 * 1024),
        cost_estimate=pl.CostEstimate(flops=0, bytes_accessed=8000000, transcendentals=0),
        name="finish",
    )(plan, moved, frac_here)
    fastest = largest(top, "gx")
    next_step = (courant / (fastest + wave_speed))[0, :1]
    return (new_frac, new_velocity, next_step)


def solution(mesh):
    placed = (
        P(None, ("runs", "gx")),
        P(None, ("runs", "gx")),
        P(("runs", "gx")),
        P(("runs", "gx")),
        P(("runs", "gx")),
        P("runs"),
    )
    return jax.shard_map(
        body,
        mesh=mesh,
        in_specs=placed,
        out_specs=(P(None, ("runs", "gx")), P(None, ("runs", "gx")), P("runs")),
        check_vma=False,
    )
```

```python
import functools

import jax
import jax.numpy as jnp
from jax import lax
from jax.experimental import pallas as pl
from jax.experimental.pallas import tpu as pltpu
from jax.sharding import PartitionSpec as P

CX = 2
NY = 32
NZ = 128
ROWS = CX * NY
BLOCK = 256
LANES = 128
UNROLL = 8
SPREAD = 32
TABLE = 16

mass_floor = 0.25
stiffness = 2.0
press_floor = 1.0
grain_size = 0.5
inertia_ref = 0.3
mu_static = 0.38
mu_limit = 0.64
rate_floor = 0.5
gravity = (0.5, 0.0, -0.866)
flip_share = 0.95
courant = 0.4
wave_speed = 2.0
components = ((0, 3, 4), (3, 1, 5), (4, 5, 2))
f32 = jnp.float32
bf16 = jnp.bfloat16


def split_pair(values):
    high = values.astype(bf16)
    low = (values - high.astype(f32)).astype(bf16)
    return high, low


def one_hot(cells_ref, block, offset):
    rel = cells_ref[pl.ds(block * 2, 2), :] - offset
    tall = (16, LANES)
    nodes = lax.broadcasted_iota(jnp.int32, tall, 0).astype(jnp.int16)
    one, zero = jnp.ones(tall, bf16), jnp.zeros(tall, bf16)
    halves = []
    for h in range(2):
        line = jnp.broadcast_to(rel[h : h + 1, :], tall).astype(jnp.int16)
        halves.append(
            jnp.concatenate(
                [
                    jnp.where(line == nodes + jnp.int16(z), one, zero)
                    for z in range(0, NZ, 16)
                ],
                axis=0,
            )
        )
    return jnp.concatenate(halves, axis=1)


def list_visits(cells_ref, count, plan_ref):
    blocks = cells_ref.shape[0] // 2
    shape = (blocks, LANES)
    number = lax.broadcasted_iota(jnp.int32, shape, 0)
    lane = lax.broadcasted_iota(jnp.int32, shape, 1)
    first_half = cells_ref[pl.ds(0, blocks, stride=2), :]
    second_half = cells_ref[pl.ds(1, blocks, stride=2), :]
    slot = number * BLOCK + lane
    reached = jnp.maximum(
        jnp.where(slot < count, first_half, 0), jnp.where(slot + LANES < count, second_half, 0)
    )
    live = number * BLOCK < count
    first = jnp.min(first_half, axis=1, keepdims=True) >> 7
    last = jnp.max(reached, axis=1, keepdims=True) >> 7
    low = jnp.where(live, first + number, 2 * LANES)
    high = jnp.where(live, last + number, -1)
    inside = (low <= lane) & (lane <= high)
    place = lane[:1]
    block = jnp.max(jnp.where(inside, number, -1), axis=0, keepdims=True)
    valid = block >= 0
    row = place - block
    plan_ref[0:1, :] = jnp.where(valid, block, 0)
    plan_ref[1:2, :] = jnp.where(valid, row + (row >> 5), 0)
    plan_ref[2:3, :] = jnp.where(valid, row, ROWS) * NZ
    plan_ref[3:4, :] = jnp.max(high, axis=0, keepdims=True) + 1
    plan_ref[4:5, :] = jnp.broadcast_to(count, (1, LANES))
    plan_ref[5:8, :] = jnp.zeros((3, LANES), jnp.int32)


def spread_kernel(
    count_ref, frac_hbm, vel_hbm, mass_hbm, cells_hbm,
    far_ref, near_ref, plan_ref, frac_ref, vel_ref, cells_ref,
    listed_ref, mass_ref, q_ref, acc_ref, sems,
):
    slots = frac_ref.shape[1]
    sources = (cells_hbm, frac_hbm, vel_hbm, mass_hbm)
    targets = (cells_ref, frac_ref, vel_ref, mass_ref)
    arrivals = [
        pltpu.make_async_copy(source, target, sems.at[k])
        for k, (source, target) in enumerate(zip(sources, targets))
    ]
    for arrival in arrivals:
        arrival.start()
    acc_ref[...] = jnp.zeros_like(acc_ref)
    arrivals[0].wait()
    count = count_ref[0]
    list_visits(cells_ref, count, plan_ref)
    listing = pltpu.make_async_copy(plan_ref, listed_ref, sems.at[4])
    listing.start()
    for arrival in arrivals[1:]:
        arrival.wait()
    sublane = lax.broadcasted_iota(jnp.int32, (8, LANES), 0)
    lane = lax.broadcasted_iota(jnp.int32, (1, LANES), 1)
    top_z = sublane >= 4
    field = sublane & 3

    def weigh(part):
        at = pl.multiple_of(part * LANES, LANES)
        here = pl.ds(at, LANES)

        def spread_out(line):
            return jnp.broadcast_to(line, (8, LANES))

        fx, fy, fz = (spread_out(frac_ref[d : d + 1, here]) for d in range(3))
        vx, vy, vz = (spread_out(vel_ref[d : d + 1, here]) for d in range(3))
        held = spread_out(jnp.where(at + lane < count, mass_ref[pl.ds(part, 1), :], 0.0))
        carried = jnp.where(
            field == 0, held, held * jnp.where(field == 1, vx, jnp.where(field == 2, vy, vz))
        )
        carried = carried * jnp.where(top_z, fz, 1.0 - fz)
        lower, upper = carried * (1.0 - fx), carried * fx
        rows = jnp.concatenate(
            [lower * (1.0 - fy), lower * fy, upper * (1.0 - fy), upper * fy], axis=0
        )
        high, low = split_pair(rows)
        q_ref[pl.ds(part, 1)] = jnp.concatenate([high, low], axis=0)[None]

    def prepare(group, carry):
        for u in range(UNROLL):
            weigh(group * UNROLL + u)
        return carry

    lax.fori_loop(0, slots // LANES // UNROLL, prepare, 0)
    listing.wait()
    total = listed_ref[3, 0]

    def visit(group, carry):
        found = []
        for u in range(UNROLL):
            v = group * UNROLL + u
            block = listed_ref[0, v]
            hot = one_hot(cells_ref, block, listed_ref[2, v])
            both = q_ref[pl.ds(block * 2, 2)]
            both = lax.dot_general(
                jnp.concatenate([both[0], both[1]], axis=1),
                hot,
                (((1,), (1,)), ((), ())),
                preferred_element_type=f32,
            )
            found.append((listed_ref[1, v], both[:SPREAD] + both[SPREAD:]))
        for base, part in found:
            for k, ahead in enumerate((0, 1, NY + 1, NY + 2)):
                at = pl.ds(pl.multiple_of((base + ahead) * 8, 8), 8)
                acc_ref[at, :] += part[8 * k : 8 * k + 8]
        return carry

    lax.fori_loop(0, (total + UNROLL - 1) // UNROLL, visit, 0)

    layers = []
    for l in range(CX + 1):
        first = l * (NY + 1) * 8
        acc_ref[first : first + 8, :] += acc_ref[first + NY * 8 : first + NY * 8 + 8, :]
        for f in range(4):
            lower = acc_ref[pl.ds(first + f, NY, stride=8), :]
            upper = acc_ref[pl.ds(first + 4 + f, NY, stride=8), :]
            layers.append(lower + pltpu.roll(upper, 1, 1))
    odd = lax.axis_index("gx") % 2 == 1
    for l in range(CX):
        for f in range(4):
            low, high = layers[l * 4 + f], layers[(l + 1) * 4 + f]
            near_ref[f * CX + l] = jnp.where(odd, low, high)
            far_ref[f * CX + l] = jnp.where(odd, high, low)


def pair_up(field, axis):
    return field + pltpu.roll(field, field.shape[axis] - 1, axis)


def step_up(field, axis):
    return pltpu.roll(field, field.shape[axis] - 1, axis) - field


def pair_down(field, axis):
    return field + pltpu.roll(field, 1, axis)


def step_down(field, axis):
    return field - pltpu.roll(field, 1, axis)


def cell_stress(vel_lo, vel_hi, mass_lo, mass_hi, keep):
    grads = []
    for a in range(3):
        diff = vel_hi[a] - vel_lo[a]
        both = vel_hi[a] + vel_lo[a]
        grads.append(
            [
                0.25 * pair_up(pair_up(diff, 0), 1),
                0.25 * pair_up(step_up(both, 0), 1),
                0.25 * step_up(pair_up(both, 0), 1),
            ]
        )
    density = 0.125 * pair_up(pair_up(mass_hi + mass_lo, 0), 1)
    dxx = grads[0][0]
    dyy = grads[1][1]
    dzz = grads[2][2]
    dxy = 0.5 * (grads[0][1] + grads[1][0])
    dxz = 0.5 * (grads[0][2] + grads[2][0])
    dyz = 0.5 * (grads[1][2] + grads[2][1])
    second = dxx * dxx + dyy * dyy + dzz * dzz + 2.0 * (dxy * dxy + dxz * dxz + dyz * dyz)
    rate = jnp.sqrt(2.0 * second + rate_floor * rate_floor)
    pressure = stiffness * density
    inertial = rate * grain_size / jnp.sqrt(pressure + press_floor)
    friction = mu_static + (mu_limit - mu_static) * inertial / (inertia_ref + inertial)
    twice = 2.0 * friction * pressure / rate
    sigma = [
        twice * dxx - pressure,
        twice * dyy - pressure,
        twice * dzz - pressure,
        twice * dxy,
        twice * dxz,
        twice * dyz,
    ]
    return [jnp.where(keep, s, 0.0) for s in sigma]


def node_force(lower, upper):
    force = []
    for a in range(3):
        sx, sy, sz = (components[a][b] for b in range(3))
        along = pair_down(pair_down(upper[sx] - lower[sx], 0), 1)
        across = step_down(pair_down(upper[sy] + lower[sy], 1), 0)
        upward = step_down(pair_down(upper[sz] + lower[sz], 0), 1)
        force.append(0.25 * (along + across + upward))
    return force


def collect_kernel(
    step_ref, plan_ref, near_ref, far_ref, far_new_ref, near_new_ref, frac_ref, vel_ref, cells_ref,
    out_ref, top_ref, listed_ref, tab_ref, pair_ref, sem,
):
    blocks = frac_ref.shape[1] // BLOCK
    listing = pltpu.make_async_copy(plan_ref, listed_ref, sem)
    listing.start()
    step = step_ref[0]
    odd = lax.axis_index("gx") % 2 == 1

    def pick(if_odd, if_even):
        return [jnp.where(odd, if_odd[k], if_even[k]) for k in range(4 * CX)]

    low, high = pick(near_ref, far_ref), pick(far_ref, near_ref)
    left, right = pick(near_new_ref, far_new_ref), pick(far_new_ref, near_new_ref)
    nodes = [
        [left[f * 2] for f in range(4)],
        [low[f * 2] + left[f * 2 + 1] for f in range(4)],
        [low[f * 2 + 1] for f in range(4)],
        [high[f * 2 + 1] + right[f * 2] for f in range(4)],
        [right[f * 2 + 1] for f in range(4)],
    ]
    height = lax.broadcasted_iota(jnp.int32, (NY, NZ), 1)
    keep = height < NZ - 1
    above_bed = height > 0
    floor = [jnp.maximum(layer[0], mass_floor) for layer in nodes]
    v_old = [[layer[1 + a] / floor[l] for a in range(3)] for l, layer in enumerate(nodes)]
    sigma = [
        cell_stress(v_old[l], v_old[l + 1], nodes[l][0], nodes[l + 1][0], keep) for l in range(4)
    ]
    blank = jnp.zeros((NY, NZ), f32)
    for l in range(CX + 1):
        force = node_force(sigma[l], sigma[l + 1])
        fields = [blank] * 8
        for a in range(3):
            layer = nodes[l + 1]
            fresh = (layer[1 + a] + step * (force[a] + layer[0] * gravity[a])) / floor[l + 1]
            fresh = jnp.where(above_bed, fresh, 0.0)
            fields[a] = fresh - flip_share * v_old[l + 1][a]
            fields[4 + a] = step * fresh
        for k, value in enumerate(fields):
            start = l * NY * TABLE + k
            tab_ref[pl.ds(start, NY, stride=TABLE), :] = value
            tab_ref[pl.ds(start + 8, NY, stride=TABLE), :] = pltpu.roll(value, NZ - 1, 1)

    for l in range(CX + 1):

        def split_row(j, carry):
            at = pl.ds(pl.multiple_of((l * NY + j) * TABLE, TABLE), TABLE)
            high, low = split_pair(tab_ref[at, :])
            pair_ref[pl.ds(l * (NY + 1) + j, 1)] = jnp.concatenate([high, low], axis=0)[None]
            return carry

        lax.fori_loop(0, NY, split_row, 0, unroll=8)
        pair_ref[l * (NY + 1) + NY] = pair_ref[l * (NY + 1)]

    out_ref[...] = jnp.zeros_like(out_ref)
    listing.wait()
    total = listed_ref[3, 0]
    count = listed_ref[4, 0]

    def visit(group, carry):
        found = []
        for u in range(UNROLL):
            v = group * UNROLL + u
            block = listed_ref[0, v]
            base = listed_ref[1, v]
            hot = one_hot(cells_ref, block, listed_ref[2, v])
            rows = [pair_ref[base + ahead] for ahead in (0, 1, NY + 1, NY + 2)]
            both = jnp.dot(jnp.concatenate(rows, axis=0), hot, preferred_element_type=f32)
            corners = []
            for k in range(4):
                four = both[4 * 8 * k : 4 * 8 * (k + 1)]
                corners += [four[0:8] + four[16:24], four[8:16] + four[24:32]]
            frac = frac_ref[:, pl.ds(pl.multiple_of(block * BLOCK, BLOCK), BLOCK)]
            for d in (2, 1, 0):
                share = frac[d : d + 1, :]
                corners = [
                    corners[k] + share * (corners[k + 1] - corners[k])
                    for k in range(0, len(corners), 2)
                ]
            found.append((block, corners[0]))
        for block, part in found:
            out_ref[pl.ds(block, 1)] += part[None]
        return carry

    lax.fori_loop(0, (total + UNROLL - 1) // UNROLL, visit, 0)

    lane = lax.broadcasted_iota(jnp.int32, (1, BLOCK), 1)

    def finish(block, top):
        at = pl.multiple_of(block * BLOCK, BLOCK)
        alive = at + lane < count
        got = out_ref[pl.ds(block, 1)][0]
        fresh = jnp.where(alive, flip_share * vel_ref[:, pl.ds(at, BLOCK)] + got[0:3], 0.0)
        out_ref[pl.ds(block, 1), 0:3] = fresh[None]
        square = fresh[0:1] * fresh[0:1] + fresh[1:2] * fresh[1:2] + fresh[2:3] * fresh[2:3]
        return jnp.maximum(top, square)

    top = lax.fori_loop(0, blocks, finish, jnp.zeros((1, BLOCK), f32), unroll=4)
    top = jnp.sqrt(jnp.max(top, axis=1, keepdims=True))
    top_ref[...] = jnp.broadcast_to(top, top_ref.shape)


def finish_kernel(plan_ref, moved_ref, frac_ref, new_frac_ref, new_vel_ref):
    blocks = frac_ref.shape[1] // BLOCK
    count = plan_ref[4:5, :]
    count = jnp.concatenate([count, count], axis=1)
    lane = lax.broadcasted_iota(jnp.int32, (1, BLOCK), 1)

    def finish(block, carry):
        at = pl.multiple_of(block * BLOCK, BLOCK)
        got = moved_ref[pl.ds(block, 1)][0]
        new_vel_ref[:, pl.ds(at, BLOCK)] = got[0:3]
        placed = jnp.where(at + lane < count, frac_ref[:, pl.ds(at, BLOCK)] + got[4:7], 0.0)
        new_frac_ref[:, pl.ds(at, BLOCK)] = placed
        return carry

    lax.fori_loop(0, blocks, finish, 0, unroll=4)


def largest(value, axis):
    devices = lax.axis_size(axis)
    reach = 1
    while reach < devices:
        if devices & (devices - 1) == 0:
            pairs = [(i, i ^ (reach | 1)) for i in range(devices)]
        else:
            pairs = [(i, (i + reach) % devices) for i in range(devices)]
        value = jnp.maximum(value, lax.ppermute(value, axis, pairs))
        reach *= 2
    return value


smem = pl.BlockSpec(memory_space=pltpu.SMEM)
vmem = pl.BlockSpec(memory_space=pltpu.VMEM)
hbm = pl.BlockSpec(memory_space=pltpu.HBM)


def body(frac, velocity, mass, particle_cell, tile_count, time_step):
    slots = frac.shape[1]
    blocks = slots // BLOCK
    rows = slots // LANES
    inputs = (frac, velocity, mass.reshape(rows, LANES), particle_cell.reshape(rows, LANES))
    layer_pair = pltpu.VMEM((4 * CX, NY, NZ), f32)
    far, near, plan, frac_here, vel_here, cells_here = pl.pallas_call(
        spread_kernel,
        out_shape=(
            layer_pair,
            layer_pair,
            pltpu.VMEM((8, LANES), jnp.int32),
            pltpu.VMEM(frac.shape, f32),
            pltpu.VMEM(velocity.shape, f32),
            pltpu.VMEM((rows, LANES), jnp.int32),
        ),
        in_specs=[smem] + [hbm] * 4,
        out_specs=(vmem,) * 6,
        scratch_shapes=[
            pltpu.SMEM((8, LANES), jnp.int32),
            pltpu.VMEM((rows, LANES), f32),
            pltpu.VMEM((rows, 2 * SPREAD, LANES), bf16),
            pltpu.VMEM(((CX + 1) * (NY + 1) * 8, NZ), f32),
            pltpu.SemaphoreType.DMA((5,)),
        ],
        compiler_params=pltpu.CompilerParams(vmem_limit_bytes=32 * 1024 * 1024),
        name="spread",
    )(tile_count, *[pltpu.with_memory_space_constraint(x, pltpu.HBM) for x in inputs])
    devices = lax.axis_size("gx")
    far_pairs = [(i, (i + (1 if i % 2 else -1)) % devices) for i in range(devices)]
    near_pairs = [(i, i ^ 1) for i in range(devices)]
    near_new = lax.ppermute(near, "gx", near_pairs)
    far_new = lax.ppermute(far, "gx", far_pairs)
    moved, top = pl.pallas_call(
        collect_kernel,
        out_shape=(
            jax.ShapeDtypeStruct((blocks, 8, BLOCK), f32),
            jax.ShapeDtypeStruct((8, LANES), f32),
        ),
        in_specs=[smem] + [vmem] * 8,
        out_specs=(vmem, vmem),
        scratch_shapes=[
            pltpu.SMEM((8, LANES), jnp.int32),
            pltpu.VMEM(((CX + 1) * NY * TABLE, NZ), f32),
            pltpu.VMEM(((CX + 1) * (NY + 1), 2 * TABLE, NZ), bf16),
            pltpu.SemaphoreType.DMA,
        ],
        compiler_params=pltpu.CompilerParams(vmem_limit_bytes=32 * 1024 * 1024),
        name="collect",
    )(time_step, plan, near, far, far_new, near_new, frac_here, vel_here, cells_here)
    new_frac, new_velocity = pl.pallas_call(
        finish_kernel,
        out_shape=(
            jax.ShapeDtypeStruct(frac.shape, f32),
            jax.ShapeDtypeStruct(velocity.shape, f32),
        ),
        in_specs=[vmem] * 3,
        out_specs=(vmem, vmem),
        compiler_params=pltpu.CompilerParams(vmem_limit_bytes=32 * 1024 * 1024),
        cost_estimate=pl.CostEstimate(flops=0, bytes_accessed=8000000, transcendentals=0),
        name="finish",
    )(plan, moved, frac_here)
    fastest = largest(top, "gx")
    next_step = (courant / (fastest + wave_speed))[0, :1]
    return (new_frac, new_velocity, next_step)


def solution(mesh):
    placed = (
        P(None, ("runs", "gx")),
        P(None, ("runs", "gx")),
        P(("runs", "gx")),
        P(("runs", "gx")),
        P(("runs", "gx")),
        P("runs"),
    )
    return jax.shard_map(
        body,
        mesh=mesh,
        in_specs=placed,
        out_specs=(P(None, ("runs", "gx")), P(None, ("runs", "gx")), P("runs")),
        check_vma=False,
    )
```

```python
import functools

import jax
import jax.numpy as jnp
from jax import lax
from jax.experimental import pallas as pl
from jax.experimental.pallas import tpu as pltpu
from jax.sharding import PartitionSpec as P

CX = 2
NY = 32
NZ = 128
ROWS = CX * NY
BLOCK = 256
LANES = 128
UNROLL = 8
FAST = 16
SPREAD = 32
TABLE = 16

mass_floor = 0.25
stiffness = 2.0
press_floor = 1.0
grain_size = 0.5
inertia_ref = 0.3
mu_static = 0.38
mu_limit = 0.64
rate_floor = 0.5
gravity = (0.5, 0.0, -0.866)
flip_share = 0.95
courant = 0.4
wave_speed = 2.0
components = ((0, 3, 4), (3, 1, 5), (4, 5, 2))
f32 = jnp.float32
bf16 = jnp.bfloat16


def split_pair(values):
    high = values.astype(bf16)
    low = (values - high.astype(f32)).astype(bf16)
    return high, low


def one_hot(cells_ref, block, offset):
    rel = cells_ref[pl.ds(block * 2, 2), :] - offset
    tall = (16, LANES)
    nodes = lax.broadcasted_iota(jnp.int32, tall, 0).astype(jnp.int16)
    one, zero = jnp.ones(tall, bf16), jnp.zeros(tall, bf16)
    halves = []
    for h in range(2):
        line = jnp.broadcast_to(rel[h : h + 1, :], tall).astype(jnp.int16)
        halves.append(
            jnp.concatenate(
                [
                    jnp.where(line == nodes + jnp.int16(z), one, zero)
                    for z in range(0, NZ, 16)
                ],
                axis=0,
            )
        )
    return jnp.concatenate(halves, axis=1)


def list_visits(cells_ref, count, plan_ref):
    blocks = cells_ref.shape[0] // 2
    shape = (blocks, LANES)
    number = lax.broadcasted_iota(jnp.int32, shape, 0)
    lane = lax.broadcasted_iota(jnp.int32, shape, 1)
    first_half = cells_ref[pl.ds(0, blocks, stride=2), :]
    second_half = cells_ref[pl.ds(1, blocks, stride=2), :]
    slot = number * BLOCK + lane
    reached = jnp.maximum(
        jnp.where(slot < count, first_half, 0), jnp.where(slot + LANES < count, second_half, 0)
    )
    live = number * BLOCK < count
    first = jnp.min(first_half, axis=1, keepdims=True) >> 7
    last = jnp.max(reached, axis=1, keepdims=True) >> 7
    low = jnp.where(live, first + number, 2 * LANES)
    high = jnp.where(live, last + number, -1)
    inside = (low <= lane) & (lane <= high)
    place = lane[:1]
    block = jnp.max(jnp.where(inside, number, -1), axis=0, keepdims=True)
    valid = block >= 0
    row = place - block
    plan_ref[0:1, :] = jnp.where(valid, block, 0)
    plan_ref[1:2, :] = jnp.where(valid, row + (row >> 5), 0)
    plan_ref[2:3, :] = jnp.where(valid, row, ROWS) * NZ
    plan_ref[3:4, :] = jnp.max(high, axis=0, keepdims=True) + 1
    plan_ref[4:5, :] = jnp.broadcast_to(count, (1, LANES))
    plan_ref[5:8, :] = jnp.zeros((3, LANES), jnp.int32)


def spread_kernel(
    count_ref, frac_hbm, vel_hbm, mass_hbm, cells_hbm,
    far_ref, near_ref, plan_ref, frac_ref, vel_ref, cells_ref,
    listed_ref, mass_ref, q_ref, acc_ref, sems,
):
    slots = frac_ref.shape[1]
    sources = (cells_hbm, frac_hbm, vel_hbm, mass_hbm)
    targets = (cells_ref, frac_ref, vel_ref, mass_ref)
    arrivals = [
        pltpu.make_async_copy(source, target, sems.at[k])
        for k, (source, target) in enumerate(zip(sources, targets))
    ]
    for arrival in arrivals:
        arrival.start()
    acc_ref[...] = jnp.zeros_like(acc_ref)
    arrivals[0].wait()
    count = count_ref[0]
    list_visits(cells_ref, count, plan_ref)
    listing = pltpu.make_async_copy(plan_ref, listed_ref, sems.at[4])
    listing.start()
    for arrival in arrivals[1:]:
        arrival.wait()
    sublane = lax.broadcasted_iota(jnp.int32, (8, LANES), 0)
    lane = lax.broadcasted_iota(jnp.int32, (1, LANES), 1)
    top_z = sublane >= 4
    field = sublane & 3

    def weigh(part):
        at = pl.multiple_of(part * LANES, LANES)
        here = pl.ds(at, LANES)

        def spread_out(line):
            return jnp.broadcast_to(line, (8, LANES))

        fx, fy, fz = (spread_out(frac_ref[d : d + 1, here]) for d in range(3))
        vx, vy, vz = (spread_out(vel_ref[d : d + 1, here]) for d in range(3))
        held = spread_out(jnp.where(at + lane < count, mass_ref[pl.ds(part, 1), :], 0.0))
        carried = jnp.where(
            field == 0, held, held * jnp.where(field == 1, vx, jnp.where(field == 2, vy, vz))
        )
        carried = carried * jnp.where(top_z, fz, 1.0 - fz)
        lower, upper = carried * (1.0 - fx), carried * fx
        rows = jnp.concatenate(
            [lower * (1.0 - fy), lower * fy, upper * (1.0 - fy), upper * fy], axis=0
        )
        high, low = split_pair(rows)
        q_ref[pl.ds(part, 1)] = jnp.concatenate([high, low], axis=0)[None]

    def prepare(group, carry):
        for u in range(UNROLL):
            weigh(group * UNROLL + u)
        return carry

    lax.fori_loop(0, slots // LANES // UNROLL, prepare, 0)
    listing.wait()
    total = listed_ref[3, 0]

    def visit(group, carry):
        found = []
        for u in range(FAST):
            v = group * FAST + u
            block = listed_ref[0, v]
            hot = one_hot(cells_ref, block, listed_ref[2, v])
            both = q_ref[pl.ds(block * 2, 2)]
            both = lax.dot_general(
                jnp.concatenate([both[0], both[1]], axis=1),
                hot,
                (((1,), (1,)), ((), ())),
                preferred_element_type=f32,
            )
            found.append((listed_ref[1, v], both[:SPREAD] + both[SPREAD:]))
        for base, part in found:
            for k, ahead in enumerate((0, 1, NY + 1, NY + 2)):
                at = pl.ds(pl.multiple_of((base + ahead) * 8, 8), 8)
                acc_ref[at, :] += part[8 * k : 8 * k + 8]
        return carry

    lax.fori_loop(0, (total + FAST - 1) // FAST, visit, 0)

    layers = []
    for l in range(CX + 1):
        first = l * (NY + 1) * 8
        acc_ref[first : first + 8, :] += acc_ref[first + NY * 8 : first + NY * 8 + 8, :]
        for f in range(4):
            lower = acc_ref[pl.ds(first + f, NY, stride=8), :]
            upper = acc_ref[pl.ds(first + 4 + f, NY, stride=8), :]
            layers.append(lower + pltpu.roll(upper, 1, 1))
    odd = lax.axis_index("gx") % 2 == 1
    for l in range(CX):
        for f in range(4):
            low, high = layers[l * 4 + f], layers[(l + 1) * 4 + f]
            near_ref[f * CX + l] = jnp.where(odd, low, high)
            far_ref[f * CX + l] = jnp.where(odd, high, low)


def pair_up(field, axis):
    return field + pltpu.roll(field, field.shape[axis] - 1, axis)


def step_up(field, axis):
    return pltpu.roll(field, field.shape[axis] - 1, axis) - field


def pair_down(field, axis):
    return field + pltpu.roll(field, 1, axis)


def step_down(field, axis):
    return field - pltpu.roll(field, 1, axis)


def cell_stress(vel_lo, vel_hi, mass_lo, mass_hi, keep):
    grads = []
    for a in range(3):
        diff = vel_hi[a] - vel_lo[a]
        both = vel_hi[a] + vel_lo[a]
        grads.append(
            [
                0.25 * pair_up(pair_up(diff, 0), 1),
                0.25 * pair_up(step_up(both, 0), 1),
                0.25 * step_up(pair_up(both, 0), 1),
            ]
        )
    density = 0.125 * pair_up(pair_up(mass_hi + mass_lo, 0), 1)
    dxx = grads[0][0]
    dyy = grads[1][1]
    dzz = grads[2][2]
    dxy = 0.5 * (grads[0][1] + grads[1][0])
    dxz = 0.5 * (grads[0][2] + grads[2][0])
    dyz = 0.5 * (grads[1][2] + grads[2][1])
    second = dxx * dxx + dyy * dyy + dzz * dzz + 2.0 * (dxy * dxy + dxz * dxz + dyz * dyz)
    rate = jnp.sqrt(2.0 * second + rate_floor * rate_floor)
    pressure = stiffness * density
    inertial = rate * grain_size / jnp.sqrt(pressure + press_floor)
    friction = mu_static + (mu_limit - mu_static) * inertial / (inertia_ref + inertial)
    twice = 2.0 * friction * pressure / rate
    sigma = [
        twice * dxx - pressure,
        twice * dyy - pressure,
        twice * dzz - pressure,
        twice * dxy,
        twice * dxz,
        twice * dyz,
    ]
    return [jnp.where(keep, s, 0.0) for s in sigma]


def node_force(lower, upper):
    force = []
    for a in range(3):
        sx, sy, sz = (components[a][b] for b in range(3))
        along = pair_down(pair_down(upper[sx] - lower[sx], 0), 1)
        across = step_down(pair_down(upper[sy] + lower[sy], 1), 0)
        upward = step_down(pair_down(upper[sz] + lower[sz], 0), 1)
        force.append(0.25 * (along + across + upward))
    return force


def collect_kernel(
    step_ref, plan_ref, near_ref, far_ref, far_new_ref, near_new_ref, frac_ref, vel_ref, cells_ref,
    out_ref, top_ref, listed_ref, tab_ref, pair_ref, sem,
):
    blocks = frac_ref.shape[1] // BLOCK
    listing = pltpu.make_async_copy(plan_ref, listed_ref, sem)
    listing.start()
    step = step_ref[0]
    odd = lax.axis_index("gx") % 2 == 1

    def pick(if_odd, if_even):
        return [jnp.where(odd, if_odd[k], if_even[k]) for k in range(4 * CX)]

    low, high = pick(near_ref, far_ref), pick(far_ref, near_ref)
    left, right = pick(near_new_ref, far_new_ref), pick(far_new_ref, near_new_ref)
    nodes = [
        [left[f * 2] for f in range(4)],
        [low[f * 2] + left[f * 2 + 1] for f in range(4)],
        [low[f * 2 + 1] for f in range(4)],
        [high[f * 2 + 1] + right[f * 2] for f in range(4)],
        [right[f * 2 + 1] for f in range(4)],
    ]
    height = lax.broadcasted_iota(jnp.int32, (NY, NZ), 1)
    keep = height < NZ - 1
    above_bed = height > 0
    floor = [jnp.maximum(layer[0], mass_floor) for layer in nodes]
    v_old = [[layer[1 + a] / floor[l] for a in range(3)] for l, layer in enumerate(nodes)]
    sigma = [
        cell_stress(v_old[l], v_old[l + 1], nodes[l][0], nodes[l + 1][0], keep) for l in range(4)
    ]
    blank = jnp.zeros((NY, NZ), f32)
    for l in range(CX + 1):
        force = node_force(sigma[l], sigma[l + 1])
        fields = [blank] * 8
        for a in range(3):
            layer = nodes[l + 1]
            fresh = (layer[1 + a] + step * (force[a] + layer[0] * gravity[a])) / floor[l + 1]
            fresh = jnp.where(above_bed, fresh, 0.0)
            fields[a] = fresh - flip_share * v_old[l + 1][a]
            fields[4 + a] = step * fresh
        for k, value in enumerate(fields):
            start = l * NY * TABLE + k
            tab_ref[pl.ds(start, NY, stride=TABLE), :] = value
            tab_ref[pl.ds(start + 8, NY, stride=TABLE), :] = pltpu.roll(value, NZ - 1, 1)

    for l in range(CX + 1):

        def split_row(j, carry):
            at = pl.ds(pl.multiple_of((l * NY + j) * TABLE, TABLE), TABLE)
            high, low = split_pair(tab_ref[at, :])
            pair_ref[pl.ds(l * (NY + 1) + j, 1)] = jnp.concatenate([high, low], axis=1)[None]
            return carry

        lax.fori_loop(0, NY, split_row, 0, unroll=8)
        pair_ref[l * (NY + 1) + NY] = pair_ref[l * (NY + 1)]

    out_ref[...] = jnp.zeros_like(out_ref)
    listing.wait()
    total = listed_ref[3, 0]
    count = listed_ref[4, 0]

    def visit(group, carry):
        found = []
        for u in range(UNROLL):
            v = group * UNROLL + u
            block = listed_ref[0, v]
            base = listed_ref[1, v]
            hot = one_hot(cells_ref, block, listed_ref[2, v])
            rows = [pair_ref[base + ahead] for ahead in (0, 1, NY + 1, NY + 2)]
            value = jnp.dot(
                jnp.concatenate(rows, axis=0),
                jnp.concatenate([hot, hot], axis=0),
                preferred_element_type=f32,
            )
            corners = [value[8 * k : 8 * k + 8] for k in range(8)]
            frac = frac_ref[:, pl.ds(pl.multiple_of(block * BLOCK, BLOCK), BLOCK)]
            for d in (2, 1, 0):
                share = frac[d : d + 1, :]
                corners = [
                    corners[k] + share * (corners[k + 1] - corners[k])
                    for k in range(0, len(corners), 2)
                ]
            found.append((block, corners[0]))
        for block, part in found:
            out_ref[pl.ds(block, 1)] += part[None]
        return carry

    lax.fori_loop(0, (total + UNROLL - 1) // UNROLL, visit, 0)

    lane = lax.broadcasted_iota(jnp.int32, (1, BLOCK), 1)

    def finish(block, top):
        at = pl.multiple_of(block * BLOCK, BLOCK)
        alive = at + lane < count
        got = out_ref[pl.ds(block, 1)][0]
        fresh = jnp.where(alive, flip_share * vel_ref[:, pl.ds(at, BLOCK)] + got[0:3], 0.0)
        out_ref[pl.ds(block, 1), 0:3] = fresh[None]
        square = fresh[0:1] * fresh[0:1] + fresh[1:2] * fresh[1:2] + fresh[2:3] * fresh[2:3]
        return jnp.maximum(top, square)

    top = lax.fori_loop(0, blocks, finish, jnp.zeros((1, BLOCK), f32), unroll=4)
    top = jnp.sqrt(jnp.max(top, axis=1, keepdims=True))
    top_ref[...] = jnp.broadcast_to(top, top_ref.shape)


def finish_kernel(plan_ref, moved_ref, frac_ref, new_frac_ref, new_vel_ref):
    blocks = frac_ref.shape[1] // BLOCK
    count = plan_ref[4:5, :]
    count = jnp.concatenate([count, count], axis=1)
    lane = lax.broadcasted_iota(jnp.int32, (1, BLOCK), 1)

    def finish(block, carry):
        at = pl.multiple_of(block * BLOCK, BLOCK)
        got = moved_ref[pl.ds(block, 1)][0]
        new_vel_ref[:, pl.ds(at, BLOCK)] = got[0:3]
        placed = jnp.where(at + lane < count, frac_ref[:, pl.ds(at, BLOCK)] + got[4:7], 0.0)
        new_frac_ref[:, pl.ds(at, BLOCK)] = placed
        return carry

    lax.fori_loop(0, blocks, finish, 0, unroll=4)


def largest(value, axis):
    devices = lax.axis_size(axis)
    reach = 1
    while reach < devices:
        if devices & (devices - 1) == 0:
            pairs = [(i, i ^ (reach | 1)) for i in range(devices)]
        else:
            pairs = [(i, (i + reach) % devices) for i in range(devices)]
        value = jnp.maximum(value, lax.ppermute(value, axis, pairs))
        reach *= 2
    return value


smem = pl.BlockSpec(memory_space=pltpu.SMEM)
vmem = pl.BlockSpec(memory_space=pltpu.VMEM)
hbm = pl.BlockSpec(memory_space=pltpu.HBM)


def body(frac, velocity, mass, particle_cell, tile_count, time_step):
    slots = frac.shape[1]
    blocks = slots // BLOCK
    rows = slots // LANES
    inputs = (frac, velocity, mass.reshape(rows, LANES), particle_cell.reshape(rows, LANES))
    layer_pair = pltpu.VMEM((4 * CX, NY, NZ), f32)
    far, near, plan, frac_here, vel_here, cells_here = pl.pallas_call(
        spread_kernel,
        out_shape=(
            layer_pair,
            layer_pair,
            pltpu.VMEM((8, LANES), jnp.int32),
            pltpu.VMEM(frac.shape, f32),
            pltpu.VMEM(velocity.shape, f32),
            pltpu.VMEM((rows, LANES), jnp.int32),
        ),
        in_specs=[smem] + [hbm] * 4,
        out_specs=(vmem,) * 6,
        scratch_shapes=[
            pltpu.SMEM((8, LANES), jnp.int32),
            pltpu.VMEM((rows, LANES), f32),
            pltpu.VMEM((rows, 2 * SPREAD, LANES), bf16),
            pltpu.VMEM(((CX + 1) * (NY + 1) * 8, NZ), f32),
            pltpu.SemaphoreType.DMA((5,)),
        ],
        compiler_params=pltpu.CompilerParams(vmem_limit_bytes=32 * 1024 * 1024),
        name="spread",
    )(tile_count, *[pltpu.with_memory_space_constraint(x, pltpu.HBM) for x in inputs])
    devices = lax.axis_size("gx")
    far_pairs = [(i, (i + (1 if i % 2 else -1)) % devices) for i in range(devices)]
    near_pairs = [(i, i ^ 1) for i in range(devices)]
    near_new = lax.ppermute(near, "gx", near_pairs)
    far_new = lax.ppermute(far, "gx", far_pairs)
    moved, top = pl.pallas_call(
        collect_kernel,
        out_shape=(
            jax.ShapeDtypeStruct((blocks, 8, BLOCK), f32),
            jax.ShapeDtypeStruct((8, LANES), f32),
        ),
        in_specs=[smem] + [vmem] * 8,
        out_specs=(vmem, vmem),
        scratch_shapes=[
            pltpu.SMEM((8, LANES), jnp.int32),
            pltpu.VMEM(((CX + 1) * NY * TABLE, NZ), f32),
            pltpu.VMEM(((CX + 1) * (NY + 1), TABLE, 2 * NZ), bf16),
            pltpu.SemaphoreType.DMA,
        ],
        compiler_params=pltpu.CompilerParams(vmem_limit_bytes=32 * 1024 * 1024),
        name="collect",
    )(time_step, plan, near, far, far_new, near_new, frac_here, vel_here, cells_here)
    new_frac, new_velocity = pl.pallas_call(
        finish_kernel,
        out_shape=(
            jax.ShapeDtypeStruct(frac.shape, f32),
            jax.ShapeDtypeStruct(velocity.shape, f32),
        ),
        in_specs=[vmem] * 3,
        out_specs=(vmem, vmem),
        compiler_params=pltpu.CompilerParams(vmem_limit_bytes=32 * 1024 * 1024),
        cost_estimate=pl.CostEstimate(flops=0, bytes_accessed=8000000, transcendentals=0),
        name="finish",
    )(plan, moved, frac_here)
    fastest = largest(top, "gx")
    next_step = (courant / (fastest + wave_speed))[0, :1]
    return (new_frac, new_velocity, next_step)


def solution(mesh):
    placed = (
        P(None, ("runs", "gx")),
        P(None, ("runs", "gx")),
        P(("runs", "gx")),
        P(("runs", "gx")),
        P(("runs", "gx")),
        P("runs"),
    )
    return jax.shard_map(
        body,
        mesh=mesh,
        in_specs=placed,
        out_specs=(P(None, ("runs", "gx")), P(None, ("runs", "gx")), P("runs")),
        check_vma=False,
    )
```

```python
import functools

import jax
import jax.numpy as jnp
from jax import lax
from jax.experimental import pallas as pl
from jax.experimental.pallas import tpu as pltpu
from jax.sharding import PartitionSpec as P

CX = 2
NY = 32
NZ = 128
ROWS = CX * NY
BLOCK = 256
LANES = 128
UNROLL = 8
GIVEN = 32
TAKEN = 16
SPREAD = 32
TABLE = 16

mass_floor = 0.25
stiffness = 2.0
press_floor = 1.0
grain_size = 0.5
inertia_ref = 0.3
mu_static = 0.38
mu_limit = 0.64
rate_floor = 0.5
gravity = (0.5, 0.0, -0.866)
flip_share = 0.95
courant = 0.4
wave_speed = 2.0
components = ((0, 3, 4), (3, 1, 5), (4, 5, 2))
f32 = jnp.float32
bf16 = jnp.bfloat16


def split_pair(values):
    high = values.astype(bf16)
    low = (values - high.astype(f32)).astype(bf16)
    return high, low


def one_hot(cells_ref, block, offset):
    rel = cells_ref[pl.ds(block * 2, 2), :] - offset
    tall = (16, LANES)
    nodes = lax.broadcasted_iota(jnp.int32, tall, 0).astype(jnp.int16)
    one, zero = jnp.ones(tall, bf16), jnp.zeros(tall, bf16)
    halves = []
    for h in range(2):
        line = jnp.broadcast_to(rel[h : h + 1, :], tall).astype(jnp.int16)
        halves.append(
            jnp.concatenate(
                [
                    jnp.where(line == nodes + jnp.int16(z), one, zero)
                    for z in range(0, NZ, 16)
                ],
                axis=0,
            )
        )
    return jnp.concatenate(halves, axis=1)


def list_visits(cells_ref, count, plan_ref):
    blocks = cells_ref.shape[0] // 2
    shape = (blocks, LANES)
    number = lax.broadcasted_iota(jnp.int32, shape, 0)
    lane = lax.broadcasted_iota(jnp.int32, shape, 1)
    first_half = cells_ref[pl.ds(0, blocks, stride=2), :]
    second_half = cells_ref[pl.ds(1, blocks, stride=2), :]
    slot = number * BLOCK + lane
    reached = jnp.maximum(
        jnp.where(slot < count, first_half, 0), jnp.where(slot + LANES < count, second_half, 0)
    )
    live = number * BLOCK < count
    first = jnp.min(first_half, axis=1, keepdims=True) >> 7
    last = jnp.max(reached, axis=1, keepdims=True) >> 7
    low = jnp.where(live, first + number, 2 * LANES)
    high = jnp.where(live, last + number, -1)
    inside = (low <= lane) & (lane <= high)
    place = lane[:1]
    block = jnp.max(jnp.where(inside, number, -1), axis=0, keepdims=True)
    valid = block >= 0
    row = place - block
    plan_ref[0:1, :] = jnp.where(valid, block, 0)
    plan_ref[1:2, :] = jnp.where(valid, row + (row >> 5), 0)
    plan_ref[2:3, :] = jnp.where(valid, row, ROWS) * NZ
    plan_ref[3:4, :] = jnp.max(high, axis=0, keepdims=True) + 1
    plan_ref[4:5, :] = jnp.broadcast_to(count, (1, LANES))
    plan_ref[5:8, :] = jnp.zeros((3, LANES), jnp.int32)


def spread_kernel(
    count_ref, frac_hbm, vel_hbm, mass_hbm, cells_hbm,
    far_ref, near_ref, plan_ref, frac_ref, vel_ref, cells_ref,
    listed_ref, mass_ref, q_ref, acc_ref, sems,
):
    slots = frac_ref.shape[1]
    sources = (cells_hbm, frac_hbm, vel_hbm, mass_hbm)
    targets = (cells_ref, frac_ref, vel_ref, mass_ref)
    arrivals = [
        pltpu.make_async_copy(source, target, sems.at[k])
        for k, (source, target) in enumerate(zip(sources, targets))
    ]
    for arrival in arrivals:
        arrival.start()
    acc_ref[...] = jnp.zeros_like(acc_ref)
    arrivals[0].wait()
    count = count_ref[0]
    list_visits(cells_ref, count, plan_ref)
    listing = pltpu.make_async_copy(plan_ref, listed_ref, sems.at[4])
    listing.start()
    for arrival in arrivals[1:]:
        arrival.wait()
    sublane = lax.broadcasted_iota(jnp.int32, (8, LANES), 0)
    lane = lax.broadcasted_iota(jnp.int32, (1, LANES), 1)
    top_z = sublane >= 4
    field = sublane & 3

    def weigh(part):
        at = pl.multiple_of(part * LANES, LANES)
        here = pl.ds(at, LANES)

        def spread_out(line):
            return jnp.broadcast_to(line, (8, LANES))

        fx, fy, fz = (spread_out(frac_ref[d : d + 1, here]) for d in range(3))
        vx, vy, vz = (spread_out(vel_ref[d : d + 1, here]) for d in range(3))
        held = spread_out(jnp.where(at + lane < count, mass_ref[pl.ds(part, 1), :], 0.0))
        carried = jnp.where(
            field == 0, held, held * jnp.where(field == 1, vx, jnp.where(field == 2, vy, vz))
        )
        carried = carried * jnp.where(top_z, fz, 1.0 - fz)
        lower, upper = carried * (1.0 - fx), carried * fx
        rows = jnp.concatenate(
            [lower * (1.0 - fy), lower * fy, upper * (1.0 - fy), upper * fy], axis=0
        )
        high, low = split_pair(rows)
        q_ref[pl.ds(part, 1)] = jnp.concatenate([high, low], axis=0)[None]

    def prepare(group, carry):
        for u in range(UNROLL):
            weigh(group * UNROLL + u)
        return carry

    lax.fori_loop(0, slots // LANES // UNROLL, prepare, 0)
    listing.wait()
    total = listed_ref[3, 0]

    def visit(group, carry):
        found = []
        for u in range(GIVEN):
            v = group * GIVEN + u
            block = listed_ref[0, v]
            hot = one_hot(cells_ref, block, listed_ref[2, v])
            both = q_ref[pl.ds(block * 2, 2)]
            both = lax.dot_general(
                jnp.concatenate([both[0], both[1]], axis=1),
                hot,
                (((1,), (1,)), ((), ())),
                preferred_element_type=f32,
            )
            found.append((listed_ref[1, v], both[:SPREAD] + both[SPREAD:]))
        for base, part in found:
            for k, ahead in enumerate((0, 1, NY + 1, NY + 2)):
                at = pl.ds(pl.multiple_of((base + ahead) * 8, 8), 8)
                acc_ref[at, :] += part[8 * k : 8 * k + 8]
        return carry

    lax.fori_loop(0, (total + GIVEN - 1) // GIVEN, visit, 0)

    layers = []
    for l in range(CX + 1):
        first = l * (NY + 1) * 8
        acc_ref[first : first + 8, :] += acc_ref[first + NY * 8 : first + NY * 8 + 8, :]
        for f in range(4):
            lower = acc_ref[pl.ds(first + f, NY, stride=8), :]
            upper = acc_ref[pl.ds(first + 4 + f, NY, stride=8), :]
            layers.append(lower + pltpu.roll(upper, 1, 1))
    odd = lax.axis_index("gx") % 2 == 1
    for l in range(CX):
        for f in range(4):
            low, high = layers[l * 4 + f], layers[(l + 1) * 4 + f]
            near_ref[f * CX + l] = jnp.where(odd, low, high)
            far_ref[f * CX + l] = jnp.where(odd, high, low)


def pair_up(field, axis):
    return field + pltpu.roll(field, field.shape[axis] - 1, axis)


def step_up(field, axis):
    return pltpu.roll(field, field.shape[axis] - 1, axis) - field


def pair_down(field, axis):
    return field + pltpu.roll(field, 1, axis)


def step_down(field, axis):
    return field - pltpu.roll(field, 1, axis)


def cell_stress(vel_lo, vel_hi, mass_lo, mass_hi, keep):
    grads = []
    for a in range(3):
        diff = vel_hi[a] - vel_lo[a]
        both = vel_hi[a] + vel_lo[a]
        grads.append(
            [
                0.25 * pair_up(pair_up(diff, 0), 1),
                0.25 * pair_up(step_up(both, 0), 1),
                0.25 * step_up(pair_up(both, 0), 1),
            ]
        )
    density = 0.125 * pair_up(pair_up(mass_hi + mass_lo, 0), 1)
    dxx = grads[0][0]
    dyy = grads[1][1]
    dzz = grads[2][2]
    dxy = 0.5 * (grads[0][1] + grads[1][0])
    dxz = 0.5 * (grads[0][2] + grads[2][0])
    dyz = 0.5 * (grads[1][2] + grads[2][1])
    second = dxx * dxx + dyy * dyy + dzz * dzz + 2.0 * (dxy * dxy + dxz * dxz + dyz * dyz)
    rate = jnp.sqrt(2.0 * second + rate_floor * rate_floor)
    pressure = stiffness * density
    inertial = rate * grain_size / jnp.sqrt(pressure + press_floor)
    friction = mu_static + (mu_limit - mu_static) * inertial / (inertia_ref + inertial)
    twice = 2.0 * friction * pressure / rate
    sigma = [
        twice * dxx - pressure,
        twice * dyy - pressure,
        twice * dzz - pressure,
        twice * dxy,
        twice * dxz,
        twice * dyz,
    ]
    return [jnp.where(keep, s, 0.0) for s in sigma]


def node_force(lower, upper):
    force = []
    for a in range(3):
        sx, sy, sz = (components[a][b] for b in range(3))
        along = pair_down(pair_down(upper[sx] - lower[sx], 0), 1)
        across = step_down(pair_down(upper[sy] + lower[sy], 1), 0)
        upward = step_down(pair_down(upper[sz] + lower[sz], 0), 1)
        force.append(0.25 * (along + across + upward))
    return force


def collect_kernel(
    step_ref, plan_ref, near_ref, far_ref, far_new_ref, near_new_ref, frac_ref, vel_ref, cells_ref,
    out_ref, top_ref, listed_ref, tab_ref, pair_ref, sem,
):
    blocks = frac_ref.shape[1] // BLOCK
    listing = pltpu.make_async_copy(plan_ref, listed_ref, sem)
    listing.start()
    step = step_ref[0]
    odd = lax.axis_index("gx") % 2 == 1

    def pick(if_odd, if_even):
        return [jnp.where(odd, if_odd[k], if_even[k]) for k in range(4 * CX)]

    low, high = pick(near_ref, far_ref), pick(far_ref, near_ref)
    left, right = pick(near_new_ref, far_new_ref), pick(far_new_ref, near_new_ref)
    nodes = [
        [left[f * 2] for f in range(4)],
        [low[f * 2] + left[f * 2 + 1] for f in range(4)],
        [low[f * 2 + 1] for f in range(4)],
        [high[f * 2 + 1] + right[f * 2] for f in range(4)],
        [right[f * 2 + 1] for f in range(4)],
    ]
    height = lax.broadcasted_iota(jnp.int32, (NY, NZ), 1)
    keep = height < NZ - 1
    above_bed = height > 0
    floor = [jnp.maximum(layer[0], mass_floor) for layer in nodes]
    v_old = [[layer[1 + a] / floor[l] for a in range(3)] for l, layer in enumerate(nodes)]
    sigma = [
        cell_stress(v_old[l], v_old[l + 1], nodes[l][0], nodes[l + 1][0], keep) for l in range(4)
    ]
    blank = jnp.zeros((NY, NZ), f32)
    for l in range(CX + 1):
        force = node_force(sigma[l], sigma[l + 1])
        fields = [blank] * 8
        for a in range(3):
            layer = nodes[l + 1]
            fresh = (layer[1 + a] + step * (force[a] + layer[0] * gravity[a])) / floor[l + 1]
            fresh = jnp.where(above_bed, fresh, 0.0)
            fields[a] = fresh - flip_share * v_old[l + 1][a]
            fields[4 + a] = step * fresh
        for k, value in enumerate(fields):
            start = l * NY * TABLE + k
            tab_ref[pl.ds(start, NY, stride=TABLE), :] = value
            tab_ref[pl.ds(start + 8, NY, stride=TABLE), :] = pltpu.roll(value, NZ - 1, 1)

    for l in range(CX + 1):

        def split_row(j, carry):
            at = pl.ds(pl.multiple_of((l * NY + j) * TABLE, TABLE), TABLE)
            high, low = split_pair(tab_ref[at, :])
            pair_ref[pl.ds(l * (NY + 1) + j, 1)] = jnp.concatenate([high, low], axis=1)[None]
            return carry

        lax.fori_loop(0, NY, split_row, 0, unroll=8)
        pair_ref[l * (NY + 1) + NY] = pair_ref[l * (NY + 1)]

    out_ref[...] = jnp.zeros_like(out_ref)
    listing.wait()
    total = listed_ref[3, 0]
    count = listed_ref[4, 0]

    def visit(group, carry):
        found = []
        for u in range(TAKEN):
            v = group * TAKEN + u
            block = listed_ref[0, v]
            base = listed_ref[1, v]
            hot = one_hot(cells_ref, block, listed_ref[2, v])
            rows = [pair_ref[base + ahead] for ahead in (0, 1, NY + 1, NY + 2)]
            value = jnp.dot(
                jnp.concatenate(rows, axis=0),
                jnp.concatenate([hot, hot], axis=0),
                preferred_element_type=f32,
            )
            corners = [value[8 * k : 8 * k + 8] for k in range(8)]
            frac = frac_ref[:, pl.ds(pl.multiple_of(block * BLOCK, BLOCK), BLOCK)]
            for d in (2, 1, 0):
                share = frac[d : d + 1, :]
                corners = [
                    corners[k] + share * (corners[k + 1] - corners[k])
                    for k in range(0, len(corners), 2)
                ]
            found.append((block, corners[0]))
        for block, part in found:
            out_ref[pl.ds(block, 1)] += part[None]
        return carry

    lax.fori_loop(0, (total + TAKEN - 1) // TAKEN, visit, 0)

    lane = lax.broadcasted_iota(jnp.int32, (1, BLOCK), 1)

    def finish(block, top):
        at = pl.multiple_of(block * BLOCK, BLOCK)
        alive = at + lane < count
        got = out_ref[pl.ds(block, 1)][0]
        fresh = jnp.where(alive, flip_share * vel_ref[:, pl.ds(at, BLOCK)] + got[0:3], 0.0)
        out_ref[pl.ds(block, 1), 0:3] = fresh[None]
        square = fresh[0:1] * fresh[0:1] + fresh[1:2] * fresh[1:2] + fresh[2:3] * fresh[2:3]
        return jnp.maximum(top, square)

    top = lax.fori_loop(0, blocks, finish, jnp.zeros((1, BLOCK), f32), unroll=4)
    top = jnp.sqrt(jnp.max(top, axis=1, keepdims=True))
    top_ref[...] = jnp.broadcast_to(top, top_ref.shape)


def finish_kernel(plan_ref, moved_ref, frac_ref, new_frac_ref, new_vel_ref):
    blocks = frac_ref.shape[1] // BLOCK
    count = plan_ref[4:5, :]
    count = jnp.concatenate([count, count], axis=1)
    lane = lax.broadcasted_iota(jnp.int32, (1, BLOCK), 1)

    def finish(block, carry):
        at = pl.multiple_of(block * BLOCK, BLOCK)
        got = moved_ref[pl.ds(block, 1)][0]
        new_vel_ref[:, pl.ds(at, BLOCK)] = got[0:3]
        placed = jnp.where(at + lane < count, frac_ref[:, pl.ds(at, BLOCK)] + got[4:7], 0.0)
        new_frac_ref[:, pl.ds(at, BLOCK)] = placed
        return carry

    lax.fori_loop(0, blocks, finish, 0, unroll=4)


def largest(value, axis):
    devices = lax.axis_size(axis)
    reach = 1
    while reach < devices:
        if devices & (devices - 1) == 0:
            pairs = [(i, i ^ (reach | 1)) for i in range(devices)]
        else:
            pairs = [(i, (i + reach) % devices) for i in range(devices)]
        value = jnp.maximum(value, lax.ppermute(value, axis, pairs))
        reach *= 2
    return value


smem = pl.BlockSpec(memory_space=pltpu.SMEM)
vmem = pl.BlockSpec(memory_space=pltpu.VMEM)
hbm = pl.BlockSpec(memory_space=pltpu.HBM)


def body(frac, velocity, mass, particle_cell, tile_count, time_step):
    slots = frac.shape[1]
    blocks = slots // BLOCK
    rows = slots // LANES
    inputs = (frac, velocity, mass.reshape(rows, LANES), particle_cell.reshape(rows, LANES))
    layer_pair = pltpu.VMEM((4 * CX, NY, NZ), f32)
    far, near, plan, frac_here, vel_here, cells_here = pl.pallas_call(
        spread_kernel,
        out_shape=(
            layer_pair,
            layer_pair,
            pltpu.VMEM((8, LANES), jnp.int32),
            pltpu.VMEM(frac.shape, f32),
            pltpu.VMEM(velocity.shape, f32),
            pltpu.VMEM((rows, LANES), jnp.int32),
        ),
        in_specs=[smem] + [hbm] * 4,
        out_specs=(vmem,) * 6,
        scratch_shapes=[
            pltpu.SMEM((8, LANES), jnp.int32),
            pltpu.VMEM((rows, LANES), f32),
            pltpu.VMEM((rows, 2 * SPREAD, LANES), bf16),
            pltpu.VMEM(((CX + 1) * (NY + 1) * 8, NZ), f32),
            pltpu.SemaphoreType.DMA((5,)),
        ],
        compiler_params=pltpu.CompilerParams(vmem_limit_bytes=32 * 1024 * 1024),
        name="spread",
    )(tile_count, *[pltpu.with_memory_space_constraint(x, pltpu.HBM) for x in inputs])
    devices = lax.axis_size("gx")
    far_pairs = [(i, (i + (1 if i % 2 else -1)) % devices) for i in range(devices)]
    near_pairs = [(i, i ^ 1) for i in range(devices)]
    near_new = lax.ppermute(near, "gx", near_pairs)
    far_new = lax.ppermute(far, "gx", far_pairs)
    moved, top = pl.pallas_call(
        collect_kernel,
        out_shape=(
            jax.ShapeDtypeStruct((blocks, 8, BLOCK), f32),
            jax.ShapeDtypeStruct((8, LANES), f32),
        ),
        in_specs=[smem] + [vmem] * 8,
        out_specs=(vmem, vmem),
        scratch_shapes=[
            pltpu.SMEM((8, LANES), jnp.int32),
            pltpu.VMEM(((CX + 1) * NY * TABLE, NZ), f32),
            pltpu.VMEM(((CX + 1) * (NY + 1), TABLE, 2 * NZ), bf16),
            pltpu.SemaphoreType.DMA,
        ],
        compiler_params=pltpu.CompilerParams(vmem_limit_bytes=32 * 1024 * 1024),
        name="collect",
    )(time_step, plan, near, far, far_new, near_new, frac_here, vel_here, cells_here)
    new_frac, new_velocity = pl.pallas_call(
        finish_kernel,
        out_shape=(
            jax.ShapeDtypeStruct(frac.shape, f32),
            jax.ShapeDtypeStruct(velocity.shape, f32),
        ),
        in_specs=[vmem] * 3,
        out_specs=(vmem, vmem),
        compiler_params=pltpu.CompilerParams(vmem_limit_bytes=32 * 1024 * 1024),
        cost_estimate=pl.CostEstimate(flops=0, bytes_accessed=8000000, transcendentals=0),
        name="finish",
    )(plan, moved, frac_here)
    fastest = largest(top, "gx")
    next_step = (courant / (fastest + wave_speed))[0, :1]
    return (new_frac, new_velocity, next_step)


def solution(mesh):
    placed = (
        P(None, ("runs", "gx")),
        P(None, ("runs", "gx")),
        P(("runs", "gx")),
        P(("runs", "gx")),
        P(("runs", "gx")),
        P("runs"),
    )
    return jax.shard_map(
        body,
        mesh=mesh,
        in_specs=placed,
        out_specs=(P(None, ("runs", "gx")), P(None, ("runs", "gx")), P("runs")),
        check_vma=False,
    )
```

```python
import functools

import jax
import jax.numpy as jnp
from jax import lax
from jax.experimental import pallas as pl
from jax.experimental.pallas import tpu as pltpu
from jax.sharding import PartitionSpec as P

CX = 2
NY = 32
NZ = 128
ROWS = CX * NY
BLOCK = 256
LANES = 128
UNROLL = 8
GIVEN = 32
TAKEN = 32
SPREAD = 32
TABLE = 16

mass_floor = 0.25
stiffness = 2.0
press_floor = 1.0
grain_size = 0.5
inertia_ref = 0.3
mu_static = 0.38
mu_limit = 0.64
rate_floor = 0.5
gravity = (0.5, 0.0, -0.866)
flip_share = 0.95
courant = 0.4
wave_speed = 2.0
components = ((0, 3, 4), (3, 1, 5), (4, 5, 2))
f32 = jnp.float32
bf16 = jnp.bfloat16


def split_pair(values):
    high = values.astype(bf16)
    low = (values - high.astype(f32)).astype(bf16)
    return high, low


def one_hot(cells_ref, block, offset):
    rel = cells_ref[pl.ds(block * 2, 2), :] - offset
    tall = (16, LANES)
    nodes = lax.broadcasted_iota(jnp.int32, tall, 0).astype(jnp.int16)
    one, zero = jnp.ones(tall, bf16), jnp.zeros(tall, bf16)
    halves = []
    for h in range(2):
        line = jnp.broadcast_to(rel[h : h + 1, :], tall).astype(jnp.int16)
        halves.append(
            jnp.concatenate(
                [
                    jnp.where(line == nodes + jnp.int16(z), one, zero)
                    for z in range(0, NZ, 16)
                ],
                axis=0,
            )
        )
    return jnp.concatenate(halves, axis=1)


def list_visits(cells_ref, count, plan_ref):
    blocks = cells_ref.shape[0] // 2
    shape = (blocks, LANES)
    number = lax.broadcasted_iota(jnp.int32, shape, 0)
    lane = lax.broadcasted_iota(jnp.int32, shape, 1)
    first_half = cells_ref[pl.ds(0, blocks, stride=2), :]
    second_half = cells_ref[pl.ds(1, blocks, stride=2), :]
    slot = number * BLOCK + lane
    reached = jnp.maximum(
        jnp.where(slot < count, first_half, 0), jnp.where(slot + LANES < count, second_half, 0)
    )
    live = number * BLOCK < count
    first = jnp.min(first_half, axis=1, keepdims=True) >> 7
    last = jnp.max(reached, axis=1, keepdims=True) >> 7
    low = jnp.where(live, first + number, 2 * LANES)
    high = jnp.where(live, last + number, -1)
    inside = (low <= lane) & (lane <= high)
    place = lane[:1]
    block = jnp.max(jnp.where(inside, number, -1), axis=0, keepdims=True)
    valid = block >= 0
    row = place - block
    plan_ref[0:1, :] = jnp.where(valid, block, 0)
    plan_ref[1:2, :] = jnp.where(valid, row + (row >> 5), 0)
    plan_ref[2:3, :] = jnp.where(valid, row, ROWS) * NZ
    plan_ref[3:4, :] = jnp.max(high, axis=0, keepdims=True) + 1
    plan_ref[4:5, :] = jnp.broadcast_to(count, (1, LANES))
    plan_ref[5:8, :] = jnp.zeros((3, LANES), jnp.int32)


def spread_kernel(
    count_ref, frac_hbm, vel_hbm, mass_hbm, cells_hbm,
    far_ref, near_ref, plan_ref, frac_ref, vel_ref, cells_ref,
    listed_ref, mass_ref, q_ref, acc_ref, sems,
):
    slots = frac_ref.shape[1]
    sources = (cells_hbm, frac_hbm, vel_hbm, mass_hbm)
    targets = (cells_ref, frac_ref, vel_ref, mass_ref)
    arrivals = [
        pltpu.make_async_copy(source, target, sems.at[k])
        for k, (source, target) in enumerate(zip(sources, targets))
    ]
    for arrival in arrivals:
        arrival.start()
    acc_ref[...] = jnp.zeros_like(acc_ref)
    arrivals[0].wait()
    count = count_ref[0]
    list_visits(cells_ref, count, plan_ref)
    listing = pltpu.make_async_copy(plan_ref, listed_ref, sems.at[4])
    listing.start()
    for arrival in arrivals[1:]:
        arrival.wait()
    sublane = lax.broadcasted_iota(jnp.int32, (8, LANES), 0)
    lane = lax.broadcasted_iota(jnp.int32, (1, LANES), 1)
    top_z = sublane >= 4
    field = sublane & 3

    def weigh(part):
        at = pl.multiple_of(part * LANES, LANES)
        here = pl.ds(at, LANES)

        def spread_out(line):
            return jnp.broadcast_to(line, (8, LANES))

        fx, fy, fz = (spread_out(frac_ref[d : d + 1, here]) for d in range(3))
        vx, vy, vz = (spread_out(vel_ref[d : d + 1, here]) for d in range(3))
        held = spread_out(jnp.where(at + lane < count, mass_ref[pl.ds(part, 1), :], 0.0))
        carried = jnp.where(
            field == 0, held, held * jnp.where(field == 1, vx, jnp.where(field == 2, vy, vz))
        )
        carried = carried * jnp.where(top_z, fz, 1.0 - fz)
        lower, upper = carried * (1.0 - fx), carried * fx
        rows = jnp.concatenate(
            [lower * (1.0 - fy), lower * fy, upper * (1.0 - fy), upper * fy], axis=0
        )
        high, low = split_pair(rows)
        q_ref[pl.ds(part, 1)] = jnp.concatenate([high, low], axis=0)[None]

    def prepare(group, carry):
        for u in range(UNROLL):
            weigh(group * UNROLL + u)
        return carry

    lax.fori_loop(0, slots // LANES // UNROLL, prepare, 0)
    listing.wait()
    total = listed_ref[3, 0]

    def visit(group, carry):
        found = []
        for u in range(GIVEN):
            v = group * GIVEN + u
            block = listed_ref[0, v]
            hot = one_hot(cells_ref, block, listed_ref[2, v])
            both = q_ref[pl.ds(block * 2, 2)]
            both = lax.dot_general(
                jnp.concatenate([both[0], both[1]], axis=1),
                hot,
                (((1,), (1,)), ((), ())),
                preferred_element_type=f32,
            )
            found.append((listed_ref[1, v], both[:SPREAD] + both[SPREAD:]))
        for base, part in found:
            here = pl.ds(pl.multiple_of(base * 8, 8), 16)
            above = pl.ds(pl.multiple_of(base * 8, 8) + (NY + 1) * 8, 16)
            lower, upper = acc_ref[here, :], acc_ref[above, :]
            acc_ref[here, :] = lower + part[:16]
            acc_ref[above, :] = upper + part[16:]
        return carry

    lax.fori_loop(0, (total + GIVEN - 1) // GIVEN, visit, 0)

    layers = []
    for l in range(CX + 1):
        first = l * (NY + 1) * 8
        acc_ref[first : first + 8, :] += acc_ref[first + NY * 8 : first + NY * 8 + 8, :]
        for f in range(4):
            lower = acc_ref[pl.ds(first + f, NY, stride=8), :]
            upper = acc_ref[pl.ds(first + 4 + f, NY, stride=8), :]
            layers.append(lower + pltpu.roll(upper, 1, 1))
    odd = lax.axis_index("gx") % 2 == 1
    for l in range(CX):
        for f in range(4):
            low, high = layers[l * 4 + f], layers[(l + 1) * 4 + f]
            near_ref[f * CX + l] = jnp.where(odd, low, high)
            far_ref[f * CX + l] = jnp.where(odd, high, low)


def pair_up(field, axis):
    return field + pltpu.roll(field, field.shape[axis] - 1, axis)


def step_up(field, axis):
    return pltpu.roll(field, field.shape[axis] - 1, axis) - field


def pair_down(field, axis):
    return field + pltpu.roll(field, 1, axis)


def step_down(field, axis):
    return field - pltpu.roll(field, 1, axis)


def cell_stress(vel_lo, vel_hi, mass_lo, mass_hi, keep):
    grads = []
    for a in range(3):
        diff = vel_hi[a] - vel_lo[a]
        both = vel_hi[a] + vel_lo[a]
        grads.append(
            [
                0.25 * pair_up(pair_up(diff, 0), 1),
                0.25 * pair_up(step_up(both, 0), 1),
                0.25 * step_up(pair_up(both, 0), 1),
            ]
        )
    density = 0.125 * pair_up(pair_up(mass_hi + mass_lo, 0), 1)
    dxx = grads[0][0]
    dyy = grads[1][1]
    dzz = grads[2][2]
    dxy = 0.5 * (grads[0][1] + grads[1][0])
    dxz = 0.5 * (grads[0][2] + grads[2][0])
    dyz = 0.5 * (grads[1][2] + grads[2][1])
    second = dxx * dxx + dyy * dyy + dzz * dzz + 2.0 * (dxy * dxy + dxz * dxz + dyz * dyz)
    rate = jnp.sqrt(2.0 * second + rate_floor * rate_floor)
    pressure = stiffness * density
    inertial = rate * grain_size / jnp.sqrt(pressure + press_floor)
    friction = mu_static + (mu_limit - mu_static) * inertial / (inertia_ref + inertial)
    twice = 2.0 * friction * pressure / rate
    sigma = [
        twice * dxx - pressure,
        twice * dyy - pressure,
        twice * dzz - pressure,
        twice * dxy,
        twice * dxz,
        twice * dyz,
    ]
    return [jnp.where(keep, s, 0.0) for s in sigma]


def node_force(lower, upper):
    force = []
    for a in range(3):
        sx, sy, sz = (components[a][b] for b in range(3))
        along = pair_down(pair_down(upper[sx] - lower[sx], 0), 1)
        across = step_down(pair_down(upper[sy] + lower[sy], 1), 0)
        upward = step_down(pair_down(upper[sz] + lower[sz], 0), 1)
        force.append(0.25 * (along + across + upward))
    return force


def collect_kernel(
    step_ref, plan_ref, near_ref, far_ref, far_new_ref, near_new_ref, frac_ref, vel_ref, cells_ref,
    out_ref, top_ref, listed_ref, tab_ref, pair_ref, sem,
):
    blocks = frac_ref.shape[1] // BLOCK
    listing = pltpu.make_async_copy(plan_ref, listed_ref, sem)
    listing.start()
    step = step_ref[0]
    odd = lax.axis_index("gx") % 2 == 1

    def pick(if_odd, if_even):
        return [jnp.where(odd, if_odd[k], if_even[k]) for k in range(4 * CX)]

    low, high = pick(near_ref, far_ref), pick(far_ref, near_ref)
    left, right = pick(near_new_ref, far_new_ref), pick(far_new_ref, near_new_ref)
    nodes = [
        [left[f * 2] for f in range(4)],
        [low[f * 2] + left[f * 2 + 1] for f in range(4)],
        [low[f * 2 + 1] for f in range(4)],
        [high[f * 2 + 1] + right[f * 2] for f in range(4)],
        [right[f * 2 + 1] for f in range(4)],
    ]
    height = lax.broadcasted_iota(jnp.int32, (NY, NZ), 1)
    keep = height < NZ - 1
    above_bed = height > 0
    floor = [jnp.maximum(layer[0], mass_floor) for layer in nodes]
    v_old = [[layer[1 + a] / floor[l] for a in range(3)] for l, layer in enumerate(nodes)]
    sigma = [
        cell_stress(v_old[l], v_old[l + 1], nodes[l][0], nodes[l + 1][0], keep) for l in range(4)
    ]
    blank = jnp.zeros((NY, NZ), f32)
    for l in range(CX + 1):
        force = node_force(sigma[l], sigma[l + 1])
        fields = [blank] * 8
        for a in range(3):
            layer = nodes[l + 1]
            fresh = (layer[1 + a] + step * (force[a] + layer[0] * gravity[a])) / floor[l + 1]
            fresh = jnp.where(above_bed, fresh, 0.0)
            fields[a] = fresh - flip_share * v_old[l + 1][a]
            fields[4 + a] = step * fresh
        for k, value in enumerate(fields):
            start = l * NY * TABLE + k
            tab_ref[pl.ds(start, NY, stride=TABLE), :] = value
            tab_ref[pl.ds(start + 8, NY, stride=TABLE), :] = pltpu.roll(value, NZ - 1, 1)

    for l in range(CX + 1):

        def split_row(j, carry):
            at = pl.ds(pl.multiple_of((l * NY + j) * TABLE, TABLE), TABLE)
            high, low = split_pair(tab_ref[at, :])
            pair_ref[pl.ds(l * (NY + 1) + j, 1)] = jnp.concatenate([high, low], axis=1)[None]
            return carry

        lax.fori_loop(0, NY, split_row, 0, unroll=8)
        pair_ref[l * (NY + 1) + NY] = pair_ref[l * (NY + 1)]

    out_ref[...] = jnp.zeros_like(out_ref)
    listing.wait()
    total = listed_ref[3, 0]
    count = listed_ref[4, 0]

    def visit(group, carry):
        found = []
        for u in range(TAKEN):
            v = group * TAKEN + u
            block = listed_ref[0, v]
            base = listed_ref[1, v]
            hot = one_hot(cells_ref, block, listed_ref[2, v])
            rows = [pair_ref[base + ahead] for ahead in (0, 1, NY + 1, NY + 2)]
            value = jnp.dot(
                jnp.concatenate(rows, axis=0),
                jnp.concatenate([hot, hot], axis=0),
                preferred_element_type=f32,
            )
            corners = [value[8 * k : 8 * k + 8] for k in range(8)]
            frac = frac_ref[:, pl.ds(pl.multiple_of(block * BLOCK, BLOCK), BLOCK)]
            for d in (2, 1, 0):
                share = frac[d : d + 1, :]
                corners = [
                    corners[k] + share * (corners[k + 1] - corners[k])
                    for k in range(0, len(corners), 2)
                ]
            found.append((block, corners[0]))
        for block, part in found:
            out_ref[pl.ds(block, 1)] += part[None]
        return carry

    lax.fori_loop(0, (total + TAKEN - 1) // TAKEN, visit, 0)

    lane = lax.broadcasted_iota(jnp.int32, (1, BLOCK), 1)

    def finish(block, top):
        at = pl.multiple_of(block * BLOCK, BLOCK)
        alive = at + lane < count
        got = out_ref[pl.ds(block, 1)][0]
        fresh = jnp.where(alive, flip_share * vel_ref[:, pl.ds(at, BLOCK)] + got[0:3], 0.0)
        out_ref[pl.ds(block, 1), 0:3] = fresh[None]
        square = fresh[0:1] * fresh[0:1] + fresh[1:2] * fresh[1:2] + fresh[2:3] * fresh[2:3]
        return jnp.maximum(top, square)

    top = lax.fori_loop(0, blocks, finish, jnp.zeros((1, BLOCK), f32), unroll=4)
    top = jnp.sqrt(jnp.max(top, axis=1, keepdims=True))
    top_ref[...] = jnp.broadcast_to(top, top_ref.shape)


def finish_kernel(plan_ref, moved_ref, frac_ref, new_frac_ref, new_vel_ref):
    blocks = frac_ref.shape[1] // BLOCK
    count = plan_ref[4:5, :]
    count = jnp.concatenate([count, count], axis=1)
    lane = lax.broadcasted_iota(jnp.int32, (1, BLOCK), 1)

    def finish(block, carry):
        at = pl.multiple_of(block * BLOCK, BLOCK)
        got = moved_ref[pl.ds(block, 1)][0]
        new_vel_ref[:, pl.ds(at, BLOCK)] = got[0:3]
        placed = jnp.where(at + lane < count, frac_ref[:, pl.ds(at, BLOCK)] + got[4:7], 0.0)
        new_frac_ref[:, pl.ds(at, BLOCK)] = placed
        return carry

    lax.fori_loop(0, blocks, finish, 0, unroll=4)


def largest(value, axis):
    devices = lax.axis_size(axis)
    reach = 1
    while reach < devices:
        if devices & (devices - 1) == 0:
            pairs = [(i, i ^ (reach | 1)) for i in range(devices)]
        else:
            pairs = [(i, (i + reach) % devices) for i in range(devices)]
        value = jnp.maximum(value, lax.ppermute(value, axis, pairs))
        reach *= 2
    return value


smem = pl.BlockSpec(memory_space=pltpu.SMEM)
vmem = pl.BlockSpec(memory_space=pltpu.VMEM)
hbm = pl.BlockSpec(memory_space=pltpu.HBM)


def body(frac, velocity, mass, particle_cell, tile_count, time_step):
    slots = frac.shape[1]
    blocks = slots // BLOCK
    rows = slots // LANES
    inputs = (frac, velocity, mass.reshape(rows, LANES), particle_cell.reshape(rows, LANES))
    layer_pair = pltpu.VMEM((4 * CX, NY, NZ), f32)
    far, near, plan, frac_here, vel_here, cells_here = pl.pallas_call(
        spread_kernel,
        out_shape=(
            layer_pair,
            layer_pair,
            pltpu.VMEM((8, LANES), jnp.int32),
            pltpu.VMEM(frac.shape, f32),
            pltpu.VMEM(velocity.shape, f32),
            pltpu.VMEM((rows, LANES), jnp.int32),
        ),
        in_specs=[smem] + [hbm] * 4,
        out_specs=(vmem,) * 6,
        scratch_shapes=[
            pltpu.SMEM((8, LANES), jnp.int32),
            pltpu.VMEM((rows, LANES), f32),
            pltpu.VMEM((rows, 2 * SPREAD, LANES), bf16),
            pltpu.VMEM(((CX + 1) * (NY + 1) * 8, NZ), f32),
            pltpu.SemaphoreType.DMA((5,)),
        ],
        compiler_params=pltpu.CompilerParams(vmem_limit_bytes=32 * 1024 * 1024),
        name="spread",
    )(tile_count, *[pltpu.with_memory_space_constraint(x, pltpu.HBM) for x in inputs])
    devices = lax.axis_size("gx")
    far_pairs = [(i, (i + (1 if i % 2 else -1)) % devices) for i in range(devices)]
    near_pairs = [(i, i ^ 1) for i in range(devices)]
    near_new = lax.ppermute(near, "gx", near_pairs)
    far_new = lax.ppermute(far, "gx", far_pairs)
    moved, top = pl.pallas_call(
        collect_kernel,
        out_shape=(
            jax.ShapeDtypeStruct((blocks, 8, BLOCK), f32),
            jax.ShapeDtypeStruct((8, LANES), f32),
        ),
        in_specs=[smem] + [vmem] * 8,
        out_specs=(vmem, vmem),
        scratch_shapes=[
            pltpu.SMEM((8, LANES), jnp.int32),
            pltpu.VMEM(((CX + 1) * NY * TABLE, NZ), f32),
            pltpu.VMEM(((CX + 1) * (NY + 1), TABLE, 2 * NZ), bf16),
            pltpu.SemaphoreType.DMA,
        ],
        compiler_params=pltpu.CompilerParams(vmem_limit_bytes=32 * 1024 * 1024),
        name="collect",
    )(time_step, plan, near, far, far_new, near_new, frac_here, vel_here, cells_here)
    new_frac, new_velocity = pl.pallas_call(
        finish_kernel,
        out_shape=(
            jax.ShapeDtypeStruct(frac.shape, f32),
            jax.ShapeDtypeStruct(velocity.shape, f32),
        ),
        in_specs=[vmem] * 3,
        out_specs=(vmem, vmem),
        compiler_params=pltpu.CompilerParams(vmem_limit_bytes=32 * 1024 * 1024),
        cost_estimate=pl.CostEstimate(flops=0, bytes_accessed=8000000, transcendentals=0),
        name="finish",
    )(plan, moved, frac_here)
    fastest = largest(top, "gx")
    next_step = (courant / (fastest + wave_speed))[0, :1]
    return (new_frac, new_velocity, next_step)


def solution(mesh):
    placed = (
        P(None, ("runs", "gx")),
        P(None, ("runs", "gx")),
        P(("runs", "gx")),
        P(("runs", "gx")),
        P(("runs", "gx")),
        P("runs"),
    )
    return jax.shard_map(
        body,
        mesh=mesh,
        in_specs=placed,
        out_specs=(P(None, ("runs", "gx")), P(None, ("runs", "gx")), P("runs")),
        check_vma=False,
    )
```

```python
import functools

import jax
import jax.numpy as jnp
from jax import lax
from jax.experimental import pallas as pl
from jax.experimental.pallas import tpu as pltpu
from jax.sharding import PartitionSpec as P

CX = 2
NY = 32
NZ = 128
ROWS = CX * NY
BLOCK = 256
LANES = 128
UNROLL = 8
GIVEN = 32
TAKEN = 32
SPREAD = 32
TABLE = 16

mass_floor = 0.25
stiffness = 2.0
press_floor = 1.0
grain_size = 0.5
inertia_ref = 0.3
mu_static = 0.38
mu_limit = 0.64
rate_floor = 0.5
gravity = (0.5, 0.0, -0.866)
flip_share = 0.95
courant = 0.4
wave_speed = 2.0
components = ((0, 3, 4), (3, 1, 5), (4, 5, 2))
f32 = jnp.float32
bf16 = jnp.bfloat16


def split_pair(values):
    high = values.astype(bf16)
    low = (values - high.astype(f32)).astype(bf16)
    return high, low


def one_hot(cells_ref, block, offset):
    rel = cells_ref[pl.ds(block * 2, 2), :] - offset
    tall = (16, LANES)
    nodes = lax.broadcasted_iota(jnp.int32, tall, 0).astype(f32)
    one, zero = jnp.ones(tall, bf16), jnp.zeros(tall, bf16)
    halves = []
    for h in range(2):
        line = jnp.broadcast_to(rel[h : h + 1, :].astype(f32), tall).astype(bf16)
        halves.append(
            jnp.concatenate(
                [
                    jnp.where(line == (nodes + z).astype(bf16), one, zero)
                    for z in range(0, NZ, 16)
                ],
                axis=0,
            )
        )
    return jnp.concatenate(halves, axis=1)


def list_visits(cells_ref, count, plan_ref):
    blocks = cells_ref.shape[0] // 2
    shape = (blocks, LANES)
    number = lax.broadcasted_iota(jnp.int32, shape, 0)
    lane = lax.broadcasted_iota(jnp.int32, shape, 1)
    first_half = cells_ref[pl.ds(0, blocks, stride=2), :]
    second_half = cells_ref[pl.ds(1, blocks, stride=2), :]
    slot = number * BLOCK + lane
    reached = jnp.maximum(
        jnp.where(slot < count, first_half, 0), jnp.where(slot + LANES < count, second_half, 0)
    )
    live = number * BLOCK < count
    first = jnp.min(first_half, axis=1, keepdims=True) >> 7
    last = jnp.max(reached, axis=1, keepdims=True) >> 7
    low = jnp.where(live, first + number, 2 * LANES)
    high = jnp.where(live, last + number, -1)
    inside = (low <= lane) & (lane <= high)
    place = lane[:1]
    block = jnp.max(jnp.where(inside, number, -1), axis=0, keepdims=True)
    valid = block >= 0
    row = place - block
    plan_ref[0:1, :] = jnp.where(valid, block, 0)
    plan_ref[1:2, :] = jnp.where(valid, row + (row >> 5), 0)
    plan_ref[2:3, :] = jnp.where(valid, row, ROWS) * NZ
    plan_ref[3:4, :] = jnp.max(high, axis=0, keepdims=True) + 1
    plan_ref[4:5, :] = jnp.broadcast_to(count, (1, LANES))
    plan_ref[5:8, :] = jnp.zeros((3, LANES), jnp.int32)


def spread_kernel(
    count_ref, frac_hbm, vel_hbm, mass_hbm, cells_hbm,
    far_ref, near_ref, plan_ref, frac_ref, vel_ref, cells_ref,
    listed_ref, mass_ref, q_ref, acc_ref, sems,
):
    slots = frac_ref.shape[1]
    sources = (cells_hbm, frac_hbm, vel_hbm, mass_hbm)
    targets = (cells_ref, frac_ref, vel_ref, mass_ref)
    arrivals = [
        pltpu.make_async_copy(source, target, sems.at[k])
        for k, (source, target) in enumerate(zip(sources, targets))
    ]
    for arrival in arrivals:
        arrival.start()
    acc_ref[...] = jnp.zeros_like(acc_ref)
    arrivals[0].wait()
    count = count_ref[0]
    list_visits(cells_ref, count, plan_ref)
    listing = pltpu.make_async_copy(plan_ref, listed_ref, sems.at[4])
    listing.start()
    for arrival in arrivals[1:]:
        arrival.wait()
    sublane = lax.broadcasted_iota(jnp.int32, (8, LANES), 0)
    lane = lax.broadcasted_iota(jnp.int32, (1, LANES), 1)
    top_z = sublane >= 4
    field = sublane & 3

    def weigh(part):
        at = pl.multiple_of(part * LANES, LANES)
        here = pl.ds(at, LANES)

        def spread_out(line):
            return jnp.broadcast_to(line, (8, LANES))

        fx, fy, fz = (spread_out(frac_ref[d : d + 1, here]) for d in range(3))
        vx, vy, vz = (spread_out(vel_ref[d : d + 1, here]) for d in range(3))
        held = spread_out(jnp.where(at + lane < count, mass_ref[pl.ds(part, 1), :], 0.0))
        carried = jnp.where(
            field == 0, held, held * jnp.where(field == 1, vx, jnp.where(field == 2, vy, vz))
        )
        carried = carried * jnp.where(top_z, fz, 1.0 - fz)
        lower, upper = carried * (1.0 - fx), carried * fx
        rows = jnp.concatenate(
            [lower * (1.0 - fy), lower * fy, upper * (1.0 - fy), upper * fy], axis=0
        )
        high, low = split_pair(rows)
        q_ref[pl.ds(part, 1)] = jnp.concatenate([high, low], axis=0)[None]

    def prepare(group, carry):
        for u in range(UNROLL):
            weigh(group * UNROLL + u)
        return carry

    lax.fori_loop(0, slots // LANES // UNROLL, prepare, 0)
    listing.wait()
    total = listed_ref[3, 0]

    def visit(group, carry):
        found = []
        for u in range(GIVEN):
            v = group * GIVEN + u
            block = listed_ref[0, v]
            hot = one_hot(cells_ref, block, listed_ref[2, v])
            both = q_ref[pl.ds(block * 2, 2)]
            both = lax.dot_general(
                jnp.concatenate([both[0], both[1]], axis=1),
                hot,
                (((1,), (1,)), ((), ())),
                preferred_element_type=f32,
            )
            found.append((listed_ref[1, v], both[:SPREAD] + both[SPREAD:]))
        for base, part in found:
            here = pl.ds(pl.multiple_of(base * 8, 8), 16)
            above = pl.ds(pl.multiple_of(base * 8, 8) + (NY + 1) * 8, 16)
            lower, upper = acc_ref[here, :], acc_ref[above, :]
            acc_ref[here, :] = lower + part[:16]
            acc_ref[above, :] = upper + part[16:]
        return carry

    lax.fori_loop(0, (total + GIVEN - 1) // GIVEN, visit, 0)

    layers = []
    for l in range(CX + 1):
        first = l * (NY + 1) * 8
        acc_ref[first : first + 8, :] += acc_ref[first + NY * 8 : first + NY * 8 + 8, :]
        for f in range(4):
            lower = acc_ref[pl.ds(first + f, NY, stride=8), :]
            upper = acc_ref[pl.ds(first + 4 + f, NY, stride=8), :]
            layers.append(lower + pltpu.roll(upper, 1, 1))
    odd = lax.axis_index("gx") % 2 == 1
    for l in range(CX):
        for f in range(4):
            low, high = layers[l * 4 + f], layers[(l + 1) * 4 + f]
            near_ref[f * CX + l] = jnp.where(odd, low, high)
            far_ref[f * CX + l] = jnp.where(odd, high, low)


def pair_up(field, axis):
    return field + pltpu.roll(field, field.shape[axis] - 1, axis)


def step_up(field, axis):
    return pltpu.roll(field, field.shape[axis] - 1, axis) - field


def pair_down(field, axis):
    return field + pltpu.roll(field, 1, axis)


def step_down(field, axis):
    return field - pltpu.roll(field, 1, axis)


def cell_stress(vel_lo, vel_hi, mass_lo, mass_hi, keep):
    grads = []
    for a in range(3):
        diff = vel_hi[a] - vel_lo[a]
        both = vel_hi[a] + vel_lo[a]
        grads.append(
            [
                0.25 * pair_up(pair_up(diff, 0), 1),
                0.25 * pair_up(step_up(both, 0), 1),
                0.25 * step_up(pair_up(both, 0), 1),
            ]
        )
    density = 0.125 * pair_up(pair_up(mass_hi + mass_lo, 0), 1)
    dxx = grads[0][0]
    dyy = grads[1][1]
    dzz = grads[2][2]
    dxy = 0.5 * (grads[0][1] + grads[1][0])
    dxz = 0.5 * (grads[0][2] + grads[2][0])
    dyz = 0.5 * (grads[1][2] + grads[2][1])
    second = dxx * dxx + dyy * dyy + dzz * dzz + 2.0 * (dxy * dxy + dxz * dxz + dyz * dyz)
    rate = jnp.sqrt(2.0 * second + rate_floor * rate_floor)
    pressure = stiffness * density
    inertial = rate * grain_size / jnp.sqrt(pressure + press_floor)
    friction = mu_static + (mu_limit - mu_static) * inertial / (inertia_ref + inertial)
    twice = 2.0 * friction * pressure / rate
    sigma = [
        twice * dxx - pressure,
        twice * dyy - pressure,
        twice * dzz - pressure,
        twice * dxy,
        twice * dxz,
        twice * dyz,
    ]
    return [jnp.where(keep, s, 0.0) for s in sigma]


def node_force(lower, upper):
    force = []
    for a in range(3):
        sx, sy, sz = (components[a][b] for b in range(3))
        along = pair_down(pair_down(upper[sx] - lower[sx], 0), 1)
        across = step_down(pair_down(upper[sy] + lower[sy], 1), 0)
        upward = step_down(pair_down(upper[sz] + lower[sz], 0), 1)
        force.append(0.25 * (along + across + upward))
    return force


def collect_kernel(
    step_ref, plan_ref, near_ref, far_ref, far_new_ref, near_new_ref, frac_ref, vel_ref, cells_ref,
    out_ref, top_ref, listed_ref, tab_ref, pair_ref, sem,
):
    blocks = frac_ref.shape[1] // BLOCK
    listing = pltpu.make_async_copy(plan_ref, listed_ref, sem)
    listing.start()
    step = step_ref[0]
    odd = lax.axis_index("gx") % 2 == 1

    def pick(if_odd, if_even):
        return [jnp.where(odd, if_odd[k], if_even[k]) for k in range(4 * CX)]

    low, high = pick(near_ref, far_ref), pick(far_ref, near_ref)
    left, right = pick(near_new_ref, far_new_ref), pick(far_new_ref, near_new_ref)
    nodes = [
        [left[f * 2] for f in range(4)],
        [low[f * 2] + left[f * 2 + 1] for f in range(4)],
        [low[f * 2 + 1] for f in range(4)],
        [high[f * 2 + 1] + right[f * 2] for f in range(4)],
        [right[f * 2 + 1] for f in range(4)],
    ]
    height = lax.broadcasted_iota(jnp.int32, (NY, NZ), 1)
    keep = height < NZ - 1
    above_bed = height > 0
    floor = [jnp.maximum(layer[0], mass_floor) for layer in nodes]
    v_old = [[layer[1 + a] / floor[l] for a in range(3)] for l, layer in enumerate(nodes)]
    sigma = [
        cell_stress(v_old[l], v_old[l + 1], nodes[l][0], nodes[l + 1][0], keep) for l in range(4)
    ]
    blank = jnp.zeros((NY, NZ), f32)
    for l in range(CX + 1):
        force = node_force(sigma[l], sigma[l + 1])
        fields = [blank] * 8
        for a in range(3):
            layer = nodes[l + 1]
            fresh = (layer[1 + a] + step * (force[a] + layer[0] * gravity[a])) / floor[l + 1]
            fresh = jnp.where(above_bed, fresh, 0.0)
            fields[a] = fresh - flip_share * v_old[l + 1][a]
            fields[4 + a] = step * fresh
        for k, value in enumerate(fields):
            start = l * NY * TABLE + k
            tab_ref[pl.ds(start, NY, stride=TABLE), :] = value
            tab_ref[pl.ds(start + 8, NY, stride=TABLE), :] = pltpu.roll(value, NZ - 1, 1)

    for l in range(CX + 1):

        def split_row(j, carry):
            at = pl.ds(pl.multiple_of((l * NY + j) * TABLE, TABLE), TABLE)
            high, low = split_pair(tab_ref[at, :])
            pair_ref[pl.ds(l * (NY + 1) + j, 1)] = jnp.concatenate([high, low], axis=1)[None]
            return carry

        lax.fori_loop(0, NY, split_row, 0, unroll=8)
        pair_ref[l * (NY + 1) + NY] = pair_ref[l * (NY + 1)]

    out_ref[...] = jnp.zeros_like(out_ref)
    listing.wait()
    total = listed_ref[3, 0]
    count = listed_ref[4, 0]

    def visit(group, carry):
        found = []
        for u in range(TAKEN):
            v = group * TAKEN + u
            block = listed_ref[0, v]
            base = listed_ref[1, v]
            hot = one_hot(cells_ref, block, listed_ref[2, v])
            rows = [pair_ref[base + ahead] for ahead in (0, 1, NY + 1, NY + 2)]
            value = jnp.dot(
                jnp.concatenate(rows, axis=0),
                jnp.concatenate([hot, hot], axis=0),
                preferred_element_type=f32,
            )
            corners = [value[8 * k : 8 * k + 8] for k in range(8)]
            frac = frac_ref[:, pl.ds(pl.multiple_of(block * BLOCK, BLOCK), BLOCK)]
            for d in (2, 1, 0):
                share = frac[d : d + 1, :]
                corners = [
                    corners[k] + share * (corners[k + 1] - corners[k])
                    for k in range(0, len(corners), 2)
                ]
            found.append((block, corners[0]))
        for block, part in found:
            out_ref[pl.ds(block, 1)] += part[None]
        return carry

    lax.fori_loop(0, (total + TAKEN - 1) // TAKEN, visit, 0)

    lane = lax.broadcasted_iota(jnp.int32, (1, BLOCK), 1)

    def finish(block, top):
        at = pl.multiple_of(block * BLOCK, BLOCK)
        alive = at + lane < count
        got = out_ref[pl.ds(block, 1)][0]
        fresh = jnp.where(alive, flip_share * vel_ref[:, pl.ds(at, BLOCK)] + got[0:3], 0.0)
        out_ref[pl.ds(block, 1), 0:3] = fresh[None]
        square = fresh[0:1] * fresh[0:1] + fresh[1:2] * fresh[1:2] + fresh[2:3] * fresh[2:3]
        return jnp.maximum(top, square)

    top = lax.fori_loop(0, blocks, finish, jnp.zeros((1, BLOCK), f32), unroll=4)
    top = jnp.sqrt(jnp.max(top, axis=1, keepdims=True))
    top_ref[...] = jnp.broadcast_to(top, top_ref.shape)


def finish_kernel(plan_ref, moved_ref, frac_ref, new_frac_ref, new_vel_ref):
    blocks = frac_ref.shape[1] // BLOCK
    count = plan_ref[4:5, :]
    count = jnp.concatenate([count, count], axis=1)
    lane = lax.broadcasted_iota(jnp.int32, (1, BLOCK), 1)

    def finish(block, carry):
        at = pl.multiple_of(block * BLOCK, BLOCK)
        got = moved_ref[pl.ds(block, 1)][0]
        new_vel_ref[:, pl.ds(at, BLOCK)] = got[0:3]
        placed = jnp.where(at + lane < count, frac_ref[:, pl.ds(at, BLOCK)] + got[4:7], 0.0)
        new_frac_ref[:, pl.ds(at, BLOCK)] = placed
        return carry

    lax.fori_loop(0, blocks, finish, 0, unroll=4)


def largest(value, axis):
    devices = lax.axis_size(axis)
    reach = 1
    while reach < devices:
        if devices & (devices - 1) == 0:
            pairs = [(i, i ^ (reach | 1)) for i in range(devices)]
        else:
            pairs = [(i, (i + reach) % devices) for i in range(devices)]
        value = jnp.maximum(value, lax.ppermute(value, axis, pairs))
        reach *= 2
    return value


smem = pl.BlockSpec(memory_space=pltpu.SMEM)
vmem = pl.BlockSpec(memory_space=pltpu.VMEM)
hbm = pl.BlockSpec(memory_space=pltpu.HBM)


def body(frac, velocity, mass, particle_cell, tile_count, time_step):
    slots = frac.shape[1]
    blocks = slots // BLOCK
    rows = slots // LANES
    inputs = (frac, velocity, mass.reshape(rows, LANES), particle_cell.reshape(rows, LANES))
    layer_pair = pltpu.VMEM((4 * CX, NY, NZ), f32)
    far, near, plan, frac_here, vel_here, cells_here = pl.pallas_call(
        spread_kernel,
        out_shape=(
            layer_pair,
            layer_pair,
            pltpu.VMEM((8, LANES), jnp.int32),
            pltpu.VMEM(frac.shape, f32),
            pltpu.VMEM(velocity.shape, f32),
            pltpu.VMEM((rows, LANES), jnp.int32),
        ),
        in_specs=[smem] + [hbm] * 4,
        out_specs=(vmem,) * 6,
        scratch_shapes=[
            pltpu.SMEM((8, LANES), jnp.int32),
            pltpu.VMEM((rows, LANES), f32),
            pltpu.VMEM((rows, 2 * SPREAD, LANES), bf16),
            pltpu.VMEM(((CX + 1) * (NY + 1) * 8, NZ), f32),
            pltpu.SemaphoreType.DMA((5,)),
        ],
        compiler_params=pltpu.CompilerParams(vmem_limit_bytes=32 * 1024 * 1024),
        name="spread",
    )(tile_count, *[pltpu.with_memory_space_constraint(x, pltpu.HBM) for x in inputs])
    devices = lax.axis_size("gx")
    far_pairs = [(i, (i + (1 if i % 2 else -1)) % devices) for i in range(devices)]
    near_pairs = [(i, i ^ 1) for i in range(devices)]
    near_new = lax.ppermute(near, "gx", near_pairs)
    far_new = lax.ppermute(far, "gx", far_pairs)
    moved, top = pl.pallas_call(
        collect_kernel,
        out_shape=(
            jax.ShapeDtypeStruct((blocks, 8, BLOCK), f32),
            jax.ShapeDtypeStruct((8, LANES), f32),
        ),
        in_specs=[smem] + [vmem] * 8,
        out_specs=(vmem, vmem),
        scratch_shapes=[
            pltpu.SMEM((8, LANES), jnp.int32),
            pltpu.VMEM(((CX + 1) * NY * TABLE, NZ), f32),
            pltpu.VMEM(((CX + 1) * (NY + 1), TABLE, 2 * NZ), bf16),
            pltpu.SemaphoreType.DMA,
        ],
        compiler_params=pltpu.CompilerParams(vmem_limit_bytes=32 * 1024 * 1024),
        name="collect",
    )(time_step, plan, near, far, far_new, near_new, frac_here, vel_here, cells_here)
    new_frac, new_velocity = pl.pallas_call(
        finish_kernel,
        out_shape=(
            jax.ShapeDtypeStruct(frac.shape, f32),
            jax.ShapeDtypeStruct(velocity.shape, f32),
        ),
        in_specs=[vmem] * 3,
        out_specs=(vmem, vmem),
        compiler_params=pltpu.CompilerParams(vmem_limit_bytes=32 * 1024 * 1024),
        cost_estimate=pl.CostEstimate(flops=0, bytes_accessed=8000000, transcendentals=0),
        name="finish",
    )(plan, moved, frac_here)
    fastest = largest(top, "gx")
    next_step = (courant / (fastest + wave_speed))[0, :1]
    return (new_frac, new_velocity, next_step)


def solution(mesh):
    placed = (
        P(None, ("runs", "gx")),
        P(None, ("runs", "gx")),
        P(("runs", "gx")),
        P(("runs", "gx")),
        P(("runs", "gx")),
        P("runs"),
    )
    return jax.shard_map(
        body,
        mesh=mesh,
        in_specs=placed,
        out_specs=(P(None, ("runs", "gx")), P(None, ("runs", "gx")), P("runs")),
        check_vma=False,
    )
```

```python
import functools

import jax
import jax.numpy as jnp
from jax import lax
from jax.experimental import pallas as pl
from jax.experimental.pallas import tpu as pltpu
from jax.sharding import PartitionSpec as P

CX = 2
NY = 32
NZ = 128
ROWS = CX * NY
BLOCK = 256
LANES = 128
UNROLL = 8
GIVEN = 32
TAKEN = 32
SPREAD = 32
TABLE = 16

mass_floor = 0.25
stiffness = 2.0
press_floor = 1.0
grain_size = 0.5
inertia_ref = 0.3
mu_static = 0.38
mu_limit = 0.64
rate_floor = 0.5
gravity = (0.5, 0.0, -0.866)
flip_share = 0.95
courant = 0.4
wave_speed = 2.0
components = ((0, 3, 4), (3, 1, 5), (4, 5, 2))
f32 = jnp.float32
bf16 = jnp.bfloat16


def split_pair(values):
    high = values.astype(bf16)
    low = (values - high.astype(f32)).astype(bf16)
    return high, low


def one_hot(cells_ref, block, offset):
    rel = cells_ref[pl.ds(block * 2, 2), :] - offset
    tall = (16, LANES)
    nodes = lax.broadcasted_iota(jnp.int32, tall, 0).astype(f32)
    one, zero = jnp.ones(tall, bf16), jnp.zeros(tall, bf16)
    halves = []
    for h in range(2):
        line = jnp.broadcast_to(rel[h : h + 1, :].astype(f32), tall).astype(bf16)
        halves.append(
            jnp.concatenate(
                [
                    jnp.where(line == (nodes + z).astype(bf16), one, zero)
                    for z in range(0, NZ, 16)
                ],
                axis=0,
            )
        )
    return jnp.concatenate(halves, axis=1)


def list_visits(cells_ref, count, plan_ref):
    blocks = cells_ref.shape[0] // 2
    shape = (blocks, LANES)
    number = lax.broadcasted_iota(jnp.int32, shape, 0)
    lane = lax.broadcasted_iota(jnp.int32, shape, 1)
    first_half = cells_ref[pl.ds(0, blocks, stride=2), :]
    second_half = cells_ref[pl.ds(1, blocks, stride=2), :]
    slot = number * BLOCK + lane
    reached = jnp.maximum(
        jnp.where(slot < count, first_half, 0), jnp.where(slot + LANES < count, second_half, 0)
    )
    live = number * BLOCK < count
    first = jnp.min(first_half, axis=1, keepdims=True) >> 7
    last = jnp.max(reached, axis=1, keepdims=True) >> 7
    low = jnp.where(live, first + number, 2 * LANES)
    high = jnp.where(live, last + number, -1)
    inside = (low <= lane) & (lane <= high)
    place = lane[:1]
    block = jnp.max(jnp.where(inside, number, -1), axis=0, keepdims=True)
    valid = block >= 0
    row = place - block
    plan_ref[0:1, :] = jnp.where(valid, block, 0)
    plan_ref[1:2, :] = jnp.where(valid, row + (row >> 5), 0)
    plan_ref[2:3, :] = jnp.where(valid, row, ROWS) * NZ
    plan_ref[3:4, :] = jnp.max(high, axis=0, keepdims=True) + 1
    plan_ref[4:5, :] = jnp.broadcast_to(count, (1, LANES))
    plan_ref[5:8, :] = jnp.zeros((3, LANES), jnp.int32)


def spread_kernel(
    count_ref, frac_hbm, vel_hbm, mass_hbm, cells_hbm,
    far_ref, near_ref, layers_ref, plan_ref, frac_ref, vel_ref, hot_ref,
    cells_ref, listed_ref, mass_ref, q_ref, acc_ref, sems,
):
    slots = frac_ref.shape[1]
    sources = (cells_hbm, frac_hbm, vel_hbm, mass_hbm)
    targets = (cells_ref, frac_ref, vel_ref, mass_ref)
    arrivals = [
        pltpu.make_async_copy(source, target, sems.at[k])
        for k, (source, target) in enumerate(zip(sources, targets))
    ]
    for arrival in arrivals:
        arrival.start()
    acc_ref[...] = jnp.zeros_like(acc_ref)
    arrivals[0].wait()
    count = count_ref[0]
    list_visits(cells_ref, count, plan_ref)
    listing = pltpu.make_async_copy(plan_ref, listed_ref, sems.at[4])
    listing.start()
    for arrival in arrivals[1:]:
        arrival.wait()
    sublane = lax.broadcasted_iota(jnp.int32, (8, LANES), 0)
    lane = lax.broadcasted_iota(jnp.int32, (1, LANES), 1)
    top_z = sublane >= 4
    field = sublane & 3

    def weigh(part):
        at = pl.multiple_of(part * LANES, LANES)
        here = pl.ds(at, LANES)

        def spread_out(line):
            return jnp.broadcast_to(line, (8, LANES))

        fx, fy, fz = (spread_out(frac_ref[d : d + 1, here]) for d in range(3))
        vx, vy, vz = (spread_out(vel_ref[d : d + 1, here]) for d in range(3))
        held = spread_out(jnp.where(at + lane < count, mass_ref[pl.ds(part, 1), :], 0.0))
        carried = jnp.where(
            field == 0, held, held * jnp.where(field == 1, vx, jnp.where(field == 2, vy, vz))
        )
        carried = carried * jnp.where(top_z, fz, 1.0 - fz)
        lower, upper = carried * (1.0 - fx), carried * fx
        rows = jnp.concatenate(
            [lower * (1.0 - fy), lower * fy, upper * (1.0 - fy), upper * fy], axis=0
        )
        high, low = split_pair(rows)
        q_ref[pl.ds(part, 1)] = jnp.concatenate([high, low], axis=0)[None]

    def prepare(group, carry):
        for u in range(UNROLL):
            weigh(group * UNROLL + u)
        return carry

    lax.fori_loop(0, slots // LANES // UNROLL, prepare, 0)
    listing.wait()
    total = listed_ref[3, 0]

    def visit(group, carry):
        found = []
        for u in range(GIVEN):
            v = group * GIVEN + u
            block = listed_ref[0, v]
            hot = one_hot(cells_ref, block, listed_ref[2, v])
            hot_ref[pl.ds(v, 1)] = hot[None]
            both = q_ref[pl.ds(block * 2, 2)]
            both = lax.dot_general(
                jnp.concatenate([both[0], both[1]], axis=1),
                hot,
                (((1,), (1,)), ((), ())),
                preferred_element_type=f32,
            )
            found.append((listed_ref[1, v], both[:SPREAD] + both[SPREAD:]))
        for base, part in found:
            here = pl.ds(pl.multiple_of(base * 8, 8), 16)
            above = pl.ds(pl.multiple_of(base * 8, 8) + (NY + 1) * 8, 16)
            lower, upper = acc_ref[here, :], acc_ref[above, :]
            acc_ref[here, :] = lower + part[:16]
            acc_ref[above, :] = upper + part[16:]
        return carry

    lax.fori_loop(0, (total + GIVEN - 1) // GIVEN, visit, 0)

    odd = lax.axis_index("gx") % 2 == 1
    layers = []
    for l in range(CX + 1):
        first = l * (NY + 1) * 8
        acc_ref[first : first + 8, :] += acc_ref[first + NY * 8 : first + NY * 8 + 8, :]
        for f in range(4):
            lower = acc_ref[pl.ds(first + f, NY, stride=8), :]
            upper = acc_ref[pl.ds(first + 4 + f, NY, stride=8), :]
            layers.append(lower + pltpu.roll(upper, 1, 1))
            layers_ref[l * 4 + f] = layers[-1]
    for k in range(CX * 4):
        far_ref[k] = jnp.where(odd, layers[k + 4], layers[k])
        near_ref[k] = jnp.where(odd, layers[k], layers[k + 4])


def pair_up(field, axis):
    return field + pltpu.roll(field, field.shape[axis] - 1, axis)


def step_up(field, axis):
    return pltpu.roll(field, field.shape[axis] - 1, axis) - field


def pair_down(field, axis):
    return field + pltpu.roll(field, 1, axis)


def step_down(field, axis):
    return field - pltpu.roll(field, 1, axis)


def cell_stress(vel_lo, vel_hi, mass_lo, mass_hi, keep):
    grads = []
    for a in range(3):
        diff = vel_hi[a] - vel_lo[a]
        both = vel_hi[a] + vel_lo[a]
        grads.append(
            [
                0.25 * pair_up(pair_up(diff, 0), 1),
                0.25 * pair_up(step_up(both, 0), 1),
                0.25 * step_up(pair_up(both, 0), 1),
            ]
        )
    density = 0.125 * pair_up(pair_up(mass_hi + mass_lo, 0), 1)
    dxx = grads[0][0]
    dyy = grads[1][1]
    dzz = grads[2][2]
    dxy = 0.5 * (grads[0][1] + grads[1][0])
    dxz = 0.5 * (grads[0][2] + grads[2][0])
    dyz = 0.5 * (grads[1][2] + grads[2][1])
    second = dxx * dxx + dyy * dyy + dzz * dzz + 2.0 * (dxy * dxy + dxz * dxz + dyz * dyz)
    rate = jnp.sqrt(2.0 * second + rate_floor * rate_floor)
    pressure = stiffness * density
    inertial = rate * grain_size / jnp.sqrt(pressure + press_floor)
    friction = mu_static + (mu_limit - mu_static) * inertial / (inertia_ref + inertial)
    twice = 2.0 * friction * pressure / rate
    sigma = [
        twice * dxx - pressure,
        twice * dyy - pressure,
        twice * dzz - pressure,
        twice * dxy,
        twice * dxz,
        twice * dyz,
    ]
    return [jnp.where(keep, s, 0.0) for s in sigma]


def node_force(lower, upper):
    force = []
    for a in range(3):
        sx, sy, sz = (components[a][b] for b in range(3))
        along = pair_down(pair_down(upper[sx] - lower[sx], 0), 1)
        across = step_down(pair_down(upper[sy] + lower[sy], 1), 0)
        upward = step_down(pair_down(upper[sz] + lower[sz], 0), 1)
        force.append(0.25 * (along + across + upward))
    return force


def collect_kernel(
    step_ref, plan_ref, layers_ref, far_new_ref, near_new_ref, frac_ref, vel_ref, hot_ref,
    out_ref, top_ref, listed_ref, tab_ref, pair_ref, sem,
):
    blocks = frac_ref.shape[1] // BLOCK
    listing = pltpu.make_async_copy(plan_ref, listed_ref, sem)
    listing.start()
    step = step_ref[0]
    odd = lax.axis_index("gx") % 2 == 1

    def pick(if_odd, if_even):
        return [jnp.where(odd, if_odd[k], if_even[k]) for k in range(4 * CX)]

    own = [layers_ref[k] for k in range(4 * (CX + 1))]
    left, right = pick(near_new_ref, far_new_ref), pick(far_new_ref, near_new_ref)
    nodes = [
        left[:4],
        [own[f] + left[4 + f] for f in range(4)],
        own[4:8],
        [own[8 + f] + right[f] for f in range(4)],
        right[4:],
    ]
    height = lax.broadcasted_iota(jnp.int32, (NY, NZ), 1)
    keep = height < NZ - 1
    above_bed = height > 0
    floor = [jnp.maximum(layer[0], mass_floor) for layer in nodes]
    v_old = [[layer[1 + a] / floor[l] for a in range(3)] for l, layer in enumerate(nodes)]
    sigma = [
        cell_stress(v_old[l], v_old[l + 1], nodes[l][0], nodes[l + 1][0], keep) for l in range(4)
    ]
    blank = jnp.zeros((NY, NZ), f32)
    for l in range(CX + 1):
        force = node_force(sigma[l], sigma[l + 1])
        fields = [blank] * 8
        for a in range(3):
            layer = nodes[l + 1]
            fresh = (layer[1 + a] + step * (force[a] + layer[0] * gravity[a])) / floor[l + 1]
            fresh = jnp.where(above_bed, fresh, 0.0)
            fields[a] = fresh - flip_share * v_old[l + 1][a]
            fields[4 + a] = step * fresh
        for k, value in enumerate(fields):
            start = l * NY * TABLE + k
            tab_ref[pl.ds(start, NY, stride=TABLE), :] = value
            tab_ref[pl.ds(start + 8, NY, stride=TABLE), :] = pltpu.roll(value, NZ - 1, 1)

    for l in range(CX + 1):

        def split_row(j, carry):
            at = pl.ds(pl.multiple_of((l * NY + j) * TABLE, TABLE), TABLE)
            high, low = split_pair(tab_ref[at, :])
            pair_ref[pl.ds(l * (NY + 1) + j, 1)] = jnp.concatenate([high, low], axis=1)[None]
            return carry

        lax.fori_loop(0, NY, split_row, 0, unroll=8)
        pair_ref[l * (NY + 1) + NY] = pair_ref[l * (NY + 1)]

    out_ref[...] = jnp.zeros_like(out_ref)
    listing.wait()
    total = listed_ref[3, 0]
    count = listed_ref[4, 0]

    def visit(group, carry):
        found = []
        for u in range(TAKEN):
            v = group * TAKEN + u
            block = listed_ref[0, v]
            base = listed_ref[1, v]
            hot = hot_ref[pl.ds(v, 1)][0]
            rows = [pair_ref[base + ahead] for ahead in (0, 1, NY + 1, NY + 2)]
            value = jnp.dot(
                jnp.concatenate(rows, axis=0),
                jnp.concatenate([hot, hot], axis=0),
                preferred_element_type=f32,
            )
            corners = [value[8 * k : 8 * k + 8] for k in range(8)]
            frac = frac_ref[:, pl.ds(pl.multiple_of(block * BLOCK, BLOCK), BLOCK)]
            for d in (2, 1, 0):
                share = frac[d : d + 1, :]
                corners = [
                    corners[k] + share * (corners[k + 1] - corners[k])
                    for k in range(0, len(corners), 2)
                ]
            found.append((block, corners[0]))
        for block, part in found:
            out_ref[pl.ds(block, 1)] += part[None]
        return carry

    lax.fori_loop(0, (total + TAKEN - 1) // TAKEN, visit, 0)

    lane = lax.broadcasted_iota(jnp.int32, (1, BLOCK), 1)

    def finish(block, top):
        at = pl.multiple_of(block * BLOCK, BLOCK)
        alive = at + lane < count
        got = out_ref[pl.ds(block, 1)][0]
        fresh = jnp.where(alive, flip_share * vel_ref[:, pl.ds(at, BLOCK)] + got[0:3], 0.0)
        out_ref[pl.ds(block, 1), 0:3] = fresh[None]
        square = fresh[0:1] * fresh[0:1] + fresh[1:2] * fresh[1:2] + fresh[2:3] * fresh[2:3]
        return jnp.maximum(top, square)

    top = lax.fori_loop(0, blocks, finish, jnp.zeros((1, BLOCK), f32), unroll=4)
    top = jnp.sqrt(jnp.max(top, axis=1, keepdims=True))
    top_ref[...] = jnp.broadcast_to(top, top_ref.shape)


def finish_kernel(plan_ref, moved_ref, frac_ref, new_frac_ref, new_vel_ref):
    blocks = frac_ref.shape[1] // BLOCK
    count = plan_ref[4:5, :]
    count = jnp.concatenate([count, count], axis=1)
    lane = lax.broadcasted_iota(jnp.int32, (1, BLOCK), 1)

    def finish(block, carry):
        at = pl.multiple_of(block * BLOCK, BLOCK)
        got = moved_ref[pl.ds(block, 1)][0]
        new_vel_ref[:, pl.ds(at, BLOCK)] = got[0:3]
        placed = jnp.where(at + lane < count, frac_ref[:, pl.ds(at, BLOCK)] + got[4:7], 0.0)
        new_frac_ref[:, pl.ds(at, BLOCK)] = placed
        return carry

    lax.fori_loop(0, blocks, finish, 0, unroll=4)


def largest(value, axis):
    devices = lax.axis_size(axis)
    reach = 1
    while reach < devices:
        if devices & (devices - 1) == 0:
            pairs = [(i, i ^ (reach | 1)) for i in range(devices)]
        else:
            pairs = [(i, (i + reach) % devices) for i in range(devices)]
        value = jnp.maximum(value, lax.ppermute(value, axis, pairs))
        reach *= 2
    return value


smem = pl.BlockSpec(memory_space=pltpu.SMEM)
vmem = pl.BlockSpec(memory_space=pltpu.VMEM)
hbm = pl.BlockSpec(memory_space=pltpu.HBM)


def body(frac, velocity, mass, particle_cell, tile_count, time_step):
    slots = frac.shape[1]
    blocks = slots // BLOCK
    rows = slots // LANES
    inputs = (frac, velocity, mass.reshape(rows, LANES), particle_cell.reshape(rows, LANES))
    far, near, layers, plan, frac_here, vel_here, hots = pl.pallas_call(
        spread_kernel,
        out_shape=(
            pltpu.VMEM((4 * CX, NY, NZ), f32),
            pltpu.VMEM((4 * CX, NY, NZ), f32),
            pltpu.VMEM((4 * (CX + 1), NY, NZ), f32),
            pltpu.VMEM((8, LANES), jnp.int32),
            pltpu.VMEM(frac.shape, f32),
            pltpu.VMEM(velocity.shape, f32),
            pltpu.VMEM((blocks + ROWS, NZ, BLOCK), bf16),
        ),
        in_specs=[smem] + [hbm] * 4,
        out_specs=(vmem,) * 7,
        scratch_shapes=[
            pltpu.VMEM((rows, LANES), jnp.int32),
            pltpu.SMEM((8, LANES), jnp.int32),
            pltpu.VMEM((rows, LANES), f32),
            pltpu.VMEM((rows, 2 * SPREAD, LANES), bf16),
            pltpu.VMEM(((CX + 1) * (NY + 1) * 8, NZ), f32),
            pltpu.SemaphoreType.DMA((5,)),
        ],
        compiler_params=pltpu.CompilerParams(vmem_limit_bytes=32 * 1024 * 1024),
        name="spread",
    )(tile_count, *[pltpu.with_memory_space_constraint(x, pltpu.HBM) for x in inputs])
    devices = lax.axis_size("gx")
    far_pairs = [(i, (i + (1 if i % 2 else -1)) % devices) for i in range(devices)]
    near_pairs = [(i, i ^ 1) for i in range(devices)]
    far_new = lax.ppermute(far, "gx", far_pairs)
    near_new = lax.ppermute(near, "gx", near_pairs)
    moved, top = pl.pallas_call(
        collect_kernel,
        out_shape=(
            jax.ShapeDtypeStruct((blocks, 8, BLOCK), f32),
            jax.ShapeDtypeStruct((8, LANES), f32),
        ),
        in_specs=[smem] + [vmem] * 7,
        out_specs=(vmem, vmem),
        scratch_shapes=[
            pltpu.SMEM((8, LANES), jnp.int32),
            pltpu.VMEM(((CX + 1) * NY * TABLE, NZ), f32),
            pltpu.VMEM(((CX + 1) * (NY + 1), TABLE, 2 * NZ), bf16),
            pltpu.SemaphoreType.DMA,
        ],
        compiler_params=pltpu.CompilerParams(vmem_limit_bytes=32 * 1024 * 1024),
        name="collect",
    )(time_step, plan, layers, far_new, near_new, frac_here, vel_here, hots)
    new_frac, new_velocity = pl.pallas_call(
        finish_kernel,
        out_shape=(
            jax.ShapeDtypeStruct(frac.shape, f32),
            jax.ShapeDtypeStruct(velocity.shape, f32),
        ),
        in_specs=[vmem] * 3,
        out_specs=(vmem, vmem),
        compiler_params=pltpu.CompilerParams(vmem_limit_bytes=32 * 1024 * 1024),
        cost_estimate=pl.CostEstimate(flops=0, bytes_accessed=8000000, transcendentals=0),
        name="finish",
    )(plan, moved, frac_here)
    fastest = largest(top, "gx")
    next_step = (courant / (fastest + wave_speed))[0, :1]
    return (new_frac, new_velocity, next_step)


def solution(mesh):
    placed = (
        P(None, ("runs", "gx")),
        P(None, ("runs", "gx")),
        P(("runs", "gx")),
        P(("runs", "gx")),
        P(("runs", "gx")),
        P("runs"),
    )
    return jax.shard_map(
        body,
        mesh=mesh,
        in_specs=placed,
        out_specs=(P(None, ("runs", "gx")), P(None, ("runs", "gx")), P("runs")),
        check_vma=False,
    )
```

```python
import functools

import jax
import jax.numpy as jnp
from jax import lax
from jax.experimental import pallas as pl
from jax.experimental.pallas import tpu as pltpu
from jax.sharding import PartitionSpec as P

CX = 2
NY = 32
NZ = 128
PAIRS = CX * NY // 2
WIDE = 2 * NZ
BLOCK = 256
LANES = 128
UNROLL = 8
GIVEN = 32
TAKEN = 32
SPREAD = 32
TABLE = 16

mass_floor = 0.25
stiffness = 2.0
press_floor = 1.0
grain_size = 0.5
inertia_ref = 0.3
mu_static = 0.38
mu_limit = 0.64
rate_floor = 0.5
gravity = (0.5, 0.0, -0.866)
flip_share = 0.95
courant = 0.4
wave_speed = 2.0
components = ((0, 3, 4), (3, 1, 5), (4, 5, 2))
f32 = jnp.float32
bf16 = jnp.bfloat16


def split_pair(values):
    high = values.astype(bf16)
    low = (values - high.astype(f32)).astype(bf16)
    return high, low


def one_hot(cells_ref, block, offset):
    rel = cells_ref[pl.ds(block * 2, 2), :] - offset
    tall = (16, LANES)
    nodes = lax.broadcasted_iota(jnp.int32, tall, 0).astype(f32)
    one, zero = jnp.ones(tall, bf16), jnp.zeros(tall, bf16)
    halves = []
    for h in range(2):
        line = jnp.broadcast_to(rel[h : h + 1, :].astype(f32), tall).astype(bf16)
        halves.append(
            jnp.concatenate(
                [
                    jnp.where(line == (nodes + z).astype(bf16), one, zero)
                    for z in range(0, WIDE, 16)
                ],
                axis=0,
            )
        )
    return jnp.concatenate(halves, axis=1)


def list_visits(cells_ref, count, plan_ref):
    blocks = cells_ref.shape[0] // 2
    shape = (blocks, LANES)
    number = lax.broadcasted_iota(jnp.int32, shape, 0)
    lane = lax.broadcasted_iota(jnp.int32, shape, 1)
    first_half = cells_ref[pl.ds(0, blocks, stride=2), :]
    second_half = cells_ref[pl.ds(1, blocks, stride=2), :]
    slot = number * BLOCK + lane
    reached = jnp.maximum(
        jnp.where(slot < count, first_half, 0), jnp.where(slot + LANES < count, second_half, 0)
    )
    live = number * BLOCK < count
    first = jnp.min(first_half, axis=1, keepdims=True) >> 8
    last = jnp.max(reached, axis=1, keepdims=True) >> 8
    low = jnp.where(live, first + number, 2 * LANES)
    high = jnp.where(live, last + number, -1)
    inside = (low <= lane) & (lane <= high)
    place = lane[:1]
    block = jnp.max(jnp.where(inside, number, -1), axis=0, keepdims=True)
    valid = block >= 0
    pair = place - block
    plan_ref[0:1, :] = jnp.where(valid, block, 0)
    plan_ref[1:2, :] = jnp.where(valid, 2 * pair + (pair >> 4), 0)
    plan_ref[2:3, :] = jnp.where(valid, pair, PAIRS) * WIDE
    plan_ref[3:4, :] = jnp.max(high, axis=0, keepdims=True) + 1
    plan_ref[4:5, :] = jnp.broadcast_to(count, (1, LANES))
    plan_ref[5:8, :] = jnp.zeros((3, LANES), jnp.int32)


def spread_kernel(
    count_ref, frac_hbm, vel_hbm, mass_hbm, cells_hbm,
    far_ref, near_ref, layers_ref, plan_ref, frac_ref, vel_ref, hot_ref,
    cells_ref, listed_ref, mass_ref, q_ref, acc_ref, sems,
):
    slots = frac_ref.shape[1]
    sources = (cells_hbm, frac_hbm, vel_hbm, mass_hbm)
    targets = (cells_ref, frac_ref, vel_ref, mass_ref)
    arrivals = [
        pltpu.make_async_copy(source, target, sems.at[k])
        for k, (source, target) in enumerate(zip(sources, targets))
    ]
    for arrival in arrivals:
        arrival.start()
    acc_ref[...] = jnp.zeros_like(acc_ref)
    arrivals[0].wait()
    count = count_ref[0]
    list_visits(cells_ref, count, plan_ref)
    listing = pltpu.make_async_copy(plan_ref, listed_ref, sems.at[4])
    listing.start()
    for arrival in arrivals[1:]:
        arrival.wait()
    sublane = lax.broadcasted_iota(jnp.int32, (8, LANES), 0)
    lane = lax.broadcasted_iota(jnp.int32, (1, LANES), 1)
    top_z = sublane >= 4
    field = sublane & 3

    def weigh(part):
        at = pl.multiple_of(part * LANES, LANES)
        here = pl.ds(at, LANES)

        def spread_out(line):
            return jnp.broadcast_to(line, (8, LANES))

        fx, fy, fz = (spread_out(frac_ref[d : d + 1, here]) for d in range(3))
        vx, vy, vz = (spread_out(vel_ref[d : d + 1, here]) for d in range(3))
        held = spread_out(jnp.where(at + lane < count, mass_ref[pl.ds(part, 1), :], 0.0))
        carried = jnp.where(
            field == 0, held, held * jnp.where(field == 1, vx, jnp.where(field == 2, vy, vz))
        )
        carried = carried * jnp.where(top_z, fz, 1.0 - fz)
        lower, upper = carried * (1.0 - fx), carried * fx
        rows = jnp.concatenate(
            [lower * (1.0 - fy), lower * fy, upper * (1.0 - fy), upper * fy], axis=0
        )
        high, low = split_pair(rows)
        q_ref[pl.ds(part, 1)] = jnp.concatenate([high, low], axis=0)[None]

    def prepare(group, carry):
        for u in range(UNROLL):
            weigh(group * UNROLL + u)
        return carry

    lax.fori_loop(0, slots // LANES // UNROLL, prepare, 0)
    listing.wait()
    total = listed_ref[3, 0]

    def visit(group, carry):
        found = []
        for u in range(GIVEN):
            v = group * GIVEN + u
            block = listed_ref[0, v]
            hot = one_hot(cells_ref, block, listed_ref[2, v])
            hot_ref[pl.ds(v, 1)] = hot[None]
            both = q_ref[pl.ds(block * 2, 2)]
            both = lax.dot_general(
                jnp.concatenate([both[0], both[1]], axis=1),
                hot,
                (((1,), (1,)), ((), ())),
                preferred_element_type=f32,
            )
            found.append((listed_ref[1, v], both[:SPREAD] + both[SPREAD:]))
        for base, part in found:
            here = pl.ds(pl.multiple_of(base * 8, 8), 24)
            above = pl.ds(pl.multiple_of(base * 8, 8) + (NY + 1) * 8, 24)
            lower, upper = acc_ref[here, :], acc_ref[above, :]
            first, second = part[:, :NZ], part[:, NZ:]
            acc_ref[here, :] = lower + jnp.concatenate(
                [first[0:8], first[8:16] + second[0:8], second[8:16]], axis=0
            )
            acc_ref[above, :] = upper + jnp.concatenate(
                [first[16:24], first[24:32] + second[16:24], second[24:32]], axis=0
            )
        return carry

    lax.fori_loop(0, (total + GIVEN - 1) // GIVEN, visit, 0)

    odd = lax.axis_index("gx") % 2 == 1
    layers = []
    for l in range(CX + 1):
        first = l * (NY + 1) * 8
        acc_ref[first : first + 8, :] += acc_ref[first + NY * 8 : first + NY * 8 + 8, :]
        for f in range(4):
            lower = acc_ref[pl.ds(first + f, NY, stride=8), :]
            upper = acc_ref[pl.ds(first + 4 + f, NY, stride=8), :]
            layers.append(lower + pltpu.roll(upper, 1, 1))
            layers_ref[l * 4 + f] = layers[-1]
    for k in range(CX * 4):
        far_ref[k] = jnp.where(odd, layers[k + 4], layers[k])
        near_ref[k] = jnp.where(odd, layers[k], layers[k + 4])


def pair_up(field, axis):
    return field + pltpu.roll(field, field.shape[axis] - 1, axis)


def step_up(field, axis):
    return pltpu.roll(field, field.shape[axis] - 1, axis) - field


def pair_down(field, axis):
    return field + pltpu.roll(field, 1, axis)


def step_down(field, axis):
    return field - pltpu.roll(field, 1, axis)


def cell_stress(vel_lo, vel_hi, mass_lo, mass_hi, keep):
    grads = []
    for a in range(3):
        diff = vel_hi[a] - vel_lo[a]
        both = vel_hi[a] + vel_lo[a]
        grads.append(
            [
                0.25 * pair_up(pair_up(diff, 0), 1),
                0.25 * pair_up(step_up(both, 0), 1),
                0.25 * step_up(pair_up(both, 0), 1),
            ]
        )
    density = 0.125 * pair_up(pair_up(mass_hi + mass_lo, 0), 1)
    dxx = grads[0][0]
    dyy = grads[1][1]
    dzz = grads[2][2]
    dxy = 0.5 * (grads[0][1] + grads[1][0])
    dxz = 0.5 * (grads[0][2] + grads[2][0])
    dyz = 0.5 * (grads[1][2] + grads[2][1])
    second = dxx * dxx + dyy * dyy + dzz * dzz + 2.0 * (dxy * dxy + dxz * dxz + dyz * dyz)
    rate = jnp.sqrt(2.0 * second + rate_floor * rate_floor)
    pressure = stiffness * density
    inertial = rate * grain_size / jnp.sqrt(pressure + press_floor)
    friction = mu_static + (mu_limit - mu_static) * inertial / (inertia_ref + inertial)
    twice = 2.0 * friction * pressure / rate
    sigma = [
        twice * dxx - pressure,
        twice * dyy - pressure,
        twice * dzz - pressure,
        twice * dxy,
        twice * dxz,
        twice * dyz,
    ]
    return [jnp.where(keep, s, 0.0) for s in sigma]


def node_force(lower, upper):
    force = []
    for a in range(3):
        sx, sy, sz = (components[a][b] for b in range(3))
        along = pair_down(pair_down(upper[sx] - lower[sx], 0), 1)
        across = step_down(pair_down(upper[sy] + lower[sy], 1), 0)
        upward = step_down(pair_down(upper[sz] + lower[sz], 0), 1)
        force.append(0.25 * (along + across + upward))
    return force


def collect_kernel(
    step_ref, plan_ref, layers_ref, far_new_ref, near_new_ref, frac_ref, vel_ref, hot_ref,
    out_ref, top_ref, listed_ref, tab_ref, pair_ref, sem,
):
    blocks = frac_ref.shape[1] // BLOCK
    listing = pltpu.make_async_copy(plan_ref, listed_ref, sem)
    listing.start()
    step = step_ref[0]
    odd = lax.axis_index("gx") % 2 == 1

    def pick(if_odd, if_even):
        return [jnp.where(odd, if_odd[k], if_even[k]) for k in range(4 * CX)]

    own = [layers_ref[k] for k in range(4 * (CX + 1))]
    left, right = pick(near_new_ref, far_new_ref), pick(far_new_ref, near_new_ref)
    nodes = [
        left[:4],
        [own[f] + left[4 + f] for f in range(4)],
        own[4:8],
        [own[8 + f] + right[f] for f in range(4)],
        right[4:],
    ]
    height = lax.broadcasted_iota(jnp.int32, (NY, NZ), 1)
    keep = height < NZ - 1
    above_bed = height > 0
    floor = [jnp.maximum(layer[0], mass_floor) for layer in nodes]
    v_old = [[layer[1 + a] / floor[l] for a in range(3)] for l, layer in enumerate(nodes)]
    sigma = [
        cell_stress(v_old[l], v_old[l + 1], nodes[l][0], nodes[l + 1][0], keep) for l in range(4)
    ]
    blank = jnp.zeros((NY, NZ), f32)
    for l in range(CX + 1):
        force = node_force(sigma[l], sigma[l + 1])
        fields = [blank] * 8
        for a in range(3):
            layer = nodes[l + 1]
            fresh = (layer[1 + a] + step * (force[a] + layer[0] * gravity[a])) / floor[l + 1]
            fresh = jnp.where(above_bed, fresh, 0.0)
            fields[a] = fresh - flip_share * v_old[l + 1][a]
            fields[4 + a] = step * fresh
        for k, value in enumerate(fields):
            start = l * NY * TABLE + k
            tab_ref[pl.ds(start, NY, stride=TABLE), :] = value
            tab_ref[pl.ds(start + 8, NY, stride=TABLE), :] = pltpu.roll(value, NZ - 1, 1)

    for l in range(CX + 1):

        def split_row(j, carry):
            at = pl.ds(pl.multiple_of((l * NY + j) * TABLE, TABLE), TABLE)
            high, low = split_pair(tab_ref[at, :])
            pair_ref[pl.ds(l * (NY + 1) + j, 1)] = jnp.concatenate([high, low], axis=0)[None]
            return carry

        lax.fori_loop(0, NY, split_row, 0, unroll=8)
        pair_ref[l * (NY + 1) + NY] = pair_ref[l * (NY + 1)]

    out_ref[...] = jnp.zeros_like(out_ref)
    listing.wait()
    total = listed_ref[3, 0]
    count = listed_ref[4, 0]

    def visit(group, carry):
        found = []
        for u in range(TAKEN):
            v = group * TAKEN + u
            block = listed_ref[0, v]
            base = listed_ref[1, v]
            hot = hot_ref[pl.ds(v, 1)][0]
            rows = []
            for a in range(2):
                three = [pair_ref[base + a * (NY + 1) + k] for k in range(3)]
                rows += [jnp.concatenate(three[b : b + 2], axis=1) for b in range(2)]
            both = jnp.dot(jnp.concatenate(rows, axis=0), hot, preferred_element_type=f32)
            corners = []
            for k in range(4):
                four = both[2 * TABLE * k : 2 * TABLE * (k + 1)]
                corners += [four[0:8] + four[16:24], four[8:16] + four[24:32]]
            frac = frac_ref[:, pl.ds(pl.multiple_of(block * BLOCK, BLOCK), BLOCK)]
            for d in (2, 1, 0):
                share = frac[d : d + 1, :]
                corners = [
                    corners[k] + share * (corners[k + 1] - corners[k])
                    for k in range(0, len(corners), 2)
                ]
            found.append((block, corners[0]))
        for block, part in found:
            out_ref[pl.ds(block, 1)] += part[None]
        return carry

    lax.fori_loop(0, (total + TAKEN - 1) // TAKEN, visit, 0)

    lane = lax.broadcasted_iota(jnp.int32, (1, BLOCK), 1)

    def finish(block, top):
        at = pl.multiple_of(block * BLOCK, BLOCK)
        alive = at + lane < count
        got = out_ref[pl.ds(block, 1)][0]
        fresh = jnp.where(alive, flip_share * vel_ref[:, pl.ds(at, BLOCK)] + got[0:3], 0.0)
        out_ref[pl.ds(block, 1), 0:3] = fresh[None]
        square = fresh[0:1] * fresh[0:1] + fresh[1:2] * fresh[1:2] + fresh[2:3] * fresh[2:3]
        return jnp.maximum(top, square)

    top = lax.fori_loop(0, blocks, finish, jnp.zeros((1, BLOCK), f32), unroll=4)
    top = jnp.sqrt(jnp.max(top, axis=1, keepdims=True))
    top_ref[...] = jnp.broadcast_to(top, top_ref.shape)


def finish_kernel(plan_ref, moved_ref, frac_ref, new_frac_ref, new_vel_ref):
    blocks = frac_ref.shape[1] // BLOCK
    count = plan_ref[4:5, :]
    count = jnp.concatenate([count, count], axis=1)
    lane = lax.broadcasted_iota(jnp.int32, (1, BLOCK), 1)

    def finish(block, carry):
        at = pl.multiple_of(block * BLOCK, BLOCK)
        got = moved_ref[pl.ds(block, 1)][0]
        new_vel_ref[:, pl.ds(at, BLOCK)] = got[0:3]
        placed = jnp.where(at + lane < count, frac_ref[:, pl.ds(at, BLOCK)] + got[4:7], 0.0)
        new_frac_ref[:, pl.ds(at, BLOCK)] = placed
        return carry

    lax.fori_loop(0, blocks, finish, 0, unroll=4)


def largest(value, axis):
    devices = lax.axis_size(axis)
    reach = 1
    while reach < devices:
        if devices & (devices - 1) == 0:
            pairs = [(i, i ^ (reach | 1)) for i in range(devices)]
        else:
            pairs = [(i, (i + reach) % devices) for i in range(devices)]
        value = jnp.maximum(value, lax.ppermute(value, axis, pairs))
        reach *= 2
    return value


smem = pl.BlockSpec(memory_space=pltpu.SMEM)
vmem = pl.BlockSpec(memory_space=pltpu.VMEM)
hbm = pl.BlockSpec(memory_space=pltpu.HBM)


def body(frac, velocity, mass, particle_cell, tile_count, time_step):
    slots = frac.shape[1]
    blocks = slots // BLOCK
    rows = slots // LANES
    inputs = (frac, velocity, mass.reshape(rows, LANES), particle_cell.reshape(rows, LANES))
    far, near, layers, plan, frac_here, vel_here, hots = pl.pallas_call(
        spread_kernel,
        out_shape=(
            pltpu.VMEM((4 * CX, NY, NZ), f32),
            pltpu.VMEM((4 * CX, NY, NZ), f32),
            pltpu.VMEM((4 * (CX + 1), NY, NZ), f32),
            pltpu.VMEM((8, LANES), jnp.int32),
            pltpu.VMEM(frac.shape, f32),
            pltpu.VMEM(velocity.shape, f32),
            pltpu.VMEM((blocks + PAIRS, WIDE, BLOCK), bf16),
        ),
        in_specs=[smem] + [hbm] * 4,
        out_specs=(vmem,) * 7,
        scratch_shapes=[
            pltpu.VMEM((rows, LANES), jnp.int32),
            pltpu.SMEM((8, LANES), jnp.int32),
            pltpu.VMEM((rows, LANES), f32),
            pltpu.VMEM((rows, 2 * SPREAD, LANES), bf16),
            pltpu.VMEM(((CX + 1) * (NY + 1) * 8, NZ), f32),
            pltpu.SemaphoreType.DMA((5,)),
        ],
        compiler_params=pltpu.CompilerParams(vmem_limit_bytes=32 * 1024 * 1024),
        name="spread",
    )(tile_count, *[pltpu.with_memory_space_constraint(x, pltpu.HBM) for x in inputs])
    devices = lax.axis_size("gx")
    far_pairs = [(i, (i + (1 if i % 2 else -1)) % devices) for i in range(devices)]
    near_pairs = [(i, i ^ 1) for i in range(devices)]
    far_new = lax.ppermute(far, "gx", far_pairs)
    near_new = lax.ppermute(near, "gx", near_pairs)
    moved, top = pl.pallas_call(
        collect_kernel,
        out_shape=(
            jax.ShapeDtypeStruct((blocks, 8, BLOCK), f32),
            jax.ShapeDtypeStruct((8, LANES), f32),
        ),
        in_specs=[smem] + [vmem] * 7,
        out_specs=(vmem, vmem),
        scratch_shapes=[
            pltpu.SMEM((8, LANES), jnp.int32),
            pltpu.VMEM(((CX + 1) * NY * TABLE, NZ), f32),
            pltpu.VMEM(((CX + 1) * (NY + 1), 2 * TABLE, NZ), bf16),
            pltpu.SemaphoreType.DMA,
        ],
        compiler_params=pltpu.CompilerParams(vmem_limit_bytes=32 * 1024 * 1024),
        name="collect",
    )(time_step, plan, layers, far_new, near_new, frac_here, vel_here, hots)
    new_frac, new_velocity = pl.pallas_call(
        finish_kernel,
        out_shape=(
            jax.ShapeDtypeStruct(frac.shape, f32),
            jax.ShapeDtypeStruct(velocity.shape, f32),
        ),
        in_specs=[vmem] * 3,
        out_specs=(vmem, vmem),
        compiler_params=pltpu.CompilerParams(vmem_limit_bytes=32 * 1024 * 1024),
        cost_estimate=pl.CostEstimate(flops=0, bytes_accessed=8000000, transcendentals=0),
        name="finish",
    )(plan, moved, frac_here)
    fastest = largest(top, "gx")
    next_step = (courant / (fastest + wave_speed))[0, :1]
    return (new_frac, new_velocity, next_step)


def solution(mesh):
    placed = (
        P(None, ("runs", "gx")),
        P(None, ("runs", "gx")),
        P(("runs", "gx")),
        P(("runs", "gx")),
        P(("runs", "gx")),
        P("runs"),
    )
    return jax.shard_map(
        body,
        mesh=mesh,
        in_specs=placed,
        out_specs=(P(None, ("runs", "gx")), P(None, ("runs", "gx")), P("runs")),
        check_vma=False,
    )
```

```python
import functools

import jax
import jax.numpy as jnp
from jax import lax
from jax.experimental import pallas as pl
from jax.experimental.pallas import tpu as pltpu
from jax.sharding import PartitionSpec as P

CX = 2
NY = 32
NZ = 128
PAIRS = CX * NY // 2
WIDE = 2 * NZ
BLOCK = 256
LANES = 128
UNROLL = 8
GIVEN = 32
TAKEN = 32
SPREAD = 32
TABLE = 16

mass_floor = 0.25
stiffness = 2.0
press_floor = 1.0
grain_size = 0.5
inertia_ref = 0.3
mu_static = 0.38
mu_limit = 0.64
rate_floor = 0.5
gravity = (0.5, 0.0, -0.866)
flip_share = 0.95
courant = 0.4
wave_speed = 2.0
components = ((0, 3, 4), (3, 1, 5), (4, 5, 2))
f32 = jnp.float32
bf16 = jnp.bfloat16


def split_pair(values):
    high = values.astype(bf16)
    low = (values - high.astype(f32)).astype(bf16)
    return high, low


def one_hot(cells_ref, block, offset):
    rel = cells_ref[pl.ds(block * 2, 2), :] - offset
    tall = (16, LANES)
    nodes = lax.broadcasted_iota(jnp.int32, tall, 0).astype(f32)
    one, zero = jnp.ones(tall, bf16), jnp.zeros(tall, bf16)
    halves = []
    for h in range(2):
        line = jnp.broadcast_to(rel[h : h + 1, :].astype(f32), tall).astype(bf16)
        parts = []
        for z in range(0, WIDE, 16):
            apart = line - (nodes + z).astype(bf16)
            parts.append(jnp.maximum(one - apart * apart, zero))
        halves.append(jnp.concatenate(parts, axis=0))
    return jnp.concatenate(halves, axis=1)


def list_visits(cells_ref, count, plan_ref):
    blocks = cells_ref.shape[0] // 2
    shape = (blocks, LANES)
    number = lax.broadcasted_iota(jnp.int32, shape, 0)
    lane = lax.broadcasted_iota(jnp.int32, shape, 1)
    first_half = cells_ref[pl.ds(0, blocks, stride=2), :]
    second_half = cells_ref[pl.ds(1, blocks, stride=2), :]
    slot = number * BLOCK + lane
    reached = jnp.maximum(
        jnp.where(slot < count, first_half, 0), jnp.where(slot + LANES < count, second_half, 0)
    )
    live = number * BLOCK < count
    first = jnp.min(first_half, axis=1, keepdims=True) >> 8
    last = jnp.max(reached, axis=1, keepdims=True) >> 8
    low = jnp.where(live, first + number, 2 * LANES)
    high = jnp.where(live, last + number, -1)
    inside = (low <= lane) & (lane <= high)
    place = lane[:1]
    block = jnp.max(jnp.where(inside, number, -1), axis=0, keepdims=True)
    valid = block >= 0
    pair = place - block
    plan_ref[0:1, :] = jnp.where(valid, block, 0)
    plan_ref[1:2, :] = jnp.where(valid, 2 * pair + (pair >> 4), 0)
    plan_ref[2:3, :] = jnp.where(valid, pair, PAIRS) * WIDE
    plan_ref[3:4, :] = jnp.max(high, axis=0, keepdims=True) + 1
    plan_ref[4:5, :] = jnp.broadcast_to(count, (1, LANES))
    plan_ref[5:8, :] = jnp.zeros((3, LANES), jnp.int32)


def spread_kernel(
    count_ref, frac_hbm, vel_hbm, mass_hbm, cells_hbm,
    far_ref, near_ref, layers_ref, plan_ref, frac_ref, vel_ref, hot_ref,
    cells_ref, listed_ref, mass_ref, q_ref, acc_ref, sems,
):
    slots = frac_ref.shape[1]
    sources = (cells_hbm, frac_hbm, vel_hbm, mass_hbm)
    targets = (cells_ref, frac_ref, vel_ref, mass_ref)
    arrivals = [
        pltpu.make_async_copy(source, target, sems.at[k])
        for k, (source, target) in enumerate(zip(sources, targets))
    ]
    for arrival in arrivals:
        arrival.start()
    acc_ref[...] = jnp.zeros_like(acc_ref)
    arrivals[0].wait()
    count = count_ref[0]
    list_visits(cells_ref, count, plan_ref)
    listing = pltpu.make_async_copy(plan_ref, listed_ref, sems.at[4])
    listing.start()
    for arrival in arrivals[1:]:
        arrival.wait()
    sublane = lax.broadcasted_iota(jnp.int32, (8, LANES), 0)
    lane = lax.broadcasted_iota(jnp.int32, (1, LANES), 1)
    top_z = sublane >= 4
    field = sublane & 3

    def weigh(part):
        at = pl.multiple_of(part * LANES, LANES)
        here = pl.ds(at, LANES)

        def spread_out(line):
            return jnp.broadcast_to(line, (8, LANES))

        fx, fy, fz = (spread_out(frac_ref[d : d + 1, here]) for d in range(3))
        vx, vy, vz = (spread_out(vel_ref[d : d + 1, here]) for d in range(3))
        held = spread_out(jnp.where(at + lane < count, mass_ref[pl.ds(part, 1), :], 0.0))
        carried = jnp.where(
            field == 0, held, held * jnp.where(field == 1, vx, jnp.where(field == 2, vy, vz))
        )
        carried = carried * jnp.where(top_z, fz, 1.0 - fz)
        lower, upper = carried * (1.0 - fx), carried * fx
        rows = jnp.concatenate(
            [lower * (1.0 - fy), lower * fy, upper * (1.0 - fy), upper * fy], axis=0
        )
        high, low = split_pair(rows)
        q_ref[pl.ds(part, 1)] = jnp.concatenate([high, low], axis=0)[None]

    def prepare(group, carry):
        for u in range(UNROLL):
            weigh(group * UNROLL + u)
        return carry

    lax.fori_loop(0, slots // LANES // UNROLL, prepare, 0)
    listing.wait()
    total = listed_ref[3, 0]

    def visit(group, carry):
        found = []
        for u in range(GIVEN):
            v = group * GIVEN + u
            block = listed_ref[0, v]
            hot = one_hot(cells_ref, block, listed_ref[2, v])
            hot_ref[pl.ds(v, 1)] = hot[None]
            both = q_ref[pl.ds(block * 2, 2)]
            both = lax.dot_general(
                jnp.concatenate([both[0], both[1]], axis=1),
                hot,
                (((1,), (1,)), ((), ())),
                preferred_element_type=f32,
            )
            found.append((listed_ref[1, v], both[:SPREAD] + both[SPREAD:]))
        for base, part in found:
            here = pl.ds(pl.multiple_of(base * 8, 8), 24)
            above = pl.ds(pl.multiple_of(base * 8, 8) + (NY + 1) * 8, 24)
            lower, upper = acc_ref[here, :], acc_ref[above, :]
            first, second = part[:, :NZ], part[:, NZ:]
            acc_ref[here, :] = lower + jnp.concatenate(
                [first[0:8], first[8:16] + second[0:8], second[8:16]], axis=0
            )
            acc_ref[above, :] = upper + jnp.concatenate(
                [first[16:24], first[24:32] + second[16:24], second[24:32]], axis=0
            )
        return carry

    lax.fori_loop(0, (total + GIVEN - 1) // GIVEN, visit, 0)

    odd = lax.axis_index("gx") % 2 == 1
    layers = []
    for l in range(CX + 1):
        first = l * (NY + 1) * 8
        acc_ref[first : first + 8, :] += acc_ref[first + NY * 8 : first + NY * 8 + 8, :]
        for f in range(4):
            lower = acc_ref[pl.ds(first + f, NY, stride=8), :]
            upper = acc_ref[pl.ds(first + 4 + f, NY, stride=8), :]
            layers.append(lower + pltpu.roll(upper, 1, 1))
            layers_ref[l * 4 + f] = layers[-1]
    for k in range(CX * 4):
        far_ref[k] = jnp.where(odd, layers[k + 4], layers[k])
        near_ref[k] = jnp.where(odd, layers[k], layers[k + 4])


def pair_up(field, axis):
    return field + pltpu.roll(field, field.shape[axis] - 1, axis)


def step_up(field, axis):
    return pltpu.roll(field, field.shape[axis] - 1, axis) - field


def pair_down(field, axis):
    return field + pltpu.roll(field, 1, axis)


def step_down(field, axis):
    return field - pltpu.roll(field, 1, axis)


def cell_stress(vel_lo, vel_hi, mass_lo, mass_hi, keep):
    grads = []
    for a in range(3):
        diff = vel_hi[a] - vel_lo[a]
        both = vel_hi[a] + vel_lo[a]
        grads.append(
            [
                0.25 * pair_up(pair_up(diff, 0), 1),
                0.25 * pair_up(step_up(both, 0), 1),
                0.25 * step_up(pair_up(both, 0), 1),
            ]
        )
    density = 0.125 * pair_up(pair_up(mass_hi + mass_lo, 0), 1)
    dxx = grads[0][0]
    dyy = grads[1][1]
    dzz = grads[2][2]
    dxy = 0.5 * (grads[0][1] + grads[1][0])
    dxz = 0.5 * (grads[0][2] + grads[2][0])
    dyz = 0.5 * (grads[1][2] + grads[2][1])
    second = dxx * dxx + dyy * dyy + dzz * dzz + 2.0 * (dxy * dxy + dxz * dxz + dyz * dyz)
    rate = jnp.sqrt(2.0 * second + rate_floor * rate_floor)
    pressure = stiffness * density
    inertial = rate * grain_size / jnp.sqrt(pressure + press_floor)
    friction = mu_static + (mu_limit - mu_static) * inertial / (inertia_ref + inertial)
    twice = 2.0 * friction * pressure / rate
    sigma = [
        twice * dxx - pressure,
        twice * dyy - pressure,
        twice * dzz - pressure,
        twice * dxy,
        twice * dxz,
        twice * dyz,
    ]
    return [jnp.where(keep, s, 0.0) for s in sigma]


def node_force(lower, upper):
    force = []
    for a in range(3):
        sx, sy, sz = (components[a][b] for b in range(3))
        along = pair_down(pair_down(upper[sx] - lower[sx], 0), 1)
        across = step_down(pair_down(upper[sy] + lower[sy], 1), 0)
        upward = step_down(pair_down(upper[sz] + lower[sz], 0), 1)
        force.append(0.25 * (along + across + upward))
    return force


def collect_kernel(
    step_ref, plan_ref, layers_ref, far_new_ref, near_new_ref, frac_ref, vel_ref, hot_ref,
    out_ref, top_ref, listed_ref, tab_ref, pair_ref, sem,
):
    blocks = frac_ref.shape[1] // BLOCK
    listing = pltpu.make_async_copy(plan_ref, listed_ref, sem)
    listing.start()
    step = step_ref[0]
    odd = lax.axis_index("gx") % 2 == 1

    def pick(if_odd, if_even):
        return [jnp.where(odd, if_odd[k], if_even[k]) for k in range(4 * CX)]

    own = [layers_ref[k] for k in range(4 * (CX + 1))]
    left, right = pick(near_new_ref, far_new_ref), pick(far_new_ref, near_new_ref)
    nodes = [
        left[:4],
        [own[f] + left[4 + f] for f in range(4)],
        own[4:8],
        [own[8 + f] + right[f] for f in range(4)],
        right[4:],
    ]
    height = lax.broadcasted_iota(jnp.int32, (NY, NZ), 1)
    keep = height < NZ - 1
    above_bed = height > 0
    floor = [jnp.maximum(layer[0], mass_floor) for layer in nodes]
    v_old = [[layer[1 + a] / floor[l] for a in range(3)] for l, layer in enumerate(nodes)]
    sigma = [
        cell_stress(v_old[l], v_old[l + 1], nodes[l][0], nodes[l + 1][0], keep) for l in range(4)
    ]
    blank = jnp.zeros((NY, NZ), f32)
    for l in range(CX + 1):
        force = node_force(sigma[l], sigma[l + 1])
        fields = [blank] * 8
        for a in range(3):
            layer = nodes[l + 1]
            fresh = (layer[1 + a] + step * (force[a] + layer[0] * gravity[a])) / floor[l + 1]
            fresh = jnp.where(above_bed, fresh, 0.0)
            fields[a] = fresh - flip_share * v_old[l + 1][a]
            fields[4 + a] = step * fresh
        for k, value in enumerate(fields):
            start = l * NY * TABLE + k
            tab_ref[pl.ds(start, NY, stride=TABLE), :] = value
            tab_ref[pl.ds(start + 8, NY, stride=TABLE), :] = pltpu.roll(value, NZ - 1, 1)

    for l in range(CX + 1):

        def split_row(j, carry):
            at = pl.ds(pl.multiple_of((l * NY + j) * TABLE, TABLE), TABLE)
            high, low = split_pair(tab_ref[at, :])
            pair_ref[pl.ds(l * (NY + 1) + j, 1)] = jnp.concatenate([high, low], axis=0)[None]
            return carry

        lax.fori_loop(0, NY, split_row, 0, unroll=8)
        pair_ref[l * (NY + 1) + NY] = pair_ref[l * (NY + 1)]

    out_ref[...] = jnp.zeros_like(out_ref)
    listing.wait()
    total = listed_ref[3, 0]
    count = listed_ref[4, 0]

    def visit(group, carry):
        found = []
        for u in range(TAKEN):
            v = group * TAKEN + u
            block = listed_ref[0, v]
            base = listed_ref[1, v]
            hot = hot_ref[pl.ds(v, 1)][0]
            rows = []
            for a in range(2):
                three = [pair_ref[base + a * (NY + 1) + k] for k in range(3)]
                rows += [jnp.concatenate(three[b : b + 2], axis=1) for b in range(2)]
            both = jnp.dot(jnp.concatenate(rows, axis=0), hot, preferred_element_type=f32)
            corners = []
            for k in range(4):
                four = both[2 * TABLE * k : 2 * TABLE * (k + 1)]
                corners += [four[0:8] + four[16:24], four[8:16] + four[24:32]]
            frac = frac_ref[:, pl.ds(pl.multiple_of(block * BLOCK, BLOCK), BLOCK)]
            for d in (2, 1, 0):
                share = frac[d : d + 1, :]
                corners = [
                    corners[k] + share * (corners[k + 1] - corners[k])
                    for k in range(0, len(corners), 2)
                ]
            found.append((block, corners[0]))
        for block, part in found:
            out_ref[pl.ds(block, 1)] += part[None]
        return carry

    lax.fori_loop(0, (total + TAKEN - 1) // TAKEN, visit, 0)

    lane = lax.broadcasted_iota(jnp.int32, (1, BLOCK), 1)

    def finish(block, top):
        at = pl.multiple_of(block * BLOCK, BLOCK)
        alive = at + lane < count
        got = out_ref[pl.ds(block, 1)][0]
        fresh = jnp.where(alive, flip_share * vel_ref[:, pl.ds(at, BLOCK)] + got[0:3], 0.0)
        out_ref[pl.ds(block, 1), 0:3] = fresh[None]
        square = fresh[0:1] * fresh[0:1] + fresh[1:2] * fresh[1:2] + fresh[2:3] * fresh[2:3]
        return jnp.maximum(top, square)

    top = lax.fori_loop(0, blocks, finish, jnp.zeros((1, BLOCK), f32), unroll=4)
    top = jnp.sqrt(jnp.max(top, axis=1, keepdims=True))
    top_ref[...] = jnp.broadcast_to(top, top_ref.shape)


def finish_kernel(plan_ref, moved_ref, frac_ref, new_frac_ref, new_vel_ref):
    blocks = frac_ref.shape[1] // BLOCK
    count = plan_ref[4:5, :]
    count = jnp.concatenate([count, count], axis=1)
    lane = lax.broadcasted_iota(jnp.int32, (1, BLOCK), 1)

    def finish(block, carry):
        at = pl.multiple_of(block * BLOCK, BLOCK)
        got = moved_ref[pl.ds(block, 1)][0]
        new_vel_ref[:, pl.ds(at, BLOCK)] = got[0:3]
        placed = jnp.where(at + lane < count, frac_ref[:, pl.ds(at, BLOCK)] + got[4:7], 0.0)
        new_frac_ref[:, pl.ds(at, BLOCK)] = placed
        return carry

    lax.fori_loop(0, blocks, finish, 0, unroll=4)


def largest(value, axis):
    devices = lax.axis_size(axis)
    reach = 1
    while reach < devices:
        if devices & (devices - 1) == 0:
            pairs = [(i, i ^ (reach | 1)) for i in range(devices)]
        else:
            pairs = [(i, (i + reach) % devices) for i in range(devices)]
        value = jnp.maximum(value, lax.ppermute(value, axis, pairs))
        reach *= 2
    return value


smem = pl.BlockSpec(memory_space=pltpu.SMEM)
vmem = pl.BlockSpec(memory_space=pltpu.VMEM)
hbm = pl.BlockSpec(memory_space=pltpu.HBM)


def body(frac, velocity, mass, particle_cell, tile_count, time_step):
    slots = frac.shape[1]
    blocks = slots // BLOCK
    rows = slots // LANES
    inputs = (frac, velocity, mass.reshape(rows, LANES), particle_cell.reshape(rows, LANES))
    far, near, layers, plan, frac_here, vel_here, hots = pl.pallas_call(
        spread_kernel,
        out_shape=(
            pltpu.VMEM((4 * CX, NY, NZ), f32),
            pltpu.VMEM((4 * CX, NY, NZ), f32),
            pltpu.VMEM((4 * (CX + 1), NY, NZ), f32),
            pltpu.VMEM((8, LANES), jnp.int32),
            pltpu.VMEM(frac.shape, f32),
            pltpu.VMEM(velocity.shape, f32),
            pltpu.VMEM((blocks + PAIRS, WIDE, BLOCK), bf16),
        ),
        in_specs=[smem] + [hbm] * 4,
        out_specs=(vmem,) * 7,
        scratch_shapes=[
            pltpu.VMEM((rows, LANES), jnp.int32),
            pltpu.SMEM((8, LANES), jnp.int32),
            pltpu.VMEM((rows, LANES), f32),
            pltpu.VMEM((rows, 2 * SPREAD, LANES), bf16),
            pltpu.VMEM(((CX + 1) * (NY + 1) * 8, NZ), f32),
            pltpu.SemaphoreType.DMA((5,)),
        ],
        compiler_params=pltpu.CompilerParams(vmem_limit_bytes=32 * 1024 * 1024),
        name="spread",
    )(tile_count, *[pltpu.with_memory_space_constraint(x, pltpu.HBM) for x in inputs])
    devices = lax.axis_size("gx")
    far_pairs = [(i, (i + (1 if i % 2 else -1)) % devices) for i in range(devices)]
    near_pairs = [(i, i ^ 1) for i in range(devices)]
    far_new = lax.ppermute(far, "gx", far_pairs)
    near_new = lax.ppermute(near, "gx", near_pairs)
    moved, top = pl.pallas_call(
        collect_kernel,
        out_shape=(
            jax.ShapeDtypeStruct((blocks, 8, BLOCK), f32),
            jax.ShapeDtypeStruct((8, LANES), f32),
        ),
        in_specs=[smem] + [vmem] * 7,
        out_specs=(vmem, vmem),
        scratch_shapes=[
            pltpu.SMEM((8, LANES), jnp.int32),
            pltpu.VMEM(((CX + 1) * NY * TABLE, NZ), f32),
            pltpu.VMEM(((CX + 1) * (NY + 1), 2 * TABLE, NZ), bf16),
            pltpu.SemaphoreType.DMA,
        ],
        compiler_params=pltpu.CompilerParams(vmem_limit_bytes=32 * 1024 * 1024),
        name="collect",
    )(time_step, plan, layers, far_new, near_new, frac_here, vel_here, hots)
    new_frac, new_velocity = pl.pallas_call(
        finish_kernel,
        out_shape=(
            jax.ShapeDtypeStruct(frac.shape, f32),
            jax.ShapeDtypeStruct(velocity.shape, f32),
        ),
        in_specs=[vmem] * 3,
        out_specs=(vmem, vmem),
        compiler_params=pltpu.CompilerParams(vmem_limit_bytes=32 * 1024 * 1024),
        cost_estimate=pl.CostEstimate(flops=0, bytes_accessed=8000000, transcendentals=0),
        name="finish",
    )(plan, moved, frac_here)
    fastest = largest(top, "gx")
    next_step = (courant / (fastest + wave_speed))[0, :1]
    return (new_frac, new_velocity, next_step)


def solution(mesh):
    placed = (
        P(None, ("runs", "gx")),
        P(None, ("runs", "gx")),
        P(("runs", "gx")),
        P(("runs", "gx")),
        P(("runs", "gx")),
        P("runs"),
    )
    return jax.shard_map(
        body,
        mesh=mesh,
        in_specs=placed,
        out_specs=(P(None, ("runs", "gx")), P(None, ("runs", "gx")), P("runs")),
        check_vma=False,
    )
```

```python
import functools

import jax
import jax.numpy as jnp
from jax import lax
from jax.experimental import pallas as pl
from jax.experimental.pallas import tpu as pltpu
from jax.sharding import PartitionSpec as P

CX = 2
NY = 32
NZ = 128
PAIRS = CX * NY // 2
WIDE = 2 * NZ
BLOCK = 256
LANES = 128
UNROLL = 8
GIVEN = 32
TAKEN = 32
SLOTS = 8
DELAY = 4
SPREAD = 32
TABLE = 16

mass_floor = 0.25
stiffness = 2.0
press_floor = 1.0
grain_size = 0.5
inertia_ref = 0.3
mu_static = 0.38
mu_limit = 0.64
rate_floor = 0.5
gravity = (0.5, 0.0, -0.866)
flip_share = 0.95
courant = 0.4
wave_speed = 2.0
components = ((0, 3, 4), (3, 1, 5), (4, 5, 2))
f32 = jnp.float32
bf16 = jnp.bfloat16


def split_pair(values):
    high = values.astype(bf16)
    low = (values - high.astype(f32)).astype(bf16)
    return high, low


def one_hot(cells_ref, block, offset):
    rel = cells_ref[pl.ds(block * 2, 2), :] - offset
    tall = (16, LANES)
    nodes = lax.broadcasted_iota(jnp.int32, tall, 0).astype(f32)
    one, zero = jnp.ones(tall, bf16), jnp.zeros(tall, bf16)
    halves = []
    for h in range(2):
        line = jnp.broadcast_to(rel[h : h + 1, :].astype(f32), tall).astype(bf16)
        parts = []
        for z in range(0, WIDE, 16):
            apart = line - (nodes + z).astype(bf16)
            parts.append(jnp.maximum(one - apart * apart, zero))
        halves.append(jnp.concatenate(parts, axis=0))
    return jnp.concatenate(halves, axis=1)


def list_visits(cells_ref, count, plan_ref):
    blocks = cells_ref.shape[0] // 2
    shape = (blocks, LANES)
    number = lax.broadcasted_iota(jnp.int32, shape, 0)
    lane = lax.broadcasted_iota(jnp.int32, shape, 1)
    first_half = cells_ref[pl.ds(0, blocks, stride=2), :]
    second_half = cells_ref[pl.ds(1, blocks, stride=2), :]
    slot = number * BLOCK + lane
    reached = jnp.maximum(
        jnp.where(slot < count, first_half, 0), jnp.where(slot + LANES < count, second_half, 0)
    )
    live = number * BLOCK < count
    first = jnp.min(first_half, axis=1, keepdims=True) >> 8
    last = jnp.max(reached, axis=1, keepdims=True) >> 8
    low = jnp.where(live, first + number, 2 * LANES)
    high = jnp.where(live, last + number, -1)
    inside = (low <= lane) & (lane <= high)
    place = lane[:1]
    block = jnp.max(jnp.where(inside, number, -1), axis=0, keepdims=True)
    valid = block >= 0
    pair = place - block
    plan_ref[0:1, :] = jnp.where(valid, block, 0)
    plan_ref[1:2, :] = jnp.where(valid, 2 * pair + (pair >> 4), 0)
    plan_ref[2:3, :] = jnp.where(valid, pair, PAIRS) * WIDE
    plan_ref[3:4, :] = jnp.max(high, axis=0, keepdims=True) + 1
    plan_ref[4:5, :] = jnp.broadcast_to(count, (1, LANES))
    plan_ref[5:8, :] = jnp.zeros((3, LANES), jnp.int32)


def spread_kernel(
    count_ref, frac_hbm, vel_hbm, mass_hbm, cells_hbm,
    far_ref, near_ref, layers_ref, plan_ref, frac_ref, vel_ref, hot_ref,
    cells_ref, listed_ref, mass_ref, q_ref, acc_ref, sems,
):
    slots = frac_ref.shape[1]
    sources = (cells_hbm, frac_hbm, vel_hbm, mass_hbm)
    targets = (cells_ref, frac_ref, vel_ref, mass_ref)
    arrivals = [
        pltpu.make_async_copy(source, target, sems.at[k])
        for k, (source, target) in enumerate(zip(sources, targets))
    ]
    for arrival in arrivals:
        arrival.start()
    acc_ref[...] = jnp.zeros_like(acc_ref)
    arrivals[0].wait()
    count = count_ref[0]
    list_visits(cells_ref, count, plan_ref)
    listing = pltpu.make_async_copy(plan_ref, listed_ref, sems.at[4])
    listing.start()
    for arrival in arrivals[1:]:
        arrival.wait()
    sublane = lax.broadcasted_iota(jnp.int32, (8, LANES), 0)
    lane = lax.broadcasted_iota(jnp.int32, (1, LANES), 1)
    top_z = sublane >= 4
    field = sublane & 3

    def weigh(part):
        at = pl.multiple_of(part * LANES, LANES)
        here = pl.ds(at, LANES)

        def spread_out(line):
            return jnp.broadcast_to(line, (8, LANES))

        fx, fy, fz = (spread_out(frac_ref[d : d + 1, here]) for d in range(3))
        vx, vy, vz = (spread_out(vel_ref[d : d + 1, here]) for d in range(3))
        held = spread_out(jnp.where(at + lane < count, mass_ref[pl.ds(part, 1), :], 0.0))
        carried = jnp.where(
            field == 0, held, held * jnp.where(field == 1, vx, jnp.where(field == 2, vy, vz))
        )
        carried = carried * jnp.where(top_z, fz, 1.0 - fz)
        lower, upper = carried * (1.0 - fx), carried * fx
        rows = jnp.concatenate(
            [lower * (1.0 - fy), lower * fy, upper * (1.0 - fy), upper * fy], axis=0
        )
        high, low = split_pair(rows)
        q_ref[pl.ds(part, 1)] = jnp.concatenate([high, low], axis=0)[None]

    def prepare(group, carry):
        for u in range(UNROLL):
            weigh(group * UNROLL + u)
        return carry

    lax.fori_loop(0, slots // LANES // UNROLL, prepare, 0)
    listing.wait()
    total = listed_ref[3, 0]

    def visit(group, carry):
        def run(*sums):
            found = []

            def take(u):
                both = pltpu.matmul_pop(sums[u % SLOTS])
                found.append((listed_ref[1, group * GIVEN + u], both[:SPREAD] + both[SPREAD:]))

            for u in range(GIVEN):
                v = group * GIVEN + u
                block = listed_ref[0, v]
                hot = one_hot(cells_ref, block, listed_ref[2, v])
                hot_ref[pl.ds(v, 1)] = hot[None]
                both = q_ref[pl.ds(block * 2, 2)]
                unit, turn = u % 2, u // 2 % 2
                pltpu.matmul_push_rhs(hot, turn, unit, transpose=True)
                pltpu.matmul_acc_lhs(
                    sums[u % SLOTS],
                    jnp.concatenate([both[0], both[1]], axis=1),
                    load_staged_rhs=turn,
                )
                if u >= DELAY:
                    take(u - DELAY)
            for u in range(GIVEN - DELAY, GIVEN):
                take(u)
            for base, part in found:
                here = pl.ds(pl.multiple_of(base * 8, 8), 24)
                above = pl.ds(pl.multiple_of(base * 8, 8) + (NY + 1) * 8, 24)
                lower, upper = acc_ref[here, :], acc_ref[above, :]
                first, second = part[:, :NZ], part[:, NZ:]
                acc_ref[here, :] = lower + jnp.concatenate(
                    [first[0:8], first[8:16] + second[0:8], second[8:16]], axis=0
                )
                acc_ref[above, :] = upper + jnp.concatenate(
                    [first[16:24], first[24:32] + second[16:24], second[24:32]], axis=0
                )

        pl.run_scoped(run, *[pltpu.ACC(k % 2)((2 * SPREAD, WIDE), f32) for k in range(SLOTS)])
        return carry

    lax.fori_loop(0, (total + GIVEN - 1) // GIVEN, visit, 0)

    odd = lax.axis_index("gx") % 2 == 1
    layers = []
    for l in range(CX + 1):
        first = l * (NY + 1) * 8
        acc_ref[first : first + 8, :] += acc_ref[first + NY * 8 : first + NY * 8 + 8, :]
        for f in range(4):
            lower = acc_ref[pl.ds(first + f, NY, stride=8), :]
            upper = acc_ref[pl.ds(first + 4 + f, NY, stride=8), :]
            layers.append(lower + pltpu.roll(upper, 1, 1))
            layers_ref[l * 4 + f] = layers[-1]
    for k in range(CX * 4):
        far_ref[k] = jnp.where(odd, layers[k + 4], layers[k])
        near_ref[k] = jnp.where(odd, layers[k], layers[k + 4])


def pair_up(field, axis):
    return field + pltpu.roll(field, field.shape[axis] - 1, axis)


def step_up(field, axis):
    return pltpu.roll(field, field.shape[axis] - 1, axis) - field


def pair_down(field, axis):
    return field + pltpu.roll(field, 1, axis)


def step_down(field, axis):
    return field - pltpu.roll(field, 1, axis)


def cell_stress(vel_lo, vel_hi, mass_lo, mass_hi, keep):
    grads = []
    for a in range(3):
        diff = vel_hi[a] - vel_lo[a]
        both = vel_hi[a] + vel_lo[a]
        grads.append(
            [
                0.25 * pair_up(pair_up(diff, 0), 1),
                0.25 * pair_up(step_up(both, 0), 1),
                0.25 * step_up(pair_up(both, 0), 1),
            ]
        )
    density = 0.125 * pair_up(pair_up(mass_hi + mass_lo, 0), 1)
    dxx = grads[0][0]
    dyy = grads[1][1]
    dzz = grads[2][2]
    dxy = 0.5 * (grads[0][1] + grads[1][0])
    dxz = 0.5 * (grads[0][2] + grads[2][0])
    dyz = 0.5 * (grads[1][2] + grads[2][1])
    second = dxx * dxx + dyy * dyy + dzz * dzz + 2.0 * (dxy * dxy + dxz * dxz + dyz * dyz)
    rate = jnp.sqrt(2.0 * second + rate_floor * rate_floor)
    pressure = stiffness * density
    inertial = rate * grain_size / jnp.sqrt(pressure + press_floor)
    friction = mu_static + (mu_limit - mu_static) * inertial / (inertia_ref + inertial)
    twice = 2.0 * friction * pressure / rate
    sigma = [
        twice * dxx - pressure,
        twice * dyy - pressure,
        twice * dzz - pressure,
        twice * dxy,
        twice * dxz,
        twice * dyz,
    ]
    return [jnp.where(keep, s, 0.0) for s in sigma]


def node_force(lower, upper):
    force = []
    for a in range(3):
        sx, sy, sz = (components[a][b] for b in range(3))
        along = pair_down(pair_down(upper[sx] - lower[sx], 0), 1)
        across = step_down(pair_down(upper[sy] + lower[sy], 1), 0)
        upward = step_down(pair_down(upper[sz] + lower[sz], 0), 1)
        force.append(0.25 * (along + across + upward))
    return force


def collect_kernel(
    step_ref, plan_ref, layers_ref, far_new_ref, near_new_ref, frac_ref, vel_ref, hot_ref,
    out_ref, top_ref, listed_ref, tab_ref, pair_ref, sem,
):
    blocks = frac_ref.shape[1] // BLOCK
    listing = pltpu.make_async_copy(plan_ref, listed_ref, sem)
    listing.start()
    step = step_ref[0]
    odd = lax.axis_index("gx") % 2 == 1

    def pick(if_odd, if_even):
        return [jnp.where(odd, if_odd[k], if_even[k]) for k in range(4 * CX)]

    own = [layers_ref[k] for k in range(4 * (CX + 1))]
    left, right = pick(near_new_ref, far_new_ref), pick(far_new_ref, near_new_ref)
    nodes = [
        left[:4],
        [own[f] + left[4 + f] for f in range(4)],
        own[4:8],
        [own[8 + f] + right[f] for f in range(4)],
        right[4:],
    ]
    height = lax.broadcasted_iota(jnp.int32, (NY, NZ), 1)
    keep = height < NZ - 1
    above_bed = height > 0
    floor = [jnp.maximum(layer[0], mass_floor) for layer in nodes]
    v_old = [[layer[1 + a] / floor[l] for a in range(3)] for l, layer in enumerate(nodes)]
    sigma = [
        cell_stress(v_old[l], v_old[l + 1], nodes[l][0], nodes[l + 1][0], keep) for l in range(4)
    ]
    blank = jnp.zeros((NY, NZ), f32)
    for l in range(CX + 1):
        force = node_force(sigma[l], sigma[l + 1])
        fields = [blank] * 8
        for a in range(3):
            layer = nodes[l + 1]
            fresh = (layer[1 + a] + step * (force[a] + layer[0] * gravity[a])) / floor[l + 1]
            fresh = jnp.where(above_bed, fresh, 0.0)
            fields[a] = fresh - flip_share * v_old[l + 1][a]
            fields[4 + a] = step * fresh
        for k, value in enumerate(fields):
            start = l * NY * TABLE + k
            tab_ref[pl.ds(start, NY, stride=TABLE), :] = value
            tab_ref[pl.ds(start + 8, NY, stride=TABLE), :] = pltpu.roll(value, NZ - 1, 1)

    for l in range(CX + 1):

        def split_row(j, carry):
            at = pl.ds(pl.multiple_of((l * NY + j) * TABLE, TABLE), TABLE)
            high, low = split_pair(tab_ref[at, :])
            pair_ref[pl.ds(l * (NY + 1) + j, 1)] = jnp.concatenate([high, low], axis=0)[None]
            return carry

        lax.fori_loop(0, NY, split_row, 0, unroll=8)
        pair_ref[l * (NY + 1) + NY] = pair_ref[l * (NY + 1)]

    out_ref[...] = jnp.zeros_like(out_ref)
    listing.wait()
    total = listed_ref[3, 0]
    count = listed_ref[4, 0]

    def visit(group, carry):
        found = []
        for u in range(TAKEN):
            v = group * TAKEN + u
            block = listed_ref[0, v]
            base = listed_ref[1, v]
            hot = hot_ref[pl.ds(v, 1)][0]
            rows = []
            for a in range(2):
                three = [pair_ref[base + a * (NY + 1) + k] for k in range(3)]
                rows += [jnp.concatenate(three[b : b + 2], axis=1) for b in range(2)]
            both = jnp.dot(jnp.concatenate(rows, axis=0), hot, preferred_element_type=f32)
            corners = []
            for k in range(4):
                four = both[2 * TABLE * k : 2 * TABLE * (k + 1)]
                corners += [four[0:8] + four[16:24], four[8:16] + four[24:32]]
            frac = frac_ref[:, pl.ds(pl.multiple_of(block * BLOCK, BLOCK), BLOCK)]
            for d in (2, 1, 0):
                share = frac[d : d + 1, :]
                corners = [
                    corners[k] + share * (corners[k + 1] - corners[k])
                    for k in range(0, len(corners), 2)
                ]
            found.append((block, corners[0]))
        for block, part in found:
            out_ref[pl.ds(block, 1)] += part[None]
        return carry

    lax.fori_loop(0, (total + TAKEN - 1) // TAKEN, visit, 0)

    lane = lax.broadcasted_iota(jnp.int32, (1, BLOCK), 1)

    def finish(block, top):
        at = pl.multiple_of(block * BLOCK, BLOCK)
        alive = at + lane < count
        got = out_ref[pl.ds(block, 1)][0]
        fresh = jnp.where(alive, flip_share * vel_ref[:, pl.ds(at, BLOCK)] + got[0:3], 0.0)
        out_ref[pl.ds(block, 1), 0:3] = fresh[None]
        square = fresh[0:1] * fresh[0:1] + fresh[1:2] * fresh[1:2] + fresh[2:3] * fresh[2:3]
        return jnp.maximum(top, square)

    top = lax.fori_loop(0, blocks, finish, jnp.zeros((1, BLOCK), f32), unroll=4)
    top = jnp.sqrt(jnp.max(top, axis=1, keepdims=True))
    top_ref[...] = jnp.broadcast_to(top, top_ref.shape)


def finish_kernel(plan_ref, moved_ref, frac_ref, new_frac_ref, new_vel_ref):
    blocks = frac_ref.shape[1] // BLOCK
    count = plan_ref[4:5, :]
    count = jnp.concatenate([count, count], axis=1)
    lane = lax.broadcasted_iota(jnp.int32, (1, BLOCK), 1)

    def finish(block, carry):
        at = pl.multiple_of(block * BLOCK, BLOCK)
        got = moved_ref[pl.ds(block, 1)][0]
        new_vel_ref[:, pl.ds(at, BLOCK)] = got[0:3]
        placed = jnp.where(at + lane < count, frac_ref[:, pl.ds(at, BLOCK)] + got[4:7], 0.0)
        new_frac_ref[:, pl.ds(at, BLOCK)] = placed
        return carry

    lax.fori_loop(0, blocks, finish, 0, unroll=4)


def largest(value, axis):
    devices = lax.axis_size(axis)
    reach = 1
    while reach < devices:
        if devices & (devices - 1) == 0:
            pairs = [(i, i ^ (reach | 1)) for i in range(devices)]
        else:
            pairs = [(i, (i + reach) % devices) for i in range(devices)]
        value = jnp.maximum(value, lax.ppermute(value, axis, pairs))
        reach *= 2
    return value


smem = pl.BlockSpec(memory_space=pltpu.SMEM)
vmem = pl.BlockSpec(memory_space=pltpu.VMEM)
hbm = pl.BlockSpec(memory_space=pltpu.HBM)


def body(frac, velocity, mass, particle_cell, tile_count, time_step):
    slots = frac.shape[1]
    blocks = slots // BLOCK
    rows = slots // LANES
    inputs = (frac, velocity, mass.reshape(rows, LANES), particle_cell.reshape(rows, LANES))
    far, near, layers, plan, frac_here, vel_here, hots = pl.pallas_call(
        spread_kernel,
        out_shape=(
            pltpu.VMEM((4 * CX, NY, NZ), f32),
            pltpu.VMEM((4 * CX, NY, NZ), f32),
            pltpu.VMEM((4 * (CX + 1), NY, NZ), f32),
            pltpu.VMEM((8, LANES), jnp.int32),
            pltpu.VMEM(frac.shape, f32),
            pltpu.VMEM(velocity.shape, f32),
            pltpu.VMEM((blocks + PAIRS, WIDE, BLOCK), bf16),
        ),
        in_specs=[smem] + [hbm] * 4,
        out_specs=(vmem,) * 7,
        scratch_shapes=[
            pltpu.VMEM((rows, LANES), jnp.int32),
            pltpu.SMEM((8, LANES), jnp.int32),
            pltpu.VMEM((rows, LANES), f32),
            pltpu.VMEM((rows, 2 * SPREAD, LANES), bf16),
            pltpu.VMEM(((CX + 1) * (NY + 1) * 8, NZ), f32),
            pltpu.SemaphoreType.DMA((5,)),
        ],
        compiler_params=pltpu.CompilerParams(vmem_limit_bytes=32 * 1024 * 1024),
        name="spread",
    )(tile_count, *[pltpu.with_memory_space_constraint(x, pltpu.HBM) for x in inputs])
    devices = lax.axis_size("gx")
    far_pairs = [(i, (i + (1 if i % 2 else -1)) % devices) for i in range(devices)]
    near_pairs = [(i, i ^ 1) for i in range(devices)]
    far_new = lax.ppermute(far, "gx", far_pairs)
    near_new = lax.ppermute(near, "gx", near_pairs)
    moved, top = pl.pallas_call(
        collect_kernel,
        out_shape=(
            jax.ShapeDtypeStruct((blocks, 8, BLOCK), f32),
            jax.ShapeDtypeStruct((8, LANES), f32),
        ),
        in_specs=[smem] + [vmem] * 7,
        out_specs=(vmem, vmem),
        scratch_shapes=[
            pltpu.SMEM((8, LANES), jnp.int32),
            pltpu.VMEM(((CX + 1) * NY * TABLE, NZ), f32),
            pltpu.VMEM(((CX + 1) * (NY + 1), 2 * TABLE, NZ), bf16),
            pltpu.SemaphoreType.DMA,
        ],
        compiler_params=pltpu.CompilerParams(vmem_limit_bytes=32 * 1024 * 1024),
        name="collect",
    )(time_step, plan, layers, far_new, near_new, frac_here, vel_here, hots)
    new_frac, new_velocity = pl.pallas_call(
        finish_kernel,
        out_shape=(
            jax.ShapeDtypeStruct(frac.shape, f32),
            jax.ShapeDtypeStruct(velocity.shape, f32),
        ),
        in_specs=[vmem] * 3,
        out_specs=(vmem, vmem),
        compiler_params=pltpu.CompilerParams(vmem_limit_bytes=32 * 1024 * 1024),
        cost_estimate=pl.CostEstimate(flops=0, bytes_accessed=8000000, transcendentals=0),
        name="finish",
    )(plan, moved, frac_here)
    fastest = largest(top, "gx")
    next_step = (courant / (fastest + wave_speed))[0, :1]
    return (new_frac, new_velocity, next_step)


def solution(mesh):
    placed = (
        P(None, ("runs", "gx")),
        P(None, ("runs", "gx")),
        P(("runs", "gx")),
        P(("runs", "gx")),
        P(("runs", "gx")),
        P("runs"),
    )
    return jax.shard_map(
        body,
        mesh=mesh,
        in_specs=placed,
        out_specs=(P(None, ("runs", "gx")), P(None, ("runs", "gx")), P("runs")),
        check_vma=False,
    )
```

```python
import functools

import jax
import jax.numpy as jnp
from jax import lax
from jax.experimental import pallas as pl
from jax.experimental.pallas import tpu as pltpu
from jax.sharding import PartitionSpec as P

CX = 2
NY = 32
NZ = 128
ROWS = CX * NY
PAIRS = ROWS // 2
WIDE = 2 * NZ
BLOCK = 256
LANES = 128
GIVEN = 32
TAKEN = 32
SPREAD = 32
TABLE = 16

mass_floor = 0.25
stiffness = 2.0
press_floor = 1.0
grain_size = 0.5
inertia_ref = 0.3
mu_static = 0.38
mu_limit = 0.64
rate_floor = 0.5
gravity = (0.5, 0.0, -0.866)
flip_share = 0.95
courant = 0.4
wave_speed = 2.0
components = ((0, 3, 4), (3, 1, 5), (4, 5, 2))
f32 = jnp.float32
bf16 = jnp.bfloat16


def split_pair(values):
    high = values.astype(bf16)
    low = (values - high.astype(f32)).astype(bf16)
    return high, low


def one_hot(cells_ref, block, offset, wide):
    rel = cells_ref[pl.ds(block * 2, 2), :] - offset
    tall = (16, LANES)
    nodes = lax.broadcasted_iota(jnp.int32, tall, 0).astype(f32)
    one, zero = jnp.ones(tall, bf16), jnp.zeros(tall, bf16)
    halves = []
    for h in range(2):
        line = jnp.broadcast_to(rel[h : h + 1, :].astype(f32), tall).astype(bf16)
        parts = [
            jnp.where(line == (nodes + z).astype(bf16), one, zero) for z in range(0, wide, 16)
        ]
        halves.append(jnp.concatenate(parts, axis=0))
    return jnp.concatenate(halves, axis=1)


def list_visits(cells_ref, count, plan_ref):
    blocks = cells_ref.shape[0] // 2
    shape = (blocks, LANES)
    number = lax.broadcasted_iota(jnp.int32, shape, 0)
    lane = lax.broadcasted_iota(jnp.int32, shape, 1)
    first_half = cells_ref[pl.ds(0, blocks, stride=2), :]
    second_half = cells_ref[pl.ds(1, blocks, stride=2), :]
    slot = number * BLOCK + lane
    reached = jnp.maximum(
        jnp.where(slot < count, first_half, 0), jnp.where(slot + LANES < count, second_half, 0)
    )
    live = number * BLOCK < count
    first = jnp.min(first_half, axis=1, keepdims=True)
    last = jnp.max(reached, axis=1, keepdims=True)
    place = lane[:1]
    for k, shift in enumerate((7, 8)):
        low = jnp.where(live, (first >> shift) + number, 2 * LANES)
        high = jnp.where(live, (last >> shift) + number, -1)
        inside = (low <= lane) & (lane <= high)
        block = jnp.max(jnp.where(inside, number, -1), axis=0, keepdims=True)
        valid = block >= 0
        row = (place - block) << (shift - 7)
        plan_ref[4 * k : 4 * k + 1, :] = jnp.where(valid, block, 0)
        plan_ref[4 * k + 1 : 4 * k + 2, :] = jnp.where(valid, row + (row >> 5), 0)
        plan_ref[4 * k + 2 : 4 * k + 3, :] = jnp.where(valid, row, ROWS) * NZ
        plan_ref[4 * k + 3 : 4 * k + 4, :] = jnp.max(high, axis=0, keepdims=True) + 1
    plan_ref[8:9, :] = jnp.broadcast_to(count, (1, LANES))
    plan_ref[9:16, :] = jnp.zeros((7, LANES), jnp.int32)


def spread_kernel(
    count_ref, frac_hbm, vel_hbm, mass_hbm, cells_hbm,
    far_ref, near_ref, layers_ref, plan_ref, frac_ref, vel_ref, cells_ref,
    listed_ref, mass_ref, acc_ref, sems,
):
    slots = frac_ref.shape[1]
    sources = (cells_hbm, frac_hbm, vel_hbm, mass_hbm)
    targets = (cells_ref, frac_ref, vel_ref, mass_ref)
    arrivals = [
        pltpu.make_async_copy(source, target, sems.at[k])
        for k, (source, target) in enumerate(zip(sources, targets))
    ]
    for arrival in arrivals:
        arrival.start()
    acc_ref[...] = jnp.zeros_like(acc_ref)
    arrivals[0].wait()
    count = count_ref[0]
    list_visits(cells_ref, count, plan_ref)
    listing = pltpu.make_async_copy(plan_ref, listed_ref, sems.at[4])
    listing.start()
    for arrival in arrivals[1:]:
        arrival.wait()
    sublane = lax.broadcasted_iota(jnp.int32, (8, LANES), 0)
    lane = lax.broadcasted_iota(jnp.int32, (1, LANES), 1)
    top_z = sublane >= 4
    field = sublane & 3

    def weigh(part):
        at = pl.multiple_of(part * LANES, LANES)
        here = pl.ds(at, LANES)

        def spread_out(line):
            return jnp.broadcast_to(line, (8, LANES))

        fx, fy, fz = (spread_out(frac_ref[d : d + 1, here]) for d in range(3))
        vx, vy, vz = (spread_out(vel_ref[d : d + 1, here]) for d in range(3))
        held = spread_out(jnp.where(at + lane < count, mass_ref[pl.ds(part, 1), :], 0.0))
        carried = jnp.where(
            field == 0, held, held * jnp.where(field == 1, vx, jnp.where(field == 2, vy, vz))
        )
        carried = carried * jnp.where(top_z, fz, 1.0 - fz)
        lower, upper = carried * (1.0 - fx), carried * fx
        rows = jnp.concatenate(
            [lower * (1.0 - fy), lower * fy, upper * (1.0 - fy), upper * fy], axis=0
        )
        return jnp.concatenate(split_pair(rows), axis=0)

    listing.wait()
    total = listed_ref[3, 0]

    def visit(group, carry):
        found = []
        for u in range(GIVEN):
            v = group * GIVEN + u
            block = listed_ref[0, v]
            hot = one_hot(cells_ref, block, listed_ref[2, v], NZ)
            both = lax.dot_general(
                jnp.concatenate([weigh(2 * block), weigh(2 * block + 1)], axis=1),
                hot,
                (((1,), (1,)), ((), ())),
                preferred_element_type=f32,
            )
            found.append((listed_ref[1, v], both[:SPREAD] + both[SPREAD:]))
        for base, part in found:
            here = pl.ds(pl.multiple_of(base * 8, 8), 16)
            above = pl.ds(pl.multiple_of(base * 8, 8) + (NY + 1) * 8, 16)
            lower, upper = acc_ref[here, :], acc_ref[above, :]
            acc_ref[here, :] = lower + part[:16]
            acc_ref[above, :] = upper + part[16:]
        return carry

    lax.fori_loop(0, (total + GIVEN - 1) // GIVEN, visit, 0)

    odd = lax.axis_index("gx") % 2 == 1
    layers = []
    for l in range(CX + 1):
        first = l * (NY + 1) * 8
        acc_ref[first : first + 8, :] += acc_ref[first + NY * 8 : first + NY * 8 + 8, :]
        for f in range(4):
            lower = acc_ref[pl.ds(first + f, NY, stride=8), :]
            upper = acc_ref[pl.ds(first + 4 + f, NY, stride=8), :]
            layers.append(lower + pltpu.roll(upper, 1, 1))
            layers_ref[l * 4 + f] = layers[-1]
    for k in range(CX * 4):
        far_ref[k] = jnp.where(odd, layers[k + 4], layers[k])
        near_ref[k] = jnp.where(odd, layers[k], layers[k + 4])


def pair_up(field, axis):
    return field + pltpu.roll(field, field.shape[axis] - 1, axis)


def step_up(field, axis):
    return pltpu.roll(field, field.shape[axis] - 1, axis) - field


def pair_down(field, axis):
    return field + pltpu.roll(field, 1, axis)


def step_down(field, axis):
    return field - pltpu.roll(field, 1, axis)


def cell_stress(vel_lo, vel_hi, mass_lo, mass_hi, keep):
    grads = []
    for a in range(3):
        diff = vel_hi[a] - vel_lo[a]
        both = vel_hi[a] + vel_lo[a]
        grads.append(
            [
                0.25 * pair_up(pair_up(diff, 0), 1),
                0.25 * pair_up(step_up(both, 0), 1),
                0.25 * step_up(pair_up(both, 0), 1),
            ]
        )
    density = 0.125 * pair_up(pair_up(mass_hi + mass_lo, 0), 1)
    dxx = grads[0][0]
    dyy = grads[1][1]
    dzz = grads[2][2]
    dxy = 0.5 * (grads[0][1] + grads[1][0])
    dxz = 0.5 * (grads[0][2] + grads[2][0])
    dyz = 0.5 * (grads[1][2] + grads[2][1])
    second = dxx * dxx + dyy * dyy + dzz * dzz + 2.0 * (dxy * dxy + dxz * dxz + dyz * dyz)
    rate = jnp.sqrt(2.0 * second + rate_floor * rate_floor)
    pressure = stiffness * density
    inertial = rate * grain_size / jnp.sqrt(pressure + press_floor)
    friction = mu_static + (mu_limit - mu_static) * inertial / (inertia_ref + inertial)
    twice = 2.0 * friction * pressure / rate
    sigma = [
        twice * dxx - pressure,
        twice * dyy - pressure,
        twice * dzz - pressure,
        twice * dxy,
        twice * dxz,
        twice * dyz,
    ]
    return [jnp.where(keep, s, 0.0) for s in sigma]


def node_force(lower, upper):
    force = []
    for a in range(3):
        sx, sy, sz = (components[a][b] for b in range(3))
        along = pair_down(pair_down(upper[sx] - lower[sx], 0), 1)
        across = step_down(pair_down(upper[sy] + lower[sy], 1), 0)
        upward = step_down(pair_down(upper[sz] + lower[sz], 0), 1)
        force.append(0.25 * (along + across + upward))
    return force


def collect_kernel(
    step_ref, plan_ref, layers_ref, far_new_ref, near_new_ref, frac_ref, vel_ref, cells_ref,
    out_ref, top_ref, listed_ref, tab_ref, pair_ref, sem,
):
    blocks = frac_ref.shape[1] // BLOCK
    listing = pltpu.make_async_copy(plan_ref, listed_ref, sem)
    listing.start()
    step = step_ref[0]
    odd = lax.axis_index("gx") % 2 == 1

    def pick(if_odd, if_even):
        return [jnp.where(odd, if_odd[k], if_even[k]) for k in range(4 * CX)]

    own = [layers_ref[k] for k in range(4 * (CX + 1))]
    left, right = pick(near_new_ref, far_new_ref), pick(far_new_ref, near_new_ref)
    nodes = [
        left[:4],
        [own[f] + left[4 + f] for f in range(4)],
        own[4:8],
        [own[8 + f] + right[f] for f in range(4)],
        right[4:],
    ]
    height = lax.broadcasted_iota(jnp.int32, (NY, NZ), 1)
    keep = height < NZ - 1
    above_bed = height > 0
    floor = [jnp.maximum(layer[0], mass_floor) for layer in nodes]
    v_old = [[layer[1 + a] / floor[l] for a in range(3)] for l, layer in enumerate(nodes)]
    sigma = [
        cell_stress(v_old[l], v_old[l + 1], nodes[l][0], nodes[l + 1][0], keep) for l in range(4)
    ]
    blank = jnp.zeros((NY, NZ), f32)
    for l in range(CX + 1):
        force = node_force(sigma[l], sigma[l + 1])
        fields = [blank] * 8
        for a in range(3):
            layer = nodes[l + 1]
            fresh = (layer[1 + a] + step * (force[a] + layer[0] * gravity[a])) / floor[l + 1]
            fresh = jnp.where(above_bed, fresh, 0.0)
            fields[a] = fresh - flip_share * v_old[l + 1][a]
            fields[4 + a] = step * fresh
        for k, value in enumerate(fields):
            start = l * NY * TABLE + k
            tab_ref[pl.ds(start, NY, stride=TABLE), :] = value
            tab_ref[pl.ds(start + 8, NY, stride=TABLE), :] = pltpu.roll(value, NZ - 1, 1)

    for l in range(CX + 1):

        def split_row(j, carry):
            at = pl.ds(pl.multiple_of((l * NY + j) * TABLE, TABLE), TABLE)
            high, low = split_pair(tab_ref[at, :])
            pair_ref[pl.ds(l * (NY + 1) + j, 1)] = jnp.concatenate([high, low], axis=0)[None]
            return carry

        lax.fori_loop(0, NY, split_row, 0, unroll=8)
        pair_ref[l * (NY + 1) + NY] = pair_ref[l * (NY + 1)]

    out_ref[...] = jnp.zeros_like(out_ref)
    listing.wait()
    total = listed_ref[7, 0]
    count = listed_ref[8, 0]

    def visit(group, carry):
        found = []
        for u in range(TAKEN):
            v = group * TAKEN + u
            block = listed_ref[4, v]
            base = listed_ref[5, v]
            hot = one_hot(cells_ref, block, listed_ref[6, v], WIDE)
            rows = []
            for a in range(2):
                three = [pair_ref[base + a * (NY + 1) + k] for k in range(3)]
                rows += [jnp.concatenate(three[b : b + 2], axis=1) for b in range(2)]
            both = jnp.dot(jnp.concatenate(rows, axis=0), hot, preferred_element_type=f32)
            corners = []
            for k in range(4):
                four = both[2 * TABLE * k : 2 * TABLE * (k + 1)]
                corners += [four[0:8] + four[16:24], four[8:16] + four[24:32]]
            frac = frac_ref[:, pl.ds(pl.multiple_of(block * BLOCK, BLOCK), BLOCK)]
            for d in (2, 1, 0):
                share = frac[d : d + 1, :]
                corners = [
                    corners[k] + share * (corners[k + 1] - corners[k])
                    for k in range(0, len(corners), 2)
                ]
            found.append((block, corners[0]))
        for block, part in found:
            out_ref[pl.ds(block, 1)] += part[None]
        return carry

    lax.fori_loop(0, (total + TAKEN - 1) // TAKEN, visit, 0)

    lane = lax.broadcasted_iota(jnp.int32, (1, BLOCK), 1)

    def finish(block, top):
        at = pl.multiple_of(block * BLOCK, BLOCK)
        alive = at + lane < count
        got = out_ref[pl.ds(block, 1)][0]
        fresh = jnp.where(alive, flip_share * vel_ref[:, pl.ds(at, BLOCK)] + got[0:3], 0.0)
        out_ref[pl.ds(block, 1), 0:3] = fresh[None]
        square = fresh[0:1] * fresh[0:1] + fresh[1:2] * fresh[1:2] + fresh[2:3] * fresh[2:3]
        return jnp.maximum(top, square)

    top = lax.fori_loop(0, blocks, finish, jnp.zeros((1, BLOCK), f32), unroll=4)
    top = jnp.sqrt(jnp.max(top, axis=1, keepdims=True))
    top_ref[...] = jnp.broadcast_to(top, top_ref.shape)


def finish_kernel(plan_ref, moved_ref, frac_ref, new_frac_ref, new_vel_ref):
    blocks = frac_ref.shape[1] // BLOCK
    count = plan_ref[8:9, :]
    count = jnp.concatenate([count, count], axis=1)
    lane = lax.broadcasted_iota(jnp.int32, (1, BLOCK), 1)

    def finish(block, carry):
        at = pl.multiple_of(block * BLOCK, BLOCK)
        got = moved_ref[pl.ds(block, 1)][0]
        new_vel_ref[:, pl.ds(at, BLOCK)] = got[0:3]
        placed = jnp.where(at + lane < count, frac_ref[:, pl.ds(at, BLOCK)] + got[4:7], 0.0)
        new_frac_ref[:, pl.ds(at, BLOCK)] = placed
        return carry

    lax.fori_loop(0, blocks, finish, 0, unroll=4)


def largest(value, axis):
    devices = lax.axis_size(axis)
    reach = 1
    while reach < devices:
        if devices & (devices - 1) == 0:
            pairs = [(i, i ^ (reach | 1)) for i in range(devices)]
        else:
            pairs = [(i, (i + reach) % devices) for i in range(devices)]
        value = jnp.maximum(value, lax.ppermute(value, axis, pairs))
        reach *= 2
    return value


smem = pl.BlockSpec(memory_space=pltpu.SMEM)
vmem = pl.BlockSpec(memory_space=pltpu.VMEM)
hbm = pl.BlockSpec(memory_space=pltpu.HBM)


def body(frac, velocity, mass, particle_cell, tile_count, time_step):
    slots = frac.shape[1]
    blocks = slots // BLOCK
    rows = slots // LANES
    inputs = (frac, velocity, mass.reshape(rows, LANES), particle_cell.reshape(rows, LANES))
    far, near, layers, plan, frac_here, vel_here, cells_here = pl.pallas_call(
        spread_kernel,
        out_shape=(
            pltpu.VMEM((4 * CX, NY, NZ), f32),
            pltpu.VMEM((4 * CX, NY, NZ), f32),
            pltpu.VMEM((4 * (CX + 1), NY, NZ), f32),
            pltpu.VMEM((16, LANES), jnp.int32),
            pltpu.VMEM(frac.shape, f32),
            pltpu.VMEM(velocity.shape, f32),
            pltpu.VMEM((rows, LANES), jnp.int32),
        ),
        in_specs=[smem] + [hbm] * 4,
        out_specs=(vmem,) * 7,
        scratch_shapes=[
            pltpu.SMEM((16, LANES), jnp.int32),
            pltpu.VMEM((rows, LANES), f32),
            pltpu.VMEM(((CX + 1) * (NY + 1) * 8, NZ), f32),
            pltpu.SemaphoreType.DMA((5,)),
        ],
        compiler_params=pltpu.CompilerParams(vmem_limit_bytes=32 * 1024 * 1024),
        name="spread",
    )(tile_count, *[pltpu.with_memory_space_constraint(x, pltpu.HBM) for x in inputs])
    devices = lax.axis_size("gx")
    far_pairs = [(i, (i + (1 if i % 2 else -1)) % devices) for i in range(devices)]
    near_pairs = [(i, i ^ 1) for i in range(devices)]
    far_new = lax.ppermute(far, "gx", far_pairs)
    near_new = lax.ppermute(near, "gx", near_pairs)
    moved, top = pl.pallas_call(
        collect_kernel,
        out_shape=(
            jax.ShapeDtypeStruct((blocks, 8, BLOCK), f32),
            jax.ShapeDtypeStruct((8, LANES), f32),
        ),
        in_specs=[smem] + [vmem] * 7,
        out_specs=(vmem, vmem),
        scratch_shapes=[
            pltpu.SMEM((16, LANES), jnp.int32),
            pltpu.VMEM(((CX + 1) * NY * TABLE, NZ), f32),
            pltpu.VMEM(((CX + 1) * (NY + 1), 2 * TABLE, NZ), bf16),
            pltpu.SemaphoreType.DMA,
        ],
        compiler_params=pltpu.CompilerParams(vmem_limit_bytes=32 * 1024 * 1024),
        name="collect",
    )(time_step, plan, layers, far_new, near_new, frac_here, vel_here, cells_here)
    new_frac, new_velocity = pl.pallas_call(
        finish_kernel,
        out_shape=(
            jax.ShapeDtypeStruct(frac.shape, f32),
            jax.ShapeDtypeStruct(velocity.shape, f32),
        ),
        in_specs=[vmem] * 3,
        out_specs=(vmem, vmem),
        compiler_params=pltpu.CompilerParams(vmem_limit_bytes=32 * 1024 * 1024),
        cost_estimate=pl.CostEstimate(flops=0, bytes_accessed=8000000, transcendentals=0),
        name="finish",
    )(plan, moved, frac_here)
    fastest = largest(top, "gx")
    next_step = (courant / (fastest + wave_speed))[0, :1]
    return (new_frac, new_velocity, next_step)


def solution(mesh):
    placed = (
        P(None, ("runs", "gx")),
        P(None, ("runs", "gx")),
        P(("runs", "gx")),
        P(("runs", "gx")),
        P(("runs", "gx")),
        P("runs"),
    )
    return jax.shard_map(
        body,
        mesh=mesh,
        in_specs=placed,
        out_specs=(P(None, ("runs", "gx")), P(None, ("runs", "gx")), P("runs")),
        check_vma=False,
    )
```

```python
import functools

import jax
import jax.numpy as jnp
from jax import lax
from jax.experimental import pallas as pl
from jax.experimental.pallas import tpu as pltpu
from jax.sharding import PartitionSpec as P

CX = 2
NY = 32
NZ = 128
ROWS = CX * NY
PAIRS = ROWS // 2
WIDE = 2 * NZ
BLOCK = 256
LANES = 128
GIVEN = 32
TAKEN = 32
SPREAD = 32
TABLE = 16

mass_floor = 0.25
stiffness = 2.0
press_floor = 1.0
grain_size = 0.5
inertia_ref = 0.3
mu_static = 0.38
mu_limit = 0.64
rate_floor = 0.5
gravity = (0.5, 0.0, -0.866)
flip_share = 0.95
courant = 0.4
wave_speed = 2.0
components = ((0, 3, 4), (3, 1, 5), (4, 5, 2))
f32 = jnp.float32
bf16 = jnp.bfloat16


def split_pair(values):
    high = values.astype(bf16)
    low = (values - high.astype(f32)).astype(bf16)
    return high, low


def relative(cells_ref, block, offset):
    return cells_ref[pl.ds(block * 2, 2), :] - offset


def one_hot(rel, wide):
    tall = (16, LANES)
    nodes = lax.broadcasted_iota(jnp.int32, tall, 0).astype(f32)
    one, zero = jnp.ones(tall, bf16), jnp.zeros(tall, bf16)
    halves = []
    for h in range(2):
        line = jnp.broadcast_to(rel[h : h + 1, :].astype(f32), tall).astype(bf16)
        parts = [
            jnp.where(line == (nodes + z).astype(bf16), one, zero) for z in range(0, wide, 16)
        ]
        halves.append(jnp.concatenate(parts, axis=0))
    return jnp.concatenate(halves, axis=1)


def list_visits(cells_ref, count, plan_ref, start_ref):
    blocks = cells_ref.shape[0] // 2
    shape = (blocks, LANES)
    number = lax.broadcasted_iota(jnp.int32, shape, 0)
    lane = lax.broadcasted_iota(jnp.int32, shape, 1)
    first_half = cells_ref[pl.ds(0, blocks, stride=2), :]
    second_half = cells_ref[pl.ds(1, blocks, stride=2), :]
    slot = number * BLOCK + lane
    reached = jnp.maximum(
        jnp.where(slot < count, first_half, 0), jnp.where(slot + LANES < count, second_half, 0)
    )
    live = number * BLOCK < count
    first = jnp.min(first_half, axis=1, keepdims=True)
    last = jnp.max(reached, axis=1, keepdims=True)
    first_row, last_row = first >> 7, last >> 7
    start_ref[...] = jnp.broadcast_to(first_row * NZ, shape)
    row = jnp.max(jnp.where(number == lane, first_row, 0), axis=0, keepdims=True)
    plan_ref[0:1, :] = row + (row >> 5)
    within = live & (first_row < lane) & (lane <= last_row)
    block = jnp.max(jnp.where(within, number, -1), axis=0, keepdims=True)
    plan_ref[1:2, :] = jnp.maximum(block, 0)
    plan_ref[2:3, :] = jnp.where(block >= 0, lane[:1], ROWS) * NZ
    low = jnp.where(live, (first >> 8) + number, 2 * LANES)
    high = jnp.where(live, (last >> 8) + number, -1)
    inside = (low <= lane) & (lane <= high)
    block = jnp.max(jnp.where(inside, number, -1), axis=0, keepdims=True)
    valid = block >= 0
    pair = lane[:1] - block
    plan_ref[3:4, :] = jnp.where(valid, block, 0)
    plan_ref[4:5, :] = jnp.where(valid, 2 * pair + (pair >> 4), 0)
    plan_ref[5:6, :] = jnp.where(valid, pair, PAIRS) * WIDE
    plan_ref[6:7, :] = jnp.max(high, axis=0, keepdims=True) + 1
    plan_ref[7:8, :] = jnp.broadcast_to(count, (1, LANES))


def spread_kernel(
    count_ref, frac_hbm, vel_hbm, mass_hbm, cells_hbm,
    far_ref, near_ref, layers_ref, plan_ref, frac_ref, vel_ref, cells_ref,
    listed_ref, start_ref, mass_ref, acc_ref, sems,
):
    slots = frac_ref.shape[1]
    sources = (cells_hbm, frac_hbm, vel_hbm, mass_hbm)
    targets = (cells_ref, frac_ref, vel_ref, mass_ref)
    arrivals = [
        pltpu.make_async_copy(source, target, sems.at[k])
        for k, (source, target) in enumerate(zip(sources, targets))
    ]
    for arrival in arrivals:
        arrival.start()
    acc_ref[...] = jnp.zeros_like(acc_ref)
    arrivals[0].wait()
    count = count_ref[0]
    list_visits(cells_ref, count, plan_ref, start_ref)
    listing = pltpu.make_async_copy(plan_ref, listed_ref, sems.at[4])
    listing.start()
    for arrival in arrivals[1:]:
        arrival.wait()
    sublane = lax.broadcasted_iota(jnp.int32, (8, LANES), 0)
    lane = lax.broadcasted_iota(jnp.int32, (1, LANES), 1)
    top_z = sublane >= 4
    field = sublane & 3

    def weigh(part):
        at = pl.multiple_of(part * LANES, LANES)
        here = pl.ds(at, LANES)

        def spread_out(line):
            return jnp.broadcast_to(line, (8, LANES))

        fx, fy, fz = (spread_out(frac_ref[d : d + 1, here]) for d in range(3))
        vx, vy, vz = (spread_out(vel_ref[d : d + 1, here]) for d in range(3))
        held = spread_out(jnp.where(at + lane < count, mass_ref[pl.ds(part, 1), :], 0.0))
        carried = jnp.where(
            field == 0, held, held * jnp.where(field == 1, vx, jnp.where(field == 2, vy, vz))
        )
        carried = carried * jnp.where(top_z, fz, 1.0 - fz)
        lower, upper = carried * (1.0 - fx), carried * fx
        rows = jnp.concatenate(
            [lower * (1.0 - fy), lower * fy, upper * (1.0 - fy), upper * fy], axis=0
        )
        return jnp.concatenate(split_pair(rows), axis=0)

    def spread_one(block, offset):
        both = lax.dot_general(
            jnp.concatenate([weigh(2 * block), weigh(2 * block + 1)], axis=1),
            one_hot(relative(cells_ref, block, offset), NZ),
            (((1,), (1,)), ((), ())),
            preferred_element_type=f32,
        )
        return both[:SPREAD] + both[SPREAD:]

    def add_to_nodes(base, part):
        here = pl.ds(pl.multiple_of(base * 8, 8), 16)
        above = pl.ds(pl.multiple_of(base * 8, 8) + (NY + 1) * 8, 16)
        lower, upper = acc_ref[here, :], acc_ref[above, :]
        acc_ref[here, :] = lower + part[:16]
        acc_ref[above, :] = upper + part[16:]

    def first_rows(group, wait):
        blocks = [group * GIVEN + u for u in range(GIVEN)]
        found = [spread_one(block, start_ref[pl.ds(block, 1), :]) for block in blocks]
        if wait:
            listing.wait()
        for block, part in zip(blocks, found):
            add_to_nodes(listed_ref[0, block], part)

    def more_first_rows(group, carry):
        first_rows(group, False)
        return carry

    def later_rows(group, carry):
        rows = [group * GIVEN + u for u in range(GIVEN)]
        found = [spread_one(listed_ref[1, row], listed_ref[2, row]) for row in rows]
        for row, part in zip(rows, found):
            add_to_nodes(row + (row >> 5), part)
        return carry

    first_rows(0, True)
    live_blocks = (count + BLOCK - 1) >> 8
    lax.fori_loop(1, (live_blocks + GIVEN - 1) // GIVEN, more_first_rows, 0)
    lax.fori_loop(0, ROWS // GIVEN, later_rows, 0)

    odd = lax.axis_index("gx") % 2 == 1
    layers = []
    for l in range(CX + 1):
        first = l * (NY + 1) * 8
        acc_ref[first : first + 8, :] += acc_ref[first + NY * 8 : first + NY * 8 + 8, :]
        for f in range(4):
            lower = acc_ref[pl.ds(first + f, NY, stride=8), :]
            upper = acc_ref[pl.ds(first + 4 + f, NY, stride=8), :]
            layers.append(lower + pltpu.roll(upper, 1, 1))
            layers_ref[l * 4 + f] = layers[-1]
    for k in range(CX * 4):
        far_ref[k] = jnp.where(odd, layers[k + 4], layers[k])
        near_ref[k] = jnp.where(odd, layers[k], layers[k + 4])


def pair_up(field, axis):
    return field + pltpu.roll(field, field.shape[axis] - 1, axis)


def step_up(field, axis):
    return pltpu.roll(field, field.shape[axis] - 1, axis) - field


def pair_down(field, axis):
    return field + pltpu.roll(field, 1, axis)


def step_down(field, axis):
    return field - pltpu.roll(field, 1, axis)


def cell_stress(vel_lo, vel_hi, mass_lo, mass_hi, keep):
    grads = []
    for a in range(3):
        diff = vel_hi[a] - vel_lo[a]
        both = vel_hi[a] + vel_lo[a]
        grads.append(
            [
                0.25 * pair_up(pair_up(diff, 0), 1),
                0.25 * pair_up(step_up(both, 0), 1),
                0.25 * step_up(pair_up(both, 0), 1),
            ]
        )
    density = 0.125 * pair_up(pair_up(mass_hi + mass_lo, 0), 1)
    dxx = grads[0][0]
    dyy = grads[1][1]
    dzz = grads[2][2]
    dxy = 0.5 * (grads[0][1] + grads[1][0])
    dxz = 0.5 * (grads[0][2] + grads[2][0])
    dyz = 0.5 * (grads[1][2] + grads[2][1])
    second = dxx * dxx + dyy * dyy + dzz * dzz + 2.0 * (dxy * dxy + dxz * dxz + dyz * dyz)
    rate = jnp.sqrt(2.0 * second + rate_floor * rate_floor)
    pressure = stiffness * density
    inertial = rate * grain_size / jnp.sqrt(pressure + press_floor)
    friction = mu_static + (mu_limit - mu_static) * inertial / (inertia_ref + inertial)
    twice = 2.0 * friction * pressure / rate
    sigma = [
        twice * dxx - pressure,
        twice * dyy - pressure,
        twice * dzz - pressure,
        twice * dxy,
        twice * dxz,
        twice * dyz,
    ]
    return [jnp.where(keep, s, 0.0) for s in sigma]


def node_force(lower, upper):
    force = []
    for a in range(3):
        sx, sy, sz = (components[a][b] for b in range(3))
        along = pair_down(pair_down(upper[sx] - lower[sx], 0), 1)
        across = step_down(pair_down(upper[sy] + lower[sy], 1), 0)
        upward = step_down(pair_down(upper[sz] + lower[sz], 0), 1)
        force.append(0.25 * (along + across + upward))
    return force


def collect_kernel(
    step_ref, plan_ref, layers_ref, far_new_ref, near_new_ref, frac_ref, vel_ref, cells_ref,
    out_ref, top_ref, listed_ref, tab_ref, pair_ref, sem,
):
    blocks = frac_ref.shape[1] // BLOCK
    listing = pltpu.make_async_copy(plan_ref, listed_ref, sem)
    listing.start()
    step = step_ref[0]
    odd = lax.axis_index("gx") % 2 == 1

    def pick(if_odd, if_even):
        return [jnp.where(odd, if_odd[k], if_even[k]) for k in range(4 * CX)]

    own = [layers_ref[k] for k in range(4 * (CX + 1))]
    left, right = pick(near_new_ref, far_new_ref), pick(far_new_ref, near_new_ref)
    nodes = [
        left[:4],
        [own[f] + left[4 + f] for f in range(4)],
        own[4:8],
        [own[8 + f] + right[f] for f in range(4)],
        right[4:],
    ]
    height = lax.broadcasted_iota(jnp.int32, (NY, NZ), 1)
    keep = height < NZ - 1
    above_bed = height > 0
    floor = [jnp.maximum(layer[0], mass_floor) for layer in nodes]
    v_old = [[layer[1 + a] / floor[l] for a in range(3)] for l, layer in enumerate(nodes)]
    sigma = [
        cell_stress(v_old[l], v_old[l + 1], nodes[l][0], nodes[l + 1][0], keep) for l in range(4)
    ]
    blank = jnp.zeros((NY, NZ), f32)
    for l in range(CX + 1):
        force = node_force(sigma[l], sigma[l + 1])
        fields = [blank] * 8
        for a in range(3):
            layer = nodes[l + 1]
            fresh = (layer[1 + a] + step * (force[a] + layer[0] * gravity[a])) / floor[l + 1]
            fresh = jnp.where(above_bed, fresh, 0.0)
            fields[a] = fresh - flip_share * v_old[l + 1][a]
            fields[4 + a] = step * fresh
        for k, value in enumerate(fields):
            start = l * NY * TABLE + k
            tab_ref[pl.ds(start, NY, stride=TABLE), :] = value
            tab_ref[pl.ds(start + 8, NY, stride=TABLE), :] = pltpu.roll(value, NZ - 1, 1)

    for l in range(CX + 1):

        def split_row(j, carry):
            at = pl.ds(pl.multiple_of((l * NY + j) * TABLE, TABLE), TABLE)
            high, low = split_pair(tab_ref[at, :])
            pair_ref[pl.ds(l * (NY + 1) + j, 1)] = jnp.concatenate([high, low], axis=0)[None]
            return carry

        lax.fori_loop(0, NY, split_row, 0, unroll=8)
        pair_ref[l * (NY + 1) + NY] = pair_ref[l * (NY + 1)]

    out_ref[...] = jnp.zeros_like(out_ref)
    listing.wait()
    total = listed_ref[6, 0]
    count = listed_ref[7, 0]
    lane = lax.broadcasted_iota(jnp.int32, (2, LANES), 1)
    half = lax.broadcasted_iota(jnp.int32, (2, LANES), 0)

    def visit(group, top):
        found = []
        for u in range(TAKEN):
            v = group * TAKEN + u
            block = listed_ref[3, v]
            base = listed_ref[4, v]
            rel = relative(cells_ref, block, listed_ref[5, v])
            hot = one_hot(rel, WIDE)
            rows = []
            for a in range(2):
                three = [pair_ref[base + a * (NY + 1) + k] for k in range(3)]
                rows += [jnp.concatenate(three[b : b + 2], axis=1) for b in range(2)]
            both = jnp.dot(jnp.concatenate(rows, axis=0), hot, preferred_element_type=f32)
            corners = []
            for k in range(4):
                four = both[2 * TABLE * k : 2 * TABLE * (k + 1)]
                corners += [four[0:8] + four[16:24], four[8:16] + four[24:32]]
            here = pl.ds(pl.multiple_of(block * BLOCK, BLOCK), BLOCK)
            frac = frac_ref[:, here]
            for d in (2, 1, 0):
                share = frac[d : d + 1, :]
                corners = [
                    corners[k] + share * (corners[k + 1] - corners[k])
                    for k in range(0, len(corners), 2)
                ]
            fresh = flip_share * vel_ref[:, here] + corners[0][0:3]
            square = jnp.sum(fresh * fresh, axis=0, keepdims=True)
            slot = block * BLOCK + half * LANES + lane
            taken = (rel >= 0) & (rel < WIDE) & (slot < count)
            for h in range(2):
                part = square[:, h * LANES : (h + 1) * LANES]
                top = jnp.maximum(top, jnp.where(taken[h : h + 1], part, 0.0))
            found.append((block, corners[0]))
        for block, part in found:
            out_ref[pl.ds(block, 1)] += part[None]
        return top

    top = jnp.zeros((1, LANES), f32)
    top = lax.fori_loop(0, (total + TAKEN - 1) // TAKEN, visit, top)
    top = jnp.sqrt(jnp.max(top, axis=1, keepdims=True))
    top_ref[...] = jnp.broadcast_to(top, top_ref.shape)


def finish_kernel(plan_ref, moved_ref, frac_ref, vel_ref, new_frac_ref, new_vel_ref):
    blocks = frac_ref.shape[1] // BLOCK
    count = plan_ref[7:8, :]
    count = jnp.concatenate([count, count], axis=1)
    lane = lax.broadcasted_iota(jnp.int32, (1, BLOCK), 1)

    def finish(block, carry):
        at = pl.multiple_of(block * BLOCK, BLOCK)
        here = pl.ds(at, BLOCK)
        alive = at + lane < count
        got = moved_ref[pl.ds(block, 1)][0]
        new_vel_ref[:, here] = jnp.where(alive, flip_share * vel_ref[:, here] + got[0:3], 0.0)
        new_frac_ref[:, here] = jnp.where(alive, frac_ref[:, here] + got[4:7], 0.0)
        return carry

    lax.fori_loop(0, blocks, finish, 0, unroll=4)


def largest(value, axis):
    devices = lax.axis_size(axis)
    reach = 1
    while reach < devices:
        if devices & (devices - 1) == 0:
            pairs = [(i, i ^ (reach | 1)) for i in range(devices)]
        else:
            pairs = [(i, (i + reach) % devices) for i in range(devices)]
        value = jnp.maximum(value, lax.ppermute(value, axis, pairs))
        reach *= 2
    return value


smem = pl.BlockSpec(memory_space=pltpu.SMEM)
vmem = pl.BlockSpec(memory_space=pltpu.VMEM)
hbm = pl.BlockSpec(memory_space=pltpu.HBM)


def body(frac, velocity, mass, particle_cell, tile_count, time_step):
    slots = frac.shape[1]
    blocks = slots // BLOCK
    rows = slots // LANES
    inputs = (frac, velocity, mass.reshape(rows, LANES), particle_cell.reshape(rows, LANES))
    far, near, layers, plan, frac_here, vel_here, cells_here = pl.pallas_call(
        spread_kernel,
        out_shape=(
            pltpu.VMEM((4 * CX, NY, NZ), f32),
            pltpu.VMEM((4 * CX, NY, NZ), f32),
            pltpu.VMEM((4 * (CX + 1), NY, NZ), f32),
            pltpu.VMEM((8, LANES), jnp.int32),
            pltpu.VMEM(frac.shape, f32),
            pltpu.VMEM(velocity.shape, f32),
            pltpu.VMEM((rows, LANES), jnp.int32),
        ),
        in_specs=[smem] + [hbm] * 4,
        out_specs=(vmem,) * 7,
        scratch_shapes=[
            pltpu.SMEM((8, LANES), jnp.int32),
            pltpu.VMEM((blocks, LANES), jnp.int32),
            pltpu.VMEM((rows, LANES), f32),
            pltpu.VMEM(((CX + 1) * (NY + 1) * 8, NZ), f32),
            pltpu.SemaphoreType.DMA((5,)),
        ],
        compiler_params=pltpu.CompilerParams(vmem_limit_bytes=32 * 1024 * 1024),
        name="spread",
    )(tile_count, *[pltpu.with_memory_space_constraint(x, pltpu.HBM) for x in inputs])
    devices = lax.axis_size("gx")
    far_pairs = [(i, (i + (1 if i % 2 else -1)) % devices) for i in range(devices)]
    near_pairs = [(i, i ^ 1) for i in range(devices)]
    far_new = lax.ppermute(far, "gx", far_pairs)
    near_new = lax.ppermute(near, "gx", near_pairs)
    moved, top = pl.pallas_call(
        collect_kernel,
        out_shape=(
            jax.ShapeDtypeStruct((blocks, 8, BLOCK), f32),
            jax.ShapeDtypeStruct((8, LANES), f32),
        ),
        in_specs=[smem] + [vmem] * 7,
        out_specs=(vmem, vmem),
        scratch_shapes=[
            pltpu.SMEM((8, LANES), jnp.int32),
            pltpu.VMEM(((CX + 1) * NY * TABLE, NZ), f32),
            pltpu.VMEM(((CX + 1) * (NY + 1), 2 * TABLE, NZ), bf16),
            pltpu.SemaphoreType.DMA,
        ],
        compiler_params=pltpu.CompilerParams(vmem_limit_bytes=32 * 1024 * 1024),
        name="collect",
    )(time_step, plan, layers, far_new, near_new, frac_here, vel_here, cells_here)
    new_frac, new_velocity = pl.pallas_call(
        finish_kernel,
        out_shape=(
            jax.ShapeDtypeStruct(frac.shape, f32),
            jax.ShapeDtypeStruct(velocity.shape, f32),
        ),
        in_specs=[vmem] * 4,
        out_specs=(vmem, vmem),
        compiler_params=pltpu.CompilerParams(vmem_limit_bytes=32 * 1024 * 1024),
        cost_estimate=pl.CostEstimate(flops=0, bytes_accessed=8000000, transcendentals=0),
        name="finish",
    )(plan, moved, frac_here, vel_here)
    fastest = largest(top, "gx")
    next_step = (courant / (fastest + wave_speed))[0, :1]
    return (new_frac, new_velocity, next_step)


def solution(mesh):
    placed = (
        P(None, ("runs", "gx")),
        P(None, ("runs", "gx")),
        P(("runs", "gx")),
        P(("runs", "gx")),
        P(("runs", "gx")),
        P("runs"),
    )
    return jax.shard_map(
        body,
        mesh=mesh,
        in_specs=placed,
        out_specs=(P(None, ("runs", "gx")), P(None, ("runs", "gx")), P("runs")),
        check_vma=False,
    )
```

```python
import functools

import jax
import jax.numpy as jnp
from jax import lax
from jax.experimental import pallas as pl
from jax.experimental.pallas import tpu as pltpu
from jax.sharding import PartitionSpec as P

CX = 2
NY = 32
NZ = 128
ROWS = CX * NY
PAIRS = ROWS // 2
WIDE = 2 * NZ
BLOCK = 256
LANES = 128
GIVEN = 32
TAKEN = 32
SPREAD = 32
TABLE = 16

mass_floor = 0.25
stiffness = 2.0
press_floor = 1.0
grain_size = 0.5
inertia_ref = 0.3
mu_static = 0.38
mu_limit = 0.64
rate_floor = 0.5
gravity = (0.5, 0.0, -0.866)
flip_share = 0.95
courant = 0.4
wave_speed = 2.0
components = ((0, 3, 4), (3, 1, 5), (4, 5, 2))
f32 = jnp.float32
bf16 = jnp.bfloat16


def split_pair(values):
    high = values.astype(bf16)
    low = (values - high.astype(f32)).astype(bf16)
    return high, low


def relative(cells_ref, block, offset):
    return cells_ref[pl.ds(block * 2, 2), :] - offset


def one_hot(rel, wide):
    tall = (16, LANES)
    nodes = lax.broadcasted_iota(jnp.int32, tall, 0).astype(f32)
    one, zero = jnp.ones(tall, bf16), jnp.zeros(tall, bf16)
    halves = []
    for h in range(2):
        line = jnp.broadcast_to(rel[h : h + 1, :].astype(f32), tall).astype(bf16)
        parts = [
            jnp.where(line == (nodes + z).astype(bf16), one, zero) for z in range(0, wide, 16)
        ]
        halves.append(jnp.concatenate(parts, axis=0))
    return jnp.concatenate(halves, axis=1)


def list_visits(cells_ref, count, plan_ref, start_ref):
    blocks = cells_ref.shape[0] // 2
    shape = (blocks, LANES)
    number = lax.broadcasted_iota(jnp.int32, shape, 0)
    lane = lax.broadcasted_iota(jnp.int32, shape, 1)
    first_half = cells_ref[pl.ds(0, blocks, stride=2), :]
    second_half = cells_ref[pl.ds(1, blocks, stride=2), :]
    slot = number * BLOCK + lane
    reached = jnp.maximum(
        jnp.where(slot < count, first_half, 0), jnp.where(slot + LANES < count, second_half, 0)
    )
    live = number * BLOCK < count
    first = jnp.min(first_half, axis=1, keepdims=True)
    last = jnp.max(reached, axis=1, keepdims=True)
    first_row, last_row = first >> 7, last >> 7
    start_ref[...] = jnp.broadcast_to(first_row * NZ, shape)
    row = jnp.max(jnp.where(number == lane, first_row, 0), axis=0, keepdims=True)
    plan_ref[0:1, :] = row + (row >> 5)
    within = live & (first_row < lane) & (lane <= last_row)
    block = jnp.max(jnp.where(within, number, -1), axis=0, keepdims=True)
    plan_ref[1:2, :] = jnp.maximum(block, 0)
    plan_ref[2:3, :] = jnp.where(block >= 0, lane[:1], ROWS) * NZ
    low = jnp.where(live, (first >> 8) + number, 2 * LANES)
    high = jnp.where(live, (last >> 8) + number, -1)
    inside = (low <= lane) & (lane <= high)
    block = jnp.max(jnp.where(inside, number, -1), axis=0, keepdims=True)
    valid = block >= 0
    pair = lane[:1] - block
    plan_ref[3:4, :] = jnp.where(valid, block, 0)
    plan_ref[4:5, :] = jnp.where(valid, 2 * pair + (pair >> 4), 0)
    plan_ref[5:6, :] = jnp.where(valid, pair, PAIRS) * WIDE
    plan_ref[6:7, :] = jnp.max(high, axis=0, keepdims=True) + 1
    plan_ref[7:8, :] = jnp.broadcast_to(count, (1, LANES))


def spread_kernel(
    count_ref, frac_hbm, vel_hbm, mass_hbm, cells_hbm,
    far_ref, near_ref, layers_ref, plan_ref, frac_ref, vel_ref, cells_ref,
    listed_ref, start_ref, tall_ref, mass_ref, acc_ref, sems,
):
    slots = frac_ref.shape[1]
    sources = (cells_hbm, frac_hbm, vel_hbm, mass_hbm)
    targets = (cells_ref, frac_ref, vel_ref, mass_ref)
    arrivals = [
        pltpu.make_async_copy(source, target, sems.at[k])
        for k, (source, target) in enumerate(zip(sources, targets))
    ]
    for arrival in arrivals:
        arrival.start()
    acc_ref[...] = jnp.zeros_like(acc_ref)
    arrivals[0].wait()
    count = count_ref[0]
    list_visits(cells_ref, count, plan_ref, start_ref)
    listing = pltpu.make_async_copy(plan_ref, listed_ref, sems.at[4])
    listing.start()
    tall_ref[...] = cells_ref[...].astype(f32).T
    for arrival in arrivals[1:]:
        arrival.wait()
    sublane = lax.broadcasted_iota(jnp.int32, (8, LANES), 0)
    lane = lax.broadcasted_iota(jnp.int32, (1, LANES), 1)
    top_z = sublane >= 4
    field = sublane & 3

    def weigh(part):
        at = pl.multiple_of(part * LANES, LANES)
        here = pl.ds(at, LANES)

        def spread_out(line):
            return jnp.broadcast_to(line, (8, LANES))

        fx, fy, fz = (spread_out(frac_ref[d : d + 1, here]) for d in range(3))
        vx, vy, vz = (spread_out(vel_ref[d : d + 1, here]) for d in range(3))
        held = spread_out(jnp.where(at + lane < count, mass_ref[pl.ds(part, 1), :], 0.0))
        carried = jnp.where(
            field == 0, held, held * jnp.where(field == 1, vx, jnp.where(field == 2, vy, vz))
        )
        carried = carried * jnp.where(top_z, fz, 1.0 - fz)
        lower, upper = carried * (1.0 - fx), carried * fx
        rows = jnp.concatenate(
            [lower * (1.0 - fy), lower * fy, upper * (1.0 - fy), upper * fy], axis=0
        )
        return jnp.concatenate(split_pair(rows), axis=0)

    def spread_one(block, offset):
        wanted = (lane + offset).astype(f32)
        halves = []
        for h in range(2):
            column = jnp.full((LANES, LANES), 2 * block + h, jnp.int32)
            numbers = jnp.take_along_axis(tall_ref[...], column, axis=1)
            halves.append(jnp.where(numbers == wanted, 1.0, 0.0).astype(bf16))
        both = jnp.dot(
            jnp.concatenate([weigh(2 * block), weigh(2 * block + 1)], axis=1),
            jnp.concatenate(halves, axis=0),
            preferred_element_type=f32,
        )
        return both[:SPREAD] + both[SPREAD:]

    def add_to_nodes(base, part):
        here = pl.ds(pl.multiple_of(base * 8, 8), 16)
        above = pl.ds(pl.multiple_of(base * 8, 8) + (NY + 1) * 8, 16)
        lower, upper = acc_ref[here, :], acc_ref[above, :]
        acc_ref[here, :] = lower + part[:16]
        acc_ref[above, :] = upper + part[16:]

    def first_rows(group, wait):
        blocks = [group * GIVEN + u for u in range(GIVEN)]
        found = [spread_one(block, start_ref[pl.ds(block, 1), :]) for block in blocks]
        if wait:
            listing.wait()
        for block, part in zip(blocks, found):
            add_to_nodes(listed_ref[0, block], part)

    def more_first_rows(group, carry):
        first_rows(group, False)
        return carry

    def later_rows(group, carry):
        rows = [group * GIVEN + u for u in range(GIVEN)]
        found = [spread_one(listed_ref[1, row], listed_ref[2, row]) for row in rows]
        for row, part in zip(rows, found):
            add_to_nodes(row + (row >> 5), part)
        return carry

    first_rows(0, True)
    live_blocks = (count + BLOCK - 1) >> 8
    lax.fori_loop(1, (live_blocks + GIVEN - 1) // GIVEN, more_first_rows, 0)
    lax.fori_loop(0, ROWS // GIVEN, later_rows, 0)

    odd = lax.axis_index("gx") % 2 == 1
    layers = []
    for l in range(CX + 1):
        first = l * (NY + 1) * 8
        acc_ref[first : first + 8, :] += acc_ref[first + NY * 8 : first + NY * 8 + 8, :]
        for f in range(4):
            lower = acc_ref[pl.ds(first + f, NY, stride=8), :]
            upper = acc_ref[pl.ds(first + 4 + f, NY, stride=8), :]
            layers.append(lower + pltpu.roll(upper, 1, 1))
            layers_ref[l * 4 + f] = layers[-1]
    for k in range(CX * 4):
        far_ref[k] = jnp.where(odd, layers[k + 4], layers[k])
        near_ref[k] = jnp.where(odd, layers[k], layers[k + 4])


def pair_up(field, axis):
    return field + pltpu.roll(field, field.shape[axis] - 1, axis)


def step_up(field, axis):
    return pltpu.roll(field, field.shape[axis] - 1, axis) - field


def pair_down(field, axis):
    return field + pltpu.roll(field, 1, axis)


def step_down(field, axis):
    return field - pltpu.roll(field, 1, axis)


def cell_stress(vel_lo, vel_hi, mass_lo, mass_hi, keep):
    grads = []
    for a in range(3):
        diff = vel_hi[a] - vel_lo[a]
        both = vel_hi[a] + vel_lo[a]
        grads.append(
            [
                0.25 * pair_up(pair_up(diff, 0), 1),
                0.25 * pair_up(step_up(both, 0), 1),
                0.25 * step_up(pair_up(both, 0), 1),
            ]
        )
    density = 0.125 * pair_up(pair_up(mass_hi + mass_lo, 0), 1)
    dxx = grads[0][0]
    dyy = grads[1][1]
    dzz = grads[2][2]
    dxy = 0.5 * (grads[0][1] + grads[1][0])
    dxz = 0.5 * (grads[0][2] + grads[2][0])
    dyz = 0.5 * (grads[1][2] + grads[2][1])
    second = dxx * dxx + dyy * dyy + dzz * dzz + 2.0 * (dxy * dxy + dxz * dxz + dyz * dyz)
    rate = jnp.sqrt(2.0 * second + rate_floor * rate_floor)
    pressure = stiffness * density
    inertial = rate * grain_size / jnp.sqrt(pressure + press_floor)
    friction = mu_static + (mu_limit - mu_static) * inertial / (inertia_ref + inertial)
    twice = 2.0 * friction * pressure / rate
    sigma = [
        twice * dxx - pressure,
        twice * dyy - pressure,
        twice * dzz - pressure,
        twice * dxy,
        twice * dxz,
        twice * dyz,
    ]
    return [jnp.where(keep, s, 0.0) for s in sigma]


def node_force(lower, upper):
    force = []
    for a in range(3):
        sx, sy, sz = (components[a][b] for b in range(3))
        along = pair_down(pair_down(upper[sx] - lower[sx], 0), 1)
        across = step_down(pair_down(upper[sy] + lower[sy], 1), 0)
        upward = step_down(pair_down(upper[sz] + lower[sz], 0), 1)
        force.append(0.25 * (along + across + upward))
    return force


def collect_kernel(
    step_ref, plan_ref, layers_ref, far_new_ref, near_new_ref, frac_ref, vel_ref, cells_ref,
    out_ref, top_ref, listed_ref, tab_ref, pair_ref, sem,
):
    blocks = frac_ref.shape[1] // BLOCK
    listing = pltpu.make_async_copy(plan_ref, listed_ref, sem)
    listing.start()
    step = step_ref[0]
    odd = lax.axis_index("gx") % 2 == 1

    def pick(if_odd, if_even):
        return [jnp.where(odd, if_odd[k], if_even[k]) for k in range(4 * CX)]

    own = [layers_ref[k] for k in range(4 * (CX + 1))]
    left, right = pick(near_new_ref, far_new_ref), pick(far_new_ref, near_new_ref)
    nodes = [
        left[:4],
        [own[f] + left[4 + f] for f in range(4)],
        own[4:8],
        [own[8 + f] + right[f] for f in range(4)],
        right[4:],
    ]
    height = lax.broadcasted_iota(jnp.int32, (NY, NZ), 1)
    keep = height < NZ - 1
    above_bed = height > 0
    floor = [jnp.maximum(layer[0], mass_floor) for layer in nodes]
    v_old = [[layer[1 + a] / floor[l] for a in range(3)] for l, layer in enumerate(nodes)]
    sigma = [
        cell_stress(v_old[l], v_old[l + 1], nodes[l][0], nodes[l + 1][0], keep) for l in range(4)
    ]
    blank = jnp.zeros((NY, NZ), f32)
    for l in range(CX + 1):
        force = node_force(sigma[l], sigma[l + 1])
        fields = [blank] * 8
        for a in range(3):
            layer = nodes[l + 1]
            fresh = (layer[1 + a] + step * (force[a] + layer[0] * gravity[a])) / floor[l + 1]
            fresh = jnp.where(above_bed, fresh, 0.0)
            fields[a] = fresh - flip_share * v_old[l + 1][a]
            fields[4 + a] = step * fresh
        for k, value in enumerate(fields):
            start = l * NY * TABLE + k
            tab_ref[pl.ds(start, NY, stride=TABLE), :] = value
            tab_ref[pl.ds(start + 8, NY, stride=TABLE), :] = pltpu.roll(value, NZ - 1, 1)

    for l in range(CX + 1):

        def split_row(j, carry):
            at = pl.ds(pl.multiple_of((l * NY + j) * TABLE, TABLE), TABLE)
            high, low = split_pair(tab_ref[at, :])
            pair_ref[pl.ds(l * (NY + 1) + j, 1)] = jnp.concatenate([high, low], axis=0)[None]
            return carry

        lax.fori_loop(0, NY, split_row, 0, unroll=8)
        pair_ref[l * (NY + 1) + NY] = pair_ref[l * (NY + 1)]

    out_ref[...] = jnp.zeros_like(out_ref)
    listing.wait()
    total = listed_ref[6, 0]
    count = listed_ref[7, 0]
    lane = lax.broadcasted_iota(jnp.int32, (2, LANES), 1)
    half = lax.broadcasted_iota(jnp.int32, (2, LANES), 0)

    def visit(group, top):
        found = []
        for u in range(TAKEN):
            v = group * TAKEN + u
            block = listed_ref[3, v]
            base = listed_ref[4, v]
            rel = relative(cells_ref, block, listed_ref[5, v])
            hot = one_hot(rel, WIDE)
            rows = []
            for a in range(2):
                three = [pair_ref[base + a * (NY + 1) + k] for k in range(3)]
                rows += [jnp.concatenate(three[b : b + 2], axis=1) for b in range(2)]
            both = jnp.dot(jnp.concatenate(rows, axis=0), hot, preferred_element_type=f32)
            corners = []
            for k in range(4):
                four = both[2 * TABLE * k : 2 * TABLE * (k + 1)]
                corners += [four[0:8] + four[16:24], four[8:16] + four[24:32]]
            here = pl.ds(pl.multiple_of(block * BLOCK, BLOCK), BLOCK)
            frac = frac_ref[:, here]
            for d in (2, 1, 0):
                share = frac[d : d + 1, :]
                corners = [
                    corners[k] + share * (corners[k + 1] - corners[k])
                    for k in range(0, len(corners), 2)
                ]
            fresh = flip_share * vel_ref[:, here] + corners[0][0:3]
            square = jnp.sum(fresh * fresh, axis=0, keepdims=True)
            slot = block * BLOCK + half * LANES + lane
            taken = (rel >= 0) & (rel < WIDE) & (slot < count)
            for h in range(2):
                part = square[:, h * LANES : (h + 1) * LANES]
                top = jnp.maximum(top, jnp.where(taken[h : h + 1], part, 0.0))
            found.append((block, corners[0]))
        for block, part in found:
            out_ref[pl.ds(block, 1)] += part[None]
        return top

    top = jnp.zeros((1, LANES), f32)
    top = lax.fori_loop(0, (total + TAKEN - 1) // TAKEN, visit, top)
    top = jnp.sqrt(jnp.max(top, axis=1, keepdims=True))
    top_ref[...] = jnp.broadcast_to(top, top_ref.shape)


def finish_kernel(plan_ref, moved_ref, frac_ref, vel_ref, new_frac_ref, new_vel_ref):
    blocks = frac_ref.shape[1] // BLOCK
    count = plan_ref[7:8, :]
    count = jnp.concatenate([count, count], axis=1)
    lane = lax.broadcasted_iota(jnp.int32, (1, BLOCK), 1)

    def finish(block, carry):
        at = pl.multiple_of(block * BLOCK, BLOCK)
        here = pl.ds(at, BLOCK)
        alive = at + lane < count
        got = moved_ref[pl.ds(block, 1)][0]
        new_vel_ref[:, here] = jnp.where(alive, flip_share * vel_ref[:, here] + got[0:3], 0.0)
        new_frac_ref[:, here] = jnp.where(alive, frac_ref[:, here] + got[4:7], 0.0)
        return carry

    lax.fori_loop(0, blocks, finish, 0, unroll=4)


def largest(value, axis):
    devices = lax.axis_size(axis)
    reach = 1
    while reach < devices:
        if devices & (devices - 1) == 0:
            pairs = [(i, i ^ (reach | 1)) for i in range(devices)]
        else:
            pairs = [(i, (i + reach) % devices) for i in range(devices)]
        value = jnp.maximum(value, lax.ppermute(value, axis, pairs))
        reach *= 2
    return value


smem = pl.BlockSpec(memory_space=pltpu.SMEM)
vmem = pl.BlockSpec(memory_space=pltpu.VMEM)
hbm = pl.BlockSpec(memory_space=pltpu.HBM)


def body(frac, velocity, mass, particle_cell, tile_count, time_step):
    slots = frac.shape[1]
    blocks = slots // BLOCK
    rows = slots // LANES
    inputs = (frac, velocity, mass.reshape(rows, LANES), particle_cell.reshape(rows, LANES))
    far, near, layers, plan, frac_here, vel_here, cells_here = pl.pallas_call(
        spread_kernel,
        out_shape=(
            pltpu.VMEM((4 * CX, NY, NZ), f32),
            pltpu.VMEM((4 * CX, NY, NZ), f32),
            pltpu.VMEM((4 * (CX + 1), NY, NZ), f32),
            pltpu.VMEM((8, LANES), jnp.int32),
            pltpu.VMEM(frac.shape, f32),
            pltpu.VMEM(velocity.shape, f32),
            pltpu.VMEM((rows, LANES), jnp.int32),
        ),
        in_specs=[smem] + [hbm] * 4,
        out_specs=(vmem,) * 7,
        scratch_shapes=[
            pltpu.SMEM((8, LANES), jnp.int32),
            pltpu.VMEM((blocks, LANES), jnp.int32),
            pltpu.VMEM((LANES, rows), f32),
            pltpu.VMEM((rows, LANES), f32),
            pltpu.VMEM(((CX + 1) * (NY + 1) * 8, NZ), f32),
            pltpu.SemaphoreType.DMA((5,)),
        ],
        compiler_params=pltpu.CompilerParams(vmem_limit_bytes=32 * 1024 * 1024),
        name="spread",
    )(tile_count, *[pltpu.with_memory_space_constraint(x, pltpu.HBM) for x in inputs])
    devices = lax.axis_size("gx")
    far_pairs = [(i, (i + (1 if i % 2 else -1)) % devices) for i in range(devices)]
    near_pairs = [(i, i ^ 1) for i in range(devices)]
    far_new = lax.ppermute(far, "gx", far_pairs)
    near_new = lax.ppermute(near, "gx", near_pairs)
    moved, top = pl.pallas_call(
        collect_kernel,
        out_shape=(
            jax.ShapeDtypeStruct((blocks, 8, BLOCK), f32),
            jax.ShapeDtypeStruct((8, LANES), f32),
        ),
        in_specs=[smem] + [vmem] * 7,
        out_specs=(vmem, vmem),
        scratch_shapes=[
            pltpu.SMEM((8, LANES), jnp.int32),
            pltpu.VMEM(((CX + 1) * NY * TABLE, NZ), f32),
            pltpu.VMEM(((CX + 1) * (NY + 1), 2 * TABLE, NZ), bf16),
            pltpu.SemaphoreType.DMA,
        ],
        compiler_params=pltpu.CompilerParams(vmem_limit_bytes=32 * 1024 * 1024),
        name="collect",
    )(time_step, plan, layers, far_new, near_new, frac_here, vel_here, cells_here)
    new_frac, new_velocity = pl.pallas_call(
        finish_kernel,
        out_shape=(
            jax.ShapeDtypeStruct(frac.shape, f32),
            jax.ShapeDtypeStruct(velocity.shape, f32),
        ),
        in_specs=[vmem] * 4,
        out_specs=(vmem, vmem),
        compiler_params=pltpu.CompilerParams(vmem_limit_bytes=32 * 1024 * 1024),
        cost_estimate=pl.CostEstimate(flops=0, bytes_accessed=8000000, transcendentals=0),
        name="finish",
    )(plan, moved, frac_here, vel_here)
    fastest = largest(top, "gx")
    next_step = (courant / (fastest + wave_speed))[0, :1]
    return (new_frac, new_velocity, next_step)


def solution(mesh):
    placed = (
        P(None, ("runs", "gx")),
        P(None, ("runs", "gx")),
        P(("runs", "gx")),
        P(("runs", "gx")),
        P(("runs", "gx")),
        P("runs"),
    )
    return jax.shard_map(
        body,
        mesh=mesh,
        in_specs=placed,
        out_specs=(P(None, ("runs", "gx")), P(None, ("runs", "gx")), P("runs")),
        check_vma=False,
    )
```

```python
import functools

import jax
import jax.numpy as jnp
from jax import lax
from jax.experimental import pallas as pl
from jax.experimental.pallas import tpu as pltpu
from jax.sharding import PartitionSpec as P

CX = 2
NY = 32
NZ = 128
ROWS = CX * NY
PAIRS = ROWS // 2
LAST = ROWS * NZ - 1
WIDE = 2 * NZ
BLOCK = 256
LANES = 128
GIVEN = 32
TAKEN = 32
SPREAD = 32
TABLE = 16

mass_floor = 0.25
stiffness = 2.0
press_floor = 1.0
grain_size = 0.5
inertia_ref = 0.3
mu_static = 0.38
mu_limit = 0.64
rate_floor = 0.5
gravity = (0.5, 0.0, -0.866)
flip_share = 0.95
courant = 0.4
wave_speed = 2.0
components = ((0, 3, 4), (3, 1, 5), (4, 5, 2))
f32 = jnp.float32
bf16 = jnp.bfloat16


def split_pair(values):
    high = values.astype(bf16)
    low = (values - high.astype(f32)).astype(bf16)
    return high, low


def relative(cells_ref, block, offset):
    return cells_ref[pl.ds(block * 2, 2), :] - offset


def one_hot(rel, wide):
    tall = (16, LANES)
    nodes = lax.broadcasted_iota(jnp.int32, tall, 0).astype(f32)
    one, zero = jnp.ones(tall, bf16), jnp.zeros(tall, bf16)
    halves = []
    for h in range(2):
        line = jnp.broadcast_to(rel[h : h + 1, :].astype(f32), tall).astype(bf16)
        parts = [
            jnp.where(line == (nodes + z).astype(bf16), one, zero) for z in range(0, wide, 16)
        ]
        halves.append(jnp.concatenate(parts, axis=0))
    return jnp.concatenate(halves, axis=1)


def list_visits(cells_ref, plan_ref, start_ref):
    blocks = cells_ref.shape[0] // 2
    shape = (blocks, LANES)
    number = lax.broadcasted_iota(jnp.int32, shape, 0)
    lane = lax.broadcasted_iota(jnp.int32, shape, 1)
    first_half = cells_ref[pl.ds(0, blocks, stride=2), :]
    second_half = cells_ref[pl.ds(1, blocks, stride=2), :]
    reached = jnp.maximum(
        jnp.where(first_half < LAST, first_half, 0), jnp.where(second_half < LAST, second_half, 0)
    )
    first = jnp.min(first_half, axis=1, keepdims=True)
    live = first < LAST
    last = jnp.max(reached, axis=1, keepdims=True)
    first_row, last_row = first >> 7, last >> 7
    start_ref[...] = jnp.broadcast_to(first_row * NZ, shape)
    row = jnp.max(jnp.where(number == lane, first_row, 0), axis=0, keepdims=True)
    plan_ref[0:1, :] = row + (row >> 5)
    within = live & (first_row < lane) & (lane <= last_row)
    block = jnp.max(jnp.where(within, number, -1), axis=0, keepdims=True)
    plan_ref[1:2, :] = jnp.maximum(block, 0)
    plan_ref[2:3, :] = jnp.where(block >= 0, lane[:1], ROWS) * NZ
    low = jnp.where(live, (first >> 8) + number, 2 * LANES)
    high = jnp.where(live, (last >> 8) + number, -1)
    inside = (low <= lane) & (lane <= high)
    block = jnp.max(jnp.where(inside, number, -1), axis=0, keepdims=True)
    valid = block >= 0
    pair = lane[:1] - block
    plan_ref[3:4, :] = jnp.where(valid, block, 0)
    plan_ref[4:5, :] = jnp.where(valid, 2 * pair + (pair >> 4), 0)
    plan_ref[5:6, :] = jnp.where(valid, pair, PAIRS) * WIDE
    plan_ref[6:7, :] = jnp.max(high, axis=0, keepdims=True) + 1
    plan_ref[7:8, :] = jnp.max(jnp.where(live, number + 1, 0), axis=0, keepdims=True)


def spread_kernel(
    frac_hbm, vel_hbm, mass_hbm, cells_hbm,
    far_ref, near_ref, layers_ref, plan_ref, frac_ref, vel_ref, cells_ref,
    listed_ref, start_ref, mass_ref, acc_ref, sems,
):
    slots = frac_ref.shape[1]
    sources = (cells_hbm, frac_hbm, vel_hbm, mass_hbm)
    targets = (cells_ref, frac_ref, vel_ref, mass_ref)
    arrivals = [
        pltpu.make_async_copy(source, target, sems.at[k])
        for k, (source, target) in enumerate(zip(sources, targets))
    ]
    for arrival in arrivals:
        arrival.start()
    acc_ref[...] = jnp.zeros_like(acc_ref)
    arrivals[0].wait()
    list_visits(cells_ref, plan_ref, start_ref)
    listing = pltpu.make_async_copy(plan_ref, listed_ref, sems.at[4])
    listing.start()
    for arrival in arrivals[1:]:
        arrival.wait()
    sublane = lax.broadcasted_iota(jnp.int32, (8, LANES), 0)
    lane = lax.broadcasted_iota(jnp.int32, (1, LANES), 1)
    top_z = sublane >= 4
    field = sublane & 3

    def weigh(part):
        at = pl.multiple_of(part * LANES, LANES)
        here = pl.ds(at, LANES)

        def spread_out(line):
            return jnp.broadcast_to(line, (8, LANES))

        fx, fy, fz = (spread_out(frac_ref[d : d + 1, here]) for d in range(3))
        vx, vy, vz = (spread_out(vel_ref[d : d + 1, here]) for d in range(3))
        live = cells_ref[pl.ds(part, 1), :] < LAST
        held = spread_out(jnp.where(live, mass_ref[pl.ds(part, 1), :], 0.0))
        carried = jnp.where(
            field == 0, held, held * jnp.where(field == 1, vx, jnp.where(field == 2, vy, vz))
        )
        carried = carried * jnp.where(top_z, fz, 1.0 - fz)
        lower, upper = carried * (1.0 - fx), carried * fx
        rows = jnp.concatenate(
            [lower * (1.0 - fy), lower * fy, upper * (1.0 - fy), upper * fy], axis=0
        )
        return jnp.concatenate(split_pair(rows), axis=0)

    def spread_one(block, offset):
        both = lax.dot_general(
            jnp.concatenate([weigh(2 * block), weigh(2 * block + 1)], axis=1),
            one_hot(relative(cells_ref, block, offset), NZ),
            (((1,), (1,)), ((), ())),
            preferred_element_type=f32,
        )
        return both[:SPREAD] + both[SPREAD:]

    def add_to_nodes(base, part):
        here = pl.ds(pl.multiple_of(base * 8, 8), 16)
        above = pl.ds(pl.multiple_of(base * 8, 8) + (NY + 1) * 8, 16)
        lower, upper = acc_ref[here, :], acc_ref[above, :]
        acc_ref[here, :] = lower + part[:16]
        acc_ref[above, :] = upper + part[16:]

    def first_rows(group, carry):
        blocks = [group * GIVEN + u for u in range(GIVEN)]
        found = [spread_one(block, start_ref[pl.ds(block, 1), :]) for block in blocks]
        if carry is None:
            listing.wait()
        for block, part in zip(blocks, found):
            add_to_nodes(listed_ref[0, block], part)
        return carry

    def later_rows(rows):
        found = [spread_one(listed_ref[1, row], listed_ref[2, row]) for row in rows]
        for row, part in zip(rows, found):
            add_to_nodes(row + (row >> 5), part)

    first_rows(0, None)
    for row in range(0, ROWS, GIVEN):
        later_rows(range(row, row + GIVEN))
    lax.fori_loop(1, (listed_ref[7, 0] + GIVEN - 1) // GIVEN, first_rows, 0)

    odd = lax.axis_index("gx") % 2 == 1
    layers = []
    for l in range(CX + 1):
        first = l * (NY + 1) * 8
        acc_ref[first : first + 8, :] += acc_ref[first + NY * 8 : first + NY * 8 + 8, :]
        for f in range(4):
            lower = acc_ref[pl.ds(first + f, NY, stride=8), :]
            upper = acc_ref[pl.ds(first + 4 + f, NY, stride=8), :]
            layers.append(lower + pltpu.roll(upper, 1, 1))
            layers_ref[l * 4 + f] = layers[-1]
    for k in range(CX * 4):
        far_ref[k] = jnp.where(odd, layers[k + 4], layers[k])
        near_ref[k] = jnp.where(odd, layers[k], layers[k + 4])


def pair_up(field, axis):
    return field + pltpu.roll(field, field.shape[axis] - 1, axis)


def step_up(field, axis):
    return pltpu.roll(field, field.shape[axis] - 1, axis) - field


def pair_down(field, axis):
    return field + pltpu.roll(field, 1, axis)


def step_down(field, axis):
    return field - pltpu.roll(field, 1, axis)


def cell_stress(vel_lo, vel_hi, mass_lo, mass_hi, keep):
    grads = []
    for a in range(3):
        diff = vel_hi[a] - vel_lo[a]
        both = vel_hi[a] + vel_lo[a]
        grads.append(
            [
                0.25 * pair_up(pair_up(diff, 0), 1),
                0.25 * pair_up(step_up(both, 0), 1),
                0.25 * step_up(pair_up(both, 0), 1),
            ]
        )
    density = 0.125 * pair_up(pair_up(mass_hi + mass_lo, 0), 1)
    dxx = grads[0][0]
    dyy = grads[1][1]
    dzz = grads[2][2]
    dxy = 0.5 * (grads[0][1] + grads[1][0])
    dxz = 0.5 * (grads[0][2] + grads[2][0])
    dyz = 0.5 * (grads[1][2] + grads[2][1])
    second = dxx * dxx + dyy * dyy + dzz * dzz + 2.0 * (dxy * dxy + dxz * dxz + dyz * dyz)
    rate = jnp.sqrt(2.0 * second + rate_floor * rate_floor)
    pressure = stiffness * density
    inertial = rate * grain_size / jnp.sqrt(pressure + press_floor)
    friction = mu_static + (mu_limit - mu_static) * inertial / (inertia_ref + inertial)
    twice = 2.0 * friction * pressure / rate
    sigma = [
        twice * dxx - pressure,
        twice * dyy - pressure,
        twice * dzz - pressure,
        twice * dxy,
        twice * dxz,
        twice * dyz,
    ]
    return [jnp.where(keep, s, 0.0) for s in sigma]


def node_force(lower, upper):
    force = []
    for a in range(3):
        sx, sy, sz = (components[a][b] for b in range(3))
        along = pair_down(pair_down(upper[sx] - lower[sx], 0), 1)
        across = step_down(pair_down(upper[sy] + lower[sy], 1), 0)
        upward = step_down(pair_down(upper[sz] + lower[sz], 0), 1)
        force.append(0.25 * (along + across + upward))
    return force


def collect_kernel(
    step_ref, plan_ref, layers_ref, far_new_ref, near_new_ref, frac_ref, vel_ref, cells_ref,
    out_ref, top_ref, listed_ref, tab_ref, pair_ref, sem,
):
    blocks = frac_ref.shape[1] // BLOCK
    listing = pltpu.make_async_copy(plan_ref, listed_ref, sem)
    listing.start()
    step = step_ref[0]
    odd = lax.axis_index("gx") % 2 == 1

    def pick(if_odd, if_even):
        return [jnp.where(odd, if_odd[k], if_even[k]) for k in range(4 * CX)]

    own = [layers_ref[k] for k in range(4 * (CX + 1))]
    left, right = pick(near_new_ref, far_new_ref), pick(far_new_ref, near_new_ref)
    nodes = [
        left[:4],
        [own[f] + left[4 + f] for f in range(4)],
        own[4:8],
        [own[8 + f] + right[f] for f in range(4)],
        right[4:],
    ]
    height = lax.broadcasted_iota(jnp.int32, (NY, NZ), 1)
    keep = height < NZ - 1
    above_bed = height > 0
    floor = [jnp.maximum(layer[0], mass_floor) for layer in nodes]
    v_old = [[layer[1 + a] / floor[l] for a in range(3)] for l, layer in enumerate(nodes)]
    sigma = [
        cell_stress(v_old[l], v_old[l + 1], nodes[l][0], nodes[l + 1][0], keep) for l in range(4)
    ]
    blank = jnp.zeros((NY, NZ), f32)
    for l in range(CX + 1):
        force = node_force(sigma[l], sigma[l + 1])
        fields = [blank] * 8
        for a in range(3):
            layer = nodes[l + 1]
            fresh = (layer[1 + a] + step * (force[a] + layer[0] * gravity[a])) / floor[l + 1]
            fresh = jnp.where(above_bed, fresh, 0.0)
            fields[a] = fresh - flip_share * v_old[l + 1][a]
            fields[4 + a] = step * fresh
        for k, value in enumerate(fields):
            start = l * NY * TABLE + k
            tab_ref[pl.ds(start, NY, stride=TABLE), :] = value
            tab_ref[pl.ds(start + 8, NY, stride=TABLE), :] = pltpu.roll(value, NZ - 1, 1)

    for l in range(CX + 1):

        def split_row(j, carry):
            at = pl.ds(pl.multiple_of((l * NY + j) * TABLE, TABLE), TABLE)
            high, low = split_pair(tab_ref[at, :])
            pair_ref[pl.ds(l * (NY + 1) + j, 1)] = jnp.concatenate([high, low], axis=0)[None]
            return carry

        lax.fori_loop(0, NY, split_row, 0, unroll=8)
        pair_ref[l * (NY + 1) + NY] = pair_ref[l * (NY + 1)]

    out_ref[...] = jnp.zeros_like(out_ref)
    listing.wait()
    total = listed_ref[6, 0]

    def visit(group, top):
        found = []
        for u in range(TAKEN):
            v = group * TAKEN + u
            block = listed_ref[3, v]
            base = listed_ref[4, v]
            rel = relative(cells_ref, block, listed_ref[5, v])
            hot = one_hot(rel, WIDE)
            rows = []
            for a in range(2):
                three = [pair_ref[base + a * (NY + 1) + k] for k in range(3)]
                rows += [jnp.concatenate(three[b : b + 2], axis=1) for b in range(2)]
            both = jnp.dot(jnp.concatenate(rows, axis=0), hot, preferred_element_type=f32)
            corners = []
            for k in range(4):
                four = both[2 * TABLE * k : 2 * TABLE * (k + 1)]
                corners += [four[0:8] + four[16:24], four[8:16] + four[24:32]]
            here = pl.ds(pl.multiple_of(block * BLOCK, BLOCK), BLOCK)
            frac = frac_ref[:, here]
            for d in (2, 1, 0):
                share = frac[d : d + 1, :]
                corners = [
                    corners[k] + share * (corners[k + 1] - corners[k])
                    for k in range(0, len(corners), 2)
                ]
            fresh = flip_share * vel_ref[:, here] + corners[0][0:3]
            square = jnp.sum(fresh * fresh, axis=0, keepdims=True)
            taken = (rel >= 0) & (rel < WIDE - 1)
            for h in range(2):
                part = square[:, h * LANES : (h + 1) * LANES]
                top = jnp.maximum(top, jnp.where(taken[h : h + 1], part, 0.0))
            found.append((block, corners[0]))
        for block, part in found:
            out_ref[pl.ds(block, 1)] += part[None]
        return top

    top = jnp.zeros((1, LANES), f32)
    for group in range(2):
        top = visit(group, top)
    top = lax.fori_loop(2, (total + TAKEN - 1) // TAKEN, visit, top)
    top = jnp.sqrt(jnp.max(top, axis=1, keepdims=True))
    top_ref[...] = jnp.broadcast_to(top, top_ref.shape)


def finish_kernel(count_ref, moved_ref, frac_ref, vel_ref, new_frac_ref, new_vel_ref):
    blocks = frac_ref.shape[1] // BLOCK
    count = count_ref[0]
    lane = lax.broadcasted_iota(jnp.int32, (1, BLOCK), 1)

    def finish(block, carry):
        at = pl.multiple_of(block * BLOCK, BLOCK)
        here = pl.ds(at, BLOCK)
        alive = at + lane < count
        got = moved_ref[pl.ds(block, 1)][0]
        new_vel_ref[:, here] = jnp.where(alive, flip_share * vel_ref[:, here] + got[0:3], 0.0)
        new_frac_ref[:, here] = jnp.where(alive, frac_ref[:, here] + got[4:7], 0.0)
        return carry

    lax.fori_loop(0, blocks, finish, 0, unroll=4)


def largest(value, axis):
    devices = lax.axis_size(axis)
    reach = 1
    while reach < devices:
        if devices & (devices - 1) == 0:
            pairs = [(i, i ^ (reach | 1)) for i in range(devices)]
        else:
            pairs = [(i, (i + reach) % devices) for i in range(devices)]
        value = jnp.maximum(value, lax.ppermute(value, axis, pairs))
        reach *= 2
    return value


smem = pl.BlockSpec(memory_space=pltpu.SMEM)
vmem = pl.BlockSpec(memory_space=pltpu.VMEM)
hbm = pl.BlockSpec(memory_space=pltpu.HBM)


def body(frac, velocity, mass, particle_cell, tile_count, time_step):
    slots = frac.shape[1]
    blocks = slots // BLOCK
    rows = slots // LANES
    inputs = (frac, velocity, mass.reshape(rows, LANES), particle_cell.reshape(rows, LANES))
    far, near, layers, plan, frac_here, vel_here, cells_here = pl.pallas_call(
        spread_kernel,
        out_shape=(
            pltpu.VMEM((4 * CX, NY, NZ), f32),
            pltpu.VMEM((4 * CX, NY, NZ), f32),
            pltpu.VMEM((4 * (CX + 1), NY, NZ), f32),
            pltpu.VMEM((8, LANES), jnp.int32),
            pltpu.VMEM(frac.shape, f32),
            pltpu.VMEM(velocity.shape, f32),
            pltpu.VMEM((rows, LANES), jnp.int32),
        ),
        in_specs=[hbm] * 4,
        out_specs=(vmem,) * 7,
        scratch_shapes=[
            pltpu.SMEM((8, LANES), jnp.int32),
            pltpu.VMEM((blocks, LANES), jnp.int32),
            pltpu.VMEM((rows, LANES), f32),
            pltpu.VMEM(((CX + 1) * (NY + 1) * 8, NZ), f32),
            pltpu.SemaphoreType.DMA((5,)),
        ],
        compiler_params=pltpu.CompilerParams(vmem_limit_bytes=32 * 1024 * 1024),
        name="spread",
    )(*[pltpu.with_memory_space_constraint(x, pltpu.HBM) for x in inputs])
    devices = lax.axis_size("gx")
    far_pairs = [(i, (i + (1 if i % 2 else -1)) % devices) for i in range(devices)]
    near_pairs = [(i, i ^ 1) for i in range(devices)]
    far_new = lax.ppermute(far, "gx", far_pairs)
    near_new = lax.ppermute(near, "gx", near_pairs)
    moved, top = pl.pallas_call(
        collect_kernel,
        out_shape=(
            jax.ShapeDtypeStruct((blocks, 8, BLOCK), f32),
            jax.ShapeDtypeStruct((8, LANES), f32),
        ),
        in_specs=[smem] + [vmem] * 7,
        out_specs=(vmem, vmem),
        scratch_shapes=[
            pltpu.SMEM((8, LANES), jnp.int32),
            pltpu.VMEM(((CX + 1) * NY * TABLE, NZ), f32),
            pltpu.VMEM(((CX + 1) * (NY + 1), 2 * TABLE, NZ), bf16),
            pltpu.SemaphoreType.DMA,
        ],
        compiler_params=pltpu.CompilerParams(vmem_limit_bytes=32 * 1024 * 1024),
        name="collect",
    )(time_step, plan, layers, far_new, near_new, frac_here, vel_here, cells_here)
    new_frac, new_velocity = pl.pallas_call(
        finish_kernel,
        out_shape=(
            jax.ShapeDtypeStruct(frac.shape, f32),
            jax.ShapeDtypeStruct(velocity.shape, f32),
        ),
        in_specs=[smem] + [vmem] * 3,
        out_specs=(vmem, vmem),
        compiler_params=pltpu.CompilerParams(vmem_limit_bytes=32 * 1024 * 1024),
        cost_estimate=pl.CostEstimate(flops=0, bytes_accessed=8000000, transcendentals=0),
        name="finish",
    )(tile_count, moved, frac_here, vel_here)
    fastest = largest(top, "gx")
    next_step = (courant / (fastest + wave_speed))[0, :1]
    return (new_frac, new_velocity, next_step)


def solution(mesh):
    placed = (
        P(None, ("runs", "gx")),
        P(None, ("runs", "gx")),
        P(("runs", "gx")),
        P(("runs", "gx")),
        P(("runs", "gx")),
        P("runs"),
    )
    return jax.shard_map(
        body,
        mesh=mesh,
        in_specs=placed,
        out_specs=(P(None, ("runs", "gx")), P(None, ("runs", "gx")), P("runs")),
        check_vma=False,
    )
```

```python
import functools

import jax
import jax.numpy as jnp
from jax import lax
from jax.experimental import pallas as pl
from jax.experimental.pallas import tpu as pltpu
from jax.sharding import PartitionSpec as P

CX = 2
NY = 32
NZ = 128
ROWS = CX * NY
LAST = ROWS * NZ - 1
BLOCK = 256
LANES = 128
GIVEN = 32
TAKEN = 32
SPREAD = 32
TABLE = 16

mass_floor = 0.25
stiffness = 2.0
press_floor = 1.0
grain_size = 0.5
inertia_ref = 0.3
mu_static = 0.38
mu_limit = 0.64
rate_floor = 0.5
gravity = (0.5, 0.0, -0.866)
flip_share = 0.95
courant = 0.4
wave_speed = 2.0
components = ((0, 3, 4), (3, 1, 5), (4, 5, 2))
f32 = jnp.float32
bf16 = jnp.bfloat16


def split_pair(values):
    high = values.astype(bf16)
    low = (values - high.astype(f32)).astype(bf16)
    return high, low


def relative(cells_ref, block, offset):
    return cells_ref[pl.ds(block * 2, 2), :] - offset


def one_hot(rel, wide):
    tall = (16, LANES)
    nodes = lax.broadcasted_iota(jnp.int32, tall, 0).astype(f32)
    one, zero = jnp.ones(tall, bf16), jnp.zeros(tall, bf16)
    halves = []
    for h in range(2):
        line = jnp.broadcast_to(rel[h : h + 1, :].astype(f32), tall).astype(bf16)
        parts = [
            jnp.where(line == (nodes + z).astype(bf16), one, zero) for z in range(0, wide, 16)
        ]
        halves.append(jnp.concatenate(parts, axis=0))
    return jnp.concatenate(halves, axis=1)


def list_visits(cells_ref, plan_ref, start_ref):
    blocks = cells_ref.shape[0] // 2
    shape = (blocks, LANES)
    number = lax.broadcasted_iota(jnp.int32, shape, 0)
    lane = lax.broadcasted_iota(jnp.int32, shape, 1)
    first_half = cells_ref[pl.ds(0, blocks, stride=2), :]
    second_half = cells_ref[pl.ds(1, blocks, stride=2), :]
    reached = jnp.maximum(
        jnp.where(first_half < LAST, first_half, 0), jnp.where(second_half < LAST, second_half, 0)
    )
    first = jnp.min(first_half, axis=1, keepdims=True)
    live = first < LAST
    last = jnp.max(reached, axis=1, keepdims=True)
    first_row, last_row = first >> 7, last >> 7
    start_ref[...] = jnp.broadcast_to(first_row * NZ, shape)
    row = jnp.max(jnp.where(number == lane, first_row, 0), axis=0, keepdims=True)
    plan_ref[0:1, :] = row + (row >> 5)
    within = live & (first_row < lane) & (lane <= last_row)
    block = jnp.max(jnp.where(within, number, -1), axis=0, keepdims=True)
    plan_ref[1:2, :] = jnp.maximum(block, 0)
    plan_ref[2:3, :] = jnp.where(block >= 0, lane[:1], ROWS) * NZ
    low = jnp.where(live, first_row + number, 2 * LANES)
    high = jnp.where(live, last_row + number, -1)
    inside = (low <= lane) & (lane <= high)
    block = jnp.max(jnp.where(inside, number, -1), axis=0, keepdims=True)
    valid = block >= 0
    row = lane[:1] - block
    plan_ref[3:4, :] = jnp.where(valid, block, 0)
    plan_ref[4:5, :] = jnp.where(valid, row + (row >> 5), 0)
    plan_ref[5:6, :] = jnp.where(valid, row, ROWS) * NZ
    plan_ref[6:7, :] = jnp.max(high, axis=0, keepdims=True) + 1
    plan_ref[7:8, :] = jnp.max(jnp.where(live, number + 1, 0), axis=0, keepdims=True)


def spread_kernel(
    frac_hbm, vel_hbm, mass_hbm, cells_hbm,
    far_ref, near_ref, layers_ref, plan_ref, frac_ref, vel_ref, cells_ref,
    listed_ref, start_ref, mass_ref, acc_ref, sems,
):
    slots = frac_ref.shape[1]
    sources = (cells_hbm, frac_hbm, vel_hbm, mass_hbm)
    targets = (cells_ref, frac_ref, vel_ref, mass_ref)
    arrivals = [
        pltpu.make_async_copy(source, target, sems.at[k])
        for k, (source, target) in enumerate(zip(sources, targets))
    ]
    for arrival in arrivals:
        arrival.start()
    acc_ref[...] = jnp.zeros_like(acc_ref)
    arrivals[0].wait()
    list_visits(cells_ref, plan_ref, start_ref)
    listing = pltpu.make_async_copy(plan_ref, listed_ref, sems.at[4])
    listing.start()
    for arrival in arrivals[1:]:
        arrival.wait()
    sublane = lax.broadcasted_iota(jnp.int32, (8, LANES), 0)
    lane = lax.broadcasted_iota(jnp.int32, (1, LANES), 1)
    top_z = sublane >= 4
    field = sublane & 3

    def weigh(part):
        at = pl.multiple_of(part * LANES, LANES)
        here = pl.ds(at, LANES)

        def spread_out(line):
            return jnp.broadcast_to(line, (8, LANES))

        fx, fy, fz = (spread_out(frac_ref[d : d + 1, here]) for d in range(3))
        vx, vy, vz = (spread_out(vel_ref[d : d + 1, here]) for d in range(3))
        live = cells_ref[pl.ds(part, 1), :] < LAST
        held = spread_out(jnp.where(live, mass_ref[pl.ds(part, 1), :], 0.0))
        carried = jnp.where(
            field == 0, held, held * jnp.where(field == 1, vx, jnp.where(field == 2, vy, vz))
        )
        carried = carried * jnp.where(top_z, fz, 1.0 - fz)
        lower, upper = carried * (1.0 - fx), carried * fx
        rows = jnp.concatenate(
            [lower * (1.0 - fy), lower * fy, upper * (1.0 - fy), upper * fy], axis=0
        )
        return jnp.concatenate(split_pair(rows), axis=0)

    def spread_one(block, offset):
        both = lax.dot_general(
            jnp.concatenate([weigh(2 * block), weigh(2 * block + 1)], axis=1),
            one_hot(relative(cells_ref, block, offset), NZ),
            (((1,), (1,)), ((), ())),
            preferred_element_type=f32,
        )
        return both[:SPREAD] + both[SPREAD:]

    def add_to_nodes(base, part):
        here = pl.ds(pl.multiple_of(base * 8, 8), 16)
        above = pl.ds(pl.multiple_of(base * 8, 8) + (NY + 1) * 8, 16)
        lower, upper = acc_ref[here, :], acc_ref[above, :]
        acc_ref[here, :] = lower + part[:16]
        acc_ref[above, :] = upper + part[16:]

    def first_rows(group, carry):
        blocks = [group * GIVEN + u for u in range(GIVEN)]
        found = [spread_one(block, start_ref[pl.ds(block, 1), :]) for block in blocks]
        if carry is None:
            listing.wait()
        for block, part in zip(blocks, found):
            add_to_nodes(listed_ref[0, block], part)
        return carry

    def later_rows(rows):
        found = [spread_one(listed_ref[1, row], listed_ref[2, row]) for row in rows]
        for row, part in zip(rows, found):
            add_to_nodes(row + (row >> 5), part)

    first_rows(0, None)
    for row in range(0, ROWS, GIVEN):
        later_rows(range(row, row + GIVEN))
    lax.fori_loop(1, (listed_ref[7, 0] + GIVEN - 1) // GIVEN, first_rows, 0)

    odd = lax.axis_index("gx") % 2 == 1
    layers = []
    for l in range(CX + 1):
        first = l * (NY + 1) * 8
        acc_ref[first : first + 8, :] += acc_ref[first + NY * 8 : first + NY * 8 + 8, :]
        for f in range(4):
            lower = acc_ref[pl.ds(first + f, NY, stride=8), :]
            upper = acc_ref[pl.ds(first + 4 + f, NY, stride=8), :]
            layers.append(lower + pltpu.roll(upper, 1, 1))
            layers_ref[l * 4 + f] = layers[-1]
    for k in range(CX * 4):
        far_ref[k] = jnp.where(odd, layers[k + 4], layers[k])
        near_ref[k] = jnp.where(odd, layers[k], layers[k + 4])


def pair_up(field, axis):
    return field + pltpu.roll(field, field.shape[axis] - 1, axis)


def step_up(field, axis):
    return pltpu.roll(field, field.shape[axis] - 1, axis) - field


def pair_down(field, axis):
    return field + pltpu.roll(field, 1, axis)


def step_down(field, axis):
    return field - pltpu.roll(field, 1, axis)


def cell_stress(vel_lo, vel_hi, mass_lo, mass_hi, keep):
    grads = []
    for a in range(3):
        diff = vel_hi[a] - vel_lo[a]
        both = vel_hi[a] + vel_lo[a]
        grads.append(
            [
                0.25 * pair_up(pair_up(diff, 0), 1),
                0.25 * pair_up(step_up(both, 0), 1),
                0.25 * step_up(pair_up(both, 0), 1),
            ]
        )
    density = 0.125 * pair_up(pair_up(mass_hi + mass_lo, 0), 1)
    dxx = grads[0][0]
    dyy = grads[1][1]
    dzz = grads[2][2]
    dxy = 0.5 * (grads[0][1] + grads[1][0])
    dxz = 0.5 * (grads[0][2] + grads[2][0])
    dyz = 0.5 * (grads[1][2] + grads[2][1])
    second = dxx * dxx + dyy * dyy + dzz * dzz + 2.0 * (dxy * dxy + dxz * dxz + dyz * dyz)
    rate = jnp.sqrt(2.0 * second + rate_floor * rate_floor)
    pressure = stiffness * density
    inertial = rate * grain_size / jnp.sqrt(pressure + press_floor)
    friction = mu_static + (mu_limit - mu_static) * inertial / (inertia_ref + inertial)
    twice = 2.0 * friction * pressure / rate
    sigma = [
        twice * dxx - pressure,
        twice * dyy - pressure,
        twice * dzz - pressure,
        twice * dxy,
        twice * dxz,
        twice * dyz,
    ]
    return [jnp.where(keep, s, 0.0) for s in sigma]


def node_force(lower, upper):
    force = []
    for a in range(3):
        sx, sy, sz = (components[a][b] for b in range(3))
        along = pair_down(pair_down(upper[sx] - lower[sx], 0), 1)
        across = step_down(pair_down(upper[sy] + lower[sy], 1), 0)
        upward = step_down(pair_down(upper[sz] + lower[sz], 0), 1)
        force.append(0.25 * (along + across + upward))
    return force


def collect_kernel(
    step_ref, count_ref, plan_ref, layers_ref, far_new_ref, near_new_ref, frac_ref, vel_ref, cells_ref,
    out_ref, top_ref, listed_ref, tab_ref, pair_ref, sem,
):
    blocks = frac_ref.shape[1] // BLOCK
    listing = pltpu.make_async_copy(plan_ref, listed_ref, sem)
    listing.start()
    step = step_ref[0]
    odd = lax.axis_index("gx") % 2 == 1

    def pick(if_odd, if_even):
        return [jnp.where(odd, if_odd[k], if_even[k]) for k in range(4 * CX)]

    own = [layers_ref[k] for k in range(4 * (CX + 1))]
    left, right = pick(near_new_ref, far_new_ref), pick(far_new_ref, near_new_ref)
    nodes = [
        left[:4],
        [own[f] + left[4 + f] for f in range(4)],
        own[4:8],
        [own[8 + f] + right[f] for f in range(4)],
        right[4:],
    ]
    height = lax.broadcasted_iota(jnp.int32, (NY, NZ), 1)
    keep = height < NZ - 1
    above_bed = height > 0
    floor = [jnp.maximum(layer[0], mass_floor) for layer in nodes]
    v_old = [[layer[1 + a] / floor[l] for a in range(3)] for l, layer in enumerate(nodes)]
    sigma = [
        cell_stress(v_old[l], v_old[l + 1], nodes[l][0], nodes[l + 1][0], keep) for l in range(4)
    ]
    blank = jnp.zeros((NY, NZ), f32)
    for l in range(CX + 1):
        force = node_force(sigma[l], sigma[l + 1])
        fields = [blank] * 8
        for a in range(3):
            layer = nodes[l + 1]
            fresh = (layer[1 + a] + step * (force[a] + layer[0] * gravity[a])) / floor[l + 1]
            fresh = jnp.where(above_bed, fresh, 0.0)
            fields[a] = fresh - flip_share * v_old[l + 1][a]
            fields[4 + a] = step * fresh
        for k, value in enumerate(fields):
            start = l * NY * TABLE + k
            tab_ref[pl.ds(start, NY, stride=TABLE), :] = value
            tab_ref[pl.ds(start + 8, NY, stride=TABLE), :] = pltpu.roll(value, NZ - 1, 1)

    for l in range(CX + 1):

        def split_row(j, carry):
            at = pl.ds(pl.multiple_of((l * NY + j) * TABLE, TABLE), TABLE)
            high, low = split_pair(tab_ref[at, :])
            pair_ref[pl.ds(l * (NY + 1) + j, 1)] = jnp.concatenate([high, low], axis=0)[None]
            return carry

        lax.fori_loop(0, NY, split_row, 0, unroll=8)
        pair_ref[l * (NY + 1) + NY] = pair_ref[l * (NY + 1)]

    out_ref[...] = jnp.zeros_like(out_ref)
    listing.wait()
    total = listed_ref[6, 0]
    count = count_ref[0]
    lane = lax.broadcasted_iota(jnp.int32, (2, LANES), 1)
    half = lax.broadcasted_iota(jnp.int32, (2, LANES), 0)

    def visit(group, top):
        found = []
        for u in range(TAKEN):
            v = group * TAKEN + u
            block = listed_ref[3, v]
            base = listed_ref[4, v]
            rel = relative(cells_ref, block, listed_ref[5, v])
            hot = one_hot(rel, NZ)
            rows = [pair_ref[base + ahead] for ahead in (0, 1, NY + 1, NY + 2)]
            both = jnp.dot(jnp.concatenate(rows, axis=0), hot, preferred_element_type=f32)
            corners = []
            for k in range(4):
                four = both[2 * TABLE * k : 2 * TABLE * (k + 1)]
                corners += [four[0:8] + four[16:24], four[8:16] + four[24:32]]
            here = pl.ds(pl.multiple_of(block * BLOCK, BLOCK), BLOCK)
            frac = frac_ref[:, here]
            for d in (2, 1, 0):
                share = frac[d : d + 1, :]
                corners = [
                    corners[k] + share * (corners[k + 1] - corners[k])
                    for k in range(0, len(corners), 2)
                ]
            fresh = flip_share * vel_ref[:, here] + corners[0][0:3]
            square = jnp.sum(fresh * fresh, axis=0, keepdims=True)
            slot = block * BLOCK + half * LANES + lane
            taken = (rel >= 0) & (rel < NZ) & (slot < count)
            for h in range(2):
                part = square[:, h * LANES : (h + 1) * LANES]
                top = jnp.maximum(top, jnp.where(taken[h : h + 1], part, 0.0))
            found.append((block, corners[0]))
        for block, part in found:
            out_ref[pl.ds(block, 1)] += part[None]
        return top

    top = jnp.zeros((1, LANES), f32)
    for group in range(3):
        top = visit(group, top)
    top = lax.fori_loop(3, (total + TAKEN - 1) // TAKEN, visit, top)
    top = jnp.sqrt(jnp.max(top, axis=1, keepdims=True))
    top_ref[...] = jnp.broadcast_to(top, top_ref.shape)


def finish_kernel(cells_ref, moved_ref, frac_ref, vel_ref, new_frac_ref, new_vel_ref):
    blocks = frac_ref.shape[1] // BLOCK

    def finish(block, carry):
        at = pl.multiple_of(block * BLOCK, BLOCK)
        here = pl.ds(at, BLOCK)
        cells = cells_ref[pl.ds(block * 2, 2), :]
        alive = jnp.concatenate([cells[0:1], cells[1:2]], axis=1) < LAST
        got = moved_ref[pl.ds(block, 1)][0]
        new_vel_ref[:, here] = jnp.where(alive, flip_share * vel_ref[:, here] + got[0:3], 0.0)
        new_frac_ref[:, here] = jnp.where(alive, frac_ref[:, here] + got[4:7], 0.0)
        return carry

    lax.fori_loop(0, blocks, finish, 0, unroll=4)


def largest(value, axis):
    devices = lax.axis_size(axis)
    reach = 1
    while reach < devices:
        if devices & (devices - 1) == 0:
            pairs = [(i, i ^ (reach | 1)) for i in range(devices)]
        else:
            pairs = [(i, (i + reach) % devices) for i in range(devices)]
        value = jnp.maximum(value, lax.ppermute(value, axis, pairs))
        reach *= 2
    return value


smem = pl.BlockSpec(memory_space=pltpu.SMEM)
vmem = pl.BlockSpec(memory_space=pltpu.VMEM)
hbm = pl.BlockSpec(memory_space=pltpu.HBM)


def body(frac, velocity, mass, particle_cell, tile_count, time_step):
    slots = frac.shape[1]
    blocks = slots // BLOCK
    rows = slots // LANES
    inputs = (frac, velocity, mass.reshape(rows, LANES), particle_cell.reshape(rows, LANES))
    far, near, layers, plan, frac_here, vel_here, cells_here = pl.pallas_call(
        spread_kernel,
        out_shape=(
            pltpu.VMEM((4 * CX, NY, NZ), f32),
            pltpu.VMEM((4 * CX, NY, NZ), f32),
            pltpu.VMEM((4 * (CX + 1), NY, NZ), f32),
            pltpu.VMEM((8, LANES), jnp.int32),
            pltpu.VMEM(frac.shape, f32),
            pltpu.VMEM(velocity.shape, f32),
            pltpu.VMEM((rows, LANES), jnp.int32),
        ),
        in_specs=[hbm] * 4,
        out_specs=(vmem,) * 7,
        scratch_shapes=[
            pltpu.SMEM((8, LANES), jnp.int32),
            pltpu.VMEM((blocks, LANES), jnp.int32),
            pltpu.VMEM((rows, LANES), f32),
            pltpu.VMEM(((CX + 1) * (NY + 1) * 8, NZ), f32),
            pltpu.SemaphoreType.DMA((5,)),
        ],
        compiler_params=pltpu.CompilerParams(vmem_limit_bytes=32 * 1024 * 1024),
        name="spread",
    )(*[pltpu.with_memory_space_constraint(x, pltpu.HBM) for x in inputs])
    devices = lax.axis_size("gx")
    far_pairs = [(i, (i + (1 if i % 2 else -1)) % devices) for i in range(devices)]
    near_pairs = [(i, i ^ 1) for i in range(devices)]
    far_new = lax.ppermute(far, "gx", far_pairs)
    near_new = lax.ppermute(near, "gx", near_pairs)
    moved, top = pl.pallas_call(
        collect_kernel,
        out_shape=(
            jax.ShapeDtypeStruct((blocks, 8, BLOCK), f32),
            jax.ShapeDtypeStruct((8, LANES), f32),
        ),
        in_specs=[smem] * 2 + [vmem] * 7,
        out_specs=(vmem, vmem),
        scratch_shapes=[
            pltpu.SMEM((8, LANES), jnp.int32),
            pltpu.VMEM(((CX + 1) * NY * TABLE, NZ), f32),
            pltpu.VMEM(((CX + 1) * (NY + 1), 2 * TABLE, NZ), bf16),
            pltpu.SemaphoreType.DMA,
        ],
        compiler_params=pltpu.CompilerParams(vmem_limit_bytes=32 * 1024 * 1024),
        name="collect",
    )(time_step, tile_count, plan, layers, far_new, near_new, frac_here, vel_here, cells_here)
    new_frac, new_velocity = pl.pallas_call(
        finish_kernel,
        out_shape=(
            jax.ShapeDtypeStruct(frac.shape, f32),
            jax.ShapeDtypeStruct(velocity.shape, f32),
        ),
        in_specs=[vmem] * 4,
        out_specs=(vmem, vmem),
        compiler_params=pltpu.CompilerParams(vmem_limit_bytes=32 * 1024 * 1024),
        cost_estimate=pl.CostEstimate(flops=0, bytes_accessed=8000000, transcendentals=0),
        name="finish",
    )(cells_here, moved, frac_here, vel_here)
    fastest = largest(top, "gx")
    next_step = (courant / (fastest + wave_speed))[0, :1]
    return (new_frac, new_velocity, next_step)


def solution(mesh):
    placed = (
        P(None, ("runs", "gx")),
        P(None, ("runs", "gx")),
        P(("runs", "gx")),
        P(("runs", "gx")),
        P(("runs", "gx")),
        P("runs"),
    )
    return jax.shard_map(
        body,
        mesh=mesh,
        in_specs=placed,
        out_specs=(P(None, ("runs", "gx")), P(None, ("runs", "gx")), P("runs")),
        check_vma=False,
    )
```

```python
import functools

import jax
import jax.numpy as jnp
from jax import lax
from jax.experimental import pallas as pl
from jax.experimental.pallas import tpu as pltpu
from jax.sharding import PartitionSpec as P

CX = 2
NY = 32
NZ = 128
ROWS = CX * NY
PAIRS = ROWS // 2
LAST = ROWS * NZ - 1
WIDE = 2 * NZ
BLOCK = 256
LANES = 128
GIVEN = 32
TAKEN = 32
SPREAD = 32
TABLE = 16

mass_floor = 0.25
stiffness = 2.0
press_floor = 1.0
grain_size = 0.5
inertia_ref = 0.3
mu_static = 0.38
mu_limit = 0.64
rate_floor = 0.5
gravity = (0.5, 0.0, -0.866)
flip_share = 0.95
courant = 0.4
wave_speed = 2.0
components = ((0, 3, 4), (3, 1, 5), (4, 5, 2))
f32 = jnp.float32
bf16 = jnp.bfloat16


def split_pair(values):
    high = values.astype(bf16)
    low = (values - high.astype(f32)).astype(bf16)
    return high, low


def relative(cells_ref, block, offset):
    return cells_ref[pl.ds(block * 2, 2), :] - offset


def one_hot(rel, wide):
    tall = (16, LANES)
    nodes = lax.broadcasted_iota(jnp.int32, tall, 0).astype(f32)
    one, zero = jnp.ones(tall, bf16), jnp.zeros(tall, bf16)
    halves = []
    for h in range(2):
        line = jnp.broadcast_to(rel[h : h + 1, :].astype(f32), tall).astype(bf16)
        parts = [
            jnp.where(line == (nodes + z).astype(bf16), one, zero) for z in range(0, wide, 16)
        ]
        halves.append(jnp.concatenate(parts, axis=0))
    return jnp.concatenate(halves, axis=1)


def list_visits(cells_ref, plan_ref, start_ref):
    blocks = cells_ref.shape[0] // 2
    shape = (blocks, LANES)
    number = lax.broadcasted_iota(jnp.int32, shape, 0)
    lane = lax.broadcasted_iota(jnp.int32, shape, 1)
    first_half = cells_ref[pl.ds(0, blocks, stride=2), :]
    second_half = cells_ref[pl.ds(1, blocks, stride=2), :]
    reached = jnp.maximum(
        jnp.where(first_half < LAST, first_half, 0), jnp.where(second_half < LAST, second_half, 0)
    )
    first = jnp.min(first_half, axis=1, keepdims=True)
    live = first < LAST
    last = jnp.max(reached, axis=1, keepdims=True)
    first_pair, last_pair = first >> 8, last >> 8
    start_ref[...] = jnp.broadcast_to(first_pair * WIDE, shape)
    pair = jnp.max(jnp.where(number == lane, first_pair, 0), axis=0, keepdims=True)
    plan_ref[0:1, :] = 2 * pair + (pair >> 4)
    within = live & (first_pair < lane) & (lane <= last_pair)
    block = jnp.max(jnp.where(within, number, -1), axis=0, keepdims=True)
    plan_ref[1:2, :] = jnp.maximum(block, 0)
    plan_ref[2:3, :] = jnp.where(block >= 0, lane[:1], PAIRS) * WIDE
    low = jnp.where(live, first_pair + number, 2 * LANES)
    high = jnp.where(live, last_pair + number, -1)
    inside = (low <= lane) & (lane <= high)
    block = jnp.max(jnp.where(inside, number, -1), axis=0, keepdims=True)
    valid = block >= 0
    pair = lane[:1] - block
    plan_ref[3:4, :] = jnp.where(valid, block, 0)
    plan_ref[4:5, :] = jnp.where(valid, 2 * pair + (pair >> 4), 0)
    plan_ref[5:6, :] = jnp.where(valid, pair, PAIRS) * WIDE
    plan_ref[6:7, :] = jnp.max(high, axis=0, keepdims=True) + 1
    plan_ref[7:8, :] = jnp.max(jnp.where(live, number + 1, 0), axis=0, keepdims=True)


def spread_kernel(
    frac_hbm, vel_hbm, mass_hbm, cells_hbm,
    far_ref, near_ref, layers_ref, plan_ref, frac_ref, vel_ref, cells_ref,
    listed_ref, start_ref, mass_ref, acc_ref, sems,
):
    slots = frac_ref.shape[1]
    sources = (cells_hbm, frac_hbm, vel_hbm, mass_hbm)
    targets = (cells_ref, frac_ref, vel_ref, mass_ref)
    arrivals = [
        pltpu.make_async_copy(source, target, sems.at[k])
        for k, (source, target) in enumerate(zip(sources, targets))
    ]
    for arrival in arrivals:
        arrival.start()
    acc_ref[...] = jnp.zeros_like(acc_ref)
    arrivals[0].wait()
    list_visits(cells_ref, plan_ref, start_ref)
    listing = pltpu.make_async_copy(plan_ref, listed_ref, sems.at[4])
    listing.start()
    for arrival in arrivals[1:]:
        arrival.wait()
    sublane = lax.broadcasted_iota(jnp.int32, (8, LANES), 0)
    lane = lax.broadcasted_iota(jnp.int32, (1, LANES), 1)
    top_z = sublane >= 4
    field = sublane & 3

    def weigh(part):
        at = pl.multiple_of(part * LANES, LANES)
        here = pl.ds(at, LANES)

        def spread_out(line):
            return jnp.broadcast_to(line, (8, LANES))

        fx, fy, fz = (spread_out(frac_ref[d : d + 1, here]) for d in range(3))
        vx, vy, vz = (spread_out(vel_ref[d : d + 1, here]) for d in range(3))
        live = cells_ref[pl.ds(part, 1), :] < LAST
        held = spread_out(jnp.where(live, mass_ref[pl.ds(part, 1), :], 0.0))
        carried = jnp.where(
            field == 0, held, held * jnp.where(field == 1, vx, jnp.where(field == 2, vy, vz))
        )
        carried = carried * jnp.where(top_z, fz, 1.0 - fz)
        lower, upper = carried * (1.0 - fx), carried * fx
        rows = jnp.concatenate(
            [lower * (1.0 - fy), lower * fy, upper * (1.0 - fy), upper * fy], axis=0
        )
        return jnp.concatenate(split_pair(rows), axis=0)

    def spread_one(block, offset):
        rel = relative(cells_ref, block, offset)
        row = (rel >> 7).astype(f32)
        shares = ([], [])
        for h in range(2):
            values = weigh(2 * block + h)
            which = jnp.broadcast_to(row[h : h + 1, :], values.shape).astype(bf16)
            for r in range(2):
                here = which == jnp.full(values.shape, r, bf16)
                shares[r].append(jnp.where(here, values, jnp.zeros_like(values)))
        both = lax.dot_general(
            jnp.concatenate([jnp.concatenate(share, axis=1) for share in shares], axis=0),
            one_hot(rel & (NZ - 1), NZ),
            (((1,), (1,)), ((), ())),
            preferred_element_type=f32,
        )
        first = both[:SPREAD] + both[SPREAD : 2 * SPREAD]
        second = both[2 * SPREAD : 3 * SPREAD] + both[3 * SPREAD :]
        return (
            jnp.concatenate([first[0:8], first[8:16] + second[0:8], second[8:16]], axis=0),
            jnp.concatenate([first[16:24], first[24:32] + second[16:24], second[24:32]], axis=0),
        )

    def add_to_nodes(base, parts):
        here = pl.ds(pl.multiple_of(base * 8, 8), 24)
        above = pl.ds(pl.multiple_of(base * 8, 8) + (NY + 1) * 8, 24)
        lower, upper = acc_ref[here, :], acc_ref[above, :]
        acc_ref[here, :] = lower + parts[0]
        acc_ref[above, :] = upper + parts[1]

    def first_pairs(group, carry):
        blocks = [group * GIVEN + u for u in range(GIVEN)]
        found = [spread_one(block, start_ref[pl.ds(block, 1), :]) for block in blocks]
        if carry is None:
            listing.wait()
        for block, parts in zip(blocks, found):
            add_to_nodes(listed_ref[0, block], parts)
        return carry

    first_pairs(0, None)
    found = [spread_one(listed_ref[1, pair], listed_ref[2, pair]) for pair in range(PAIRS)]
    for pair, parts in enumerate(found):
        add_to_nodes(2 * pair + (pair >> 4), parts)
    lax.fori_loop(1, (listed_ref[7, 0] + GIVEN - 1) // GIVEN, first_pairs, 0)

    odd = lax.axis_index("gx") % 2 == 1
    layers = []
    for l in range(CX + 1):
        first = l * (NY + 1) * 8
        acc_ref[first : first + 8, :] += acc_ref[first + NY * 8 : first + NY * 8 + 8, :]
        for f in range(4):
            lower = acc_ref[pl.ds(first + f, NY, stride=8), :]
            upper = acc_ref[pl.ds(first + 4 + f, NY, stride=8), :]
            layers.append(lower + pltpu.roll(upper, 1, 1))
            layers_ref[l * 4 + f] = layers[-1]
    for k in range(CX * 4):
        far_ref[k] = jnp.where(odd, layers[k + 4], layers[k])
        near_ref[k] = jnp.where(odd, layers[k], layers[k + 4])


def pair_up(field, axis):
    return field + pltpu.roll(field, field.shape[axis] - 1, axis)


def step_up(field, axis):
    return pltpu.roll(field, field.shape[axis] - 1, axis) - field


def pair_down(field, axis):
    return field + pltpu.roll(field, 1, axis)


def step_down(field, axis):
    return field - pltpu.roll(field, 1, axis)


def cell_stress(vel_lo, vel_hi, mass_lo, mass_hi, keep):
    grads = []
    for a in range(3):
        diff = vel_hi[a] - vel_lo[a]
        both = vel_hi[a] + vel_lo[a]
        grads.append(
            [
                0.25 * pair_up(pair_up(diff, 0), 1),
                0.25 * pair_up(step_up(both, 0), 1),
                0.25 * step_up(pair_up(both, 0), 1),
            ]
        )
    density = 0.125 * pair_up(pair_up(mass_hi + mass_lo, 0), 1)
    dxx = grads[0][0]
    dyy = grads[1][1]
    dzz = grads[2][2]
    dxy = 0.5 * (grads[0][1] + grads[1][0])
    dxz = 0.5 * (grads[0][2] + grads[2][0])
    dyz = 0.5 * (grads[1][2] + grads[2][1])
    second = dxx * dxx + dyy * dyy + dzz * dzz + 2.0 * (dxy * dxy + dxz * dxz + dyz * dyz)
    rate = jnp.sqrt(2.0 * second + rate_floor * rate_floor)
    pressure = stiffness * density
    inertial = rate * grain_size / jnp.sqrt(pressure + press_floor)
    friction = mu_static + (mu_limit - mu_static) * inertial / (inertia_ref + inertial)
    twice = 2.0 * friction * pressure / rate
    sigma = [
        twice * dxx - pressure,
        twice * dyy - pressure,
        twice * dzz - pressure,
        twice * dxy,
        twice * dxz,
        twice * dyz,
    ]
    return [jnp.where(keep, s, 0.0) for s in sigma]


def node_force(lower, upper):
    force = []
    for a in range(3):
        sx, sy, sz = (components[a][b] for b in range(3))
        along = pair_down(pair_down(upper[sx] - lower[sx], 0), 1)
        across = step_down(pair_down(upper[sy] + lower[sy], 1), 0)
        upward = step_down(pair_down(upper[sz] + lower[sz], 0), 1)
        force.append(0.25 * (along + across + upward))
    return force


def collect_kernel(
    step_ref, count_ref, plan_ref, layers_ref, far_new_ref, near_new_ref, frac_ref, vel_ref, cells_ref,
    out_ref, top_ref, listed_ref, tab_ref, pair_ref, sem,
):
    blocks = frac_ref.shape[1] // BLOCK
    listing = pltpu.make_async_copy(plan_ref, listed_ref, sem)
    listing.start()
    step = step_ref[0]
    odd = lax.axis_index("gx") % 2 == 1

    def pick(if_odd, if_even):
        return [jnp.where(odd, if_odd[k], if_even[k]) for k in range(4 * CX)]

    own = [layers_ref[k] for k in range(4 * (CX + 1))]
    left, right = pick(near_new_ref, far_new_ref), pick(far_new_ref, near_new_ref)
    nodes = [
        left[:4],
        [own[f] + left[4 + f] for f in range(4)],
        own[4:8],
        [own[8 + f] + right[f] for f in range(4)],
        right[4:],
    ]
    height = lax.broadcasted_iota(jnp.int32, (NY, NZ), 1)
    keep = height < NZ - 1
    above_bed = height > 0
    floor = [jnp.maximum(layer[0], mass_floor) for layer in nodes]
    v_old = [[layer[1 + a] / floor[l] for a in range(3)] for l, layer in enumerate(nodes)]
    sigma = [
        cell_stress(v_old[l], v_old[l + 1], nodes[l][0], nodes[l + 1][0], keep) for l in range(4)
    ]
    blank = jnp.zeros((NY, NZ), f32)
    for l in range(CX + 1):
        force = node_force(sigma[l], sigma[l + 1])
        fields = [blank] * 8
        for a in range(3):
            layer = nodes[l + 1]
            fresh = (layer[1 + a] + step * (force[a] + layer[0] * gravity[a])) / floor[l + 1]
            fresh = jnp.where(above_bed, fresh, 0.0)
            fields[a] = fresh - flip_share * v_old[l + 1][a]
            fields[4 + a] = step * fresh
        for k, value in enumerate(fields):
            start = l * NY * TABLE + k
            tab_ref[pl.ds(start, NY, stride=TABLE), :] = value
            tab_ref[pl.ds(start + 8, NY, stride=TABLE), :] = pltpu.roll(value, NZ - 1, 1)

    for l in range(CX + 1):

        def split_row(j, carry):
            at = pl.ds(pl.multiple_of((l * NY + j) * TABLE, TABLE), TABLE)
            high, low = split_pair(tab_ref[at, :])
            pair_ref[pl.ds(l * (NY + 1) + j, 1)] = jnp.concatenate([high, low], axis=0)[None]
            return carry

        lax.fori_loop(0, NY, split_row, 0, unroll=8)
        pair_ref[l * (NY + 1) + NY] = pair_ref[l * (NY + 1)]

    out_ref[...] = jnp.zeros_like(out_ref)
    listing.wait()
    total = listed_ref[6, 0]
    count = count_ref[0]
    lane = lax.broadcasted_iota(jnp.int32, (2, LANES), 1)
    half = lax.broadcasted_iota(jnp.int32, (2, LANES), 0)

    def visit(group, top):
        found = []
        for u in range(TAKEN):
            v = group * TAKEN + u
            block = listed_ref[3, v]
            base = listed_ref[4, v]
            rel = relative(cells_ref, block, listed_ref[5, v])
            hot = one_hot(rel, WIDE)
            rows = []
            for a in range(2):
                three = [pair_ref[base + a * (NY + 1) + k] for k in range(3)]
                rows += [jnp.concatenate(three[b : b + 2], axis=1) for b in range(2)]
            both = jnp.dot(jnp.concatenate(rows, axis=0), hot, preferred_element_type=f32)
            corners = []
            for k in range(4):
                four = both[2 * TABLE * k : 2 * TABLE * (k + 1)]
                corners += [four[0:8] + four[16:24], four[8:16] + four[24:32]]
            here = pl.ds(pl.multiple_of(block * BLOCK, BLOCK), BLOCK)
            frac = frac_ref[:, here]
            for d in (2, 1, 0):
                share = frac[d : d + 1, :]
                corners = [
                    corners[k] + share * (corners[k + 1] - corners[k])
                    for k in range(0, len(corners), 2)
                ]
            fresh = flip_share * vel_ref[:, here] + corners[0][0:3]
            square = jnp.sum(fresh * fresh, axis=0, keepdims=True)
            slot = block * BLOCK + half * LANES + lane
            taken = (rel >= 0) & (rel < WIDE) & (slot < count)
            for h in range(2):
                part = square[:, h * LANES : (h + 1) * LANES]
                top = jnp.maximum(top, jnp.where(taken[h : h + 1], part, 0.0))
            found.append((block, corners[0]))
        for block, part in found:
            out_ref[pl.ds(block, 1)] += part[None]
        return top

    top = jnp.zeros((1, LANES), f32)
    for group in range(2):
        top = visit(group, top)
    top = lax.fori_loop(2, (total + TAKEN - 1) // TAKEN, visit, top)
    top = jnp.sqrt(jnp.max(top, axis=1, keepdims=True))
    top_ref[...] = jnp.broadcast_to(top, top_ref.shape)


def finish_kernel(cells_ref, moved_ref, frac_ref, vel_ref, new_frac_ref, new_vel_ref):
    blocks = frac_ref.shape[1] // BLOCK

    def finish(block, carry):
        at = pl.multiple_of(block * BLOCK, BLOCK)
        here = pl.ds(at, BLOCK)
        cells = cells_ref[pl.ds(block * 2, 2), :]
        alive = jnp.concatenate([cells[0:1], cells[1:2]], axis=1) < LAST
        got = moved_ref[pl.ds(block, 1)][0]
        new_vel_ref[:, here] = jnp.where(alive, flip_share * vel_ref[:, here] + got[0:3], 0.0)
        new_frac_ref[:, here] = jnp.where(alive, frac_ref[:, here] + got[4:7], 0.0)
        return carry

    lax.fori_loop(0, blocks, finish, 0, unroll=4)


def largest(value, axis):
    devices = lax.axis_size(axis)
    reach = 1
    while reach < devices:
        if devices & (devices - 1) == 0:
            pairs = [(i, i ^ (reach | 1)) for i in range(devices)]
        else:
            pairs = [(i, (i + reach) % devices) for i in range(devices)]
        value = jnp.maximum(value, lax.ppermute(value, axis, pairs))
        reach *= 2
    return value


smem = pl.BlockSpec(memory_space=pltpu.SMEM)
vmem = pl.BlockSpec(memory_space=pltpu.VMEM)
hbm = pl.BlockSpec(memory_space=pltpu.HBM)


def body(frac, velocity, mass, particle_cell, tile_count, time_step):
    slots = frac.shape[1]
    blocks = slots // BLOCK
    rows = slots // LANES
    inputs = (frac, velocity, mass.reshape(rows, LANES), particle_cell.reshape(rows, LANES))
    far, near, layers, plan, frac_here, vel_here, cells_here = pl.pallas_call(
        spread_kernel,
        out_shape=(
            pltpu.VMEM((4 * CX, NY, NZ), f32),
            pltpu.VMEM((4 * CX, NY, NZ), f32),
            pltpu.VMEM((4 * (CX + 1), NY, NZ), f32),
            pltpu.VMEM((8, LANES), jnp.int32),
            pltpu.VMEM(frac.shape, f32),
            pltpu.VMEM(velocity.shape, f32),
            pltpu.VMEM((rows, LANES), jnp.int32),
        ),
        in_specs=[hbm] * 4,
        out_specs=(vmem,) * 7,
        scratch_shapes=[
            pltpu.SMEM((8, LANES), jnp.int32),
            pltpu.VMEM((blocks, LANES), jnp.int32),
            pltpu.VMEM((rows, LANES), f32),
            pltpu.VMEM(((CX + 1) * (NY + 1) * 8, NZ), f32),
            pltpu.SemaphoreType.DMA((5,)),
        ],
        compiler_params=pltpu.CompilerParams(vmem_limit_bytes=32 * 1024 * 1024),
        name="spread",
    )(*[pltpu.with_memory_space_constraint(x, pltpu.HBM) for x in inputs])
    devices = lax.axis_size("gx")
    far_pairs = [(i, (i + (1 if i % 2 else -1)) % devices) for i in range(devices)]
    near_pairs = [(i, i ^ 1) for i in range(devices)]
    far_new = lax.ppermute(far, "gx", far_pairs)
    near_new = lax.ppermute(near, "gx", near_pairs)
    moved, top = pl.pallas_call(
        collect_kernel,
        out_shape=(
            jax.ShapeDtypeStruct((blocks, 8, BLOCK), f32),
            jax.ShapeDtypeStruct((8, LANES), f32),
        ),
        in_specs=[smem] * 2 + [vmem] * 7,
        out_specs=(vmem, vmem),
        scratch_shapes=[
            pltpu.SMEM((8, LANES), jnp.int32),
            pltpu.VMEM(((CX + 1) * NY * TABLE, NZ), f32),
            pltpu.VMEM(((CX + 1) * (NY + 1), 2 * TABLE, NZ), bf16),
            pltpu.SemaphoreType.DMA,
        ],
        compiler_params=pltpu.CompilerParams(vmem_limit_bytes=32 * 1024 * 1024),
        name="collect",
    )(time_step, tile_count, plan, layers, far_new, near_new, frac_here, vel_here, cells_here)
    new_frac, new_velocity = pl.pallas_call(
        finish_kernel,
        out_shape=(
            jax.ShapeDtypeStruct(frac.shape, f32),
            jax.ShapeDtypeStruct(velocity.shape, f32),
        ),
        in_specs=[vmem] * 4,
        out_specs=(vmem, vmem),
        compiler_params=pltpu.CompilerParams(vmem_limit_bytes=32 * 1024 * 1024),
        cost_estimate=pl.CostEstimate(flops=0, bytes_accessed=8000000, transcendentals=0),
        name="finish",
    )(cells_here, moved, frac_here, vel_here)
    fastest = largest(top, "gx")
    next_step = (courant / (fastest + wave_speed))[0, :1]
    return (new_frac, new_velocity, next_step)


def solution(mesh):
    placed = (
        P(None, ("runs", "gx")),
        P(None, ("runs", "gx")),
        P(("runs", "gx")),
        P(("runs", "gx")),
        P(("runs", "gx")),
        P("runs"),
    )
    return jax.shard_map(
        body,
        mesh=mesh,
        in_specs=placed,
        out_specs=(P(None, ("runs", "gx")), P(None, ("runs", "gx")), P("runs")),
        check_vma=False,
    )
```

```python
import functools

import jax
import jax.numpy as jnp
from jax import lax
from jax.experimental import pallas as pl
from jax.experimental.pallas import tpu as pltpu
from jax.sharding import PartitionSpec as P

CX = 2
NY = 32
NZ = 128
ROWS = CX * NY
PAIRS = ROWS // 2
LAST = ROWS * NZ - 1
WIDE = 2 * NZ
TALL = 4
BLOCK = 256
LANES = 128
GIVEN = 32
TAKEN = 32
SPREAD = 32
TABLE = 16

mass_floor = 0.25
stiffness = 2.0
press_floor = 1.0
grain_size = 0.5
inertia_ref = 0.3
mu_static = 0.38
mu_limit = 0.64
rate_floor = 0.5
gravity = (0.5, 0.0, -0.866)
flip_share = 0.95
courant = 0.4
wave_speed = 2.0
components = ((0, 3, 4), (3, 1, 5), (4, 5, 2))
f32 = jnp.float32
bf16 = jnp.bfloat16


def split_pair(values):
    high = values.astype(bf16)
    low = (values - high.astype(f32)).astype(bf16)
    return high, low


def relative(cells_ref, block, offset):
    return cells_ref[pl.ds(block * 2, 2), :] - offset


def one_hot(rel, wide):
    tall = (16, LANES)
    nodes = lax.broadcasted_iota(jnp.int32, tall, 0).astype(f32)
    one, zero = jnp.ones(tall, bf16), jnp.zeros(tall, bf16)
    halves = []
    for h in range(2):
        line = jnp.broadcast_to(rel[h : h + 1, :].astype(f32), tall).astype(bf16)
        parts = [
            jnp.where(line == (nodes + z).astype(bf16), one, zero) for z in range(0, wide, 16)
        ]
        halves.append(jnp.concatenate(parts, axis=0))
    return jnp.concatenate(halves, axis=1)


def list_visits(cells_ref, plan_ref, start_ref):
    blocks = cells_ref.shape[0] // 2
    shape = (blocks, LANES)
    number = lax.broadcasted_iota(jnp.int32, shape, 0)
    lane = lax.broadcasted_iota(jnp.int32, shape, 1)
    first_half = cells_ref[pl.ds(0, blocks, stride=2), :]
    second_half = cells_ref[pl.ds(1, blocks, stride=2), :]
    reached = jnp.maximum(
        jnp.where(first_half < LAST, first_half, 0), jnp.where(second_half < LAST, second_half, 0)
    )
    first = jnp.min(first_half, axis=1, keepdims=True)
    live = first < LAST
    last = jnp.max(reached, axis=1, keepdims=True)
    first_four, last_four = first >> 9, last >> 9
    start_ref[...] = jnp.broadcast_to(first_four * (TALL * NZ), shape)
    four = jnp.max(jnp.where(number == lane, first_four, 0), axis=0, keepdims=True)
    plan_ref[0:1, :] = TALL * four + (four >> 3)
    within = live & (first_four < lane) & (lane <= last_four)
    block = jnp.max(jnp.where(within, number, -1), axis=0, keepdims=True)
    plan_ref[1:2, :] = jnp.maximum(block, 0)
    plan_ref[2:3, :] = jnp.where(block >= 0, lane[:1] * TALL, ROWS) * NZ
    first_pair, last_pair = first >> 8, last >> 8
    low = jnp.where(live, first_pair + number, 2 * LANES)
    high = jnp.where(live, last_pair + number, -1)
    inside = (low <= lane) & (lane <= high)
    block = jnp.max(jnp.where(inside, number, -1), axis=0, keepdims=True)
    valid = block >= 0
    pair = lane[:1] - block
    plan_ref[3:4, :] = jnp.where(valid, block, 0)
    plan_ref[4:5, :] = jnp.where(valid, 2 * pair + (pair >> 4), 0)
    plan_ref[5:6, :] = jnp.where(valid, pair, PAIRS) * WIDE
    plan_ref[6:7, :] = jnp.max(high, axis=0, keepdims=True) + 1
    plan_ref[7:8, :] = jnp.max(jnp.where(live, number + 1, 0), axis=0, keepdims=True)


def spread_kernel(
    frac_hbm, vel_hbm, mass_hbm, cells_hbm,
    far_ref, near_ref, layers_ref, plan_ref, frac_ref, vel_ref, cells_ref,
    listed_ref, start_ref, mass_ref, acc_ref, sems,
):
    slots = frac_ref.shape[1]
    sources = (cells_hbm, frac_hbm, vel_hbm, mass_hbm)
    targets = (cells_ref, frac_ref, vel_ref, mass_ref)
    arrivals = [
        pltpu.make_async_copy(source, target, sems.at[k])
        for k, (source, target) in enumerate(zip(sources, targets))
    ]
    for arrival in arrivals:
        arrival.start()
    acc_ref[...] = jnp.zeros_like(acc_ref)
    arrivals[0].wait()
    list_visits(cells_ref, plan_ref, start_ref)
    listing = pltpu.make_async_copy(plan_ref, listed_ref, sems.at[4])
    listing.start()
    for arrival in arrivals[1:]:
        arrival.wait()
    sublane = lax.broadcasted_iota(jnp.int32, (8, LANES), 0)
    lane = lax.broadcasted_iota(jnp.int32, (1, LANES), 1)
    top_z = sublane >= 4
    field = sublane & 3

    def weigh(part):
        at = pl.multiple_of(part * LANES, LANES)
        here = pl.ds(at, LANES)

        def spread_out(line):
            return jnp.broadcast_to(line, (8, LANES))

        fx, fy, fz = (spread_out(frac_ref[d : d + 1, here]) for d in range(3))
        vx, vy, vz = (spread_out(vel_ref[d : d + 1, here]) for d in range(3))
        live = cells_ref[pl.ds(part, 1), :] < LAST
        held = spread_out(jnp.where(live, mass_ref[pl.ds(part, 1), :], 0.0))
        carried = jnp.where(
            field == 0, held, held * jnp.where(field == 1, vx, jnp.where(field == 2, vy, vz))
        )
        carried = carried * jnp.where(top_z, fz, 1.0 - fz)
        lower, upper = carried * (1.0 - fx), carried * fx
        rows = jnp.concatenate(
            [lower * (1.0 - fy), lower * fy, upper * (1.0 - fy), upper * fy], axis=0
        )
        return jnp.concatenate(split_pair(rows), axis=0)

    def spread_one(block, offset):
        rel = relative(cells_ref, block, offset)
        row = (rel >> 7).astype(f32)
        shares = [[] for _ in range(TALL)]
        for h in range(2):
            values = weigh(2 * block + h)
            which = jnp.broadcast_to(row[h : h + 1, :], values.shape).astype(bf16)
            for r in range(TALL):
                here = which == jnp.full(values.shape, r, bf16)
                shares[r].append(jnp.where(here, values, jnp.zeros_like(values)))
        both = lax.dot_general(
            jnp.concatenate([jnp.concatenate(share, axis=1) for share in shares], axis=0),
            one_hot(rel & (NZ - 1), NZ),
            (((1,), (1,)), ((), ())),
            preferred_element_type=f32,
        )
        sums = []
        for r in range(TALL):
            at = 2 * SPREAD * r
            sums.append(both[at : at + SPREAD] + both[at + SPREAD : at + 2 * SPREAD])
        parts = []
        for a in (0, 16):
            lines = [sums[0][a : a + 8]]
            lines += [sums[r - 1][a + 8 : a + 16] + sums[r][a : a + 8] for r in range(1, TALL)]
            parts.append(jnp.concatenate(lines + [sums[-1][a + 8 : a + 16]], axis=0))
        return parts

    def add_to_nodes(base, parts):
        here = pl.ds(pl.multiple_of(base * 8, 8), (TALL + 1) * 8)
        above = pl.ds(pl.multiple_of(base * 8, 8) + (NY + 1) * 8, (TALL + 1) * 8)
        lower, upper = acc_ref[here, :], acc_ref[above, :]
        acc_ref[here, :] = lower + parts[0]
        acc_ref[above, :] = upper + parts[1]

    def first_fours(group, carry):
        blocks = [group * GIVEN + u for u in range(GIVEN)]
        found = [spread_one(block, start_ref[pl.ds(block, 1), :]) for block in blocks]
        if carry is None:
            listing.wait()
        for block, parts in zip(blocks, found):
            add_to_nodes(listed_ref[0, block], parts)
        return carry

    first_fours(0, None)
    found = [spread_one(listed_ref[1, k], listed_ref[2, k]) for k in range(ROWS // TALL)]
    for k, parts in enumerate(found):
        add_to_nodes(TALL * k + (k >> 3), parts)
    lax.fori_loop(1, (listed_ref[7, 0] + GIVEN - 1) // GIVEN, first_fours, 0)

    odd = lax.axis_index("gx") % 2 == 1
    layers = []
    for l in range(CX + 1):
        first = l * (NY + 1) * 8
        acc_ref[first : first + 8, :] += acc_ref[first + NY * 8 : first + NY * 8 + 8, :]
        for f in range(4):
            lower = acc_ref[pl.ds(first + f, NY, stride=8), :]
            upper = acc_ref[pl.ds(first + 4 + f, NY, stride=8), :]
            layers.append(lower + pltpu.roll(upper, 1, 1))
            layers_ref[l * 4 + f] = layers[-1]
    for k in range(CX * 4):
        far_ref[k] = jnp.where(odd, layers[k + 4], layers[k])
        near_ref[k] = jnp.where(odd, layers[k], layers[k + 4])


def pair_up(field, axis):
    return field + pltpu.roll(field, field.shape[axis] - 1, axis)


def step_up(field, axis):
    return pltpu.roll(field, field.shape[axis] - 1, axis) - field


def pair_down(field, axis):
    return field + pltpu.roll(field, 1, axis)


def step_down(field, axis):
    return field - pltpu.roll(field, 1, axis)


def cell_stress(vel_lo, vel_hi, mass_lo, mass_hi, keep):
    grads = []
    for a in range(3):
        diff = vel_hi[a] - vel_lo[a]
        both = vel_hi[a] + vel_lo[a]
        grads.append(
            [
                0.25 * pair_up(pair_up(diff, 0), 1),
                0.25 * pair_up(step_up(both, 0), 1),
                0.25 * step_up(pair_up(both, 0), 1),
            ]
        )
    density = 0.125 * pair_up(pair_up(mass_hi + mass_lo, 0), 1)
    dxx = grads[0][0]
    dyy = grads[1][1]
    dzz = grads[2][2]
    dxy = 0.5 * (grads[0][1] + grads[1][0])
    dxz = 0.5 * (grads[0][2] + grads[2][0])
    dyz = 0.5 * (grads[1][2] + grads[2][1])
    second = dxx * dxx + dyy * dyy + dzz * dzz + 2.0 * (dxy * dxy + dxz * dxz + dyz * dyz)
    rate = jnp.sqrt(2.0 * second + rate_floor * rate_floor)
    pressure = stiffness * density
    inertial = rate * grain_size / jnp.sqrt(pressure + press_floor)
    friction = mu_static + (mu_limit - mu_static) * inertial / (inertia_ref + inertial)
    twice = 2.0 * friction * pressure / rate
    sigma = [
        twice * dxx - pressure,
        twice * dyy - pressure,
        twice * dzz - pressure,
        twice * dxy,
        twice * dxz,
        twice * dyz,
    ]
    return [jnp.where(keep, s, 0.0) for s in sigma]


def node_force(lower, upper):
    force = []
    for a in range(3):
        sx, sy, sz = (components[a][b] for b in range(3))
        along = pair_down(pair_down(upper[sx] - lower[sx], 0), 1)
        across = step_down(pair_down(upper[sy] + lower[sy], 1), 0)
        upward = step_down(pair_down(upper[sz] + lower[sz], 0), 1)
        force.append(0.25 * (along + across + upward))
    return force


def collect_kernel(
    step_ref, count_ref, plan_ref, layers_ref, far_new_ref, near_new_ref, frac_ref, vel_ref, cells_ref,
    out_ref, top_ref, listed_ref, tab_ref, pair_ref, sem,
):
    blocks = frac_ref.shape[1] // BLOCK
    listing = pltpu.make_async_copy(plan_ref, listed_ref, sem)
    listing.start()
    step = step_ref[0]
    odd = lax.axis_index("gx") % 2 == 1

    def pick(if_odd, if_even):
        return [jnp.where(odd, if_odd[k], if_even[k]) for k in range(4 * CX)]

    own = [layers_ref[k] for k in range(4 * (CX + 1))]
    left, right = pick(near_new_ref, far_new_ref), pick(far_new_ref, near_new_ref)
    nodes = [
        left[:4],
        [own[f] + left[4 + f] for f in range(4)],
        own[4:8],
        [own[8 + f] + right[f] for f in range(4)],
        right[4:],
    ]
    height = lax.broadcasted_iota(jnp.int32, (NY, NZ), 1)
    keep = height < NZ - 1
    above_bed = height > 0
    floor = [jnp.maximum(layer[0], mass_floor) for layer in nodes]
    v_old = [[layer[1 + a] / floor[l] for a in range(3)] for l, layer in enumerate(nodes)]
    sigma = [
        cell_stress(v_old[l], v_old[l + 1], nodes[l][0], nodes[l + 1][0], keep) for l in range(4)
    ]
    blank = jnp.zeros((NY, NZ), f32)
    for l in range(CX + 1):
        force = node_force(sigma[l], sigma[l + 1])
        fields = [blank] * 8
        for a in range(3):
            layer = nodes[l + 1]
            fresh = (layer[1 + a] + step * (force[a] + layer[0] * gravity[a])) / floor[l + 1]
            fresh = jnp.where(above_bed, fresh, 0.0)
            fields[a] = fresh - flip_share * v_old[l + 1][a]
            fields[4 + a] = step * fresh
        for k, value in enumerate(fields):
            start = l * NY * TABLE + k
            tab_ref[pl.ds(start, NY, stride=TABLE), :] = value
            tab_ref[pl.ds(start + 8, NY, stride=TABLE), :] = pltpu.roll(value, NZ - 1, 1)

    for l in range(CX + 1):

        def split_row(j, carry):
            at = pl.ds(pl.multiple_of((l * NY + j) * TABLE, TABLE), TABLE)
            high, low = split_pair(tab_ref[at, :])
            pair_ref[pl.ds(l * (NY + 1) + j, 1)] = jnp.concatenate([high, low], axis=0)[None]
            return carry

        lax.fori_loop(0, NY, split_row, 0, unroll=8)
        pair_ref[l * (NY + 1) + NY] = pair_ref[l * (NY + 1)]

    out_ref[...] = jnp.zeros_like(out_ref)
    listing.wait()
    total = listed_ref[6, 0]
    count = count_ref[0]
    lane = lax.broadcasted_iota(jnp.int32, (2, LANES), 1)
    half = lax.broadcasted_iota(jnp.int32, (2, LANES), 0)

    def visit(group, top):
        found = []
        for u in range(TAKEN):
            v = group * TAKEN + u
            block = listed_ref[3, v]
            base = listed_ref[4, v]
            rel = relative(cells_ref, block, listed_ref[5, v])
            hot = one_hot(rel, WIDE)
            rows = []
            for a in range(2):
                three = [pair_ref[base + a * (NY + 1) + k] for k in range(3)]
                rows += [jnp.concatenate(three[b : b + 2], axis=1) for b in range(2)]
            both = jnp.dot(jnp.concatenate(rows, axis=0), hot, preferred_element_type=f32)
            corners = []
            for k in range(4):
                four = both[2 * TABLE * k : 2 * TABLE * (k + 1)]
                corners += [four[0:8] + four[16:24], four[8:16] + four[24:32]]
            here = pl.ds(pl.multiple_of(block * BLOCK, BLOCK), BLOCK)
            frac = frac_ref[:, here]
            for d in (2, 1, 0):
                share = frac[d : d + 1, :]
                corners = [
                    corners[k] + share * (corners[k + 1] - corners[k])
                    for k in range(0, len(corners), 2)
                ]
            fresh = flip_share * vel_ref[:, here] + corners[0][0:3]
            square = jnp.sum(fresh * fresh, axis=0, keepdims=True)
            slot = block * BLOCK + half * LANES + lane
            taken = (rel >= 0) & (rel < WIDE) & (slot < count)
            for h in range(2):
                part = square[:, h * LANES : (h + 1) * LANES]
                top = jnp.maximum(top, jnp.where(taken[h : h + 1], part, 0.0))
            found.append((block, corners[0]))
        for block, part in found:
            out_ref[pl.ds(block, 1)] += part[None]
        return top

    top = jnp.zeros((1, LANES), f32)
    for group in range(2):
        top = visit(group, top)
    top = lax.fori_loop(2, (total + TAKEN - 1) // TAKEN, visit, top)
    top = jnp.sqrt(jnp.max(top, axis=1, keepdims=True))
    top_ref[...] = jnp.broadcast_to(top, top_ref.shape)


def finish_kernel(cells_ref, moved_ref, frac_ref, vel_ref, new_frac_ref, new_vel_ref):
    blocks = frac_ref.shape[1] // BLOCK

    def finish(block, carry):
        at = pl.multiple_of(block * BLOCK, BLOCK)
        here = pl.ds(at, BLOCK)
        cells = cells_ref[pl.ds(block * 2, 2), :]
        alive = jnp.concatenate([cells[0:1], cells[1:2]], axis=1) < LAST
        got = moved_ref[pl.ds(block, 1)][0]
        new_vel_ref[:, here] = jnp.where(alive, flip_share * vel_ref[:, here] + got[0:3], 0.0)
        new_frac_ref[:, here] = jnp.where(alive, frac_ref[:, here] + got[4:7], 0.0)
        return carry

    lax.fori_loop(0, blocks, finish, 0, unroll=4)


def largest(value, axis):
    devices = lax.axis_size(axis)
    reach = 1
    while reach < devices:
        if devices & (devices - 1) == 0:
            pairs = [(i, i ^ (reach | 1)) for i in range(devices)]
        else:
            pairs = [(i, (i + reach) % devices) for i in range(devices)]
        value = jnp.maximum(value, lax.ppermute(value, axis, pairs))
        reach *= 2
    return value


smem = pl.BlockSpec(memory_space=pltpu.SMEM)
vmem = pl.BlockSpec(memory_space=pltpu.VMEM)
hbm = pl.BlockSpec(memory_space=pltpu.HBM)


def body(frac, velocity, mass, particle_cell, tile_count, time_step):
    slots = frac.shape[1]
    blocks = slots // BLOCK
    rows = slots // LANES
    inputs = (frac, velocity, mass.reshape(rows, LANES), particle_cell.reshape(rows, LANES))
    far, near, layers, plan, frac_here, vel_here, cells_here = pl.pallas_call(
        spread_kernel,
        out_shape=(
            pltpu.VMEM((4 * CX, NY, NZ), f32),
            pltpu.VMEM((4 * CX, NY, NZ), f32),
            pltpu.VMEM((4 * (CX + 1), NY, NZ), f32),
            pltpu.VMEM((8, LANES), jnp.int32),
            pltpu.VMEM(frac.shape, f32),
            pltpu.VMEM(velocity.shape, f32),
            pltpu.VMEM((rows, LANES), jnp.int32),
        ),
        in_specs=[hbm] * 4,
        out_specs=(vmem,) * 7,
        scratch_shapes=[
            pltpu.SMEM((8, LANES), jnp.int32),
            pltpu.VMEM((blocks, LANES), jnp.int32),
            pltpu.VMEM((rows, LANES), f32),
            pltpu.VMEM(((CX + 1) * (NY + 1) * 8, NZ), f32),
            pltpu.SemaphoreType.DMA((5,)),
        ],
        compiler_params=pltpu.CompilerParams(vmem_limit_bytes=32 * 1024 * 1024),
        name="spread",
    )(*[pltpu.with_memory_space_constraint(x, pltpu.HBM) for x in inputs])
    devices = lax.axis_size("gx")
    far_pairs = [(i, (i + (1 if i % 2 else -1)) % devices) for i in range(devices)]
    near_pairs = [(i, i ^ 1) for i in range(devices)]
    far_new = lax.ppermute(far, "gx", far_pairs)
    near_new = lax.ppermute(near, "gx", near_pairs)
    moved, top = pl.pallas_call(
        collect_kernel,
        out_shape=(
            jax.ShapeDtypeStruct((blocks, 8, BLOCK), f32),
            jax.ShapeDtypeStruct((8, LANES), f32),
        ),
        in_specs=[smem] * 2 + [vmem] * 7,
        out_specs=(vmem, vmem),
        scratch_shapes=[
            pltpu.SMEM((8, LANES), jnp.int32),
            pltpu.VMEM(((CX + 1) * NY * TABLE, NZ), f32),
            pltpu.VMEM(((CX + 1) * (NY + 1), 2 * TABLE, NZ), bf16),
            pltpu.SemaphoreType.DMA,
        ],
        compiler_params=pltpu.CompilerParams(vmem_limit_bytes=32 * 1024 * 1024),
        name="collect",
    )(time_step, tile_count, plan, layers, far_new, near_new, frac_here, vel_here, cells_here)
    new_frac, new_velocity = pl.pallas_call(
        finish_kernel,
        out_shape=(
            jax.ShapeDtypeStruct(frac.shape, f32),
            jax.ShapeDtypeStruct(velocity.shape, f32),
        ),
        in_specs=[vmem] * 4,
        out_specs=(vmem, vmem),
        compiler_params=pltpu.CompilerParams(vmem_limit_bytes=32 * 1024 * 1024),
        cost_estimate=pl.CostEstimate(flops=0, bytes_accessed=8000000, transcendentals=0),
        name="finish",
    )(cells_here, moved, frac_here, vel_here)
    fastest = largest(top, "gx")
    next_step = (courant / (fastest + wave_speed))[0, :1]
    return (new_frac, new_velocity, next_step)


def solution(mesh):
    placed = (
        P(None, ("runs", "gx")),
        P(None, ("runs", "gx")),
        P(("runs", "gx")),
        P(("runs", "gx")),
        P(("runs", "gx")),
        P("runs"),
    )
    return jax.shard_map(
        body,
        mesh=mesh,
        in_specs=placed,
        out_specs=(P(None, ("runs", "gx")), P(None, ("runs", "gx")), P("runs")),
        check_vma=False,
    )
```

```python
import functools

import jax
import jax.numpy as jnp
from jax import lax
from jax.experimental import pallas as pl
from jax.experimental.pallas import tpu as pltpu
from jax.sharding import PartitionSpec as P

CX = 2
NY = 32
NZ = 128
ROWS = CX * NY
PAIRS = ROWS // 2
LAST = ROWS * NZ - 1
WIDE = 2 * NZ
BLOCK = 256
LANES = 128
GIVEN = 16
TAKEN = 16
SPREAD = 32
TABLE = 16

mass_floor = 0.25
stiffness = 2.0
press_floor = 1.0
grain_size = 0.5
inertia_ref = 0.3
mu_static = 0.38
mu_limit = 0.64
rate_floor = 0.5
gravity = (0.5, 0.0, -0.866)
flip_share = 0.95
courant = 0.4
wave_speed = 2.0
components = ((0, 3, 4), (3, 1, 5), (4, 5, 2))
f32 = jnp.float32
bf16 = jnp.bfloat16


def split_pair(values):
    high = values.astype(bf16)
    low = (values - high.astype(f32)).astype(bf16)
    return high, low


def relative(cells_ref, block, offset):
    return cells_ref[pl.ds(block * 2, 2), :] - offset


def one_hot(rel, wide):
    tall = (16, LANES)
    nodes = lax.broadcasted_iota(jnp.int32, tall, 0).astype(f32)
    one, zero = jnp.ones(tall, bf16), jnp.zeros(tall, bf16)
    halves = []
    for h in range(2):
        line = jnp.broadcast_to(rel[h : h + 1, :].astype(f32), tall).astype(bf16)
        parts = [
            jnp.where(line == (nodes + z).astype(bf16), one, zero) for z in range(0, wide, 16)
        ]
        halves.append(jnp.concatenate(parts, axis=0))
    return jnp.concatenate(halves, axis=1)


def list_visits(cells_ref, plan_ref, start_ref):
    blocks = cells_ref.shape[0] // 2
    shape = (blocks, LANES)
    number = lax.broadcasted_iota(jnp.int32, shape, 0)
    lane = lax.broadcasted_iota(jnp.int32, shape, 1)
    first_half = cells_ref[pl.ds(0, blocks, stride=2), :]
    second_half = cells_ref[pl.ds(1, blocks, stride=2), :]
    reached = jnp.maximum(
        jnp.where(first_half < LAST, first_half, 0), jnp.where(second_half < LAST, second_half, 0)
    )
    first = jnp.min(first_half, axis=1, keepdims=True)
    live = first < LAST
    last = jnp.max(reached, axis=1, keepdims=True)
    first_pair, last_pair = first >> 8, last >> 8
    start_ref[...] = jnp.broadcast_to(first_pair * WIDE, shape)
    pair = jnp.max(jnp.where(number == lane, first_pair, 0), axis=0, keepdims=True)
    plan_ref[0:1, :] = 2 * pair + (pair >> 4)
    within = live & (first_pair < lane) & (lane <= last_pair)
    block = jnp.max(jnp.where(within, number, -1), axis=0, keepdims=True)
    plan_ref[1:2, :] = jnp.maximum(block, 0)
    plan_ref[2:3, :] = jnp.where(block >= 0, lane[:1], PAIRS) * WIDE
    low = jnp.where(live, first_pair + number, 2 * LANES)
    high = jnp.where(live, last_pair + number, -1)
    inside = (low <= lane) & (lane <= high)
    block = jnp.max(jnp.where(inside, number, -1), axis=0, keepdims=True)
    valid = block >= 0
    pair = lane[:1] - block
    plan_ref[3:4, :] = jnp.where(valid, block, 0)
    plan_ref[4:5, :] = jnp.where(valid, 2 * pair + (pair >> 4), 0)
    plan_ref[5:6, :] = jnp.where(valid, pair, PAIRS) * WIDE
    plan_ref[6:7, :] = jnp.max(high, axis=0, keepdims=True) + 1
    plan_ref[7:8, :] = jnp.max(jnp.where(live, number + 1, 0), axis=0, keepdims=True)


def spread_kernel(
    frac_hbm, vel_hbm, mass_hbm, cells_hbm,
    far_ref, near_ref, layers_ref, plan_ref, frac_ref, vel_ref, cells_ref,
    listed_ref, start_ref, mass_ref, acc_ref, sems,
):
    slots = frac_ref.shape[1]
    sources = (cells_hbm, frac_hbm, vel_hbm, mass_hbm)
    targets = (cells_ref, frac_ref, vel_ref, mass_ref)
    arrivals = [
        pltpu.make_async_copy(source, target, sems.at[k])
        for k, (source, target) in enumerate(zip(sources, targets))
    ]
    for arrival in arrivals:
        arrival.start()
    acc_ref[...] = jnp.zeros_like(acc_ref)
    arrivals[0].wait()
    list_visits(cells_ref, plan_ref, start_ref)
    listing = pltpu.make_async_copy(plan_ref, listed_ref, sems.at[4])
    listing.start()
    for arrival in arrivals[1:]:
        arrival.wait()
    sublane = lax.broadcasted_iota(jnp.int32, (8, LANES), 0)
    lane = lax.broadcasted_iota(jnp.int32, (1, LANES), 1)
    top_z = sublane >= 4
    field = sublane & 3

    def weigh(part):
        at = pl.multiple_of(part * LANES, LANES)
        here = pl.ds(at, LANES)

        def spread_out(line):
            return jnp.broadcast_to(line, (8, LANES))

        fx, fy, fz = (spread_out(frac_ref[d : d + 1, here]) for d in range(3))
        vx, vy, vz = (spread_out(vel_ref[d : d + 1, here]) for d in range(3))
        live = cells_ref[pl.ds(part, 1), :] < LAST
        held = spread_out(jnp.where(live, mass_ref[pl.ds(part, 1), :], 0.0))
        carried = jnp.where(
            field == 0, held, held * jnp.where(field == 1, vx, jnp.where(field == 2, vy, vz))
        )
        carried = carried * jnp.where(top_z, fz, 1.0 - fz)
        lower, upper = carried * (1.0 - fx), carried * fx
        rows = jnp.concatenate(
            [lower * (1.0 - fy), lower * fy, upper * (1.0 - fy), upper * fy], axis=0
        )
        return jnp.concatenate(split_pair(rows), axis=0)

    def spread_one(block, offset):
        rel = relative(cells_ref, block, offset)
        row = (rel >> 7).astype(f32)
        shares = ([], [])
        for h in range(2):
            values = weigh(2 * block + h)
            which = jnp.broadcast_to(row[h : h + 1, :], values.shape).astype(bf16)
            for r in range(2):
                here = which == jnp.full(values.shape, r, bf16)
                shares[r].append(jnp.where(here, values, jnp.zeros_like(values)))
        both = lax.dot_general(
            jnp.concatenate([jnp.concatenate(share, axis=1) for share in shares], axis=0),
            one_hot(rel & (NZ - 1), NZ),
            (((1,), (1,)), ((), ())),
            preferred_element_type=f32,
        )
        first = both[:SPREAD] + both[SPREAD : 2 * SPREAD]
        second = both[2 * SPREAD : 3 * SPREAD] + both[3 * SPREAD :]
        return (
            jnp.concatenate([first[0:8], first[8:16] + second[0:8], second[8:16]], axis=0),
            jnp.concatenate([first[16:24], first[24:32] + second[16:24], second[24:32]], axis=0),
        )

    def add_to_nodes(base, parts):
        here = pl.ds(pl.multiple_of(base * 8, 8), 24)
        above = pl.ds(pl.multiple_of(base * 8, 8) + (NY + 1) * 8, 24)
        lower, upper = acc_ref[here, :], acc_ref[above, :]
        acc_ref[here, :] = lower + parts[0]
        acc_ref[above, :] = upper + parts[1]

    def first_pairs(group, carry):
        blocks = [group * GIVEN + u for u in range(GIVEN)]
        found = [spread_one(block, start_ref[pl.ds(block, 1), :]) for block in blocks]
        if carry is None:
            listing.wait()
        for block, parts in zip(blocks, found):
            add_to_nodes(listed_ref[0, block], parts)
        return carry

    first_pairs(0, None)
    found = [spread_one(listed_ref[1, pair], listed_ref[2, pair]) for pair in range(PAIRS)]
    for pair, parts in enumerate(found):
        add_to_nodes(2 * pair + (pair >> 4), parts)
    lax.fori_loop(1, (listed_ref[7, 0] + GIVEN - 1) // GIVEN, first_pairs, 0)

    odd = lax.axis_index("gx") % 2 == 1
    layers = []
    for l in range(CX + 1):
        first = l * (NY + 1) * 8
        acc_ref[first : first + 8, :] += acc_ref[first + NY * 8 : first + NY * 8 + 8, :]
        for f in range(4):
            lower = acc_ref[pl.ds(first + f, NY, stride=8), :]
            upper = acc_ref[pl.ds(first + 4 + f, NY, stride=8), :]
            layers.append(lower + pltpu.roll(upper, 1, 1))
            layers_ref[l * 4 + f] = layers[-1]
    for k in range(CX * 4):
        far_ref[k] = jnp.where(odd, layers[k + 4], layers[k])
        near_ref[k] = jnp.where(odd, layers[k], layers[k + 4])


def pair_up(field, axis):
    return field + pltpu.roll(field, field.shape[axis] - 1, axis)


def step_up(field, axis):
    return pltpu.roll(field, field.shape[axis] - 1, axis) - field


def pair_down(field, axis):
    return field + pltpu.roll(field, 1, axis)


def step_down(field, axis):
    return field - pltpu.roll(field, 1, axis)


def cell_stress(vel_lo, vel_hi, mass_lo, mass_hi, keep):
    grads = []
    for a in range(3):
        diff = vel_hi[a] - vel_lo[a]
        both = vel_hi[a] + vel_lo[a]
        grads.append(
            [
                0.25 * pair_up(pair_up(diff, 0), 1),
                0.25 * pair_up(step_up(both, 0), 1),
                0.25 * step_up(pair_up(both, 0), 1),
            ]
        )
    density = 0.125 * pair_up(pair_up(mass_hi + mass_lo, 0), 1)
    dxx = grads[0][0]
    dyy = grads[1][1]
    dzz = grads[2][2]
    dxy = 0.5 * (grads[0][1] + grads[1][0])
    dxz = 0.5 * (grads[0][2] + grads[2][0])
    dyz = 0.5 * (grads[1][2] + grads[2][1])
    second = dxx * dxx + dyy * dyy + dzz * dzz + 2.0 * (dxy * dxy + dxz * dxz + dyz * dyz)
    rate = jnp.sqrt(2.0 * second + rate_floor * rate_floor)
    pressure = stiffness * density
    inertial = rate * grain_size / jnp.sqrt(pressure + press_floor)
    friction = mu_static + (mu_limit - mu_static) * inertial / (inertia_ref + inertial)
    twice = 2.0 * friction * pressure / rate
    sigma = [
        twice * dxx - pressure,
        twice * dyy - pressure,
        twice * dzz - pressure,
        twice * dxy,
        twice * dxz,
        twice * dyz,
    ]
    return [jnp.where(keep, s, 0.0) for s in sigma]


def node_force(lower, upper):
    force = []
    for a in range(3):
        sx, sy, sz = (components[a][b] for b in range(3))
        along = pair_down(pair_down(upper[sx] - lower[sx], 0), 1)
        across = step_down(pair_down(upper[sy] + lower[sy], 1), 0)
        upward = step_down(pair_down(upper[sz] + lower[sz], 0), 1)
        force.append(0.25 * (along + across + upward))
    return force


def collect_kernel(
    step_ref, count_ref, plan_ref, layers_ref, far_new_ref, near_new_ref, frac_ref, vel_ref, cells_ref,
    out_ref, top_ref, listed_ref, tab_ref, pair_ref, sem,
):
    blocks = frac_ref.shape[1] // BLOCK
    listing = pltpu.make_async_copy(plan_ref, listed_ref, sem)
    listing.start()
    step = step_ref[0]
    odd = lax.axis_index("gx") % 2 == 1

    def pick(if_odd, if_even):
        return [jnp.where(odd, if_odd[k], if_even[k]) for k in range(4 * CX)]

    own = [layers_ref[k] for k in range(4 * (CX + 1))]
    left, right = pick(near_new_ref, far_new_ref), pick(far_new_ref, near_new_ref)
    nodes = [
        left[:4],
        [own[f] + left[4 + f] for f in range(4)],
        own[4:8],
        [own[8 + f] + right[f] for f in range(4)],
        right[4:],
    ]
    height = lax.broadcasted_iota(jnp.int32, (NY, NZ), 1)
    keep = height < NZ - 1
    above_bed = height > 0
    floor = [jnp.maximum(layer[0], mass_floor) for layer in nodes]
    v_old = [[layer[1 + a] / floor[l] for a in range(3)] for l, layer in enumerate(nodes)]
    sigma = [
        cell_stress(v_old[l], v_old[l + 1], nodes[l][0], nodes[l + 1][0], keep) for l in range(4)
    ]
    blank = jnp.zeros((NY, NZ), f32)
    for l in range(CX + 1):
        force = node_force(sigma[l], sigma[l + 1])
        fields = [blank] * 8
        for a in range(3):
            layer = nodes[l + 1]
            fresh = (layer[1 + a] + step * (force[a] + layer[0] * gravity[a])) / floor[l + 1]
            fresh = jnp.where(above_bed, fresh, 0.0)
            fields[a] = fresh - flip_share * v_old[l + 1][a]
            fields[4 + a] = step * fresh
        for k, value in enumerate(fields):
            start = l * NY * TABLE + k
            tab_ref[pl.ds(start, NY, stride=TABLE), :] = value
            tab_ref[pl.ds(start + 8, NY, stride=TABLE), :] = pltpu.roll(value, NZ - 1, 1)

    for l in range(CX + 1):

        def split_row(j, carry):
            at = pl.ds(pl.multiple_of((l * NY + j) * TABLE, TABLE), TABLE)
            high, low = split_pair(tab_ref[at, :])
            pair_ref[pl.ds(l * (NY + 1) + j, 1)] = jnp.concatenate([high, low], axis=0)[None]
            return carry

        lax.fori_loop(0, NY, split_row, 0, unroll=8)
        pair_ref[l * (NY + 1) + NY] = pair_ref[l * (NY + 1)]

    out_ref[...] = jnp.zeros_like(out_ref)
    listing.wait()
    total = listed_ref[6, 0]
    count = count_ref[0]
    lane = lax.broadcasted_iota(jnp.int32, (2, LANES), 1)
    half = lax.broadcasted_iota(jnp.int32, (2, LANES), 0)

    def visit(group, top):
        found = []
        for u in range(TAKEN):
            v = group * TAKEN + u
            block = listed_ref[3, v]
            base = listed_ref[4, v]
            rel = relative(cells_ref, block, listed_ref[5, v])
            hot = one_hot(rel, WIDE)
            rows = []
            for a in range(2):
                three = [pair_ref[base + a * (NY + 1) + k] for k in range(3)]
                rows += [jnp.concatenate(three[b : b + 2], axis=1) for b in range(2)]
            both = jnp.dot(jnp.concatenate(rows, axis=0), hot, preferred_element_type=f32)
            corners = []
            for k in range(4):
                four = both[2 * TABLE * k : 2 * TABLE * (k + 1)]
                corners += [four[0:8] + four[16:24], four[8:16] + four[24:32]]
            here = pl.ds(pl.multiple_of(block * BLOCK, BLOCK), BLOCK)
            frac = frac_ref[:, here]
            for d in (2, 1, 0):
                share = frac[d : d + 1, :]
                corners = [
                    corners[k] + share * (corners[k + 1] - corners[k])
                    for k in range(0, len(corners), 2)
                ]
            fresh = flip_share * vel_ref[:, here] + corners[0][0:3]
            square = jnp.sum(fresh * fresh, axis=0, keepdims=True)
            slot = block * BLOCK + half * LANES + lane
            taken = (rel >= 0) & (rel < WIDE) & (slot < count)
            for h in range(2):
                part = square[:, h * LANES : (h + 1) * LANES]
                top = jnp.maximum(top, jnp.where(taken[h : h + 1], part, 0.0))
            found.append((block, corners[0]))
        for block, part in found:
            out_ref[pl.ds(block, 1)] += part[None]
        return top

    top = jnp.zeros((1, LANES), f32)
    for group in range(3):
        top = visit(group, top)
    top = lax.fori_loop(3, (total + TAKEN - 1) // TAKEN, visit, top)
    top = jnp.sqrt(jnp.max(top, axis=1, keepdims=True))
    top_ref[...] = jnp.broadcast_to(top, top_ref.shape)


def finish_kernel(cells_ref, moved_ref, frac_ref, vel_ref, new_frac_ref, new_vel_ref):
    blocks = frac_ref.shape[1] // BLOCK

    def finish(block, carry):
        at = pl.multiple_of(block * BLOCK, BLOCK)
        here = pl.ds(at, BLOCK)
        cells = cells_ref[pl.ds(block * 2, 2), :]
        alive = jnp.concatenate([cells[0:1], cells[1:2]], axis=1) < LAST
        got = moved_ref[pl.ds(block, 1)][0]
        new_vel_ref[:, here] = jnp.where(alive, flip_share * vel_ref[:, here] + got[0:3], 0.0)
        new_frac_ref[:, here] = jnp.where(alive, frac_ref[:, here] + got[4:7], 0.0)
        return carry

    lax.fori_loop(0, blocks, finish, 0, unroll=4)


def largest(value, axis):
    devices = lax.axis_size(axis)
    reach = 1
    while reach < devices:
        if devices & (devices - 1) == 0:
            pairs = [(i, i ^ (reach | 1)) for i in range(devices)]
        else:
            pairs = [(i, (i + reach) % devices) for i in range(devices)]
        value = jnp.maximum(value, lax.ppermute(value, axis, pairs))
        reach *= 2
    return value


smem = pl.BlockSpec(memory_space=pltpu.SMEM)
vmem = pl.BlockSpec(memory_space=pltpu.VMEM)
hbm = pl.BlockSpec(memory_space=pltpu.HBM)


def body(frac, velocity, mass, particle_cell, tile_count, time_step):
    slots = frac.shape[1]
    blocks = slots // BLOCK
    rows = slots // LANES
    inputs = (frac, velocity, mass.reshape(rows, LANES), particle_cell.reshape(rows, LANES))
    far, near, layers, plan, frac_here, vel_here, cells_here = pl.pallas_call(
        spread_kernel,
        out_shape=(
            pltpu.VMEM((4 * CX, NY, NZ), f32),
            pltpu.VMEM((4 * CX, NY, NZ), f32),
            pltpu.VMEM((4 * (CX + 1), NY, NZ), f32),
            pltpu.VMEM((8, LANES), jnp.int32),
            pltpu.VMEM(frac.shape, f32),
            pltpu.VMEM(velocity.shape, f32),
            pltpu.VMEM((rows, LANES), jnp.int32),
        ),
        in_specs=[hbm] * 4,
        out_specs=(vmem,) * 7,
        scratch_shapes=[
            pltpu.SMEM((8, LANES), jnp.int32),
            pltpu.VMEM((blocks, LANES), jnp.int32),
            pltpu.VMEM((rows, LANES), f32),
            pltpu.VMEM(((CX + 1) * (NY + 1) * 8, NZ), f32),
            pltpu.SemaphoreType.DMA((5,)),
        ],
        compiler_params=pltpu.CompilerParams(vmem_limit_bytes=32 * 1024 * 1024),
        name="spread",
    )(*[pltpu.with_memory_space_constraint(x, pltpu.HBM) for x in inputs])
    devices = lax.axis_size("gx")
    far_pairs = [(i, (i + (1 if i % 2 else -1)) % devices) for i in range(devices)]
    near_pairs = [(i, i ^ 1) for i in range(devices)]
    far_new = lax.ppermute(far, "gx", far_pairs)
    near_new = lax.ppermute(near, "gx", near_pairs)
    moved, top = pl.pallas_call(
        collect_kernel,
        out_shape=(
            jax.ShapeDtypeStruct((blocks, 8, BLOCK), f32),
            jax.ShapeDtypeStruct((8, LANES), f32),
        ),
        in_specs=[smem] * 2 + [vmem] * 7,
        out_specs=(vmem, vmem),
        scratch_shapes=[
            pltpu.SMEM((8, LANES), jnp.int32),
            pltpu.VMEM(((CX + 1) * NY * TABLE, NZ), f32),
            pltpu.VMEM(((CX + 1) * (NY + 1), 2 * TABLE, NZ), bf16),
            pltpu.SemaphoreType.DMA,
        ],
        compiler_params=pltpu.CompilerParams(vmem_limit_bytes=32 * 1024 * 1024),
        name="collect",
    )(time_step, tile_count, plan, layers, far_new, near_new, frac_here, vel_here, cells_here)
    new_frac, new_velocity = pl.pallas_call(
        finish_kernel,
        out_shape=(
            jax.ShapeDtypeStruct(frac.shape, f32),
            jax.ShapeDtypeStruct(velocity.shape, f32),
        ),
        in_specs=[vmem] * 4,
        out_specs=(vmem, vmem),
        compiler_params=pltpu.CompilerParams(vmem_limit_bytes=32 * 1024 * 1024),
        cost_estimate=pl.CostEstimate(flops=0, bytes_accessed=8000000, transcendentals=0),
        name="finish",
    )(cells_here, moved, frac_here, vel_here)
    fastest = largest(top, "gx")
    next_step = (courant / (fastest + wave_speed))[0, :1]
    return (new_frac, new_velocity, next_step)


def solution(mesh):
    placed = (
        P(None, ("runs", "gx")),
        P(None, ("runs", "gx")),
        P(("runs", "gx")),
        P(("runs", "gx")),
        P(("runs", "gx")),
        P("runs"),
    )
    return jax.shard_map(
        body,
        mesh=mesh,
        in_specs=placed,
        out_specs=(P(None, ("runs", "gx")), P(None, ("runs", "gx")), P("runs")),
        check_vma=False,
    )
```

```python
import functools

import jax
import jax.numpy as jnp
from jax import lax
from jax.experimental import pallas as pl
from jax.experimental.pallas import tpu as pltpu
from jax.sharding import PartitionSpec as P

CX = 2
NY = 32
NZ = 128
ROWS = CX * NY
PAIRS = ROWS // 2
LAST = ROWS * NZ - 1
WIDE = 2 * NZ
BLOCK = 256
LANES = 128
GIVEN = 32
TAKEN = 32
SLOTS = 8
DELAY = 4
SPREAD = 32
TABLE = 16

mass_floor = 0.25
stiffness = 2.0
press_floor = 1.0
grain_size = 0.5
inertia_ref = 0.3
mu_static = 0.38
mu_limit = 0.64
rate_floor = 0.5
gravity = (0.5, 0.0, -0.866)
flip_share = 0.95
courant = 0.4
wave_speed = 2.0
components = ((0, 3, 4), (3, 1, 5), (4, 5, 2))
f32 = jnp.float32
bf16 = jnp.bfloat16


def split_pair(values):
    high = values.astype(bf16)
    low = (values - high.astype(f32)).astype(bf16)
    return high, low


def relative(cells_ref, block, offset):
    return cells_ref[pl.ds(block * 2, 2), :] - offset


def one_hot(rel, wide):
    tall = (16, LANES)
    nodes = lax.broadcasted_iota(jnp.int32, tall, 0).astype(f32)
    one, zero = jnp.ones(tall, bf16), jnp.zeros(tall, bf16)
    halves = []
    for h in range(2):
        line = jnp.broadcast_to(rel[h : h + 1, :].astype(f32), tall).astype(bf16)
        parts = [
            jnp.where(line == (nodes + z).astype(bf16), one, zero) for z in range(0, wide, 16)
        ]
        halves.append(jnp.concatenate(parts, axis=0))
    return jnp.concatenate(halves, axis=1)


def list_visits(cells_ref, plan_ref, start_ref):
    blocks = cells_ref.shape[0] // 2
    shape = (blocks, LANES)
    number = lax.broadcasted_iota(jnp.int32, shape, 0)
    lane = lax.broadcasted_iota(jnp.int32, shape, 1)
    first_half = cells_ref[pl.ds(0, blocks, stride=2), :]
    second_half = cells_ref[pl.ds(1, blocks, stride=2), :]
    reached = jnp.maximum(
        jnp.where(first_half < LAST, first_half, 0), jnp.where(second_half < LAST, second_half, 0)
    )
    first = jnp.min(first_half, axis=1, keepdims=True)
    live = first < LAST
    last = jnp.max(reached, axis=1, keepdims=True)
    first_pair, last_pair = first >> 8, last >> 8
    start_ref[...] = jnp.broadcast_to(first_pair * WIDE, shape)
    pair = jnp.max(jnp.where(number == lane, first_pair, 0), axis=0, keepdims=True)
    plan_ref[0:1, :] = 2 * pair + (pair >> 4)
    within = live & (first_pair < lane) & (lane <= last_pair)
    block = jnp.max(jnp.where(within, number, -1), axis=0, keepdims=True)
    plan_ref[1:2, :] = jnp.maximum(block, 0)
    plan_ref[2:3, :] = jnp.where(block >= 0, lane[:1], PAIRS) * WIDE
    low = jnp.where(live, first_pair + number, 2 * LANES)
    high = jnp.where(live, last_pair + number, -1)
    inside = (low <= lane) & (lane <= high)
    block = jnp.max(jnp.where(inside, number, -1), axis=0, keepdims=True)
    valid = block >= 0
    pair = lane[:1] - block
    plan_ref[3:4, :] = jnp.where(valid, block, 0)
    plan_ref[4:5, :] = jnp.where(valid, 2 * pair + (pair >> 4), 0)
    plan_ref[5:6, :] = jnp.where(valid, pair, PAIRS) * WIDE
    plan_ref[6:7, :] = jnp.max(high, axis=0, keepdims=True) + 1
    plan_ref[7:8, :] = jnp.max(jnp.where(live, number + 1, 0), axis=0, keepdims=True)


def spread_kernel(
    frac_hbm, vel_hbm, mass_hbm, cells_hbm,
    far_ref, near_ref, layers_ref, plan_ref, frac_ref, vel_ref, cells_ref,
    listed_ref, start_ref, mass_ref, acc_ref, sems,
):
    slots = frac_ref.shape[1]
    sources = (cells_hbm, frac_hbm, vel_hbm, mass_hbm)
    targets = (cells_ref, frac_ref, vel_ref, mass_ref)
    arrivals = [
        pltpu.make_async_copy(source, target, sems.at[k])
        for k, (source, target) in enumerate(zip(sources, targets))
    ]
    for arrival in arrivals:
        arrival.start()
    acc_ref[...] = jnp.zeros_like(acc_ref)
    arrivals[0].wait()
    list_visits(cells_ref, plan_ref, start_ref)
    listing = pltpu.make_async_copy(plan_ref, listed_ref, sems.at[4])
    listing.start()
    for arrival in arrivals[1:]:
        arrival.wait()
    sublane = lax.broadcasted_iota(jnp.int32, (8, LANES), 0)
    lane = lax.broadcasted_iota(jnp.int32, (1, LANES), 1)
    top_z = sublane >= 4
    field = sublane & 3

    def weigh(part):
        at = pl.multiple_of(part * LANES, LANES)
        here = pl.ds(at, LANES)

        def spread_out(line):
            return jnp.broadcast_to(line, (8, LANES))

        fx, fy, fz = (spread_out(frac_ref[d : d + 1, here]) for d in range(3))
        vx, vy, vz = (spread_out(vel_ref[d : d + 1, here]) for d in range(3))
        live = cells_ref[pl.ds(part, 1), :] < LAST
        held = spread_out(jnp.where(live, mass_ref[pl.ds(part, 1), :], 0.0))
        carried = jnp.where(
            field == 0, held, held * jnp.where(field == 1, vx, jnp.where(field == 2, vy, vz))
        )
        carried = carried * jnp.where(top_z, fz, 1.0 - fz)
        lower, upper = carried * (1.0 - fx), carried * fx
        rows = jnp.concatenate(
            [lower * (1.0 - fy), lower * fy, upper * (1.0 - fy), upper * fy], axis=0
        )
        return jnp.concatenate(split_pair(rows), axis=0)

    def spread_one(block, offset):
        rel = relative(cells_ref, block, offset)
        row = (rel >> 7).astype(f32)
        shares = ([], [])
        for h in range(2):
            values = weigh(2 * block + h)
            which = jnp.broadcast_to(row[h : h + 1, :], values.shape).astype(bf16)
            for r in range(2):
                here = which == jnp.full(values.shape, r, bf16)
                shares[r].append(jnp.where(here, values, jnp.zeros_like(values)))
        both = lax.dot_general(
            jnp.concatenate([jnp.concatenate(share, axis=1) for share in shares], axis=0),
            one_hot(rel & (NZ - 1), NZ),
            (((1,), (1,)), ((), ())),
            preferred_element_type=f32,
        )
        first = both[:SPREAD] + both[SPREAD : 2 * SPREAD]
        second = both[2 * SPREAD : 3 * SPREAD] + both[3 * SPREAD :]
        return (
            jnp.concatenate([first[0:8], first[8:16] + second[0:8], second[8:16]], axis=0),
            jnp.concatenate([first[16:24], first[24:32] + second[16:24], second[24:32]], axis=0),
        )

    def add_to_nodes(base, parts):
        here = pl.ds(pl.multiple_of(base * 8, 8), 24)
        above = pl.ds(pl.multiple_of(base * 8, 8) + (NY + 1) * 8, 24)
        lower, upper = acc_ref[here, :], acc_ref[above, :]
        acc_ref[here, :] = lower + parts[0]
        acc_ref[above, :] = upper + parts[1]

    def first_pairs(group, carry):
        blocks = [group * GIVEN + u for u in range(GIVEN)]
        found = [spread_one(block, start_ref[pl.ds(block, 1), :]) for block in blocks]
        if carry is None:
            listing.wait()
        for block, parts in zip(blocks, found):
            add_to_nodes(listed_ref[0, block], parts)
        return carry

    first_pairs(0, None)
    found = [spread_one(listed_ref[1, pair], listed_ref[2, pair]) for pair in range(PAIRS)]
    for pair, parts in enumerate(found):
        add_to_nodes(2 * pair + (pair >> 4), parts)
    lax.fori_loop(1, (listed_ref[7, 0] + GIVEN - 1) // GIVEN, first_pairs, 0)

    odd = lax.axis_index("gx") % 2 == 1
    layers = []
    for l in range(CX + 1):
        first = l * (NY + 1) * 8
        acc_ref[first : first + 8, :] += acc_ref[first + NY * 8 : first + NY * 8 + 8, :]
        for f in range(4):
            lower = acc_ref[pl.ds(first + f, NY, stride=8), :]
            upper = acc_ref[pl.ds(first + 4 + f, NY, stride=8), :]
            layers.append(lower + pltpu.roll(upper, 1, 1))
            layers_ref[l * 4 + f] = layers[-1]
    for k in range(CX * 4):
        far_ref[k] = jnp.where(odd, layers[k + 4], layers[k])
        near_ref[k] = jnp.where(odd, layers[k], layers[k + 4])


def pair_up(field, axis):
    return field + pltpu.roll(field, field.shape[axis] - 1, axis)


def step_up(field, axis):
    return pltpu.roll(field, field.shape[axis] - 1, axis) - field


def pair_down(field, axis):
    return field + pltpu.roll(field, 1, axis)


def step_down(field, axis):
    return field - pltpu.roll(field, 1, axis)


def cell_stress(vel_lo, vel_hi, mass_lo, mass_hi, keep):
    grads = []
    for a in range(3):
        diff = vel_hi[a] - vel_lo[a]
        both = vel_hi[a] + vel_lo[a]
        grads.append(
            [
                0.25 * pair_up(pair_up(diff, 0), 1),
                0.25 * pair_up(step_up(both, 0), 1),
                0.25 * step_up(pair_up(both, 0), 1),
            ]
        )
    density = 0.125 * pair_up(pair_up(mass_hi + mass_lo, 0), 1)
    dxx = grads[0][0]
    dyy = grads[1][1]
    dzz = grads[2][2]
    dxy = 0.5 * (grads[0][1] + grads[1][0])
    dxz = 0.5 * (grads[0][2] + grads[2][0])
    dyz = 0.5 * (grads[1][2] + grads[2][1])
    second = dxx * dxx + dyy * dyy + dzz * dzz + 2.0 * (dxy * dxy + dxz * dxz + dyz * dyz)
    rate = jnp.sqrt(2.0 * second + rate_floor * rate_floor)
    pressure = stiffness * density
    inertial = rate * grain_size / jnp.sqrt(pressure + press_floor)
    friction = mu_static + (mu_limit - mu_static) * inertial / (inertia_ref + inertial)
    twice = 2.0 * friction * pressure / rate
    sigma = [
        twice * dxx - pressure,
        twice * dyy - pressure,
        twice * dzz - pressure,
        twice * dxy,
        twice * dxz,
        twice * dyz,
    ]
    return [jnp.where(keep, s, 0.0) for s in sigma]


def node_force(lower, upper):
    force = []
    for a in range(3):
        sx, sy, sz = (components[a][b] for b in range(3))
        along = pair_down(pair_down(upper[sx] - lower[sx], 0), 1)
        across = step_down(pair_down(upper[sy] + lower[sy], 1), 0)
        upward = step_down(pair_down(upper[sz] + lower[sz], 0), 1)
        force.append(0.25 * (along + across + upward))
    return force


def collect_kernel(
    step_ref, count_ref, plan_ref, layers_ref, far_new_ref, near_new_ref, frac_ref, vel_ref, cells_ref,
    out_ref, top_ref, listed_ref, tab_ref, pair_ref, sem,
):
    blocks = frac_ref.shape[1] // BLOCK
    listing = pltpu.make_async_copy(plan_ref, listed_ref, sem)
    listing.start()
    step = step_ref[0]
    odd = lax.axis_index("gx") % 2 == 1

    def pick(if_odd, if_even):
        return [jnp.where(odd, if_odd[k], if_even[k]) for k in range(4 * CX)]

    own = [layers_ref[k] for k in range(4 * (CX + 1))]
    left, right = pick(near_new_ref, far_new_ref), pick(far_new_ref, near_new_ref)
    nodes = [
        left[:4],
        [own[f] + left[4 + f] for f in range(4)],
        own[4:8],
        [own[8 + f] + right[f] for f in range(4)],
        right[4:],
    ]
    height = lax.broadcasted_iota(jnp.int32, (NY, NZ), 1)
    keep = height < NZ - 1
    above_bed = height > 0
    floor = [jnp.maximum(layer[0], mass_floor) for layer in nodes]
    v_old = [[layer[1 + a] / floor[l] for a in range(3)] for l, layer in enumerate(nodes)]
    sigma = [
        cell_stress(v_old[l], v_old[l + 1], nodes[l][0], nodes[l + 1][0], keep) for l in range(4)
    ]
    blank = jnp.zeros((NY, NZ), f32)
    for l in range(CX + 1):
        force = node_force(sigma[l], sigma[l + 1])
        fields = [blank] * 8
        for a in range(3):
            layer = nodes[l + 1]
            fresh = (layer[1 + a] + step * (force[a] + layer[0] * gravity[a])) / floor[l + 1]
            fresh = jnp.where(above_bed, fresh, 0.0)
            fields[a] = fresh - flip_share * v_old[l + 1][a]
            fields[4 + a] = step * fresh
        for k, value in enumerate(fields):
            start = l * NY * TABLE + k
            tab_ref[pl.ds(start, NY, stride=TABLE), :] = value
            tab_ref[pl.ds(start + 8, NY, stride=TABLE), :] = pltpu.roll(value, NZ - 1, 1)

    for l in range(CX + 1):

        def split_row(j, carry):
            at = pl.ds(pl.multiple_of((l * NY + j) * TABLE, TABLE), TABLE)
            high, low = split_pair(tab_ref[at, :])
            pair_ref[pl.ds(l * (NY + 1) + j, 1)] = jnp.concatenate([high, low], axis=0)[None]
            return carry

        lax.fori_loop(0, NY, split_row, 0, unroll=8)
        pair_ref[l * (NY + 1) + NY] = pair_ref[l * (NY + 1)]

    out_ref[...] = jnp.zeros_like(out_ref)
    listing.wait()
    total = listed_ref[6, 0]
    count = count_ref[0]
    lane = lax.broadcasted_iota(jnp.int32, (2, LANES), 1)
    half = lax.broadcasted_iota(jnp.int32, (2, LANES), 0)

    def visit(group, top):
        best = [top]

        def run(*sums):
            found = []
            begun = []

            def take(u):
                block, rel = begun[u]
                both = pltpu.matmul_pop(sums[u % SLOTS])
                corners = []
                for k in range(4):
                    four = both[2 * TABLE * k : 2 * TABLE * (k + 1)]
                    corners += [four[0:8] + four[16:24], four[8:16] + four[24:32]]
                here = pl.ds(pl.multiple_of(block * BLOCK, BLOCK), BLOCK)
                frac = frac_ref[:, here]
                for d in (2, 1, 0):
                    share = frac[d : d + 1, :]
                    corners = [
                        corners[k] + share * (corners[k + 1] - corners[k])
                        for k in range(0, len(corners), 2)
                    ]
                fresh = flip_share * vel_ref[:, here] + corners[0][0:3]
                square = jnp.sum(fresh * fresh, axis=0, keepdims=True)
                slot = block * BLOCK + half * LANES + lane
                taken = (rel >= 0) & (rel < WIDE) & (slot < count)
                for h in range(2):
                    part = square[:, h * LANES : (h + 1) * LANES]
                    best[0] = jnp.maximum(best[0], jnp.where(taken[h : h + 1], part, 0.0))
                found.append((block, corners[0]))

            for u in range(TAKEN):
                v = group * TAKEN + u
                block = listed_ref[3, v]
                base = listed_ref[4, v]
                rel = relative(cells_ref, block, listed_ref[5, v])
                begun.append((block, rel))
                rows = []
                for a in range(2):
                    three = [pair_ref[base + a * (NY + 1) + k] for k in range(3)]
                    rows += [jnp.concatenate(three[b : b + 2], axis=1) for b in range(2)]
                unit, turn = u % 2, u // 2 % 2
                pltpu.matmul_push_rhs(one_hot(rel, WIDE), turn, unit)
                pltpu.matmul_acc_lhs(
                    sums[u % SLOTS], jnp.concatenate(rows, axis=0), load_staged_rhs=turn
                )
                if u >= DELAY:
                    take(u - DELAY)
            for u in range(TAKEN - DELAY, TAKEN):
                take(u)
            for block, part in found:
                out_ref[pl.ds(block, 1)] += part[None]
            return best[0]

        return pl.run_scoped(
            run, *[pltpu.ACC(k % 2)((8 * TABLE, WIDE), f32) for k in range(SLOTS)]
        )

    top = jnp.zeros((1, LANES), f32)
    for group in range(2):
        top = visit(group, top)
    top = lax.fori_loop(2, (total + TAKEN - 1) // TAKEN, visit, top)
    top = jnp.sqrt(jnp.max(top, axis=1, keepdims=True))
    top_ref[...] = jnp.broadcast_to(top, top_ref.shape)


def finish_kernel(cells_ref, moved_ref, frac_ref, vel_ref, new_frac_ref, new_vel_ref):
    blocks = frac_ref.shape[1] // BLOCK

    def finish(block, carry):
        at = pl.multiple_of(block * BLOCK, BLOCK)
        here = pl.ds(at, BLOCK)
        cells = cells_ref[pl.ds(block * 2, 2), :]
        alive = jnp.concatenate([cells[0:1], cells[1:2]], axis=1) < LAST
        got = moved_ref[pl.ds(block, 1)][0]
        new_vel_ref[:, here] = jnp.where(alive, flip_share * vel_ref[:, here] + got[0:3], 0.0)
        new_frac_ref[:, here] = jnp.where(alive, frac_ref[:, here] + got[4:7], 0.0)
        return carry

    lax.fori_loop(0, blocks, finish, 0, unroll=4)


def largest(value, axis):
    devices = lax.axis_size(axis)
    reach = 1
    while reach < devices:
        if devices & (devices - 1) == 0:
            pairs = [(i, i ^ (reach | 1)) for i in range(devices)]
        else:
            pairs = [(i, (i + reach) % devices) for i in range(devices)]
        value = jnp.maximum(value, lax.ppermute(value, axis, pairs))
        reach *= 2
    return value


smem = pl.BlockSpec(memory_space=pltpu.SMEM)
vmem = pl.BlockSpec(memory_space=pltpu.VMEM)
hbm = pl.BlockSpec(memory_space=pltpu.HBM)


def body(frac, velocity, mass, particle_cell, tile_count, time_step):
    slots = frac.shape[1]
    blocks = slots // BLOCK
    rows = slots // LANES
    inputs = (frac, velocity, mass.reshape(rows, LANES), particle_cell.reshape(rows, LANES))
    far, near, layers, plan, frac_here, vel_here, cells_here = pl.pallas_call(
        spread_kernel,
        out_shape=(
            pltpu.VMEM((4 * CX, NY, NZ), f32),
            pltpu.VMEM((4 * CX, NY, NZ), f32),
            pltpu.VMEM((4 * (CX + 1), NY, NZ), f32),
            pltpu.VMEM((8, LANES), jnp.int32),
            pltpu.VMEM(frac.shape, f32),
            pltpu.VMEM(velocity.shape, f32),
            pltpu.VMEM((rows, LANES), jnp.int32),
        ),
        in_specs=[hbm] * 4,
        out_specs=(vmem,) * 7,
        scratch_shapes=[
            pltpu.SMEM((8, LANES), jnp.int32),
            pltpu.VMEM((blocks, LANES), jnp.int32),
            pltpu.VMEM((rows, LANES), f32),
            pltpu.VMEM(((CX + 1) * (NY + 1) * 8, NZ), f32),
            pltpu.SemaphoreType.DMA((5,)),
        ],
        compiler_params=pltpu.CompilerParams(vmem_limit_bytes=32 * 1024 * 1024),
        name="spread",
    )(*[pltpu.with_memory_space_constraint(x, pltpu.HBM) for x in inputs])
    devices = lax.axis_size("gx")
    far_pairs = [(i, (i + (1 if i % 2 else -1)) % devices) for i in range(devices)]
    near_pairs = [(i, i ^ 1) for i in range(devices)]
    far_new = lax.ppermute(far, "gx", far_pairs)
    near_new = lax.ppermute(near, "gx", near_pairs)
    moved, top = pl.pallas_call(
        collect_kernel,
        out_shape=(
            jax.ShapeDtypeStruct((blocks, 8, BLOCK), f32),
            jax.ShapeDtypeStruct((8, LANES), f32),
        ),
        in_specs=[smem] * 2 + [vmem] * 7,
        out_specs=(vmem, vmem),
        scratch_shapes=[
            pltpu.SMEM((8, LANES), jnp.int32),
            pltpu.VMEM(((CX + 1) * NY * TABLE, NZ), f32),
            pltpu.VMEM(((CX + 1) * (NY + 1), 2 * TABLE, NZ), bf16),
            pltpu.SemaphoreType.DMA,
        ],
        compiler_params=pltpu.CompilerParams(vmem_limit_bytes=32 * 1024 * 1024),
        name="collect",
    )(time_step, tile_count, plan, layers, far_new, near_new, frac_here, vel_here, cells_here)
    new_frac, new_velocity = pl.pallas_call(
        finish_kernel,
        out_shape=(
            jax.ShapeDtypeStruct(frac.shape, f32),
            jax.ShapeDtypeStruct(velocity.shape, f32),
        ),
        in_specs=[vmem] * 4,
        out_specs=(vmem, vmem),
        compiler_params=pltpu.CompilerParams(vmem_limit_bytes=32 * 1024 * 1024),
        cost_estimate=pl.CostEstimate(flops=0, bytes_accessed=8000000, transcendentals=0),
        name="finish",
    )(cells_here, moved, frac_here, vel_here)
    fastest = largest(top, "gx")
    next_step = (courant / (fastest + wave_speed))[0, :1]
    return (new_frac, new_velocity, next_step)


def solution(mesh):
    placed = (
        P(None, ("runs", "gx")),
        P(None, ("runs", "gx")),
        P(("runs", "gx")),
        P(("runs", "gx")),
        P(("runs", "gx")),
        P("runs"),
    )
    return jax.shard_map(
        body,
        mesh=mesh,
        in_specs=placed,
        out_specs=(P(None, ("runs", "gx")), P(None, ("runs", "gx")), P("runs")),
        check_vma=False,
    )
```

```python
import functools

import jax
import jax.numpy as jnp
from jax import lax
from jax.experimental import pallas as pl
from jax.experimental.pallas import tpu as pltpu
from jax.sharding import PartitionSpec as P

CX = 2
NY = 32
NZ = 128
ROWS = CX * NY
PAIRS = ROWS // 2
LAST = ROWS * NZ - 1
WIDE = 2 * NZ
BLOCK = 256
LANES = 128
GIVEN = 32
TAKEN = 32
SPREAD = 32
TABLE = 16

mass_floor = 0.25
stiffness = 2.0
press_floor = 1.0
grain_size = 0.5
inertia_ref = 0.3
mu_static = 0.38
mu_limit = 0.64
rate_floor = 0.5
gravity = (0.5, 0.0, -0.866)
flip_share = 0.95
courant = 0.4
wave_speed = 2.0
components = ((0, 3, 4), (3, 1, 5), (4, 5, 2))
f32 = jnp.float32
bf16 = jnp.bfloat16


def split_pair(values):
    high = values.astype(bf16)
    low = (values - high.astype(f32)).astype(bf16)
    return high, low


def relative(cells_ref, block, offset):
    return cells_ref[pl.ds(block * 2, 2), :] - offset


def one_hot(rel, wide):
    tall = (16, LANES)
    nodes = lax.broadcasted_iota(jnp.int32, tall, 0).astype(f32)
    one, zero = jnp.ones(tall, bf16), jnp.zeros(tall, bf16)
    halves = []
    for h in range(2):
        line = jnp.broadcast_to(rel[h : h + 1, :].astype(f32), tall).astype(bf16)
        parts = [
            jnp.where(line == (nodes + z).astype(bf16), one, zero) for z in range(0, wide, 16)
        ]
        halves.append(jnp.concatenate(parts, axis=0))
    return jnp.concatenate(halves, axis=1)


def list_visits(cells_ref, plan_ref, start_ref):
    blocks = cells_ref.shape[0] // 2
    shape = (blocks, LANES)
    number = lax.broadcasted_iota(jnp.int32, shape, 0)
    lane = lax.broadcasted_iota(jnp.int32, shape, 1)
    first_half = cells_ref[pl.ds(0, blocks, stride=2), :]
    second_half = cells_ref[pl.ds(1, blocks, stride=2), :]
    reached = jnp.maximum(
        jnp.where(first_half < LAST, first_half, 0), jnp.where(second_half < LAST, second_half, 0)
    )
    first = jnp.min(first_half, axis=1, keepdims=True)
    live = first < LAST
    last = jnp.max(reached, axis=1, keepdims=True)
    first_pair, last_pair = first >> 8, last >> 8
    start_ref[...] = jnp.broadcast_to(first_pair * WIDE, shape)
    pair = jnp.max(jnp.where(number == lane, first_pair, 0), axis=0, keepdims=True)
    plan_ref[0:1, :] = 2 * pair + (pair >> 4)
    within = live & (first_pair < lane) & (lane <= last_pair)
    block = jnp.max(jnp.where(within, number, -1), axis=0, keepdims=True)
    plan_ref[1:2, :] = jnp.maximum(block, 0)
    plan_ref[2:3, :] = jnp.where(block >= 0, lane[:1], PAIRS) * WIDE
    low = jnp.where(live, first_pair + number, 2 * LANES)
    high = jnp.where(live, last_pair + number, -1)
    inside = (low <= lane) & (lane <= high)
    block = jnp.max(jnp.where(inside, number, -1), axis=0, keepdims=True)
    valid = block >= 0
    pair = lane[:1] - block
    plan_ref[3:4, :] = jnp.where(valid, block, 0)
    plan_ref[4:5, :] = jnp.where(valid, 2 * pair + (pair >> 4), 0)
    plan_ref[5:6, :] = jnp.where(valid, pair, PAIRS) * WIDE
    plan_ref[6:7, :] = jnp.max(high, axis=0, keepdims=True) + 1
    plan_ref[7:8, :] = jnp.max(jnp.where(live, number + 1, 0), axis=0, keepdims=True)


def spread_kernel(
    frac_hbm, vel_hbm, mass_hbm, cells_hbm,
    far_ref, near_ref, layers_ref, plan_ref, frac_ref, vel_ref, cells_ref,
    listed_ref, start_ref, mass_ref, acc_ref, sems,
):
    slots = frac_ref.shape[1]
    sources = (cells_hbm, frac_hbm, vel_hbm, mass_hbm)
    targets = (cells_ref, frac_ref, vel_ref, mass_ref)
    arrivals = [
        pltpu.make_async_copy(source, target, sems.at[k])
        for k, (source, target) in enumerate(zip(sources, targets))
    ]
    for arrival in arrivals:
        arrival.start()
    acc_ref[...] = jnp.zeros_like(acc_ref)
    arrivals[0].wait()
    list_visits(cells_ref, plan_ref, start_ref)
    listing = pltpu.make_async_copy(plan_ref, listed_ref, sems.at[4])
    listing.start()
    for arrival in arrivals[1:]:
        arrival.wait()
    sublane = lax.broadcasted_iota(jnp.int32, (8, LANES), 0)
    lane = lax.broadcasted_iota(jnp.int32, (1, LANES), 1)
    top_z = sublane >= 4
    field = sublane & 3

    def weigh(part):
        at = pl.multiple_of(part * LANES, LANES)
        here = pl.ds(at, LANES)

        def spread_out(line):
            return jnp.broadcast_to(line, (8, LANES))

        fx, fy, fz = (spread_out(frac_ref[d : d + 1, here]) for d in range(3))
        vx, vy, vz = (spread_out(vel_ref[d : d + 1, here]) for d in range(3))
        live = cells_ref[pl.ds(part, 1), :] < LAST
        held = spread_out(jnp.where(live, mass_ref[pl.ds(part, 1), :], 0.0))
        carried = jnp.where(
            field == 0, held, held * jnp.where(field == 1, vx, jnp.where(field == 2, vy, vz))
        )
        carried = carried * jnp.where(top_z, fz, 1.0 - fz)
        lower, upper = carried * (1.0 - fx), carried * fx
        rows = jnp.concatenate(
            [lower * (1.0 - fy), lower * fy, upper * (1.0 - fy), upper * fy], axis=0
        )
        return jnp.concatenate(split_pair(rows), axis=0)

    def spread_one(block, offset):
        rel = relative(cells_ref, block, offset)
        row = (rel >> 7).astype(f32)
        shares = ([], [])
        for h in range(2):
            values = weigh(2 * block + h)
            which = jnp.broadcast_to(row[h : h + 1, :], values.shape).astype(bf16)
            for r in range(2):
                here = which == jnp.full(values.shape, r, bf16)
                shares[r].append(jnp.where(here, values, jnp.zeros_like(values)))
        both = lax.dot_general(
            jnp.concatenate([jnp.concatenate(share, axis=1) for share in shares], axis=0),
            one_hot(rel & (NZ - 1), NZ),
            (((1,), (1,)), ((), ())),
            preferred_element_type=f32,
        )
        first = both[:SPREAD] + both[SPREAD : 2 * SPREAD]
        second = both[2 * SPREAD : 3 * SPREAD] + both[3 * SPREAD :]
        return (
            jnp.concatenate([first[0:8], first[8:16] + second[0:8], second[8:16]], axis=0),
            jnp.concatenate([first[16:24], first[24:32] + second[16:24], second[24:32]], axis=0),
        )

    def add_to_nodes(base, parts):
        here = pl.ds(pl.multiple_of(base * 8, 8), 24)
        above = pl.ds(pl.multiple_of(base * 8, 8) + (NY + 1) * 8, 24)
        lower, upper = acc_ref[here, :], acc_ref[above, :]
        acc_ref[here, :] = lower + parts[0]
        acc_ref[above, :] = upper + parts[1]

    def first_pairs(group, carry):
        blocks = [group * GIVEN + u for u in range(GIVEN)]
        found = [spread_one(block, start_ref[pl.ds(block, 1), :]) for block in blocks]
        if carry is None:
            listing.wait()
        for block, parts in zip(blocks, found):
            add_to_nodes(listed_ref[0, block], parts)
        return carry

    first_pairs(0, None)
    found = [spread_one(listed_ref[1, pair], listed_ref[2, pair]) for pair in range(PAIRS)]
    for pair, parts in enumerate(found):
        add_to_nodes(2 * pair + (pair >> 4), parts)
    lax.fori_loop(1, (listed_ref[7, 0] + GIVEN - 1) // GIVEN, first_pairs, 0)

    odd = lax.axis_index("gx") % 2 == 1
    layers = []
    for l in range(CX + 1):
        first = l * (NY + 1) * 8
        acc_ref[first : first + 8, :] += acc_ref[first + NY * 8 : first + NY * 8 + 8, :]
        for f in range(4):
            lower = acc_ref[pl.ds(first + f, NY, stride=8), :]
            upper = acc_ref[pl.ds(first + 4 + f, NY, stride=8), :]
            layers.append(lower + pltpu.roll(upper, 1, 1))
            layers_ref[l * 4 + f] = layers[-1]
    for k in range(CX * 4):
        far_ref[k] = jnp.where(odd, layers[k + 4], layers[k])
        near_ref[k] = jnp.where(odd, layers[k], layers[k + 4])


def pair_up(field, axis):
    return field + pltpu.roll(field, field.shape[axis] - 1, axis)


def step_up(field, axis):
    return pltpu.roll(field, field.shape[axis] - 1, axis) - field


def pair_down(field, axis):
    return field + pltpu.roll(field, 1, axis)


def step_down(field, axis):
    return field - pltpu.roll(field, 1, axis)


def cell_stress(vel_lo, vel_hi, mass_lo, mass_hi, keep):
    grads = []
    for a in range(3):
        diff = vel_hi[a] - vel_lo[a]
        both = vel_hi[a] + vel_lo[a]
        grads.append(
            [
                0.25 * pair_up(pair_up(diff, 0), 1),
                0.25 * pair_up(step_up(both, 0), 1),
                0.25 * step_up(pair_up(both, 0), 1),
            ]
        )
    density = 0.125 * pair_up(pair_up(mass_hi + mass_lo, 0), 1)
    dxx = grads[0][0]
    dyy = grads[1][1]
    dzz = grads[2][2]
    dxy = 0.5 * (grads[0][1] + grads[1][0])
    dxz = 0.5 * (grads[0][2] + grads[2][0])
    dyz = 0.5 * (grads[1][2] + grads[2][1])
    second = dxx * dxx + dyy * dyy + dzz * dzz + 2.0 * (dxy * dxy + dxz * dxz + dyz * dyz)
    rate = jnp.sqrt(2.0 * second + rate_floor * rate_floor)
    pressure = stiffness * density
    inertial = rate * grain_size / jnp.sqrt(pressure + press_floor)
    friction = mu_static + (mu_limit - mu_static) * inertial / (inertia_ref + inertial)
    twice = 2.0 * friction * pressure / rate
    sigma = [
        twice * dxx - pressure,
        twice * dyy - pressure,
        twice * dzz - pressure,
        twice * dxy,
        twice * dxz,
        twice * dyz,
    ]
    return [jnp.where(keep, s, 0.0) for s in sigma]


def node_force(lower, upper):
    force = []
    for a in range(3):
        sx, sy, sz = (components[a][b] for b in range(3))
        along = pair_down(pair_down(upper[sx] - lower[sx], 0), 1)
        across = step_down(pair_down(upper[sy] + lower[sy], 1), 0)
        upward = step_down(pair_down(upper[sz] + lower[sz], 0), 1)
        force.append(0.25 * (along + across + upward))
    return force


def collect_kernel(
    step_ref, count_ref, plan_ref, layers_ref, far_new_ref, near_new_ref, frac_ref, vel_ref, cells_ref,
    out_ref, top_ref, listed_ref, tab_ref, pair_ref, sem,
):
    blocks = frac_ref.shape[1] // BLOCK
    listing = pltpu.make_async_copy(plan_ref, listed_ref, sem)
    listing.start()
    step = step_ref[0]
    odd = lax.axis_index("gx") % 2 == 1

    def pick(if_odd, if_even):
        return [jnp.where(odd, if_odd[k], if_even[k]) for k in range(4 * CX)]

    own = [layers_ref[k] for k in range(4 * (CX + 1))]
    left, right = pick(near_new_ref, far_new_ref), pick(far_new_ref, near_new_ref)
    nodes = [
        left[:4],
        [own[f] + left[4 + f] for f in range(4)],
        own[4:8],
        [own[8 + f] + right[f] for f in range(4)],
        right[4:],
    ]
    height = lax.broadcasted_iota(jnp.int32, (NY, NZ), 1)
    keep = height < NZ - 1
    above_bed = height > 0
    floor = [jnp.maximum(layer[0], mass_floor) for layer in nodes]
    v_old = [[layer[1 + a] / floor[l] for a in range(3)] for l, layer in enumerate(nodes)]
    sigma = [
        cell_stress(v_old[l], v_old[l + 1], nodes[l][0], nodes[l + 1][0], keep) for l in range(4)
    ]
    blank = jnp.zeros((NY, NZ), f32)
    for l in range(CX + 1):
        force = node_force(sigma[l], sigma[l + 1])
        fields = [blank] * 8
        for a in range(3):
            layer = nodes[l + 1]
            fresh = (layer[1 + a] + step * (force[a] + layer[0] * gravity[a])) / floor[l + 1]
            fresh = jnp.where(above_bed, fresh, 0.0)
            fields[a] = fresh - flip_share * v_old[l + 1][a]
            fields[4 + a] = step * fresh
        for k, value in enumerate(fields):
            start = l * NY * TABLE + k
            tab_ref[pl.ds(start, NY, stride=TABLE), :] = value
            tab_ref[pl.ds(start + 8, NY, stride=TABLE), :] = pltpu.roll(value, NZ - 1, 1)

    for l in range(CX + 1):

        def split_row(j, carry):
            at = pl.ds(pl.multiple_of((l * NY + j) * TABLE, TABLE), TABLE)
            high, low = split_pair(tab_ref[at, :])
            pair_ref[pl.ds(l * (NY + 1) + j, 1)] = jnp.concatenate([high, low], axis=0)[None]
            return carry

        lax.fori_loop(0, NY, split_row, 0, unroll=8)
        pair_ref[l * (NY + 1) + NY] = pair_ref[l * (NY + 1)]

    out_ref[...] = jnp.zeros_like(out_ref)
    listing.wait()
    total = listed_ref[6, 0]
    count = count_ref[0]
    lane = lax.broadcasted_iota(jnp.int32, (2, LANES), 1)
    half = lax.broadcasted_iota(jnp.int32, (2, LANES), 0)

    def visit(group, top):
        found = []
        for u in range(TAKEN):
            v = group * TAKEN + u
            block = listed_ref[3, v]
            base = listed_ref[4, v]
            rel = relative(cells_ref, block, listed_ref[5, v])
            hot = one_hot(rel, WIDE)
            rows = []
            for a in range(2):
                three = [pair_ref[base + a * (NY + 1) + k] for k in range(3)]
                rows += [jnp.concatenate(three[b : b + 2], axis=1) for b in range(2)]
            both = jnp.dot(jnp.concatenate(rows, axis=0), hot, preferred_element_type=f32)
            corners = []
            for k in range(4):
                four = both[2 * TABLE * k : 2 * TABLE * (k + 1)]
                corners += [four[0:8] + four[16:24], four[8:16] + four[24:32]]
            here = pl.ds(pl.multiple_of(block * BLOCK, BLOCK), BLOCK)
            frac = frac_ref[:, here]
            for d in (2, 1, 0):
                share = frac[d : d + 1, :]
                corners = [
                    corners[k] + share * (corners[k + 1] - corners[k])
                    for k in range(0, len(corners), 2)
                ]
            fresh = flip_share * vel_ref[:, here] + corners[0][0:3]
            square = jnp.sum(fresh * fresh, axis=0, keepdims=True)
            slot = block * BLOCK + half * LANES + lane
            taken = (rel >= 0) & (rel < WIDE) & (slot < count)
            for h in range(2):
                part = square[:, h * LANES : (h + 1) * LANES]
                top = jnp.maximum(top, jnp.where(taken[h : h + 1], part, 0.0))
            found.append((block, corners[0]))
        for block, part in found:
            out_ref[pl.ds(block, 1)] += part[None]
        return top

    top = jnp.zeros((1, LANES), f32)
    for group in range(2):
        top = visit(group, top)
    top = lax.fori_loop(2, (total + TAKEN - 1) // TAKEN, visit, top)
    top = jnp.sqrt(jnp.max(top, axis=1, keepdims=True))
    top_ref[...] = jnp.broadcast_to(top[None], top_ref.shape)


def finish_kernel(cells_ref, moved_ref, frac_ref, vel_ref, new_frac_ref, new_vel_ref):
    blocks = frac_ref.shape[1] // BLOCK

    def finish(block, carry):
        at = pl.multiple_of(block * BLOCK, BLOCK)
        here = pl.ds(at, BLOCK)
        cells = cells_ref[pl.ds(block * 2, 2), :]
        alive = jnp.concatenate([cells[0:1], cells[1:2]], axis=1) < LAST
        got = moved_ref[pl.ds(block, 1)][0]
        new_vel_ref[:, here] = jnp.where(alive, flip_share * vel_ref[:, here] + got[0:3], 0.0)
        new_frac_ref[:, here] = jnp.where(alive, frac_ref[:, here] + got[4:7], 0.0)
        return carry

    lax.fori_loop(0, blocks, finish, 0, unroll=4)


smem = pl.BlockSpec(memory_space=pltpu.SMEM)
vmem = pl.BlockSpec(memory_space=pltpu.VMEM)
hbm = pl.BlockSpec(memory_space=pltpu.HBM)


def body(frac, velocity, mass, particle_cell, tile_count, time_step):
    slots = frac.shape[1]
    blocks = slots // BLOCK
    rows = slots // LANES
    inputs = (frac, velocity, mass.reshape(rows, LANES), particle_cell.reshape(rows, LANES))
    far, near, layers, plan, frac_here, vel_here, cells_here = pl.pallas_call(
        spread_kernel,
        out_shape=(
            pltpu.VMEM((4 * CX, NY, NZ), f32),
            pltpu.VMEM((4 * CX, NY, NZ), f32),
            pltpu.VMEM((4 * (CX + 1), NY, NZ), f32),
            pltpu.VMEM((8, LANES), jnp.int32),
            pltpu.VMEM(frac.shape, f32),
            pltpu.VMEM(velocity.shape, f32),
            pltpu.VMEM((rows, LANES), jnp.int32),
        ),
        in_specs=[hbm] * 4,
        out_specs=(vmem,) * 7,
        scratch_shapes=[
            pltpu.SMEM((8, LANES), jnp.int32),
            pltpu.VMEM((blocks, LANES), jnp.int32),
            pltpu.VMEM((rows, LANES), f32),
            pltpu.VMEM(((CX + 1) * (NY + 1) * 8, NZ), f32),
            pltpu.SemaphoreType.DMA((5,)),
        ],
        compiler_params=pltpu.CompilerParams(vmem_limit_bytes=32 * 1024 * 1024),
        name="spread",
    )(*[pltpu.with_memory_space_constraint(x, pltpu.HBM) for x in inputs])
    devices = lax.axis_size("gx")
    far_pairs = [(i, (i + (1 if i % 2 else -1)) % devices) for i in range(devices)]
    near_pairs = [(i, i ^ 1) for i in range(devices)]
    far_new = lax.ppermute(far, "gx", far_pairs)
    near_new = lax.ppermute(near, "gx", near_pairs)
    moved, top = pl.pallas_call(
        collect_kernel,
        out_shape=(
            jax.ShapeDtypeStruct((blocks, 8, BLOCK), f32),
            jax.ShapeDtypeStruct((devices, 1, LANES), f32),
        ),
        in_specs=[smem] * 2 + [vmem] * 7,
        out_specs=(vmem, vmem),
        scratch_shapes=[
            pltpu.SMEM((8, LANES), jnp.int32),
            pltpu.VMEM(((CX + 1) * NY * TABLE, NZ), f32),
            pltpu.VMEM(((CX + 1) * (NY + 1), 2 * TABLE, NZ), bf16),
            pltpu.SemaphoreType.DMA,
        ],
        compiler_params=pltpu.CompilerParams(vmem_limit_bytes=32 * 1024 * 1024),
        name="collect",
    )(time_step, tile_count, plan, layers, far_new, near_new, frac_here, vel_here, cells_here)
    new_frac, new_velocity = pl.pallas_call(
        finish_kernel,
        out_shape=(
            jax.ShapeDtypeStruct(frac.shape, f32),
            jax.ShapeDtypeStruct(velocity.shape, f32),
        ),
        in_specs=[vmem] * 4,
        out_specs=(vmem, vmem),
        compiler_params=pltpu.CompilerParams(vmem_limit_bytes=32 * 1024 * 1024),
        cost_estimate=pl.CostEstimate(flops=0, bytes_accessed=8000000, transcendentals=0),
        name="finish",
    )(cells_here, moved, frac_here, vel_here)
    tops = lax.all_to_all(top, "gx", 0, 0, tiled=True)
    next_step = (courant / (jnp.max(tops, axis=0) + wave_speed))[0, :1]
    return (new_frac, new_velocity, next_step)


def solution(mesh):
    placed = (
        P(None, ("runs", "gx")),
        P(None, ("runs", "gx")),
        P(("runs", "gx")),
        P(("runs", "gx")),
        P(("runs", "gx")),
        P("runs"),
    )
    return jax.shard_map(
        body,
        mesh=mesh,
        in_specs=placed,
        out_specs=(P(None, ("runs", "gx")), P(None, ("runs", "gx")), P("runs")),
        check_vma=False,
    )
```
